32 devices in a mesh: grp: 8 (over z, x), fsdp: 4 (over y, core).
Axes of the slice: x: 2, y: 2, z: 4, core: 2. Of those that a mesh axis runs over, the one named last changes fastest.
Arguments:
- patches: bfloat16 [48, 4, 16384], P(None, None, ('grp', 'fsdp')), may hold values from -6 to 6
- patch_counts: int32 [8], P('grp'), may hold values from 682 to 2048, as said below
- var_present: int32 [8, 48], P('grp'), may hold values from 0 to 1, as said below
- item_dataset: int32 [8], P('grp'), may hold values from 0 to 5
- var_ids: int32 [6, 48], replicated, may hold values from 0 to 47, each once within a row
- patch_weight: bfloat16 [48, 4, 1024], P('fsdp'), may hold values from -3 to 3
- var_embed: bfloat16 [48, 1024], P('fsdp'), may hold values from -6 to 6
- agg_query: bfloat16 [1024], replicated, may hold values from -6 to 6
- query_weight: bfloat16 [1024, 1024], P('fsdp'), may hold values from -0.1875 to 0.1875
- key_weight: bfloat16 [1024, 1024], P('fsdp'), may hold values from -0.1875 to 0.1875
- value_weight: bfloat16 [1024, 1024], P('fsdp'), may hold values from -0.1875 to 0.1875
- agg_proj: bfloat16 [1024, 1024], P('fsdp'), may hold values from -0.375 to 0.375
- agg_bias: float32 [1024], replicated, may hold values from -2 to 2
- norm1_gain: float32 [1024], replicated, may hold values from 0.1 to 1.9
- norm1_shift: float32 [1024], replicated, may hold values from -2 to 2
- qkv_weight: bfloat16 [1024, 3072], P('fsdp'), may hold values from -0.1875 to 0.1875
- proj_weight: bfloat16 [1024, 1024], P('fsdp'), may hold values from -4 to 4
- proj_bias: float32 [1024], replicated, may hold values from -2 to 2
- norm2_gain: float32 [1024], replicated, may hold values from 0.1 to 1.9
- norm2_shift: float32 [1024], replicated, may hold values from -2 to 2
- up_weight: bfloat16 [1024, 4096], P(None, 'fsdp'), may hold values from -0.1875 to 0.1875
- up_bias: bfloat16 [4096], P('fsdp'), may hold values from -3 to 3
- down_weight: bfloat16 [4096, 1024], P('fsdp'), may hold values from -0.09375 to 0.09375
- down_bias: float32 [1024], replicated, may hold values from -2 to 2
- out_grad: bfloat16 [16384, 1024], P(('grp', 'fsdp')), may hold values from -6 to 6
Outputs:
- output: bfloat16 [16384, 1024], P(('grp', 'fsdp'))
- patches_grad: float32 [48, 4, 16384], P(None, None, ('grp', 'fsdp'))
- patch_weight_grad: float32 [48, 4, 1024], P('fsdp')
- var_embed_grad: float32 [48, 1024], P('fsdp')
- agg_query_grad: float32 [1024], P('fsdp')
- query_weight_grad: float32 [1024, 1024], P('fsdp')
- key_weight_grad: float32 [1024, 1024], P('fsdp')
- value_weight_grad: float32 [1024, 1024], P('fsdp')
- agg_proj_grad: float32 [1024, 1024], P('fsdp')
- agg_bias_grad: float32 [1024], P('fsdp')
- norm1_gain_grad: float32 [1024], P('fsdp')
- norm1_shift_grad: float32 [1024], P('fsdp')
- qkv_weight_grad: float32 [1024, 3072], P('fsdp')
- proj_weight_grad: float32 [1024, 1024], P('fsdp')
- proj_bias_grad: float32 [1024], P('fsdp')
- norm2_gain_grad: float32 [1024], P('fsdp')
- norm2_shift_grad: float32 [1024], P('fsdp')
- up_weight_grad: float32 [1024, 4096], P(None, 'fsdp')
- up_bias_grad: float32 [4096], P('fsdp')
- down_weight_grad: float32 [4096, 1024], P('fsdp')
- down_bias_grad: float32 [1024], P('fsdp')
The draws below stay inside these ranges and needn't reach their ends.
Inputs may be any that keep to these rules, and one draw needn't show every extreme that they name: Rows of a group's item at positions from patch_counts[g] on are padding; group g's count lies within 128 below 682 + 1366 * g // 7, and never under 2048 // 3; the first group has exactly 682 valid rows and the last group a full item. `var_present`: each item has 30 to 48 present variables; in every draw one item has all and one has exactly 30. `var_ids`: each dataset's row is a permutation of the 48 variables.
All inputs are finite; a program needn't handle non-finite values.
Results may differ from the reference program's by a relative error of at most 0.019.
Values may be sent and summed in bfloat16 or wider, within the bound.
A program may use at most 512 MiB of HBM per device.

```python
import jax
import jax.numpy as jnp
from jax import lax

D = 1024
HEADS = 16
FF = 4096
VTOT = 48
PIX = 4
DSETS = 6
HD = 64
LEN = 2048
GROUPS = 8
PATCHES = 16384


def draw_patch_counts(key, part):
    key = jax.random.fold_in(key, 11)
    order = jnp.arange(GROUPS, dtype=jnp.int32)
    lowest = LEN // 3
    rising = lowest + (LEN - lowest) * order // (GROUPS - 1)
    shortfall = jax.random.randint(key, (GROUPS,), 0, LEN // 16 + 1, dtype=jnp.int32)
    counts = jnp.maximum(rising - shortfall, lowest)
    counts = jnp.where(order == 0, lowest, counts)
    counts = jnp.where(order == GROUPS - 1, LEN, counts)
    return counts.astype(jnp.int32)


def draw_var_present(key, part):
    key = jax.random.fold_in(key, 23)
    first_key, second_key, third_key = jax.random.split(key, 3)
    present_count = jax.random.randint(first_key, (GROUPS,), 30, VTOT + 1, dtype=jnp.int32)
    full_at = jax.random.randint(second_key, (), 0, GROUPS, dtype=jnp.int32)
    order = jnp.arange(GROUPS, dtype=jnp.int32)
    present_count = jnp.where(order == full_at, VTOT, present_count)
    present_count = jnp.where(order == (full_at + 1) % GROUPS, 30, present_count)
    row_keys = jax.random.split(third_key, GROUPS)
    ranks = jax.vmap(lambda row_key: jax.random.permutation(row_key, VTOT))(row_keys).astype(jnp.int32)
    return (ranks < present_count[:, None]).astype(jnp.int32)


def set_ends(array, key, smallest, high):
    dims = array.shape
    index_at = [jax.random.randint(jax.random.fold_in(key, axis), (), 0, dims[axis]) for axis in range(len(dims))]
    array = array.at[tuple(index_at)].set(smallest)
    longest = dims.index(max(dims))
    index_at[longest] = (index_at[longest] + 1) % dims[longest]
    return array.at[tuple(index_at)].set(high)


def levels(stream_key, dims, cuts, least, largest):
    def one(dim, parts):
        draws = jax.random.uniform(jax.random.fold_in(jax.random.fold_in(stream_key, 6), dim), (parts,), jnp.float32, least / len(cuts), largest / len(cuts))
        return jnp.repeat(jnp.exp(draws), dims[dim] // parts).reshape((-1,) + (1,) * (len(dims) - dim - 1))

    factor_of = one(*cuts[0])
    for cut in cuts[1:]:
        factor_of = factor_of * one(*cut)
    return factor_of


def noise(stream_key, shape, scale, most, cuts=(), kind=jnp.bfloat16):
    gain = levels(stream_key, shape, cuts, -0.22, 0.18) if cuts else 1.0
    array = jax.random.normal(stream_key, shape, jnp.float32) * scale * gain
    return jnp.minimum(jnp.maximum(array, -most), most).astype(kind)


def setup_inputs(seed: int = 0) -> dict:
    arg_keys = jax.random.split(jax.random.key(seed), 26)
    patches = noise(arg_keys[0], (VTOT, PIX, PATCHES), 1.0, 6.0, ((2, 32),))
    patch_counts = draw_patch_counts(jax.random.fold_in(arg_keys[25], 71), 0)
    var_present = draw_var_present(jax.random.fold_in(arg_keys[25], 71), 0)
    item_dataset = set_ends(jax.random.randint(arg_keys[3], (GROUPS,), 0, DSETS), jax.random.fold_in(arg_keys[3], 1), 0, DSETS - 1).astype(jnp.int32)
    var_ids = jax.vmap(lambda own: jax.random.permutation(own, VTOT))(jax.random.split(arg_keys[4], DSETS)).reshape((DSETS, VTOT)).astype(jnp.int32)
    patch_weight = noise(arg_keys[5], (VTOT, PIX, D), PIX ** -0.5, 3.0, ((0, 4),))
    var_embed = noise(arg_keys[6], (VTOT, D), 1.0, 6.0, ((0, 4),))
    agg_query = noise(arg_keys[7], (D,), 1.0, 6.0)
    query_weight = noise(arg_keys[8], (D, D), D ** -0.5, 0.1875, ((0, 4),))
    key_weight = noise(arg_keys[9], (D, D), D ** -0.5, 0.1875, ((0, 4),))
    value_weight = noise(arg_keys[10], (D, D), D ** -0.5, 0.1875, ((0, 4),))
    agg_proj = noise(arg_keys[11], (D, D), (D // 4) ** -0.5, 0.375, ((0, 4),))
    agg_bias = noise(arg_keys[12], (D,), 0.3, 2.0, (), jnp.float32)
    norm1_gain = jnp.clip(1.0 + 0.18 * jax.random.normal(arg_keys[13], (D,), jnp.float32), 0.1, 1.9)
    norm1_shift = noise(arg_keys[14], (D,), 0.3, 2.0, (), jnp.float32)
    qkv_weight = noise(arg_keys[15], (D, 3 * D), D ** -0.5, 0.1875, ((0, 4),))
    proj_weight = noise(arg_keys[16], (D, D), (max(D // 512, 1)) ** -0.5, 4.0, ((0, 4),))
    proj_bias = noise(arg_keys[17], (D,), 0.3, 2.0, (), jnp.float32)
    norm2_gain = jnp.clip(1.0 + 0.18 * jax.random.normal(arg_keys[18], (D,), jnp.float32), 0.1, 1.9)
    norm2_shift = noise(arg_keys[19], (D,), 0.3, 2.0, (), jnp.float32)
    up_weight = noise(arg_keys[20], (D, FF), D ** -0.5, 0.1875, ((1, 4),))
    up_bias = noise(arg_keys[21], (FF,), 0.5, 3.0, ((0, 4),))
    down_weight = noise(arg_keys[22], (FF, D), FF ** -0.5, 0.09375, ((0, 4),))
    down_bias = noise(arg_keys[23], (D,), 0.3, 2.0, (), jnp.float32)
    out_grad = noise(arg_keys[24], (PATCHES, D), 1.0, 6.0, ((0, 32),))
    return {"patches": patches, "patch_counts": patch_counts, "var_present": var_present, "item_dataset": item_dataset, "var_ids": var_ids, "patch_weight": patch_weight, "var_embed": var_embed, "agg_query": agg_query, "query_weight": query_weight, "key_weight": key_weight, "value_weight": value_weight, "agg_proj": agg_proj, "agg_bias": agg_bias, "norm1_gain": norm1_gain, "norm1_shift": norm1_shift, "qkv_weight": qkv_weight, "proj_weight": proj_weight, "proj_bias": proj_bias, "norm2_gain": norm2_gain, "norm2_shift": norm2_shift, "up_weight": up_weight, "up_bias": up_bias, "down_weight": down_weight, "down_bias": down_bias, "out_grad": out_grad}


@jax.custom_vjp
def low(v):
    return lax.optimization_barrier(v.astype(jnp.bfloat16)).astype(jnp.float32)

@jax.custom_vjp
def low_back(v):
    return v

def low_keep(v):
    return (low(v), None)

def low_pass(kept, grad):
    return (grad,)

def back_keep(v):
    return (v, None)

def back_low(kept, grad):
    return (low(grad),)
low.defvjp(low_keep, low_pass)
low_back.defvjp(back_keep, back_low)
exact_mode = lax.Precision.HIGHEST
masked_out = -1e+30
head_group = 4

def layer_norm(values_in, gain_vec, shift_vec):
    row_mean = lax.optimization_barrier(jnp.mean(values_in, axis=-1, keepdims=True))
    centred = values_in - row_mean
    spread = lax.optimization_barrier(jnp.mean(centred * centred, axis=-1, keepdims=True))
    return centred * lax.rsqrt(spread + 1e-05) * gain_vec + shift_vec

def group_forward(inputs, weights, selector, present, key_valid):
    patch_weight, var_embed, agg_query, query_weight, key_weight, value_weight, agg_proj, agg_bias, norm1_gain, norm1_shift, qkv_weight, proj_weight, proj_bias, norm2_gain, norm2_shift, up_weight, up_bias, down_weight, down_bias = weights
    score_scale = HD ** (-0.5)
    stacked = jnp.concatenate([patch_weight.reshape(VTOT, PIX * D), var_embed], axis=1)
    var_table = jnp.dot(selector, stacked, precision=exact_mode).reshape(VTOT, PIX + 1, D)
    query_vec = low(low_back(jnp.dot(agg_query, query_weight, precision=exact_mode)))
    key_query = jnp.einsum('dhj,hj->dh', key_weight.reshape(D, HEADS, HD), query_vec.reshape(HEADS, HD), precision=exact_mode) * score_scale
    key_query = low(low_back(key_query))
    extended = jnp.concatenate([inputs, jnp.ones((VTOT, 1, LEN), inputs.dtype)], axis=1)
    coeffs = jnp.einsum('vkd,dh->vkh', var_table, key_query, precision=exact_mode)
    var_scores = jnp.einsum('vkp,vkh->vhp', extended, coeffs, precision=exact_mode)
    var_scores = jnp.where(present[:, None, None], var_scores, masked_out)
    var_weights = jax.nn.softmax(var_scores, axis=0)
    mixed_terms = low(var_weights[:, None, :, :] * extended[:, :, None, :])
    pooled = jnp.einsum('vkhp,vkd->hpd', mixed_terms, var_table, precision=exact_mode)
    pooled = low(low_back(pooled))
    agg_heads = jnp.einsum('hpd,dhj->phj', pooled, value_weight.reshape(D, HEADS, HD), precision=exact_mode)
    agg_heads = low(low_back(agg_heads.reshape(LEN, D)))
    embedded = low_back(jnp.dot(agg_heads, agg_proj, precision=exact_mode) + agg_bias)
    normed1 = low(layer_norm(embedded, norm1_gain, norm1_shift))
    qkv_rows = low(low_back(jnp.dot(normed1, qkv_weight, precision=exact_mode)))
    blocks = HEADS // head_group
    queries = qkv_rows[:, :D].reshape(LEN, blocks, head_group, HD).transpose(1, 0, 2, 3)
    keys_all = qkv_rows[:, D:2 * D].reshape(LEN, blocks, head_group, HD).transpose(1, 0, 2, 3)
    values_all = qkv_rows[:, 2 * D:].reshape(LEN, blocks, head_group, HD).transpose(1, 0, 2, 3)

    def attend(query_block, key_block, value_block):
        raw_scores = low_back(jnp.einsum('qhe,khe->hqk', query_block, key_block, precision=exact_mode))
        logits = jnp.where(key_valid[None, None, :], raw_scores * score_scale, masked_out)
        attn_probs = jax.nn.softmax(logits, axis=-1)
        return jnp.einsum('hqk,khe->qhe', low(attn_probs), value_block, precision=exact_mode)
    checked = jax.checkpoint(attend)
    context = lax.map(lambda block_parts: checked(block_parts[0], block_parts[1], block_parts[2]), (queries, keys_all, values_all))
    context = low(low_back(context.transpose(1, 0, 2, 3).reshape(LEN, D)))
    attended = low_back(jnp.dot(context, proj_weight, precision=exact_mode) + proj_bias)
    middle = embedded + attended
    normed2 = low(layer_norm(middle, norm2_gain, norm2_shift))
    pre_act = low_back(jnp.dot(normed2, up_weight, precision=exact_mode) + up_bias)
    gelu_out = low(jax.nn.gelu(pre_act, approximate=False))
    down_out = low_back(jnp.dot(gelu_out, down_weight, precision=exact_mode) + down_bias)
    return middle + down_out

def reference(patches, patch_counts, var_present, item_dataset, var_ids, patch_weight, var_embed, agg_query, query_weight, key_weight, value_weight, agg_proj, agg_bias, norm1_gain, norm1_shift, qkv_weight, proj_weight, proj_bias, norm2_gain, norm2_shift, up_weight, up_bias, down_weight, down_bias, out_grad):
    weights = tuple((array_in.astype(jnp.float32) for array_in in (patch_weight, var_embed, agg_query, query_weight, key_weight, value_weight, agg_proj, agg_bias, norm1_gain, norm1_shift, qkv_weight, proj_weight, proj_bias, norm2_gain, norm2_shift, up_weight, up_bias, down_weight, down_bias)))
    count_total = jnp.sum(patch_counts.astype(jnp.float32))
    inputs_all = patches.astype(jnp.float32).reshape(VTOT, PIX, GROUPS, LEN).transpose(2, 0, 1, 3)
    upstream_all = out_grad.astype(jnp.float32).reshape(GROUPS, LEN, D)
    positions = jnp.arange(LEN, dtype=jnp.int32)
    var_range = jnp.arange(VTOT, dtype=jnp.int32)

    def visit_group(summed, pieces):
        inputs, upstream, item_count, present_row, dataset = pieces
        slot_vars = lax.dynamic_index_in_dim(var_ids, dataset, 0, keepdims=False)
        selector = (slot_vars[:, None] == var_range[None, :]).astype(jnp.float32)
        key_valid = positions < item_count

        def forward(inputs_in, weights_in):
            return group_forward(inputs_in, weights_in, selector, present_row > 0, key_valid)
        result, pull_back = jax.vjp(forward, inputs, weights)
        masked_up = upstream * key_valid[:, None].astype(upstream.dtype)
        inputs_grad, weight_grads = pull_back(masked_up)
        count_share = item_count.astype(jnp.float32) / count_total
        summed = jax.tree.map(lambda before, added: before + count_share * added, summed, weight_grads)
        return (summed, (result.astype(jnp.bfloat16), inputs_grad * (GROUPS * count_share)))
    start = jax.tree.map(jnp.zeros_like, weights)
    summed, (results, input_grads) = lax.scan(visit_group, start, (inputs_all, upstream_all, patch_counts, var_present, item_dataset))
    output = results.reshape(GROUPS * LEN, D)
    patches_grad = input_grads.transpose(1, 2, 0, 3).reshape(VTOT, PIX, GROUPS * LEN)
    return (output, patches_grad, summed[0], summed[1], summed[2], summed[3], summed[4], summed[5], summed[6], summed[7], summed[8], summed[9], summed[10], summed[11], summed[12], summed[13], summed[14], summed[15], summed[16], summed[17], summed[18])
```

```python
import functools

import jax
import jax.numpy as jnp
from jax import lax
from jax.experimental import pallas as pl
from jax.experimental.pallas import tpu as pltpu
from jax.sharding import PartitionSpec as P

HEADS = 16
VTOT = 48
PIX = 4

exact_mode = lax.Precision.HIGHEST
masked_out = -1e30
VMEM_LIMIT = 56 * 1024 * 1024


def swap(value, axis, bit):
    size = lax.axis_size(axis)
    return lax.ppermute(value, axis, [(i, i ^ bit) for i in range(size)])


def has_bit(axis, bit):
    return (lax.axis_index(axis) // bit) % 2 == 1


def merge(mine, other, axis, bit):
    return jnp.where(
        has_bit(axis, bit),
        jnp.concatenate([other, mine], axis=0),
        jnp.concatenate([mine, other], axis=0),
    )


def product(left_side, right_side):
    return jnp.dot(left_side, right_side, preferred_element_type=jnp.float32)


def left_product(left_side, right_side):
    return lax.dot_general(
        left_side, right_side, (((0,), (0,)), ((), ())), preferred_element_type=jnp.float32
    )


def right_product(left_side, right_side):
    return lax.dot_general(
        left_side, right_side, (((1,), (1,)), ((), ())), preferred_element_type=jnp.float32
    )


def column_sums(values_in):
    return jnp.sum(values_in.astype(jnp.float32), axis=0)


def gather_far_half(own):
    rows = own.shape[0]
    half = rows // 2
    which = lax.axis_index("grp") % 2
    sent = lax.dynamic_slice_in_dim(own, which * half, half, 0)
    got = swap(sent, "fsdp", 2)
    rest = swap(got, "grp", 1)
    return merge(got, rest, "grp", 1)


def gather_far_eighth(own):
    rows = own.shape[0]
    part = rows // 8
    which = lax.axis_index("grp") % 8
    sent = lax.dynamic_slice_in_dim(own, which * part, part, 0)
    got = swap(sent, "fsdp", 2)[None]
    for bit in (2, 4):
        got = merge(got, swap(got, "grp", bit), "grp", bit)
    rest = swap(got, "grp", 1)
    odd = has_bit("grp", 1)
    both = jnp.where(odd, jnp.stack([rest, got], axis=1), jnp.stack([got, rest], axis=1))
    return both.reshape(own.shape)


def four_shards(own, far):
    return [own, swap(own, "fsdp", 1), far, swap(far, "fsdp", 1)]


def in_order(shards, axis=0):
    me = lax.axis_index("fsdp")
    size = shards[0].shape[axis]
    shape = list(shards[0].shape)
    shape[axis] = size * len(shards)
    whole = jnp.zeros(shape, shards[0].dtype)
    for j, shard in enumerate(shards):
        whole = lax.dynamic_update_slice_in_dim(whole, shard, (me ^ j) * size, axis)
    return whole


def reduce_gradient(quarter, share):
    def low(value):
        return value.astype(jnp.bfloat16)

    sent = jnp.stack([low(quarter(1) * share), low(quarter(3) * share)])
    got = swap(sent, "fsdp", 1)
    far = swap(low(quarter(2) * share + got[1].astype(jnp.float32)), "fsdp", 2)
    held = low(quarter(0) * share + got[0].astype(jnp.float32) + far.astype(jnp.float32))
    return reduce_groups(held)


def group_bits():
    bits = []
    bit = 1
    while bit < lax.axis_size("grp"):
        bits.append(bit)
        bit *= 2
    return bits


def halve(held, axis, bit):
    half = held.shape[0] // 2
    upper = has_bit(axis, bit).astype(jnp.int32)
    keep = lax.dynamic_slice_in_dim(held, upper * half, half, 0)
    give = lax.dynamic_slice_in_dim(held, (1 - upper) * half, half, 0)
    got = swap(give, axis, bit)
    return (keep.astype(jnp.float32) + got.astype(jnp.float32)).astype(held.dtype)


def reduce_groups(held):
    bits = group_bits()
    for bit in bits:
        held = halve(held, "grp", bit)
    for bit in reversed(bits):
        held = merge(held, swap(held, "grp", bit), "grp", bit)
    return held.astype(jnp.float32)


def slot_softmax(patch_ref, coeff_ref, mask_ref):
    scores = coeff_ref[0, PIX] + mask_ref[...]
    for k in range(PIX):
        scores = scores + patch_ref[k].astype(jnp.float32) * coeff_ref[0, k]
    top = jnp.max(scores, axis=0, keepdims=True)
    terms = jnp.exp(scores - top)
    return terms / jnp.sum(terms, axis=0, keepdims=True)


def mixed_of(patch_ref, weights):
    parts = [
        (weights * patch_ref[k].astype(jnp.float32)).astype(jnp.bfloat16) for k in range(PIX)
    ]
    parts.append(weights.astype(jnp.bfloat16))
    return jnp.concatenate(parts, axis=0)


def aggregate_kernel(patch_ref, coeff_ref, mask_ref, table_ref, out_ref):
    weights = slot_softmax(patch_ref, coeff_ref, mask_ref)
    mixed = mixed_of(patch_ref, weights)
    out_ref[...] = jnp.dot(
        table_ref[...], mixed, preferred_element_type=jnp.float32
    ).astype(jnp.bfloat16)


def aggregate(patch_rows, coeff_heads, slot_mask, table_values):
    rows = patch_rows.shape[2]
    width = table_values.shape[0]
    head_dim = width // HEADS
    slots = slot_mask.shape[0]
    return pl.pallas_call(
        aggregate_kernel,
        grid=(HEADS,),
        in_specs=[
            pl.BlockSpec((PIX, slots, rows), lambda h: (0, 0, 0)),
            pl.BlockSpec((1, PIX + 1, slots, 1), lambda h: (h, 0, 0, 0)),
            pl.BlockSpec((slots, 1), lambda h: (0, 0)),
            pl.BlockSpec((head_dim, (PIX + 1) * slots), lambda h: (h, 0)),
        ],
        out_specs=pl.BlockSpec((head_dim, rows), lambda h: (h, 0)),
        out_shape=jax.ShapeDtypeStruct((width, rows), jnp.bfloat16),
        compiler_params=pltpu.CompilerParams(vmem_limit_bytes=VMEM_LIMIT),
        cost_estimate=pl.CostEstimate(
            flops=2 * (PIX + 1) * slots * rows * width * 4,
            bytes_accessed=4 * width * rows,
            transcendentals=HEADS * slots * rows,
        ),
        name="aggregate",
    )(patch_rows, coeff_heads, slot_mask, table_values)


def aggregate_back_kernel(
    patch_ref, coeff_ref, mask_ref, table_ref, heads_ref, scale_ref, table_grad_ref, coeff_grad_ref, patch_grad_ref
):
    head = pl.program_id(0)
    slots = mask_ref.shape[0]
    weights = slot_softmax(patch_ref, coeff_ref, mask_ref)
    mixed = mixed_of(patch_ref, weights)
    heads_grad = heads_ref[...]
    table_grad_ref[...] = lax.dot_general(
        heads_grad, mixed, (((1,), (1,)), ((), ())), preferred_element_type=jnp.float32
    )
    mixed_grad = lax.dot_general(
        table_ref[...], heads_grad, (((0,), (0,)), ((), ())), preferred_element_type=jnp.float32
    )
    parts = [mixed_grad[k * slots : (k + 1) * slots] for k in range(PIX + 1)]
    values = [patch_ref[k].astype(jnp.float32) for k in range(PIX)]
    weights_grad = parts[PIX]
    for k in range(PIX):
        weights_grad = weights_grad + parts[k] * values[k]
    mean_grad = jnp.sum(weights * weights_grad, axis=0, keepdims=True)
    scores_grad = weights * (weights_grad - mean_grad)
    for k in range(PIX):
        coeff_grad_ref[0, k] = jnp.sum(scores_grad * values[k], axis=1, keepdims=True)
    coeff_grad_ref[0, PIX] = jnp.sum(scores_grad, axis=1, keepdims=True)

    @pl.when(head == 0)
    def _():
        patch_grad_ref[...] = jnp.zeros_like(patch_grad_ref)

    scale = scale_ref[0]
    for k in range(PIX):
        patch_grad_ref[k] += scale * (parts[k] * weights + scores_grad * coeff_ref[0, k])


def aggregate_back(patch_rows, coeff_heads, slot_mask, table_values, heads_grad, scale):
    rows = patch_rows.shape[2]
    width = table_values.shape[0]
    head_dim = width // HEADS
    slots = slot_mask.shape[0]
    return pl.pallas_call(
        aggregate_back_kernel,
        grid=(HEADS,),
        in_specs=[
            pl.BlockSpec((PIX, slots, rows), lambda h: (0, 0, 0)),
            pl.BlockSpec((1, PIX + 1, slots, 1), lambda h: (h, 0, 0, 0)),
            pl.BlockSpec((slots, 1), lambda h: (0, 0)),
            pl.BlockSpec((head_dim, (PIX + 1) * slots), lambda h: (h, 0)),
            pl.BlockSpec((head_dim, rows), lambda h: (h, 0)),
            pl.BlockSpec(memory_space=pltpu.SMEM),
        ],
        out_specs=[
            pl.BlockSpec((head_dim, (PIX + 1) * slots), lambda h: (h, 0)),
            pl.BlockSpec((1, PIX + 1, slots, 1), lambda h: (h, 0, 0, 0)),
            pl.BlockSpec((PIX, slots, rows), lambda h: (0, 0, 0)),
        ],
        out_shape=[
            jax.ShapeDtypeStruct((width, (PIX + 1) * slots), jnp.float32),
            jax.ShapeDtypeStruct((HEADS, PIX + 1, slots, 1), jnp.float32),
            jax.ShapeDtypeStruct((PIX, slots, rows), jnp.float32),
        ],
        compiler_params=pltpu.CompilerParams(vmem_limit_bytes=VMEM_LIMIT),
        cost_estimate=pl.CostEstimate(
            flops=4 * (PIX + 1) * slots * rows * width * 4,
            bytes_accessed=8 * width * rows,
            transcendentals=HEADS * slots * rows,
        ),
        name="aggregate_back",
    )(patch_rows, coeff_heads, slot_mask, table_values, heads_grad, scale)


def lane_half(rows, pair, head_dim):
    lane = lax.broadcasted_iota(jnp.int32, (rows, 2 * head_dim), 1)
    return (lane // head_dim) == pair


def attend_kernel(shards, head_dim, first, last, *refs):
    valid_ref, q_ref = refs[:2]
    keys = refs[2 : 2 + shards]
    values = refs[2 + shards : 2 + 2 * shards]
    rest = refs[2 + 2 * shards :]
    if not first:
        old_sum_ref, old_top_ref, old_total_ref = rest[:3]
        rest = rest[3:]
    rows = q_ref.shape[0]
    tile = min(rows, 256)
    scale = head_dim ** (-0.5)
    for start in range(0, rows, tile):
        block = q_ref[start : start + tile, :] * jnp.asarray(scale, jnp.bfloat16)
        sums, tops, totals = [], [], []
        for pair in range(2):
            side = lane_half(tile, pair, head_dim)
            query = jnp.where(side, block, jnp.zeros_like(block))
            logits = []
            for j in range(shards):
                raw = lax.dot_general(
                    query, keys[j][...], (((1,), (1,)), ((), ())), preferred_element_type=jnp.float32
                )
                place = lax.broadcasted_iota(jnp.int32, (1, raw.shape[1]), 1)
                logits.append(jnp.where(place < valid_ref[j], raw, masked_out))
            top = functools.reduce(
                jnp.maximum, [jnp.max(part, axis=1, keepdims=True) for part in logits]
            )
            total = 0.0
            weighted = 0.0
            for j in range(shards):
                terms = jnp.exp(logits[j] - top)
                total = total + jnp.sum(terms, axis=1, keepdims=True)
                weighted = weighted + jnp.dot(
                    terms.astype(jnp.bfloat16), values[j][...], preferred_element_type=jnp.float32
                )
            sums.append(weighted)
            tops.append(top)
            totals.append(total)
        side = lane_half(tile, 0, head_dim)
        weighted = jnp.where(side, sums[0], sums[1])
        top = jnp.where(side, tops[0], tops[1])
        total = jnp.where(side, totals[0], totals[1])
        at = slice(start, start + tile)
        if not first:
            old_top = old_top_ref[at, :]
            new_top = jnp.maximum(top, old_top)
            mine = jnp.exp(top - new_top)
            others = jnp.exp(old_top - new_top)
            weighted = weighted * mine + old_sum_ref[at, :] * others
            total = total * mine + old_total_ref[at, :] * others
            top = new_top
        if last:
            rest[0][at, :] = (weighted / total).astype(jnp.bfloat16)
            rest[1][at, :] = top + jnp.log(total)
        else:
            rest[0][at, :] = weighted
            rest[1][at, :] = top
            rest[2][at, :] = total


def attend(queries, key_values, valid, width, old=None, last=False):
    rows = queries.shape[0]
    head_dim = width // HEADS
    lanes = 2 * head_dim
    shards = len(key_values)
    whole = pl.BlockSpec((rows, lanes), lambda i: (0, i))

    def at(array, offset):
        start = offset // lanes
        return pl.BlockSpec((array.shape[0], lanes), lambda i: (0, start + i))

    in_specs = [pl.BlockSpec(memory_space=pltpu.SMEM), whole]
    in_specs += [at(array, k) for array, k, v in key_values]
    in_specs += [at(array, v) for array, k, v in key_values]
    operands = [valid, queries]
    operands += [array for array, k, v in key_values] * 2
    if old is not None:
        in_specs += [whole] * 3
        operands += list(old)
    wide = jax.ShapeDtypeStruct((rows, width), jnp.float32)
    if last:
        out_shape = [jax.ShapeDtypeStruct((rows, width), jnp.bfloat16), wide]
    else:
        out_shape = [wide] * 3
    length = sum(array.shape[0] for array, k, v in key_values)
    return pl.pallas_call(
        functools.partial(attend_kernel, shards, head_dim, old is None, last),
        grid=(HEADS // 2,),
        in_specs=in_specs,
        out_specs=[whole] * len(out_shape),
        out_shape=out_shape,
        compiler_params=pltpu.CompilerParams(vmem_limit_bytes=VMEM_LIMIT),
        cost_estimate=pl.CostEstimate(
            flops=4 * rows * length * width * 4,
            bytes_accessed=4 * length * width,
            transcendentals=HEADS * rows * length,
        ),
        name="attend",
    )(*operands)


def attend_back_kernel(shards, head_dim, first, *refs):
    valid_ref, q_ref, grad_ref, out_ref, log_ref = refs[:5]
    keys = refs[5 : 5 + shards]
    values = refs[5 + shards : 5 + 2 * shards]
    rest = refs[5 + 2 * shards :]
    old_ref = None
    if not first:
        old_ref, rest = rest[0], rest[1:]
    q_grad_ref = rest[0]
    k_grads = rest[1 : 1 + shards]
    v_grads = rest[1 + shards : 1 + 2 * shards]
    rows = q_ref.shape[0]
    lanes = 2 * head_dim
    scale = head_dim ** (-0.5)
    query = q_ref[...]
    grad = grad_ref[...]
    log_rows = jnp.transpose(log_ref[...])
    dots = jnp.transpose(grad.astype(jnp.float32) * out_ref[...].astype(jnp.float32))
    q_grad = jnp.zeros((rows, lanes), jnp.float32)
    k_sums = [0.0] * shards
    v_sums = [0.0] * shards
    for pair in range(2):
        side = lane_half(rows, pair, head_dim)
        here = slice(pair * head_dim, (pair + 1) * head_dim)
        log_row = log_rows[pair * head_dim : pair * head_dim + 1, :]
        dot_row = jnp.sum(dots[here, :], axis=0, keepdims=True)
        one_query = jnp.where(side, query, jnp.zeros_like(query))
        one_grad = jnp.where(side, grad, jnp.zeros_like(grad))
        scaled = one_query * jnp.asarray(scale, jnp.bfloat16)
        for j in range(shards):
            key = keys[j][...]
            one_key = jnp.where(lane_half(key.shape[0], pair, head_dim), key, jnp.zeros_like(key))
            raw = lax.dot_general(
                key, scaled, (((1,), (1,)), ((), ())), preferred_element_type=jnp.float32
            )
            place = lax.broadcasted_iota(jnp.int32, raw.shape, 0)
            probs = jnp.exp(jnp.where(place < valid_ref[j], raw - log_row, masked_out))
            probs_grad = lax.dot_general(
                values[j][...], one_grad, (((1,), (1,)), ((), ())), preferred_element_type=jnp.float32
            )
            raw_grad = (probs * (probs_grad - dot_row)).astype(jnp.bfloat16)
            v_sums[j] = v_sums[j] + jnp.dot(
                probs.astype(jnp.bfloat16), one_grad, preferred_element_type=jnp.float32
            )
            k_sums[j] = k_sums[j] + jnp.dot(raw_grad, scaled, preferred_element_type=jnp.float32)
            q_grad = q_grad + lax.dot_general(
                raw_grad, one_key, (((0,), (0,)), ((), ())), preferred_element_type=jnp.float32
            )
    q_grad = q_grad * scale
    if old_ref is not None:
        q_grad = q_grad + old_ref[...]
    q_grad_ref[...] = q_grad.astype(q_grad_ref.dtype)
    for j in range(shards):
        k_grads[j][...] = k_sums[j].astype(jnp.bfloat16)
        v_grads[j][...] = v_sums[j].astype(jnp.bfloat16)


def attend_back(queries, grad, out, logs, key_values, valid, old=None, last=False):
    rows, width = grad.shape
    head_dim = width // HEADS
    lanes = 2 * head_dim
    shards = len(key_values)
    whole = pl.BlockSpec((rows, lanes), lambda i: (0, i))

    def at(array, offset):
        start = offset // lanes
        return pl.BlockSpec((array.shape[0], lanes), lambda i: (0, start + i))

    in_specs = [pl.BlockSpec(memory_space=pltpu.SMEM), whole, whole, whole, whole]
    in_specs += [at(array, k) for array, k, v in key_values]
    in_specs += [at(array, v) for array, k, v in key_values]
    operands = [valid, queries, grad, out, logs]
    operands += [array for array, k, v in key_values] * 2
    if old is not None:
        in_specs.append(whole)
        operands.append(old)
    out_shape = [jax.ShapeDtypeStruct((rows, width), jnp.bfloat16 if last else jnp.float32)]
    out_shape += [
        jax.ShapeDtypeStruct((array.shape[0], width), jnp.bfloat16) for array, k, v in key_values
    ] * 2
    length = sum(array.shape[0] for array, k, v in key_values)
    result = pl.pallas_call(
        functools.partial(attend_back_kernel, shards, head_dim, old is None),
        grid=(HEADS // 2,),
        in_specs=in_specs,
        out_specs=[whole]
        + [
            pl.BlockSpec((array.shape[0], lanes), lambda i: (0, i)) for array, k, v in key_values
        ]
        * 2,
        out_shape=out_shape,
        compiler_params=pltpu.CompilerParams(vmem_limit_bytes=VMEM_LIMIT),
        cost_estimate=pl.CostEstimate(
            flops=10 * rows * length * width * 4,
            bytes_accessed=8 * length * width,
            transcendentals=HEADS * rows * length,
        ),
        name="attend_back",
    )(*operands)
    return result[0], result[1 : 1 + shards], result[1 + shards :]


def normalise(values_in):
    row_mean = jnp.mean(values_in, axis=-1, keepdims=True)
    centred = values_in - row_mean
    spread = jnp.mean(centred * centred, axis=-1, keepdims=True)
    inverse = lax.rsqrt(spread + 1e-05)
    return centred * inverse, inverse


def norm_back(grad, xhat, inverse, gain_vec):
    scaled = grad * gain_vec
    first = jnp.mean(scaled, axis=-1, keepdims=True)
    second = jnp.mean(scaled * xhat, axis=-1, keepdims=True)
    return (scaled - first - xhat * second) * inverse


def on_device(
    patches,
    patch_counts,
    var_present,
    item_dataset,
    var_ids,
    patch_weight,
    var_embed,
    agg_query,
    query_weight,
    key_weight,
    value_weight,
    agg_proj,
    agg_bias,
    norm1_gain,
    norm1_shift,
    qkv_weight,
    proj_weight,
    proj_bias,
    norm2_gain,
    norm2_shift,
    up_weight,
    up_bias,
    down_weight,
    down_bias,
    out_grad,
):
    low = jnp.bfloat16
    wide = jnp.float32
    rows = patches.shape[2]
    me = lax.axis_index("fsdp")
    group_count = lax.axis_size("grp")
    width = proj_weight.shape[1]
    head_dim = width // HEADS
    own_width = width // 4
    own_vars = patch_weight.shape[0]
    score_scale = head_dim ** (-0.5)

    counts = patch_counts.astype(wide)
    count_total = counts
    for bit in group_bits():
        count_total = count_total + swap(count_total, "grp", bit)
    count_share = counts[0] / count_total[0]
    item_count = patch_counts[0]
    own_valid = me * rows + jnp.arange(rows, dtype=jnp.int32) < item_count
    shard_valid = jnp.clip(
        item_count - (me ^ jnp.arange(4, dtype=jnp.int32)) * rows, 0, rows
    ).astype(jnp.int32)

    present = var_present[0] > 0
    slot_vars = lax.dynamic_index_in_dim(var_ids, item_dataset[0], 0, keepdims=False)
    selector = slot_vars[:, None] == jnp.arange(VTOT, dtype=jnp.int32)[None, :]
    own_rows = jnp.concatenate(
        [
            patch_weight.reshape(own_vars * PIX, width),
            var_embed,
            up_bias[None, :],
        ],
        axis=0,
    )
    near_rows = swap(own_rows, "fsdp", 1)
    far_rows = swap(jnp.stack([own_rows, near_rows]), "fsdp", 2)
    row_sets = [own_rows, near_rows, far_rows[0], far_rows[1]]
    table_parts = []
    for part in row_sets:
        pixels = part[: own_vars * PIX].reshape(own_vars, PIX, width)
        embeds = part[own_vars * PIX : own_vars * (PIX + 1)][:, None, :]
        table_parts.append(jnp.concatenate([pixels, embeds], axis=1).transpose(1, 0, 2))
    stacked = in_order(table_parts, axis=1)
    stacked_rows = stacked.reshape((PIX + 1) * VTOT, width)
    up_biases = [part[own_vars * (PIX + 1)].astype(wide) for part in row_sets]

    own_query = lax.dynamic_slice_in_dim(agg_query, me * own_width, own_width, 0)
    query_sum = product(own_query[None, :], query_weight)
    query_sum = query_sum + swap(query_sum, "fsdp", 1)
    query_sum = query_sum + swap(query_sum, "fsdp", 2)
    query_vec = query_sum[0].astype(low)
    own_key_query = (
        jnp.einsum(
            "dhj,hj->hd",
            key_weight.reshape(own_width, HEADS, head_dim),
            query_vec.reshape(HEADS, head_dim),
            preferred_element_type=wide,
        )
        * score_scale
    ).astype(low)
    near_key_query = swap(own_key_query, "fsdp", 1)
    far_key_query = swap(jnp.stack([own_key_query, near_key_query]), "fsdp", 2)
    key_query = in_order(
        [own_key_query, near_key_query, far_key_query[0], far_key_query[1]], axis=1
    )
    coeffs_by_var = right_product(key_query, stacked_rows).reshape(HEADS, PIX + 1, VTOT)
    coeff_heads = jnp.einsum(
        "hku,su->hks", coeffs_by_var, selector.astype(wide), precision=exact_mode
    )[..., None]

    value_shards = four_shards(value_weight, gather_far_half(value_weight))
    full_value = in_order(value_shards)
    table_by_var = left_product(full_value, stacked_rows.T).astype(low)
    table_values = (
        jnp.einsum(
            "hku,su->hks",
            table_by_var.reshape(width, PIX + 1, VTOT),
            selector.astype(low),
            preferred_element_type=wide,
        )
        .astype(low)
        .reshape(width, (PIX + 1) * VTOT)
    )
    own_table = lax.dynamic_slice_in_dim(stacked_rows, me * own_width, own_width, 1)
    key_table = product(own_table, key_weight)
    key_table = key_table + swap(key_table.astype(low), "fsdp", 1).astype(wide)
    key_table = key_table + swap(key_table.astype(low), "fsdp", 2).astype(wide)

    agg_proj_shards = four_shards(agg_proj, gather_far_half(agg_proj))
    full_agg_proj = in_order(agg_proj_shards)
    qkv_shards = four_shards(qkv_weight, gather_far_half(qkv_weight))
    full_qkv = in_order(qkv_shards)
    proj_shards = four_shards(proj_weight, gather_far_half(proj_weight))
    full_proj = in_order(proj_shards)
    up_shards = four_shards(up_weight, gather_far_eighth(up_weight))
    down_shards = four_shards(down_weight, gather_far_eighth(down_weight))

    patch_rows = patches.transpose(1, 0, 2)
    slot_mask = jnp.where(present, 0.0, masked_out).astype(wide)[:, None]
    heads_t = aggregate(patch_rows, coeff_heads, slot_mask, table_values)
    embedded = left_product(heads_t, full_agg_proj) + agg_bias
    xhat1, inverse1 = normalise(embedded)
    normed1 = (xhat1 * norm1_gain + norm1_shift).astype(low)
    qkv_rows = product(normed1, full_qkv).astype(low)
    kv_own = qkv_rows[:, width:]
    kv_near = swap(kv_own, "fsdp", 1)
    kv_far = swap(kv_own, "fsdp", 2)
    kv_last = swap(kv_far, "fsdp", 1)
    near_set = [(qkv_rows, width, 2 * width), (kv_near, 0, width)]
    far_set = [(kv_far, 0, width), (kv_last, 0, width)]
    partial_out = attend(qkv_rows, near_set, shard_valid[:2], width)
    context, logs = attend(qkv_rows, far_set, shard_valid[2:], width, old=partial_out, last=True)
    middle = embedded + (product(context, full_proj) + proj_bias)
    xhat2, inverse2 = normalise(middle)
    normed2 = (xhat2 * norm2_gain + norm2_shift).astype(low)
    gelu_parts = []
    slope_parts = []
    down_sum = 0.0
    for j in range(4):
        pre_act = product(normed2, up_shards[j]) + up_biases[j]
        cdf = 0.5 * (1.0 + lax.erf(pre_act * 0.7071067811865476))
        density = jnp.exp(-0.5 * pre_act * pre_act) * 0.3989422804014327
        gelu_parts.append((pre_act * cdf).astype(low))
        slope_parts.append(cdf + pre_act * density)
        down_sum = down_sum + product(gelu_parts[j], down_shards[j])
    output = (middle + down_sum + down_bias).astype(low)

    upstream = out_grad.astype(wide) * own_valid[:, None].astype(wide)
    down_grad = upstream.astype(low)
    down_bias_grad = column_sums(down_grad)
    down_weight_grad = reduce_gradient(
        lambda j: left_product(gelu_parts[j], down_grad), count_share
    )
    pre_grads = []
    up_bias_parts = []
    normed2_grad = 0.0
    for j in range(4):
        act_grad = right_product(down_grad, down_shards[j])
        pre_grads.append((act_grad * slope_parts[j]).astype(low))
        up_bias_parts.append(column_sums(pre_grads[j])[None, :])
        normed2_grad = normed2_grad + right_product(pre_grads[j], up_shards[j])
    up_bias_grad = in_order(up_bias_parts)
    up_weight_grad = reduce_gradient(lambda j: left_product(normed2, pre_grads[j]), count_share)
    norm2_gain_grad = jnp.sum(normed2_grad * xhat2, axis=0)
    norm2_shift_grad = jnp.sum(normed2_grad, axis=0)
    middle_grad = upstream + norm_back(normed2_grad, xhat2, inverse2, norm2_gain)
    attended_grad = middle_grad.astype(low)
    proj_bias_grad = column_sums(attended_grad)

    def columns(array, j):
        return lax.dynamic_slice_in_dim(array, (me ^ j) * own_width, own_width, 1)

    proj_weight_grad = reduce_gradient(
        lambda j: left_product(columns(context, j), attended_grad), count_share
    )
    context_grad = right_product(attended_grad, full_proj).astype(low)

    q_part, far_k, far_v = attend_back(
        qkv_rows, context_grad, context, logs, far_set, shard_valid[2:]
    )
    far_kv = [jnp.concatenate([far_k[i], far_v[i]], axis=1) for i in range(2)]
    far_got = swap(far_kv[1], "fsdp", 1)
    far_sum = (far_kv[0].astype(wide) + far_got.astype(wide)).astype(low)
    from_far = swap(far_sum, "fsdp", 2)
    q_grad, near_k, near_v = attend_back(
        qkv_rows, context_grad, context, logs, near_set, shard_valid[:2], old=q_part, last=True
    )
    near_kv = [jnp.concatenate([near_k[i], near_v[i]], axis=1) for i in range(2)]
    near_got = swap(near_kv[1], "fsdp", 1)
    kv_grad = (near_kv[0].astype(wide) + near_got.astype(wide) + from_far.astype(wide)).astype(low)
    qkv_grad = jnp.concatenate([q_grad, kv_grad], axis=1)
    normed1_grad = right_product(qkv_grad, full_qkv)
    norm1_gain_grad = jnp.sum(normed1_grad * xhat1, axis=0)
    norm1_shift_grad = jnp.sum(normed1_grad, axis=0)
    embedded_grad = (middle_grad + norm_back(normed1_grad, xhat1, inverse1, norm1_gain)).astype(low)
    agg_bias_grad = column_sums(embedded_grad)
    qkv_weight_grad = reduce_gradient(
        lambda j: left_product(columns(normed1, j), qkv_grad), count_share
    )

    def head_rows(j):
        return lax.dynamic_slice_in_dim(heads_t, (me ^ j) * own_width, own_width, 0)

    agg_proj_grad = reduce_gradient(lambda j: product(head_rows(j), embedded_grad), count_share)
    heads_grad = right_product(full_agg_proj, embedded_grad).astype(low)
    input_scale = (group_count * count_share)[None]
    table_grad, coeff_grad, patch_grad = aggregate_back(
        patch_rows, coeff_heads, slot_mask, table_values, heads_grad, input_scale
    )
    patches_grad = patch_grad.transpose(1, 0, 2)

    table_sum = jnp.einsum(
        "hks,su->kuh",
        table_grad.reshape(width, PIX + 1, VTOT),
        selector.astype(wide),
        precision=exact_mode,
    ).reshape((PIX + 1) * VTOT, width)
    coeff_sum = jnp.einsum(
        "hks,su->hku", coeff_grad[..., 0], selector.astype(wide), precision=exact_mode
    ).reshape(-1)
    coeff_rows = -(-coeff_sum.shape[0] // width)
    coeff_flat = jnp.pad(coeff_sum, (0, coeff_rows * width - coeff_sum.shape[0]))
    vectors = [
        agg_bias_grad,
        norm1_gain_grad,
        norm1_shift_grad,
        proj_bias_grad,
        norm2_gain_grad,
        norm2_shift_grad,
        down_bias_grad,
    ]
    pieces = [table_sum, coeff_flat.reshape(coeff_rows, width), jnp.stack(vectors), up_bias_grad]
    bundle = jnp.concatenate(pieces, axis=0) * count_share
    used = bundle.shape[0]
    step = 4 * group_count
    bundle = jnp.pad(bundle, ((0, -used % step), (0, 0)))
    for bit in (1, 2):
        bundle = halve(bundle, "fsdp", bit)
    bits = group_bits()
    for bit in bits:
        bundle = halve(bundle, "grp", bit)
    for bit in reversed(bits):
        bundle = merge(bundle, swap(bundle, "grp", bit), "grp", bit)
    for bit in (2, 1):
        bundle = merge(bundle, swap(bundle, "fsdp", bit), "fsdp", bit)
    table_total = bundle[: table_sum.shape[0]]
    at = table_sum.shape[0]
    coeff_total = bundle[at : at + coeff_rows].reshape(-1)[: coeff_sum.shape[0]]
    coeff_total = coeff_total.reshape(HEADS, (PIX + 1) * VTOT)
    at += coeff_rows
    vector_total = bundle[at : at + len(vectors)]
    at += len(vectors)
    up_bias_total = lax.dynamic_slice_in_dim(bundle, at + me, 1, 0)[0]
    vector_own = lax.dynamic_slice_in_dim(vector_total, me * own_width, own_width, 1)

    value_weight_grad = left_product(own_table, table_total.astype(low))
    key_query_grad = jnp.dot(coeff_total, own_table.astype(wide), precision=exact_mode)
    key_weight_grad = (
        key_query_grad.T[:, :, None]
        * query_vec.astype(wide).reshape(1, HEADS, head_dim)
        * score_scale
    ).reshape(own_width, width)
    query_grad = (
        jnp.einsum(
            "hx,xhj->hj",
            coeff_total,
            key_table.reshape((PIX + 1) * VTOT, HEADS, head_dim),
            precision=exact_mode,
        ).reshape(width)
        * score_scale
    )
    query_weight_grad = own_query.astype(wide)[:, None] * query_grad[None, :]
    agg_query_grad = jnp.dot(
        query_weight.astype(wide), query_grad, precision=exact_mode
    )
    own_totals = lax.dynamic_slice_in_dim(
        table_total.reshape(PIX + 1, VTOT, width), me * own_vars, own_vars, 1
    ).reshape((PIX + 1) * own_vars, width)
    own_coeffs = lax.dynamic_slice_in_dim(
        coeff_total.reshape(HEADS, PIX + 1, VTOT), me * own_vars, own_vars, 2
    ).reshape(HEADS, (PIX + 1) * own_vars)
    var_grads = right_product(own_totals.astype(low), full_value) + lax.dot_general(
        own_coeffs, key_query.astype(wide), (((0,), (0,)), ((), ())), precision=exact_mode
    )
    var_grads = var_grads.reshape(PIX + 1, own_vars, width)
    patch_weight_grad = var_grads[:PIX].transpose(1, 0, 2)
    var_embed_grad = var_grads[PIX]
    return (
        output,
        patches_grad,
        patch_weight_grad,
        var_embed_grad,
        agg_query_grad,
        query_weight_grad,
        key_weight_grad,
        value_weight_grad,
        agg_proj_grad,
        vector_own[0],
        vector_own[1],
        vector_own[2],
        qkv_weight_grad,
        proj_weight_grad,
        vector_own[3],
        vector_own[4],
        vector_own[5],
        up_weight_grad,
        up_bias_total,
        down_weight_grad,
        vector_own[6],
    )


def solution(mesh):
    shard = P("fsdp")
    shard_rows = P("fsdp", None)
    return jax.shard_map(
        on_device,
        mesh=mesh,
        in_specs=(
            P(None, None, ("grp", "fsdp")),
            P("grp"),
            P("grp", None),
            P("grp"),
            P(),
            P("fsdp", None, None),
            shard_rows,
            P(),
            shard_rows,
            shard_rows,
            shard_rows,
            shard_rows,
            P(),
            P(),
            P(),
            shard_rows,
            shard_rows,
            P(),
            P(),
            P(),
            P(None, "fsdp"),
            shard,
            shard_rows,
            P(),
            P(("grp", "fsdp"), None),
        ),
        out_specs=(
            P(("grp", "fsdp"), None),
            P(None, None, ("grp", "fsdp")),
            P("fsdp", None, None),
            shard_rows,
            shard,
            shard_rows,
            shard_rows,
            shard_rows,
            shard_rows,
            shard,
            shard,
            shard,
            shard_rows,
            shard_rows,
            shard,
            shard,
            shard,
            P(None, "fsdp"),
            shard,
            shard_rows,
            shard,
        ),
        check_vma=False,
    )
```

```python
import functools

import jax
import jax.numpy as jnp
from jax import lax
from jax.experimental import pallas as pl
from jax.experimental.pallas import tpu as pltpu
from jax.sharding import PartitionSpec as P

HEADS = 16
VTOT = 48
PIX = 4

exact_mode = lax.Precision.HIGHEST
masked_out = -1e30
VMEM_LIMIT = 56 * 1024 * 1024


def swap(value, axis, bit):
    size = lax.axis_size(axis)
    return lax.ppermute(value, axis, [(i, i ^ bit) for i in range(size)])


def has_bit(axis, bit):
    return (lax.axis_index(axis) // bit) % 2 == 1


def merge(mine, other, axis, bit):
    return jnp.where(
        has_bit(axis, bit),
        jnp.concatenate([other, mine], axis=0),
        jnp.concatenate([mine, other], axis=0),
    )


def product(left_side, right_side):
    return jnp.dot(left_side, right_side, preferred_element_type=jnp.float32)


def left_product(left_side, right_side):
    return lax.dot_general(
        left_side, right_side, (((0,), (0,)), ((), ())), preferred_element_type=jnp.float32
    )


def right_product(left_side, right_side):
    return lax.dot_general(
        left_side, right_side, (((1,), (1,)), ((), ())), preferred_element_type=jnp.float32
    )


def column_sums(values_in):
    return jnp.sum(values_in.astype(jnp.float32), axis=0)


def gather_far_half(own):
    rows = own.shape[0]
    half = rows // 2
    which = lax.axis_index("grp") % 2
    sent = lax.dynamic_slice_in_dim(own, which * half, half, 0)
    got = swap(sent, "fsdp", 2)
    rest = swap(got, "grp", 1)
    return merge(got, rest, "grp", 1)


def four_shards(own, far):
    return [own, swap(own, "fsdp", 1), far, swap(far, "fsdp", 1)]


def in_order(shards, axis=0):
    me = lax.axis_index("fsdp")
    size = shards[0].shape[axis]
    shape = list(shards[0].shape)
    shape[axis] = size * len(shards)
    whole = jnp.zeros(shape, shards[0].dtype)
    for j, shard in enumerate(shards):
        whole = lax.dynamic_update_slice_in_dim(whole, shard, (me ^ j) * size, axis)
    return whole


def group_bits():
    bits = []
    bit = 1
    while bit < lax.axis_size("grp"):
        bits.append(bit)
        bit *= 2
    return bits


def slot_softmax(patch_ref, coeff_ref, mask_ref):
    scores = coeff_ref[0, PIX] + mask_ref[...]
    for k in range(PIX):
        scores = scores + patch_ref[k].astype(jnp.float32) * coeff_ref[0, k]
    top = jnp.max(scores, axis=0, keepdims=True)
    terms = jnp.exp(scores - top)
    return terms / jnp.sum(terms, axis=0, keepdims=True)


def mixed_of(patch_ref, weights):
    parts = [
        (weights * patch_ref[k].astype(jnp.float32)).astype(jnp.bfloat16) for k in range(PIX)
    ]
    parts.append(weights.astype(jnp.bfloat16))
    return jnp.concatenate(parts, axis=0)


def aggregate_kernel(patch_ref, coeff_ref, mask_ref, table_ref, out_ref):
    weights = slot_softmax(patch_ref, coeff_ref, mask_ref)
    mixed = mixed_of(patch_ref, weights)
    out_ref[...] = jnp.dot(
        table_ref[...], mixed, preferred_element_type=jnp.float32
    ).astype(jnp.bfloat16)


def aggregate(patch_rows, coeff_heads, slot_mask, table_values):
    rows = patch_rows.shape[2]
    width = table_values.shape[0]
    head_dim = width // HEADS
    slots = slot_mask.shape[0]
    return pl.pallas_call(
        aggregate_kernel,
        grid=(HEADS,),
        in_specs=[
            pl.BlockSpec((PIX, slots, rows), lambda h: (0, 0, 0)),
            pl.BlockSpec((1, PIX + 1, slots, 1), lambda h: (h, 0, 0, 0)),
            pl.BlockSpec((slots, 1), lambda h: (0, 0)),
            pl.BlockSpec((head_dim, (PIX + 1) * slots), lambda h: (h, 0)),
        ],
        out_specs=pl.BlockSpec((head_dim, rows), lambda h: (h, 0)),
        out_shape=jax.ShapeDtypeStruct((width, rows), jnp.bfloat16),
        compiler_params=pltpu.CompilerParams(vmem_limit_bytes=VMEM_LIMIT),
        cost_estimate=pl.CostEstimate(
            flops=2 * (PIX + 1) * slots * rows * width * 4,
            bytes_accessed=4 * width * rows,
            transcendentals=HEADS * slots * rows,
        ),
        name="aggregate",
    )(patch_rows, coeff_heads, slot_mask, table_values)


def aggregate_back_kernel(
    patch_ref, coeff_ref, mask_ref, table_ref, heads_ref, scale_ref, table_grad_ref, coeff_grad_ref, patch_grad_ref
):
    head = pl.program_id(0)
    slots = mask_ref.shape[0]
    weights = slot_softmax(patch_ref, coeff_ref, mask_ref)
    mixed = mixed_of(patch_ref, weights)
    heads_grad = heads_ref[...]
    table_grad_ref[...] = lax.dot_general(
        heads_grad, mixed, (((1,), (1,)), ((), ())), preferred_element_type=jnp.float32
    )
    mixed_grad = lax.dot_general(
        table_ref[...], heads_grad, (((0,), (0,)), ((), ())), preferred_element_type=jnp.float32
    )
    parts = [mixed_grad[k * slots : (k + 1) * slots] for k in range(PIX + 1)]
    values = [patch_ref[k].astype(jnp.float32) for k in range(PIX)]
    weights_grad = parts[PIX]
    for k in range(PIX):
        weights_grad = weights_grad + parts[k] * values[k]
    mean_grad = jnp.sum(weights * weights_grad, axis=0, keepdims=True)
    scores_grad = weights * (weights_grad - mean_grad)
    for k in range(PIX):
        coeff_grad_ref[0, k] = jnp.sum(scores_grad * values[k], axis=1, keepdims=True)
    coeff_grad_ref[0, PIX] = jnp.sum(scores_grad, axis=1, keepdims=True)

    @pl.when(head == 0)
    def _():
        patch_grad_ref[...] = jnp.zeros_like(patch_grad_ref)

    scale = scale_ref[0]
    for k in range(PIX):
        patch_grad_ref[k] += scale * (parts[k] * weights + scores_grad * coeff_ref[0, k])


def aggregate_back(patch_rows, coeff_heads, slot_mask, table_values, heads_grad, scale):
    rows = patch_rows.shape[2]
    width = table_values.shape[0]
    head_dim = width // HEADS
    slots = slot_mask.shape[0]
    return pl.pallas_call(
        aggregate_back_kernel,
        grid=(HEADS,),
        in_specs=[
            pl.BlockSpec((PIX, slots, rows), lambda h: (0, 0, 0)),
            pl.BlockSpec((1, PIX + 1, slots, 1), lambda h: (h, 0, 0, 0)),
            pl.BlockSpec((slots, 1), lambda h: (0, 0)),
            pl.BlockSpec((head_dim, (PIX + 1) * slots), lambda h: (h, 0)),
            pl.BlockSpec((head_dim, rows), lambda h: (h, 0)),
            pl.BlockSpec(memory_space=pltpu.SMEM),
        ],
        out_specs=[
            pl.BlockSpec((head_dim, (PIX + 1) * slots), lambda h: (h, 0)),
            pl.BlockSpec((1, PIX + 1, slots, 1), lambda h: (h, 0, 0, 0)),
            pl.BlockSpec((PIX, slots, rows), lambda h: (0, 0, 0)),
        ],
        out_shape=[
            jax.ShapeDtypeStruct((width, (PIX + 1) * slots), jnp.float32),
            jax.ShapeDtypeStruct((HEADS, PIX + 1, slots, 1), jnp.float32),
            jax.ShapeDtypeStruct((PIX, slots, rows), jnp.float32),
        ],
        compiler_params=pltpu.CompilerParams(vmem_limit_bytes=VMEM_LIMIT),
        cost_estimate=pl.CostEstimate(
            flops=4 * (PIX + 1) * slots * rows * width * 4,
            bytes_accessed=8 * width * rows,
            transcendentals=HEADS * slots * rows,
        ),
        name="aggregate_back",
    )(patch_rows, coeff_heads, slot_mask, table_values, heads_grad, scale)


def lane_half(rows, pair, head_dim):
    lane = lax.broadcasted_iota(jnp.int32, (rows, 2 * head_dim), 1)
    return (lane // head_dim) == pair


def attend_kernel(shards, head_dim, first, last, *refs):
    valid_ref, q_ref = refs[:2]
    keys = refs[2 : 2 + shards]
    values = refs[2 + shards : 2 + 2 * shards]
    rest = refs[2 + 2 * shards :]
    if not first:
        old_sum_ref, old_top_ref, old_total_ref = rest[:3]
        rest = rest[3:]
    rows = q_ref.shape[0]
    tile = min(rows, 256)
    scale = head_dim ** (-0.5)
    for start in range(0, rows, tile):
        block = q_ref[start : start + tile, :] * jnp.asarray(scale, jnp.bfloat16)
        sums, tops, totals = [], [], []
        for pair in range(2):
            side = lane_half(tile, pair, head_dim)
            query = jnp.where(side, block, jnp.zeros_like(block))
            logits = []
            for j in range(shards):
                raw = lax.dot_general(
                    query, keys[j][...], (((1,), (1,)), ((), ())), preferred_element_type=jnp.float32
                )
                place = lax.broadcasted_iota(jnp.int32, (1, raw.shape[1]), 1)
                logits.append(jnp.where(place < valid_ref[j], raw, masked_out))
            top = functools.reduce(
                jnp.maximum, [jnp.max(part, axis=1, keepdims=True) for part in logits]
            )
            total = 0.0
            weighted = 0.0
            for j in range(shards):
                terms = jnp.exp(logits[j] - top)
                total = total + jnp.sum(terms, axis=1, keepdims=True)
                weighted = weighted + jnp.dot(
                    terms.astype(jnp.bfloat16), values[j][...], preferred_element_type=jnp.float32
                )
            sums.append(weighted)
            tops.append(top)
            totals.append(total)
        side = lane_half(tile, 0, head_dim)
        weighted = jnp.where(side, sums[0], sums[1])
        top = jnp.where(side, tops[0], tops[1])
        total = jnp.where(side, totals[0], totals[1])
        at = slice(start, start + tile)
        if not first:
            old_top = old_top_ref[at, :]
            new_top = jnp.maximum(top, old_top)
            mine = jnp.exp(top - new_top)
            others = jnp.exp(old_top - new_top)
            weighted = weighted * mine + old_sum_ref[at, :] * others
            total = total * mine + old_total_ref[at, :] * others
            top = new_top
        if last:
            rest[0][at, :] = (weighted / total).astype(jnp.bfloat16)
            rest[1][at, :] = top + jnp.log(total)
        else:
            rest[0][at, :] = weighted
            rest[1][at, :] = top
            rest[2][at, :] = total


def attend(queries, key_values, valid, width, old=None, last=False):
    rows = queries.shape[0]
    head_dim = width // HEADS
    lanes = 2 * head_dim
    shards = len(key_values)
    whole = pl.BlockSpec((rows, lanes), lambda i: (0, i))

    def at(array, offset):
        start = offset // lanes
        return pl.BlockSpec((array.shape[0], lanes), lambda i: (0, start + i))

    in_specs = [pl.BlockSpec(memory_space=pltpu.SMEM), whole]
    in_specs += [at(array, k) for array, k, v in key_values]
    in_specs += [at(array, v) for array, k, v in key_values]
    operands = [valid, queries]
    operands += [array for array, k, v in key_values] * 2
    if old is not None:
        in_specs += [whole] * 3
        operands += list(old)
    wide = jax.ShapeDtypeStruct((rows, width), jnp.float32)
    if last:
        out_shape = [jax.ShapeDtypeStruct((rows, width), jnp.bfloat16), wide]
    else:
        out_shape = [wide] * 3
    length = sum(array.shape[0] for array, k, v in key_values)
    return pl.pallas_call(
        functools.partial(attend_kernel, shards, head_dim, old is None, last),
        grid=(HEADS // 2,),
        in_specs=in_specs,
        out_specs=[whole] * len(out_shape),
        out_shape=out_shape,
        compiler_params=pltpu.CompilerParams(vmem_limit_bytes=VMEM_LIMIT),
        cost_estimate=pl.CostEstimate(
            flops=4 * rows * length * width * 4,
            bytes_accessed=4 * length * width,
            transcendentals=HEADS * rows * length,
        ),
        name="attend",
    )(*operands)


def attend_back_kernel(shards, head_dim, first, *refs):
    valid_ref, q_ref, grad_ref, out_ref, log_ref = refs[:5]
    keys = refs[5 : 5 + shards]
    values = refs[5 + shards : 5 + 2 * shards]
    rest = refs[5 + 2 * shards :]
    old_ref = None
    if not first:
        old_ref, rest = rest[0], rest[1:]
    q_grad_ref = rest[0]
    k_grads = rest[1 : 1 + shards]
    v_grads = rest[1 + shards : 1 + 2 * shards]
    rows = q_ref.shape[0]
    lanes = 2 * head_dim
    scale = head_dim ** (-0.5)
    query = q_ref[...]
    grad = grad_ref[...]
    log_rows = jnp.transpose(log_ref[...])
    dots = jnp.transpose(grad.astype(jnp.float32) * out_ref[...].astype(jnp.float32))
    q_grad = jnp.zeros((rows, lanes), jnp.float32)
    k_sums = [0.0] * shards
    v_sums = [0.0] * shards
    for pair in range(2):
        side = lane_half(rows, pair, head_dim)
        here = slice(pair * head_dim, (pair + 1) * head_dim)
        log_row = log_rows[pair * head_dim : pair * head_dim + 1, :]
        dot_row = jnp.sum(dots[here, :], axis=0, keepdims=True)
        one_query = jnp.where(side, query, jnp.zeros_like(query))
        one_grad = jnp.where(side, grad, jnp.zeros_like(grad))
        scaled = one_query * jnp.asarray(scale, jnp.bfloat16)
        for j in range(shards):
            key = keys[j][...]
            one_key = jnp.where(lane_half(key.shape[0], pair, head_dim), key, jnp.zeros_like(key))
            raw = lax.dot_general(
                key, scaled, (((1,), (1,)), ((), ())), preferred_element_type=jnp.float32
            )
            place = lax.broadcasted_iota(jnp.int32, raw.shape, 0)
            probs = jnp.exp(jnp.where(place < valid_ref[j], raw - log_row, masked_out))
            probs_grad = lax.dot_general(
                values[j][...], one_grad, (((1,), (1,)), ((), ())), preferred_element_type=jnp.float32
            )
            raw_grad = (probs * (probs_grad - dot_row)).astype(jnp.bfloat16)
            v_sums[j] = v_sums[j] + jnp.dot(
                probs.astype(jnp.bfloat16), one_grad, preferred_element_type=jnp.float32
            )
            k_sums[j] = k_sums[j] + jnp.dot(raw_grad, scaled, preferred_element_type=jnp.float32)
            q_grad = q_grad + lax.dot_general(
                raw_grad, one_key, (((0,), (0,)), ((), ())), preferred_element_type=jnp.float32
            )
    q_grad = q_grad * scale
    if old_ref is not None:
        q_grad = q_grad + old_ref[...]
    q_grad_ref[...] = q_grad.astype(q_grad_ref.dtype)
    for j in range(shards):
        k_grads[j][...] = k_sums[j].astype(jnp.bfloat16)
        v_grads[j][...] = v_sums[j].astype(jnp.bfloat16)


def attend_back(queries, grad, out, logs, key_values, valid, old=None, last=False):
    rows, width = grad.shape
    head_dim = width // HEADS
    lanes = 2 * head_dim
    shards = len(key_values)
    whole = pl.BlockSpec((rows, lanes), lambda i: (0, i))

    def at(array, offset):
        start = offset // lanes
        return pl.BlockSpec((array.shape[0], lanes), lambda i: (0, start + i))

    in_specs = [pl.BlockSpec(memory_space=pltpu.SMEM), whole, whole, whole, whole]
    in_specs += [at(array, k) for array, k, v in key_values]
    in_specs += [at(array, v) for array, k, v in key_values]
    operands = [valid, queries, grad, out, logs]
    operands += [array for array, k, v in key_values] * 2
    if old is not None:
        in_specs.append(whole)
        operands.append(old)
    out_shape = [jax.ShapeDtypeStruct((rows, width), jnp.bfloat16 if last else jnp.float32)]
    out_shape += [
        jax.ShapeDtypeStruct((array.shape[0], width), jnp.bfloat16) for array, k, v in key_values
    ] * 2
    length = sum(array.shape[0] for array, k, v in key_values)
    result = pl.pallas_call(
        functools.partial(attend_back_kernel, shards, head_dim, old is None),
        grid=(HEADS // 2,),
        in_specs=in_specs,
        out_specs=[whole]
        + [
            pl.BlockSpec((array.shape[0], lanes), lambda i: (0, i)) for array, k, v in key_values
        ]
        * 2,
        out_shape=out_shape,
        compiler_params=pltpu.CompilerParams(vmem_limit_bytes=VMEM_LIMIT),
        cost_estimate=pl.CostEstimate(
            flops=10 * rows * length * width * 4,
            bytes_accessed=8 * length * width,
            transcendentals=HEADS * rows * length,
        ),
        name="attend_back",
    )(*operands)
    return result[0], result[1 : 1 + shards], result[1 + shards :]


def feed_kernel(
    first_ref, second_ref, grad_ref, up_ref, down_ref, bias_ref, rows_ref, gelu_ref, pre_ref, out_ref, back_ref, bias_grad_ref
):
    tile = first_ref.shape[0]
    entry = jnp.concatenate([first_ref[...], second_ref[...]], axis=0)
    grad = jnp.concatenate([grad_ref[0], grad_ref[1]], axis=0)
    pre_act = jnp.dot(entry, up_ref[...], preferred_element_type=jnp.float32) + bias_ref[...]
    cdf = 0.5 * (1.0 + lax.erf(pre_act * 0.7071067811865476))
    density = jnp.exp(-0.5 * pre_act * pre_act) * 0.3989422804014327
    gelu = (pre_act * cdf).astype(jnp.bfloat16)
    act_grad = lax.dot_general(
        grad, down_ref[...], (((1,), (1,)), ((), ())), preferred_element_type=jnp.float32
    )
    pre_grad = (act_grad * (cdf + pre_act * density)).astype(jnp.bfloat16)
    out = jnp.dot(gelu, down_ref[...], preferred_element_type=jnp.float32).astype(jnp.bfloat16)
    back = lax.dot_general(
        pre_grad, up_ref[...], (((1,), (1,)), ((), ())), preferred_element_type=jnp.float32
    ).astype(jnp.bfloat16)

    @pl.when(pl.program_id(0) == 0)
    def _():
        bias_grad_ref[...] = jnp.zeros_like(bias_grad_ref)

    bias_grad_ref[...] += jnp.sum(pre_grad.astype(jnp.float32), axis=0, keepdims=True)
    for ref, value in (
        (rows_ref, entry),
        (gelu_ref, gelu),
        (pre_ref, pre_grad),
        (out_ref, out),
        (back_ref, back),
    ):
        ref[0] = value[:tile]
        ref[1] = value[tile:]


def feed(first, second, grads, up, down, bias):
    rows, width = first.shape
    hidden = up.shape[1]
    tile = min(rows, 128)
    one = pl.BlockSpec((tile, width), lambda i: (i, 0))
    pair = pl.BlockSpec((2, tile, width), lambda i: (0, i, 0))
    pair_hidden = pl.BlockSpec((2, tile, hidden), lambda i: (0, i, 0))

    def fixed(shape):
        return pl.BlockSpec(shape, lambda i: (0, 0))

    out = jax.ShapeDtypeStruct((2, rows, width), jnp.bfloat16)
    out_hidden = jax.ShapeDtypeStruct((2, rows, hidden), jnp.bfloat16)
    return pl.pallas_call(
        feed_kernel,
        grid=(rows // tile,),
        in_specs=[
            one,
            one,
            pair,
            fixed(up.shape),
            fixed(down.shape),
            fixed((1, hidden)),
        ],
        out_specs=[pair, pair_hidden, pair_hidden, pair, pair, fixed((1, hidden))],
        out_shape=[
            out,
            out_hidden,
            out_hidden,
            out,
            out,
            jax.ShapeDtypeStruct((1, hidden), jnp.float32),
        ],
        compiler_params=pltpu.CompilerParams(vmem_limit_bytes=VMEM_LIMIT),
        cost_estimate=pl.CostEstimate(
            flops=16 * rows * width * hidden * 2,
            bytes_accessed=16 * rows * width,
            transcendentals=4 * rows * hidden,
        ),
        name="feed",
    )(first, second, grads, up, down, bias)


def flip(index, bit):
    bit_set = (index // bit) % 2
    return index + bit - 2 * bit * bit_set, bit_set


def total_kernel(group_size, widths, share_ref, *refs):
    pairs = [(refs[2 * i], refs[2 * i + 1]) for i in range(3)]
    bundle_ref = refs[6]
    outs = refs[7:10]
    bundle_out = refs[10]
    send1, recv1, own1, send2, recv2, hold, halves, done, full, send_sem, recv_sem = refs[11:]
    me = lax.axis_index("fsdp")
    group = lax.axis_index("grp")
    core_partner, core = flip(me, 1)
    far_partner, far = flip(me, 2)
    quarter = own1.shape[2]
    wide = jnp.float32
    low = jnp.bfloat16

    steps = []
    size, bit, offset = quarter, 1, 0
    while bit < group_size:
        partner, bit_set = flip(group, bit)
        halving = size >= 64
        steps.append((partner, bit_set, halving, size, offset))
        if halving:
            size = size // 2
            offset = offset + bit_set * size
        bit *= 2
    halvings = [i for i, step in enumerate(steps) if step[2]]

    barrier = pltpu.get_barrier_semaphore()
    partners = [{"fsdp": core_partner}, {"fsdp": far_partner}]
    partners += [{"grp": step[0]} for step in steps]
    for partner in partners:
        pl.semaphore_signal(
            barrier, inc=1, device_id=partner, device_id_type=pl.DeviceIdType.MESH
        )
    pl.semaphore_wait(barrier, len(partners))

    chunks = [(None, None, None, 0, bundle_ref.shape[1])]
    for (left, right), out in zip(pairs, outs):
        for start in range(0, right.shape[1], widths):
            chunks.append((left, right, out, start, widths))

    def copy(stage, c, src, dst, device):
        return pltpu.make_async_remote_copy(
            src_ref=src,
            dst_ref=dst,
            send_sem=send_sem.at[stage, c],
            recv_sem=recv_sem.at[stage, c],
            device_id=device,
            device_id_type=pl.DeviceIdType.MESH,
        )

    def span(start, size):
        return pl.ds(pl.multiple_of(start, 16), size)

    def columns(c):
        return pl.ds(0, chunks[c][4])

    def core_copy(c):
        cols = columns(c)
        return copy(
            0, c, send1.at[c, :, :, cols], recv1.at[c, :, :, cols], {"fsdp": core_partner}
        )

    def far_copy(c):
        cols = columns(c)
        return copy(1, c, send2.at[c, :, cols], recv2.at[c, :, cols], {"fsdp": far_partner})

    def step_copy(i, c):
        partner, bit_set, halving, size, offset = steps[i]
        cols = columns(c)
        if halving:
            size = size // 2
            offset = offset + (1 - bit_set) * size
        src = hold.at[c, span(offset, size), cols]
        dst = halves[i].at[c, :, cols]
        return copy(2 + i, c, src, dst, {"grp": partner})

    def back_copy(i, c):
        partner, bit_set, halving, size, offset = steps[i]
        size = size // 2
        offset = offset + bit_set * size
        at = done.at[c, span(offset, size), columns(c)]
        return copy(2 + len(steps) + i, c, at, at, {"grp": partner})

    def begin(c):
        left, right, out, start, width = chunks[c]
        cols = columns(c)

        def part(q):
            rows = span(q * quarter, quarter)
            if left is None:
                return bundle_ref[rows, :]
            value = jnp.dot(
                left[rows, :], right[:, start : start + width], preferred_element_type=wide
            )
            return (value * share_ref[0]).astype(low)

        for y in range(2):
            send1[c, y, :, cols] = part(2 * y + 1 - core)
        core_copy(c).start()
        for y in range(2):
            own1[c, y, :, cols] = part(2 * y + core)

    def after_core(c):
        cols = columns(c)
        core_copy(c).wait()
        value = own1[c, 1 - far, :, cols].astype(wide) + recv1[c, 1 - far, :, cols].astype(wide)
        send2[c, :, cols] = value.astype(low)
        far_copy(c).start()

    def after_far(c):
        cols = columns(c)
        far_copy(c).wait()
        value = own1[c, far, :, cols].astype(wide) + recv1[c, far, :, cols].astype(wide)
        hold[c, :, cols] = (value + recv2[c, :, cols].astype(wide)).astype(low)
        step_copy(0, c).start()

    def after_step(i, c):
        cols = columns(c)
        step_copy(i, c).wait()
        partner, bit_set, halving, size, offset = steps[i]
        if halving:
            size = size // 2
            offset = offset + bit_set * size
        at = span(offset, size)
        value = hold[c, at, cols].astype(wide) + halves[i][c, :, cols].astype(wide)
        if i + 1 < len(steps):
            hold[c, at, cols] = value.astype(low)
            step_copy(i + 1, c).start()
        else:
            done[c, at, cols] = value.astype(low)
            back_copy(halvings[-1], c).start()

    def after_back(k, c):
        back_copy(halvings[k], c).wait()
        if k > 0:
            back_copy(halvings[k - 1], c).start()
        else:
            left, right, out, start, width = chunks[c]
            if out is None:
                full[me] = done[c, :, columns(c)]
                bundle_core().start()
            else:
                out[:, start : start + width] = done[c].astype(wide)

    last = 2 + 2 * len(steps)

    def bundle_core():
        return copy(last, 0, full.at[me], full.at[me], {"fsdp": core_partner})

    def bundle_far():
        at = full.at[pl.ds(me - core, 2)]
        return copy(last, 1, at, at, {"fsdp": far_partner})

    def finish_core(c):
        bundle_core().wait()
        bundle_far().start()

    def finish_far(c):
        bundle_far().wait()
        for q in range(4):
            bundle_out[q * quarter : (q + 1) * quarter, :] = full[q].astype(wide)

    stages = [begin, after_core, after_far]
    stages += [functools.partial(after_step, i) for i in range(len(steps))]
    stages += [functools.partial(after_back, k) for k in reversed(range(len(halvings)))]
    order = [1, 0] + list(range(2, len(stages)))
    extra = [finish_core, finish_far]
    for t in range(len(chunks) + len(stages) - 1):
        for s in order:
            if 0 <= t - s < len(chunks):
                stages[s](t - s)
        if 0 <= t - len(stages) < len(extra):
            extra[t - len(stages)](0)


def total(group_size, share, qkv_pair, agg_pair, proj_pair, bundle):
    pairs = [qkv_pair, agg_pair, proj_pair]
    width = qkv_pair[0].shape[0]
    quarter = width // 4
    widths = 512
    count = 1 + sum(right.shape[1] // widths for left, right in pairs)
    steps = 0
    halves = []
    size = quarter
    while 2**steps < group_size:
        if size >= 64:
            size //= 2
        halves.append(pltpu.VMEM((count, size, widths), jnp.bfloat16))
        steps += 1
    low = jnp.bfloat16
    whole = pl.BlockSpec(memory_space=pltpu.VMEM)
    scratch = [
        pltpu.VMEM((count, 2, quarter, widths), low),
        pltpu.VMEM((count, 2, quarter, widths), low),
        pltpu.VMEM((count, 2, quarter, widths), low),
        pltpu.VMEM((count, quarter, widths), low),
        pltpu.VMEM((count, quarter, widths), low),
        pltpu.VMEM((count, quarter, widths), low),
        halves,
        pltpu.VMEM((count, quarter, widths), low),
        pltpu.VMEM((4, quarter, bundle.shape[1]), low),
        pltpu.SemaphoreType.DMA((3 + 2 * steps, count)),
        pltpu.SemaphoreType.DMA((3 + 2 * steps, count)),
    ]
    return pl.pallas_call(
        functools.partial(total_kernel, group_size, widths),
        in_specs=[pl.BlockSpec(memory_space=pltpu.SMEM)] + [whole] * 7,
        out_specs=[whole] * 4,
        out_shape=[
            jax.ShapeDtypeStruct((quarter, right.shape[1]), jnp.float32) for left, right in pairs
        ]
        + [jax.ShapeDtypeStruct(bundle.shape, jnp.float32)],
        scratch_shapes=scratch,
        compiler_params=pltpu.CompilerParams(
            collective_id=0, has_side_effects=True, vmem_limit_bytes=VMEM_LIMIT
        ),
        cost_estimate=pl.CostEstimate(
            flops=sum(2 * left.size * right.shape[1] for left, right in pairs),
            bytes_accessed=200_000_000,
            transcendentals=0,
        ),
        name="total",
    )(share, *[array for pair in pairs for array in pair], bundle)


def normalise(values_in):
    row_mean = jnp.mean(values_in, axis=-1, keepdims=True)
    centred = values_in - row_mean
    spread = jnp.mean(centred * centred, axis=-1, keepdims=True)
    inverse = lax.rsqrt(spread + 1e-05)
    return centred * inverse, inverse


def norm_back(grad, xhat, inverse, gain_vec):
    scaled = grad * gain_vec
    first = jnp.mean(scaled, axis=-1, keepdims=True)
    second = jnp.mean(scaled * xhat, axis=-1, keepdims=True)
    return (scaled - first - xhat * second) * inverse


def on_device(
    patches,
    patch_counts,
    var_present,
    item_dataset,
    var_ids,
    patch_weight,
    var_embed,
    agg_query,
    query_weight,
    key_weight,
    value_weight,
    agg_proj,
    agg_bias,
    norm1_gain,
    norm1_shift,
    qkv_weight,
    proj_weight,
    proj_bias,
    norm2_gain,
    norm2_shift,
    up_weight,
    up_bias,
    down_weight,
    down_bias,
    out_grad,
):
    low = jnp.bfloat16
    wide = jnp.float32
    rows = patches.shape[2]
    me = lax.axis_index("fsdp")
    group_count = lax.axis_size("grp")
    width = proj_weight.shape[1]
    head_dim = width // HEADS
    own_width = width // 4
    own_vars = patch_weight.shape[0]
    score_scale = head_dim ** (-0.5)

    counts = patch_counts.astype(wide)
    count_total = counts
    for bit in group_bits():
        count_total = count_total + swap(count_total, "grp", bit)
    count_share = counts[0] / count_total[0]
    item_count = patch_counts[0]
    own_valid = me * rows + jnp.arange(rows, dtype=jnp.int32) < item_count
    shard_valid = jnp.clip(
        item_count - (me ^ jnp.arange(4, dtype=jnp.int32)) * rows, 0, rows
    ).astype(jnp.int32)

    present = var_present[0] > 0
    slot_vars = lax.dynamic_index_in_dim(var_ids, item_dataset[0], 0, keepdims=False)
    selector = slot_vars[:, None] == jnp.arange(VTOT, dtype=jnp.int32)[None, :]
    own_rows = jnp.concatenate(
        [
            patch_weight.reshape(own_vars * PIX, width),
            var_embed,
        ],
        axis=0,
    )
    near_rows = swap(own_rows, "fsdp", 1)
    far_rows = swap(jnp.stack([own_rows, near_rows]), "fsdp", 2)
    row_sets = [own_rows, near_rows, far_rows[0], far_rows[1]]
    table_parts = []
    for part in row_sets:
        pixels = part[: own_vars * PIX].reshape(own_vars, PIX, width)
        embeds = part[own_vars * PIX : own_vars * (PIX + 1)][:, None, :]
        table_parts.append(jnp.concatenate([pixels, embeds], axis=1).transpose(1, 0, 2))
    stacked = in_order(table_parts, axis=1)
    stacked_rows = stacked.reshape((PIX + 1) * VTOT, width)

    own_query = lax.dynamic_slice_in_dim(agg_query, me * own_width, own_width, 0)
    query_sum = product(own_query[None, :], query_weight)
    query_sum = query_sum + swap(query_sum, "fsdp", 1)
    query_sum = query_sum + swap(query_sum, "fsdp", 2)
    query_vec = query_sum[0].astype(low)
    own_key_query = (
        jnp.einsum(
            "dhj,hj->hd",
            key_weight.reshape(own_width, HEADS, head_dim),
            query_vec.reshape(HEADS, head_dim),
            preferred_element_type=wide,
        )
        * score_scale
    ).astype(low)
    near_key_query = swap(own_key_query, "fsdp", 1)
    far_key_query = swap(jnp.stack([own_key_query, near_key_query]), "fsdp", 2)
    key_query = in_order(
        [own_key_query, near_key_query, far_key_query[0], far_key_query[1]], axis=1
    )
    coeffs_by_var = right_product(key_query, stacked_rows).reshape(HEADS, PIX + 1, VTOT)
    coeff_heads = jnp.einsum(
        "hku,su->hks", coeffs_by_var, selector.astype(wide), precision=exact_mode
    )[..., None]

    value_shards = four_shards(value_weight, gather_far_half(value_weight))
    full_value = in_order(value_shards)
    table_by_var = left_product(full_value, stacked_rows.T).astype(low)
    table_values = (
        jnp.einsum(
            "hku,su->hks",
            table_by_var.reshape(width, PIX + 1, VTOT),
            selector.astype(low),
            preferred_element_type=wide,
        )
        .astype(low)
        .reshape(width, (PIX + 1) * VTOT)
    )
    own_table = lax.dynamic_slice_in_dim(stacked_rows, me * own_width, own_width, 1)
    key_table = product(own_table, key_weight)
    key_table = key_table + swap(key_table.astype(low), "fsdp", 1).astype(wide)
    key_table = key_table + swap(key_table.astype(low), "fsdp", 2).astype(wide)

    agg_proj_shards = four_shards(agg_proj, gather_far_half(agg_proj))
    full_agg_proj = in_order(agg_proj_shards)
    qkv_shards = four_shards(qkv_weight, gather_far_half(qkv_weight))
    full_qkv = in_order(qkv_shards)
    proj_shards = four_shards(proj_weight, gather_far_half(proj_weight))
    full_proj = in_order(proj_shards)
    upstream = out_grad.astype(wide) * own_valid[:, None].astype(wide)
    down_grad = upstream.astype(low)
    near_down_grad = swap(down_grad, "fsdp", 1)
    far_down_grad = swap(down_grad, "fsdp", 2)
    last_down_grad = swap(far_down_grad, "fsdp", 1)
    near_grads = jnp.stack([down_grad, near_down_grad])
    far_grads = jnp.stack([far_down_grad, last_down_grad])

    patch_rows = patches.transpose(1, 0, 2)
    slot_mask = jnp.where(present, 0.0, masked_out).astype(wide)[:, None]
    heads_t = aggregate(patch_rows, coeff_heads, slot_mask, table_values)
    embedded = left_product(heads_t, full_agg_proj) + agg_bias
    xhat1, inverse1 = normalise(embedded)
    normed1 = (xhat1 * norm1_gain + norm1_shift).astype(low)
    qkv_rows = product(normed1, full_qkv).astype(low)
    kv_own = qkv_rows[:, width:]
    kv_near = swap(kv_own, "fsdp", 1)
    kv_far = swap(kv_own, "fsdp", 2)
    kv_last = swap(kv_far, "fsdp", 1)
    near_set = [(qkv_rows, width, 2 * width), (kv_near, 0, width)]
    far_set = [(kv_far, 0, width), (kv_last, 0, width)]
    partial_out = attend(qkv_rows, near_set, shard_valid[:2], width)
    context, logs = attend(qkv_rows, far_set, shard_valid[2:], width, old=partial_out, last=True)
    middle = embedded + (product(context, full_proj) + proj_bias)
    xhat2, inverse2 = normalise(middle)
    normed2 = (xhat2 * norm2_gain + norm2_shift).astype(low)
    near_normed2 = swap(normed2, "fsdp", 1)
    far_normed2 = swap(normed2, "fsdp", 2)
    last_normed2 = swap(far_normed2, "fsdp", 1)
    bias_row = up_bias.astype(wide)[None, :]
    near = feed(normed2, near_normed2, near_grads, up_weight, down_weight, bias_row)
    far = feed(far_normed2, last_normed2, far_grads, up_weight, down_weight, bias_row)
    far_got = swap(far[4][1], "fsdp", 1)
    far_sum = (far[4][0].astype(wide) + far_got.astype(wide)).astype(low)
    far_back = swap(far_sum, "fsdp", 2)
    near_back = swap(near[4][1], "fsdp", 1)

    def both_left(left, right):
        def one(i):
            return left_product(
                left[i].reshape(-1, left[i].shape[2]), right[i].reshape(-1, right[i].shape[2])
            )

        return ((one(0) + one(1)) * count_share).astype(low)

    down_weight_part = both_left([near[1], far[1]], [near_grads, far_grads])
    up_weight_part = both_left([near[0], far[0]], [near[2], far[2]])
    down_weight_grad = lax.psum(down_weight_part, "grp").astype(wide)
    up_weight_grad = lax.psum(up_weight_part, "grp").astype(wide)
    up_bias_grad = near[5] + far[5]
    down_bias_grad = column_sums(down_grad)
    normed2_grad = near[4][0].astype(wide) + near_back.astype(wide) + far_back.astype(wide)
    out_got = swap(jnp.stack([near[3][1], far[3][1]]), "fsdp", 1)
    out_far = swap((far[3][0].astype(wide) + out_got[1].astype(wide)).astype(low), "fsdp", 2)
    down_sum = near[3][0].astype(wide) + out_got[0].astype(wide) + out_far.astype(wide)
    output = (middle + down_sum + down_bias).astype(low)
    norm2_gain_grad = jnp.sum(normed2_grad * xhat2, axis=0)
    norm2_shift_grad = jnp.sum(normed2_grad, axis=0)
    middle_grad = upstream + norm_back(normed2_grad, xhat2, inverse2, norm2_gain)
    attended_grad = middle_grad.astype(low)
    proj_bias_grad = column_sums(attended_grad)

    context_grad = right_product(attended_grad, full_proj).astype(low)

    q_part, far_k, far_v = attend_back(
        qkv_rows, context_grad, context, logs, far_set, shard_valid[2:]
    )
    far_kv = [jnp.concatenate([far_k[i], far_v[i]], axis=1) for i in range(2)]
    far_got = swap(far_kv[1], "fsdp", 1)
    far_sum = (far_kv[0].astype(wide) + far_got.astype(wide)).astype(low)
    from_far = swap(far_sum, "fsdp", 2)
    q_grad, near_k, near_v = attend_back(
        qkv_rows, context_grad, context, logs, near_set, shard_valid[:2], old=q_part, last=True
    )
    near_kv = [jnp.concatenate([near_k[i], near_v[i]], axis=1) for i in range(2)]
    near_got = swap(near_kv[1], "fsdp", 1)
    kv_grad = (near_kv[0].astype(wide) + near_got.astype(wide) + from_far.astype(wide)).astype(low)
    qkv_grad = jnp.concatenate([q_grad, kv_grad], axis=1)
    normed1_grad = right_product(qkv_grad, full_qkv)
    norm1_gain_grad = jnp.sum(normed1_grad * xhat1, axis=0)
    norm1_shift_grad = jnp.sum(normed1_grad, axis=0)
    embedded_grad = (middle_grad + norm_back(normed1_grad, xhat1, inverse1, norm1_gain)).astype(low)
    agg_bias_grad = column_sums(embedded_grad)
    heads_grad = right_product(full_agg_proj, embedded_grad).astype(low)
    input_scale = (group_count * count_share)[None]
    table_grad, coeff_grad, patch_grad = aggregate_back(
        patch_rows, coeff_heads, slot_mask, table_values, heads_grad, input_scale
    )
    patches_grad = patch_grad.transpose(1, 0, 2)

    table_sum = jnp.einsum(
        "hks,su->kuh",
        table_grad.reshape(width, PIX + 1, VTOT),
        selector.astype(wide),
        precision=exact_mode,
    ).reshape((PIX + 1) * VTOT, width)
    coeff_sum = jnp.einsum(
        "hks,su->hku", coeff_grad[..., 0], selector.astype(wide), precision=exact_mode
    ).reshape(-1)
    coeff_rows = -(-coeff_sum.shape[0] // width)
    coeff_flat = jnp.pad(coeff_sum, (0, coeff_rows * width - coeff_sum.shape[0]))
    vectors = [
        agg_bias_grad,
        norm1_gain_grad,
        norm1_shift_grad,
        proj_bias_grad,
        norm2_gain_grad,
        norm2_shift_grad,
        down_bias_grad,
    ]
    up_bias_rows = lax.dynamic_update_slice_in_dim(jnp.zeros((4, width), wide), up_bias_grad, me, 0)
    pieces = [table_sum, coeff_flat.reshape(coeff_rows, width), jnp.stack(vectors), up_bias_rows]
    bundle = jnp.concatenate(pieces, axis=0) * count_share
    bundle = jnp.pad(bundle, ((0, -bundle.shape[0] % 128), (0, 0))).astype(low)
    bundle_shape = bundle.shape
    qkv_weight_grad, agg_proj_grad, proj_weight_grad, bundle = total(
        group_count,
        count_share[None],
        (normed1.T, qkv_grad),
        (heads_t, embedded_grad),
        (context.T, attended_grad),
        bundle.reshape(width, -1),
    )
    bundle = bundle.reshape(bundle_shape)
    table_total = bundle[: table_sum.shape[0]]
    at = table_sum.shape[0]
    coeff_total = bundle[at : at + coeff_rows].reshape(-1)[: coeff_sum.shape[0]]
    coeff_total = coeff_total.reshape(HEADS, (PIX + 1) * VTOT)
    at += coeff_rows
    vector_total = bundle[at : at + len(vectors)]
    at += len(vectors)
    up_bias_total = lax.dynamic_slice_in_dim(bundle, at + me, 1, 0)[0]
    vector_own = lax.dynamic_slice_in_dim(vector_total, me * own_width, own_width, 1)

    value_weight_grad = left_product(own_table, table_total.astype(low))
    key_query_grad = jnp.dot(coeff_total, own_table.astype(wide), precision=exact_mode)
    key_weight_grad = (
        key_query_grad.T[:, :, None]
        * query_vec.astype(wide).reshape(1, HEADS, head_dim)
        * score_scale
    ).reshape(own_width, width)
    query_grad = (
        jnp.einsum(
            "hx,xhj->hj",
            coeff_total,
            key_table.reshape((PIX + 1) * VTOT, HEADS, head_dim),
            precision=exact_mode,
        ).reshape(width)
        * score_scale
    )
    query_weight_grad = own_query.astype(wide)[:, None] * query_grad[None, :]
    agg_query_grad = jnp.dot(
        query_weight.astype(wide), query_grad, precision=exact_mode
    )
    own_totals = lax.dynamic_slice_in_dim(
        table_total.reshape(PIX + 1, VTOT, width), me * own_vars, own_vars, 1
    ).reshape((PIX + 1) * own_vars, width)
    own_coeffs = lax.dynamic_slice_in_dim(
        coeff_total.reshape(HEADS, PIX + 1, VTOT), me * own_vars, own_vars, 2
    ).reshape(HEADS, (PIX + 1) * own_vars)
    var_grads = right_product(own_totals.astype(low), full_value) + lax.dot_general(
        own_coeffs, key_query.astype(wide), (((0,), (0,)), ((), ())), precision=exact_mode
    )
    var_grads = var_grads.reshape(PIX + 1, own_vars, width)
    patch_weight_grad = var_grads[:PIX].transpose(1, 0, 2)
    var_embed_grad = var_grads[PIX]
    return (
        output,
        patches_grad,
        patch_weight_grad,
        var_embed_grad,
        agg_query_grad,
        query_weight_grad,
        key_weight_grad,
        value_weight_grad,
        agg_proj_grad,
        vector_own[0],
        vector_own[1],
        vector_own[2],
        qkv_weight_grad,
        proj_weight_grad,
        vector_own[3],
        vector_own[4],
        vector_own[5],
        up_weight_grad,
        up_bias_total,
        down_weight_grad,
        vector_own[6],
    )


def solution(mesh):
    shard = P("fsdp")
    shard_rows = P("fsdp", None)
    return jax.shard_map(
        on_device,
        mesh=mesh,
        in_specs=(
            P(None, None, ("grp", "fsdp")),
            P("grp"),
            P("grp", None),
            P("grp"),
            P(),
            P("fsdp", None, None),
            shard_rows,
            P(),
            shard_rows,
            shard_rows,
            shard_rows,
            shard_rows,
            P(),
            P(),
            P(),
            shard_rows,
            shard_rows,
            P(),
            P(),
            P(),
            P(None, "fsdp"),
            shard,
            shard_rows,
            P(),
            P(("grp", "fsdp"), None),
        ),
        out_specs=(
            P(("grp", "fsdp"), None),
            P(None, None, ("grp", "fsdp")),
            P("fsdp", None, None),
            shard_rows,
            shard,
            shard_rows,
            shard_rows,
            shard_rows,
            shard_rows,
            shard,
            shard,
            shard,
            shard_rows,
            shard_rows,
            shard,
            shard,
            shard,
            P(None, "fsdp"),
            shard,
            shard_rows,
            shard,
        ),
        check_vma=False,
    )
```

```python
import functools

import jax
import jax.numpy as jnp
from jax import lax
from jax.experimental import pallas as pl
from jax.experimental.pallas import tpu as pltpu
from jax.sharding import PartitionSpec as P

HEADS = 16
VTOT = 48
PIX = 4

exact_mode = lax.Precision.HIGHEST
masked_out = -1e30
VMEM_LIMIT = 56 * 1024 * 1024


def swap(value, axis, bit):
    size = lax.axis_size(axis)
    return lax.ppermute(value, axis, [(i, i ^ bit) for i in range(size)])


def has_bit(axis, bit):
    return (lax.axis_index(axis) // bit) % 2 == 1


def merge(mine, other, axis, bit):
    return jnp.where(
        has_bit(axis, bit),
        jnp.concatenate([other, mine], axis=0),
        jnp.concatenate([mine, other], axis=0),
    )


def product(left_side, right_side):
    return jnp.dot(left_side, right_side, preferred_element_type=jnp.float32)


def left_product(left_side, right_side):
    return lax.dot_general(
        left_side, right_side, (((0,), (0,)), ((), ())), preferred_element_type=jnp.float32
    )


def right_product(left_side, right_side):
    return lax.dot_general(
        left_side, right_side, (((1,), (1,)), ((), ())), preferred_element_type=jnp.float32
    )


def column_sums(values_in):
    return jnp.sum(values_in.astype(jnp.float32), axis=0)


def gather_far_half(own):
    rows = own.shape[0]
    half = rows // 2
    which = lax.axis_index("grp") % 2
    sent = lax.dynamic_slice_in_dim(own, which * half, half, 0)
    got = swap(sent, "fsdp", 2)
    rest = swap(got, "grp", 1)
    return merge(got, rest, "grp", 1)


def four_shards(own, far):
    return [own, swap(own, "fsdp", 1), far, swap(far, "fsdp", 1)]


def in_order(shards, axis=0):
    me = lax.axis_index("fsdp")
    size = shards[0].shape[axis]
    shape = list(shards[0].shape)
    shape[axis] = size * len(shards)
    whole = jnp.zeros(shape, shards[0].dtype)
    for j, shard in enumerate(shards):
        whole = lax.dynamic_update_slice_in_dim(whole, shard, (me ^ j) * size, axis)
    return whole


def group_bits():
    bits = []
    bit = 1
    while bit < lax.axis_size("grp"):
        bits.append(bit)
        bit *= 2
    return bits


def slot_softmax(patch_ref, coeff_ref, mask_ref):
    scores = coeff_ref[0, PIX] + mask_ref[...]
    for k in range(PIX):
        scores = scores + patch_ref[k].astype(jnp.float32) * coeff_ref[0, k]
    top = jnp.max(scores, axis=0, keepdims=True)
    terms = jnp.exp(scores - top)
    return terms / jnp.sum(terms, axis=0, keepdims=True)


def mixed_of(patch_ref, weights):
    parts = [
        (weights * patch_ref[k].astype(jnp.float32)).astype(jnp.bfloat16) for k in range(PIX)
    ]
    parts.append(weights.astype(jnp.bfloat16))
    return jnp.concatenate(parts, axis=0)


def aggregate_kernel(patch_ref, coeff_ref, mask_ref, table_ref, out_ref):
    weights = slot_softmax(patch_ref, coeff_ref, mask_ref)
    mixed = mixed_of(patch_ref, weights)
    out_ref[...] = jnp.dot(
        table_ref[...], mixed, preferred_element_type=jnp.float32
    ).astype(jnp.bfloat16)


def aggregate(patch_rows, coeff_heads, slot_mask, table_values):
    rows = patch_rows.shape[2]
    width = table_values.shape[0]
    head_dim = width // HEADS
    slots = slot_mask.shape[0]
    return pl.pallas_call(
        aggregate_kernel,
        grid=(HEADS,),
        in_specs=[
            pl.BlockSpec((PIX, slots, rows), lambda h: (0, 0, 0)),
            pl.BlockSpec((1, PIX + 1, slots, 1), lambda h: (h, 0, 0, 0)),
            pl.BlockSpec((slots, 1), lambda h: (0, 0)),
            pl.BlockSpec((head_dim, (PIX + 1) * slots), lambda h: (h, 0)),
        ],
        out_specs=pl.BlockSpec((head_dim, rows), lambda h: (h, 0)),
        out_shape=jax.ShapeDtypeStruct((width, rows), jnp.bfloat16),
        compiler_params=pltpu.CompilerParams(vmem_limit_bytes=VMEM_LIMIT),
        cost_estimate=pl.CostEstimate(
            flops=2 * (PIX + 1) * slots * rows * width * 4,
            bytes_accessed=4 * width * rows,
            transcendentals=HEADS * slots * rows,
        ),
        name="aggregate",
    )(patch_rows, coeff_heads, slot_mask, table_values)


def aggregate_back_kernel(
    patch_ref, coeff_ref, mask_ref, table_ref, heads_ref, scale_ref, table_grad_ref, coeff_grad_ref, patch_grad_ref
):
    head = pl.program_id(0)
    slots = mask_ref.shape[0]
    weights = slot_softmax(patch_ref, coeff_ref, mask_ref)
    mixed = mixed_of(patch_ref, weights)
    heads_grad = heads_ref[...]
    table_grad_ref[...] = lax.dot_general(
        heads_grad, mixed, (((1,), (1,)), ((), ())), preferred_element_type=jnp.float32
    )
    mixed_grad = lax.dot_general(
        table_ref[...], heads_grad, (((0,), (0,)), ((), ())), preferred_element_type=jnp.float32
    )
    parts = [mixed_grad[k * slots : (k + 1) * slots] for k in range(PIX + 1)]
    values = [patch_ref[k].astype(jnp.float32) for k in range(PIX)]
    weights_grad = parts[PIX]
    for k in range(PIX):
        weights_grad = weights_grad + parts[k] * values[k]
    mean_grad = jnp.sum(weights * weights_grad, axis=0, keepdims=True)
    scores_grad = weights * (weights_grad - mean_grad)
    for k in range(PIX):
        coeff_grad_ref[0, k] = jnp.sum(scores_grad * values[k], axis=1, keepdims=True)
    coeff_grad_ref[0, PIX] = jnp.sum(scores_grad, axis=1, keepdims=True)

    @pl.when(head == 0)
    def _():
        patch_grad_ref[...] = jnp.zeros_like(patch_grad_ref)

    scale = scale_ref[0]
    for k in range(PIX):
        patch_grad_ref[k] += scale * (parts[k] * weights + scores_grad * coeff_ref[0, k])


def aggregate_back(patch_rows, coeff_heads, slot_mask, table_values, heads_grad, scale):
    rows = patch_rows.shape[2]
    width = table_values.shape[0]
    head_dim = width // HEADS
    slots = slot_mask.shape[0]
    return pl.pallas_call(
        aggregate_back_kernel,
        grid=(HEADS,),
        in_specs=[
            pl.BlockSpec((PIX, slots, rows), lambda h: (0, 0, 0)),
            pl.BlockSpec((1, PIX + 1, slots, 1), lambda h: (h, 0, 0, 0)),
            pl.BlockSpec((slots, 1), lambda h: (0, 0)),
            pl.BlockSpec((head_dim, (PIX + 1) * slots), lambda h: (h, 0)),
            pl.BlockSpec((head_dim, rows), lambda h: (h, 0)),
            pl.BlockSpec(memory_space=pltpu.SMEM),
        ],
        out_specs=[
            pl.BlockSpec((head_dim, (PIX + 1) * slots), lambda h: (h, 0)),
            pl.BlockSpec((1, PIX + 1, slots, 1), lambda h: (h, 0, 0, 0)),
            pl.BlockSpec((PIX, slots, rows), lambda h: (0, 0, 0)),
        ],
        out_shape=[
            jax.ShapeDtypeStruct((width, (PIX + 1) * slots), jnp.float32),
            jax.ShapeDtypeStruct((HEADS, PIX + 1, slots, 1), jnp.float32),
            jax.ShapeDtypeStruct((PIX, slots, rows), jnp.float32),
        ],
        compiler_params=pltpu.CompilerParams(vmem_limit_bytes=VMEM_LIMIT),
        cost_estimate=pl.CostEstimate(
            flops=4 * (PIX + 1) * slots * rows * width * 4,
            bytes_accessed=8 * width * rows,
            transcendentals=HEADS * slots * rows,
        ),
        name="aggregate_back",
    )(patch_rows, coeff_heads, slot_mask, table_values, heads_grad, scale)


def flip(index, bit):
    bit_set = (index // bit) % 2
    return index + bit - 2 * bit * bit_set, bit_set


def meet(partners):
    barrier = pltpu.get_barrier_semaphore()
    for partner in partners:
        pl.semaphore_signal(
            barrier, inc=1, device_id=partner, device_id_type=pl.DeviceIdType.MESH
        )
    pl.semaphore_wait(barrier, len(partners))


def lane_half(rows, pair, head_dim):
    lane = lax.broadcasted_iota(jnp.int32, (rows, 2 * head_dim), 1)
    return (lane // head_dim) == pair


def attend_kernel(
    head_dim, valid_ref, rows_ref, weight_ref, q_ref, kv_ref, out_ref, log_ref, sum_s, top_s, total_s, send_sem, recv_sem
):
    me = lax.axis_index("fsdp")
    near = {"fsdp": flip(me, 1)[0]}
    far = {"fsdp": flip(me, 2)[0]}
    wide = jnp.float32
    low = jnp.bfloat16
    rows, width = rows_ref.shape
    lanes = 2 * head_dim
    pairs = width // lanes
    scale = head_dim ** (-0.5)
    meet([near, far])

    def copy(kind, i, source, target, device):
        return pltpu.make_async_remote_copy(
            src_ref=kv_ref.at[source, i],
            dst_ref=kv_ref.at[target, i],
            send_sem=send_sem.at[kind, i],
            recv_sem=recv_sem.at[kind, i],
            device_id=device,
            device_id_type=pl.DeviceIdType.MESH,
        )

    def near_copy(i):
        return copy(0, i, 0, 1, near)

    def far_copy(i):
        return copy(1, i, 0, 2, far)

    def last_copy(i):
        return copy(2, i, 2, 3, near)

    entry = rows_ref[...]
    for g in range(pairs // 2):
        for part in range(2):
            start = (part + 1) * width + g * 2 * lanes
            value = jnp.dot(
                entry, weight_ref[:, start : start + 2 * lanes], preferred_element_type=wide
            ).astype(low)
            kv_ref[0, 2 * g, part] = value[:, :lanes]
            kv_ref[0, 2 * g + 1, part] = value[:, lanes:]
        for i in (2 * g, 2 * g + 1):
            far_copy(i).start()
            near_copy(i).start()
    for g in range(pairs // 2):
        start = g * 2 * lanes
        value = jnp.dot(
            entry, weight_ref[:, start : start + 2 * lanes], preferred_element_type=wide
        ).astype(low)
        value = value * jnp.asarray(scale, low)
        q_ref[2 * g] = value[:, :lanes]
        q_ref[2 * g + 1] = value[:, lanes:]

    tile = min(rows, 256)

    def attend(i, shards, first):
        for start in range(0, rows, tile):
            at = slice(start, start + tile)
            block = q_ref[i, at, :]
            sums, tops, totals = [], [], []
            for pair in range(2):
                query = jnp.where(lane_half(tile, pair, head_dim), block, jnp.zeros_like(block))
                logits = []
                for j in shards:
                    raw = lax.dot_general(
                        query, kv_ref[j, i, 0], (((1,), (1,)), ((), ())), preferred_element_type=wide
                    )
                    place = lax.broadcasted_iota(jnp.int32, (1, rows), 1)
                    logits.append(jnp.where(place < valid_ref[j], raw, masked_out))
                top = functools.reduce(
                    jnp.maximum, [jnp.max(part, axis=1, keepdims=True) for part in logits]
                )
                sum_now, total_now = 0.0, 0.0
                for j, part in zip(shards, logits):
                    terms = jnp.exp(part - top)
                    total_now = total_now + jnp.sum(terms, axis=1, keepdims=True)
                    sum_now = sum_now + jnp.dot(
                        terms.astype(low), kv_ref[j, i, 1], preferred_element_type=wide
                    )
                sums.append(sum_now)
                tops.append(top)
                totals.append(total_now)
            side = lane_half(tile, 0, head_dim)
            sum_now = jnp.where(side, sums[0], sums[1])
            top = jnp.where(side, tops[0], tops[1])
            total_now = jnp.where(side, totals[0], totals[1])
            if not first:
                old_top = top_s[at, :]
                new_top = jnp.maximum(top, old_top)
                mine = jnp.exp(top - new_top)
                others = jnp.exp(old_top - new_top)
                sum_now = sum_now * mine + sum_s[at, :] * others
                total_now = total_now * mine + total_s[at, :] * others
                top = new_top
            sum_s[at, :] = sum_now
            top_s[at, :] = top
            total_s[at, :] = total_now

    def one_pair(i, carry):
        near_copy(i).wait_recv()
        attend(i, (0, 1), True)
        far_copy(i).wait_recv()
        last_copy(i).start()
        attend(i, (2,), False)
        last_copy(i).wait_recv()
        attend(i, (3,), False)
        out_ref[i] = (sum_s[...] / total_s[...]).astype(low)
        log_ref[i] = top_s[...] + jnp.log(total_s[...])
        return carry

    lax.fori_loop(0, pairs, one_pair, 0)

    def end(i, carry):
        near_copy(i).wait_send()
        far_copy(i).wait_send()
        last_copy(i).wait_send()
        return carry

    lax.fori_loop(0, pairs, end, 0)


def attend(rows_in, weight, valid):
    rows, width = rows_in.shape
    head_dim = width // HEADS
    lanes = 2 * head_dim
    pairs = HEADS // 2
    whole = pl.BlockSpec(memory_space=pltpu.VMEM)
    low = jnp.bfloat16
    wide = jnp.float32
    return pl.pallas_call(
        functools.partial(attend_kernel, head_dim),
        in_specs=[pl.BlockSpec(memory_space=pltpu.SMEM), whole, whole],
        out_specs=[whole] * 4,
        out_shape=[
            jax.ShapeDtypeStruct((pairs, rows, lanes), low),
            jax.ShapeDtypeStruct((4, pairs, 2, rows, lanes), low),
            jax.ShapeDtypeStruct((pairs, rows, lanes), low),
            jax.ShapeDtypeStruct((pairs, rows, lanes), wide),
        ],
        scratch_shapes=[
            pltpu.VMEM((rows, lanes), wide),
            pltpu.VMEM((rows, lanes), wide),
            pltpu.VMEM((rows, lanes), wide),
            pltpu.SemaphoreType.DMA((3, pairs)),
            pltpu.SemaphoreType.DMA((3, pairs)),
        ],
        compiler_params=pltpu.CompilerParams(
            collective_id=1, has_side_effects=True, vmem_limit_bytes=VMEM_LIMIT
        ),
        cost_estimate=pl.CostEstimate(
            flops=64 * rows * rows * width, bytes_accessed=100_000_000, transcendentals=0
        ),
        name="attend",
    )(valid, rows_in, weight)


def attend_back_kernel(
    head_dim, valid_ref, q_ref, kv_ref, grad_ref, out_ref, log_ref, *refs
):
    result_ref, q_sum, own_s, far_s, last_s, near_s, got_far, got_last, got_near, log_rows, dot_rows = refs[:11]
    send_sem, recv_sem = refs[11:]
    me = lax.axis_index("fsdp")
    near = {"fsdp": flip(me, 1)[0]}
    far = {"fsdp": flip(me, 2)[0]}
    wide = jnp.float32
    low = jnp.bfloat16
    pairs, rows, lanes = q_ref.shape
    width = pairs * lanes
    scale = head_dim ** (-0.5)
    meet([near, far])

    def copy(kind, i, source, target, device):
        return pltpu.make_async_remote_copy(
            src_ref=source.at[i],
            dst_ref=target.at[i],
            send_sem=send_sem.at[kind, i],
            recv_sem=recv_sem.at[kind, i],
            device_id=device,
            device_id_type=pl.DeviceIdType.MESH,
        )

    def last_copy(i):
        return copy(0, i, last_s, got_last, near)

    def near_copy(i):
        return copy(1, i, near_s, got_near, near)

    def far_copy(i):
        return copy(2, i, far_s, got_far, far)

    def back(i, shards, targets):
        query = q_ref[i]
        grad = grad_ref[i]
        q_grad = None
        k_sums = [None, None]
        v_sums = [None, None]

        def plus(old, new):
            return new if old is None else old + new

        for pair in range(2):
            side = lane_half(rows, pair, head_dim)
            log_row = log_rows[i, pair : pair + 1, :]
            dot_row = dot_rows[i, pair : pair + 1, :]
            one_query = jnp.where(side, query, jnp.zeros_like(query))
            one_grad = jnp.where(side, grad, jnp.zeros_like(grad))
            for n, j in enumerate(shards):
                key = kv_ref[j, i, 0]
                one_key = jnp.where(side, key, jnp.zeros_like(key))
                raw = lax.dot_general(
                    key, one_query, (((1,), (1,)), ((), ())), preferred_element_type=wide
                )
                place = lax.broadcasted_iota(jnp.int32, raw.shape, 0)
                probs = jnp.exp(jnp.where(place < valid_ref[j], raw - log_row, masked_out))
                probs_grad = lax.dot_general(
                    kv_ref[j, i, 1], one_grad, (((1,), (1,)), ((), ())), preferred_element_type=wide
                )
                raw_grad = (probs * (probs_grad - dot_row)).astype(low)
                v_sums[n] = plus(
                    v_sums[n], jnp.dot(probs.astype(low), one_grad, preferred_element_type=wide)
                )
                k_sums[n] = plus(
                    k_sums[n], jnp.dot(raw_grad, one_query, preferred_element_type=wide)
                )
                q_grad = plus(
                    q_grad,
                    lax.dot_general(
                        raw_grad, one_key, (((0,), (0,)), ((), ())), preferred_element_type=wide
                    ),
                )
        for n, target in enumerate(targets):
            target[i, 0] = k_sums[n].astype(target.dtype)
            target[i, 1] = v_sums[n].astype(target.dtype)
        return q_grad

    def send_far(i):
        last_copy(i).wait()
        far_s[i] = (far_s[i].astype(wide) + got_last[i].astype(wide)).astype(low)
        far_copy(i).start()

    def first_loop(i, carry):
        log_t = jnp.transpose(log_ref[i])
        dots = jnp.transpose(grad_ref[i].astype(wide) * out_ref[i].astype(wide))
        for pair in range(2):
            here = slice(pair * head_dim, (pair + 1) * head_dim)
            log_rows[i, pair : pair + 1, :] = log_t[pair * head_dim : pair * head_dim + 1, :]
            dot_rows[i, pair : pair + 1, :] = jnp.sum(dots[here, :], axis=0, keepdims=True)
        q_sum[i] = back(i, (3, 2), (last_s, far_s))
        last_copy(i).start()

        @pl.when(i > 0)
        def _():
            send_far(i - 1)

        return carry

    lax.fori_loop(0, pairs, first_loop, 0)
    send_far(pairs - 1)

    def second_loop(i, carry):
        q_sum[i] = (q_sum[i] + back(i, (1, 0), (near_s, own_s))) * scale
        near_copy(i).start()
        return carry

    lax.fori_loop(0, pairs, second_loop, 0)
    for i in range(pairs):
        near_copy(i).wait()
        far_copy(i).wait()
        at = slice(i * lanes, (i + 1) * lanes)
        result_ref[:, at] = q_sum[i].astype(low)
        for part in range(2):
            value = own_s[i, part] + got_near[i, part].astype(wide) + got_far[i, part].astype(wide)
            start = (part + 1) * width + i * lanes
            result_ref[:, start : start + lanes] = value.astype(low)


def attend_back(queries, key_values, grad, out, logs, valid):
    pairs, rows, lanes = queries.shape
    head_dim = lanes // 2
    whole = pl.BlockSpec(memory_space=pltpu.VMEM)
    low = jnp.bfloat16
    wide = jnp.float32
    slab = (pairs, 2, rows, lanes)
    return pl.pallas_call(
        functools.partial(attend_back_kernel, head_dim),
        in_specs=[pl.BlockSpec(memory_space=pltpu.SMEM)] + [whole] * 5,
        out_specs=whole,
        out_shape=jax.ShapeDtypeStruct((rows, 3 * pairs * lanes), low),
        scratch_shapes=[
            pltpu.VMEM((pairs, rows, lanes), wide),
            pltpu.VMEM(slab, wide),
            pltpu.VMEM(slab, low),
            pltpu.VMEM(slab, low),
            pltpu.VMEM(slab, low),
            pltpu.VMEM(slab, low),
            pltpu.VMEM(slab, low),
            pltpu.VMEM(slab, low),
            pltpu.VMEM((pairs, 8, rows), wide),
            pltpu.VMEM((pairs, 8, rows), wide),
            pltpu.SemaphoreType.DMA((3, pairs)),
            pltpu.SemaphoreType.DMA((3, pairs)),
        ],
        compiler_params=pltpu.CompilerParams(
            collective_id=2, has_side_effects=True, vmem_limit_bytes=VMEM_LIMIT
        ),
        cost_estimate=pl.CostEstimate(
            flops=160 * rows * rows * pairs * lanes, bytes_accessed=100_000_000, transcendentals=0
        ),
        name="attend_back",
    )(valid, queries, key_values, grad, out, logs)


def feed_kernel(
    first_ref, second_ref, grad_ref, up_ref, down_ref, bias_ref, rows_ref, gelu_ref, pre_ref, out_ref, back_ref, bias_grad_ref
):
    tile = first_ref.shape[0]
    entry = jnp.concatenate([first_ref[...], second_ref[...]], axis=0)
    grad = jnp.concatenate([grad_ref[0], grad_ref[1]], axis=0)
    pre_act = jnp.dot(entry, up_ref[...], preferred_element_type=jnp.float32) + bias_ref[...]
    cdf = 0.5 * (1.0 + lax.erf(pre_act * 0.7071067811865476))
    density = jnp.exp(-0.5 * pre_act * pre_act) * 0.3989422804014327
    gelu = (pre_act * cdf).astype(jnp.bfloat16)
    act_grad = lax.dot_general(
        grad, down_ref[...], (((1,), (1,)), ((), ())), preferred_element_type=jnp.float32
    )
    pre_grad = (act_grad * (cdf + pre_act * density)).astype(jnp.bfloat16)
    out = jnp.dot(gelu, down_ref[...], preferred_element_type=jnp.float32).astype(jnp.bfloat16)
    back = lax.dot_general(
        pre_grad, up_ref[...], (((1,), (1,)), ((), ())), preferred_element_type=jnp.float32
    ).astype(jnp.bfloat16)

    @pl.when(pl.program_id(0) == 0)
    def _():
        bias_grad_ref[...] = jnp.zeros_like(bias_grad_ref)

    bias_grad_ref[...] += jnp.sum(pre_grad.astype(jnp.float32), axis=0, keepdims=True)
    for ref, value in (
        (rows_ref, entry),
        (gelu_ref, gelu),
        (pre_ref, pre_grad),
        (out_ref, out),
        (back_ref, back),
    ):
        ref[0] = value[:tile]
        ref[1] = value[tile:]


def feed(first, second, grads, up, down, bias):
    rows, width = first.shape
    hidden = up.shape[1]
    tile = min(rows, 128)
    one = pl.BlockSpec((tile, width), lambda i: (i, 0))
    pair = pl.BlockSpec((2, tile, width), lambda i: (0, i, 0))
    pair_hidden = pl.BlockSpec((2, tile, hidden), lambda i: (0, i, 0))

    def fixed(shape):
        return pl.BlockSpec(shape, lambda i: (0, 0))

    out = jax.ShapeDtypeStruct((2, rows, width), jnp.bfloat16)
    out_hidden = jax.ShapeDtypeStruct((2, rows, hidden), jnp.bfloat16)
    return pl.pallas_call(
        feed_kernel,
        grid=(rows // tile,),
        in_specs=[
            one,
            one,
            pair,
            fixed(up.shape),
            fixed(down.shape),
            fixed((1, hidden)),
        ],
        out_specs=[pair, pair_hidden, pair_hidden, pair, pair, fixed((1, hidden))],
        out_shape=[
            out,
            out_hidden,
            out_hidden,
            out,
            out,
            jax.ShapeDtypeStruct((1, hidden), jnp.float32),
        ],
        compiler_params=pltpu.CompilerParams(vmem_limit_bytes=VMEM_LIMIT),
        cost_estimate=pl.CostEstimate(
            flops=16 * rows * width * hidden * 2,
            bytes_accessed=16 * rows * width,
            transcendentals=4 * rows * hidden,
        ),
        name="feed",
    )(first, second, grads, up, down, bias)


def total_kernel(group_size, widths, share_ref, *refs):
    pairs = [(refs[2 * i], refs[2 * i + 1]) for i in range(3)]
    bundle_ref = refs[6]
    outs = refs[7:10]
    bundle_out = refs[10]
    send1, recv1, own1, send2, recv2, hold, halves, done, full, send_sem, recv_sem = refs[11:]
    me = lax.axis_index("fsdp")
    group = lax.axis_index("grp")
    core_partner, core = flip(me, 1)
    far_partner, far = flip(me, 2)
    quarter = own1.shape[2]
    wide = jnp.float32
    low = jnp.bfloat16

    steps = []
    size, bit, offset = quarter, 1, 0
    while bit < group_size:
        partner, bit_set = flip(group, bit)
        halving = size >= 64
        steps.append((partner, bit_set, halving, size, offset))
        if halving:
            size = size // 2
            offset = offset + bit_set * size
        bit *= 2
    halvings = [i for i, step in enumerate(steps) if step[2]]

    meet([{"fsdp": core_partner}, {"fsdp": far_partner}] + [{"grp": step[0]} for step in steps])

    chunks = [(None, None, None, 0, bundle_ref.shape[1])]
    for (left, right), out in zip(pairs, outs):
        for start in range(0, right.shape[1], widths):
            chunks.append((left, right, out, start, widths))

    def copy(stage, c, src, dst, device):
        return pltpu.make_async_remote_copy(
            src_ref=src,
            dst_ref=dst,
            send_sem=send_sem.at[stage, c],
            recv_sem=recv_sem.at[stage, c],
            device_id=device,
            device_id_type=pl.DeviceIdType.MESH,
        )

    def span(start, size):
        return pl.ds(pl.multiple_of(start, 16), size)

    def columns(c):
        return pl.ds(0, chunks[c][4])

    def core_copy(c):
        cols = columns(c)
        return copy(
            0, c, send1.at[c, :, :, cols], recv1.at[c, :, :, cols], {"fsdp": core_partner}
        )

    def far_copy(c):
        cols = columns(c)
        return copy(1, c, send2.at[c, :, cols], recv2.at[c, :, cols], {"fsdp": far_partner})

    def step_copy(i, c):
        partner, bit_set, halving, size, offset = steps[i]
        cols = columns(c)
        if halving:
            size = size // 2
            offset = offset + (1 - bit_set) * size
        src = hold.at[c, span(offset, size), cols]
        dst = halves[i].at[c, :, cols]
        return copy(2 + i, c, src, dst, {"grp": partner})

    def back_copy(i, c):
        partner, bit_set, halving, size, offset = steps[i]
        size = size // 2
        offset = offset + bit_set * size
        at = done.at[c, span(offset, size), columns(c)]
        return copy(2 + len(steps) + i, c, at, at, {"grp": partner})

    def begin(c):
        left, right, out, start, width = chunks[c]
        cols = columns(c)

        def part(q):
            rows = span(q * quarter, quarter)
            if left is None:
                return bundle_ref[rows, :]
            value = jnp.dot(
                left[rows, :], right[:, start : start + width], preferred_element_type=wide
            )
            return (value * share_ref[0]).astype(low)

        for y in range(2):
            send1[c, y, :, cols] = part(2 * y + 1 - core)
        core_copy(c).start()
        for y in range(2):
            own1[c, y, :, cols] = part(2 * y + core)

    def after_core(c):
        cols = columns(c)
        core_copy(c).wait()
        value = own1[c, 1 - far, :, cols].astype(wide) + recv1[c, 1 - far, :, cols].astype(wide)
        send2[c, :, cols] = value.astype(low)
        far_copy(c).start()

    def after_far(c):
        cols = columns(c)
        far_copy(c).wait()
        value = own1[c, far, :, cols].astype(wide) + recv1[c, far, :, cols].astype(wide)
        hold[c, :, cols] = (value + recv2[c, :, cols].astype(wide)).astype(low)
        step_copy(0, c).start()

    def after_step(i, c):
        cols = columns(c)
        step_copy(i, c).wait()
        partner, bit_set, halving, size, offset = steps[i]
        if halving:
            size = size // 2
            offset = offset + bit_set * size
        at = span(offset, size)
        value = hold[c, at, cols].astype(wide) + halves[i][c, :, cols].astype(wide)
        if i + 1 < len(steps):
            hold[c, at, cols] = value.astype(low)
            step_copy(i + 1, c).start()
        else:
            done[c, at, cols] = value.astype(low)
            back_copy(halvings[-1], c).start()

    def after_back(k, c):
        back_copy(halvings[k], c).wait()
        if k > 0:
            back_copy(halvings[k - 1], c).start()
        else:
            left, right, out, start, width = chunks[c]
            if out is None:
                full[me] = done[c, :, columns(c)]
                bundle_core().start()
            else:
                out[:, start : start + width] = done[c].astype(wide)

    last = 2 + 2 * len(steps)

    def bundle_core():
        return copy(last, 0, full.at[me], full.at[me], {"fsdp": core_partner})

    def bundle_far():
        at = full.at[pl.ds(me - core, 2)]
        return copy(last, 1, at, at, {"fsdp": far_partner})

    def finish_core(c):
        bundle_core().wait()
        bundle_far().start()

    def finish_far(c):
        bundle_far().wait()
        for q in range(4):
            bundle_out[q * quarter : (q + 1) * quarter, :] = full[q].astype(wide)

    stages = [begin, after_core, after_far]
    stages += [functools.partial(after_step, i) for i in range(len(steps))]
    stages += [functools.partial(after_back, k) for k in reversed(range(len(halvings)))]
    order = [1, 0] + list(range(2, len(stages)))
    extra = [finish_core, finish_far]
    for t in range(len(chunks) + len(stages) - 1):
        for s in order:
            if 0 <= t - s < len(chunks):
                stages[s](t - s)
        if 0 <= t - len(stages) < len(extra):
            extra[t - len(stages)](0)


def total(group_size, share, qkv_pair, agg_pair, proj_pair, bundle):
    pairs = [qkv_pair, agg_pair, proj_pair]
    width = qkv_pair[0].shape[0]
    quarter = width // 4
    widths = 512
    count = 1 + sum(right.shape[1] // widths for left, right in pairs)
    steps = 0
    halves = []
    size = quarter
    while 2**steps < group_size:
        if size >= 64:
            size //= 2
        halves.append(pltpu.VMEM((count, size, widths), jnp.bfloat16))
        steps += 1
    low = jnp.bfloat16
    whole = pl.BlockSpec(memory_space=pltpu.VMEM)
    scratch = [
        pltpu.VMEM((count, 2, quarter, widths), low),
        pltpu.VMEM((count, 2, quarter, widths), low),
        pltpu.VMEM((count, 2, quarter, widths), low),
        pltpu.VMEM((count, quarter, widths), low),
        pltpu.VMEM((count, quarter, widths), low),
        pltpu.VMEM((count, quarter, widths), low),
        halves,
        pltpu.VMEM((count, quarter, widths), low),
        pltpu.VMEM((4, quarter, bundle.shape[1]), low),
        pltpu.SemaphoreType.DMA((3 + 2 * steps, count)),
        pltpu.SemaphoreType.DMA((3 + 2 * steps, count)),
    ]
    return pl.pallas_call(
        functools.partial(total_kernel, group_size, widths),
        in_specs=[pl.BlockSpec(memory_space=pltpu.SMEM)] + [whole] * 7,
        out_specs=[whole] * 4,
        out_shape=[
            jax.ShapeDtypeStruct((quarter, right.shape[1]), jnp.float32) for left, right in pairs
        ]
        + [jax.ShapeDtypeStruct(bundle.shape, jnp.float32)],
        scratch_shapes=scratch,
        compiler_params=pltpu.CompilerParams(
            collective_id=0, has_side_effects=True, vmem_limit_bytes=VMEM_LIMIT
        ),
        cost_estimate=pl.CostEstimate(
            flops=sum(2 * left.size * right.shape[1] for left, right in pairs),
            bytes_accessed=200_000_000,
            transcendentals=0,
        ),
        name="total",
    )(share, *[array for pair in pairs for array in pair], bundle)


def normalise(values_in):
    row_mean = jnp.mean(values_in, axis=-1, keepdims=True)
    centred = values_in - row_mean
    spread = jnp.mean(centred * centred, axis=-1, keepdims=True)
    inverse = lax.rsqrt(spread + 1e-05)
    return centred * inverse, inverse


def norm_back(grad, xhat, inverse, gain_vec):
    scaled = grad * gain_vec
    first = jnp.mean(scaled, axis=-1, keepdims=True)
    second = jnp.mean(scaled * xhat, axis=-1, keepdims=True)
    return (scaled - first - xhat * second) * inverse


def on_device(
    patches,
    patch_counts,
    var_present,
    item_dataset,
    var_ids,
    patch_weight,
    var_embed,
    agg_query,
    query_weight,
    key_weight,
    value_weight,
    agg_proj,
    agg_bias,
    norm1_gain,
    norm1_shift,
    qkv_weight,
    proj_weight,
    proj_bias,
    norm2_gain,
    norm2_shift,
    up_weight,
    up_bias,
    down_weight,
    down_bias,
    out_grad,
):
    low = jnp.bfloat16
    wide = jnp.float32
    rows = patches.shape[2]
    me = lax.axis_index("fsdp")
    group_count = lax.axis_size("grp")
    width = proj_weight.shape[1]
    head_dim = width // HEADS
    own_width = width // 4
    own_vars = patch_weight.shape[0]
    score_scale = head_dim ** (-0.5)

    counts = patch_counts.astype(wide)
    count_total = counts
    for bit in group_bits():
        count_total = count_total + swap(count_total, "grp", bit)
    count_share = counts[0] / count_total[0]
    item_count = patch_counts[0]
    own_valid = me * rows + jnp.arange(rows, dtype=jnp.int32) < item_count
    shard_valid = jnp.clip(
        item_count - (me ^ jnp.arange(4, dtype=jnp.int32)) * rows, 0, rows
    ).astype(jnp.int32)

    present = var_present[0] > 0
    slot_vars = lax.dynamic_index_in_dim(var_ids, item_dataset[0], 0, keepdims=False)
    selector = slot_vars[:, None] == jnp.arange(VTOT, dtype=jnp.int32)[None, :]
    own_rows = jnp.concatenate(
        [
            patch_weight.reshape(own_vars * PIX, width),
            var_embed,
        ],
        axis=0,
    )
    near_rows = swap(own_rows, "fsdp", 1)
    far_rows = swap(jnp.stack([own_rows, near_rows]), "fsdp", 2)
    row_sets = [own_rows, near_rows, far_rows[0], far_rows[1]]
    table_parts = []
    for part in row_sets:
        pixels = part[: own_vars * PIX].reshape(own_vars, PIX, width)
        embeds = part[own_vars * PIX : own_vars * (PIX + 1)][:, None, :]
        table_parts.append(jnp.concatenate([pixels, embeds], axis=1).transpose(1, 0, 2))
    stacked = in_order(table_parts, axis=1)
    stacked_rows = stacked.reshape((PIX + 1) * VTOT, width)

    own_query = lax.dynamic_slice_in_dim(agg_query, me * own_width, own_width, 0)
    query_sum = product(own_query[None, :], query_weight)
    query_sum = query_sum + swap(query_sum, "fsdp", 1)
    query_sum = query_sum + swap(query_sum, "fsdp", 2)
    query_vec = query_sum[0].astype(low)
    own_key_query = (
        jnp.einsum(
            "dhj,hj->hd",
            key_weight.reshape(own_width, HEADS, head_dim),
            query_vec.reshape(HEADS, head_dim),
            preferred_element_type=wide,
        )
        * score_scale
    ).astype(low)
    near_key_query = swap(own_key_query, "fsdp", 1)
    far_key_query = swap(jnp.stack([own_key_query, near_key_query]), "fsdp", 2)
    key_query = in_order(
        [own_key_query, near_key_query, far_key_query[0], far_key_query[1]], axis=1
    )
    coeffs_by_var = right_product(key_query, stacked_rows).reshape(HEADS, PIX + 1, VTOT)
    coeff_heads = jnp.einsum(
        "hku,su->hks", coeffs_by_var, selector.astype(wide), precision=exact_mode
    )[..., None]

    value_shards = four_shards(value_weight, gather_far_half(value_weight))
    full_value = in_order(value_shards)
    table_by_var = left_product(full_value, stacked_rows.T).astype(low)
    table_values = (
        jnp.einsum(
            "hku,su->hks",
            table_by_var.reshape(width, PIX + 1, VTOT),
            selector.astype(low),
            preferred_element_type=wide,
        )
        .astype(low)
        .reshape(width, (PIX + 1) * VTOT)
    )
    own_table = lax.dynamic_slice_in_dim(stacked_rows, me * own_width, own_width, 1)
    key_table = product(own_table, key_weight)
    key_table = key_table + swap(key_table.astype(low), "fsdp", 1).astype(wide)
    key_table = key_table + swap(key_table.astype(low), "fsdp", 2).astype(wide)

    agg_proj_shards = four_shards(agg_proj, gather_far_half(agg_proj))
    full_agg_proj = in_order(agg_proj_shards)
    qkv_shards = four_shards(qkv_weight, gather_far_half(qkv_weight))
    full_qkv = in_order(qkv_shards)
    proj_shards = four_shards(proj_weight, gather_far_half(proj_weight))
    full_proj = in_order(proj_shards)
    upstream = out_grad.astype(wide) * own_valid[:, None].astype(wide)
    down_grad = upstream.astype(low)
    near_down_grad = swap(down_grad, "fsdp", 1)
    far_down_grad = swap(down_grad, "fsdp", 2)
    last_down_grad = swap(far_down_grad, "fsdp", 1)
    near_grads = jnp.stack([down_grad, near_down_grad])
    far_grads = jnp.stack([far_down_grad, last_down_grad])

    patch_rows = patches.transpose(1, 0, 2)
    slot_mask = jnp.where(present, 0.0, masked_out).astype(wide)[:, None]
    heads_t = aggregate(patch_rows, coeff_heads, slot_mask, table_values)
    embedded = left_product(heads_t, full_agg_proj) + agg_bias
    xhat1, inverse1 = normalise(embedded)
    normed1 = (xhat1 * norm1_gain + norm1_shift).astype(low)
    queries, key_values, context_pairs, logs = attend(normed1, full_qkv, shard_valid)
    context = context_pairs.transpose(1, 0, 2).reshape(rows, width)
    middle = embedded + (product(context, full_proj) + proj_bias)
    xhat2, inverse2 = normalise(middle)
    normed2 = (xhat2 * norm2_gain + norm2_shift).astype(low)
    near_normed2 = swap(normed2, "fsdp", 1)
    far_normed2 = swap(normed2, "fsdp", 2)
    last_normed2 = swap(far_normed2, "fsdp", 1)
    bias_row = up_bias.astype(wide)[None, :]
    near = feed(normed2, near_normed2, near_grads, up_weight, down_weight, bias_row)
    far = feed(far_normed2, last_normed2, far_grads, up_weight, down_weight, bias_row)
    far_got = swap(far[4][1], "fsdp", 1)
    far_sum = (far[4][0].astype(wide) + far_got.astype(wide)).astype(low)
    far_back = swap(far_sum, "fsdp", 2)
    near_back = swap(near[4][1], "fsdp", 1)

    def both_left(left, right):
        def one(i):
            return left_product(
                left[i].reshape(-1, left[i].shape[2]), right[i].reshape(-1, right[i].shape[2])
            )

        return ((one(0) + one(1)) * count_share).astype(low)

    down_weight_part = both_left([near[1], far[1]], [near_grads, far_grads])
    up_weight_part = both_left([near[0], far[0]], [near[2], far[2]])
    down_weight_grad = lax.psum(down_weight_part, "grp").astype(wide)
    up_weight_grad = lax.psum(up_weight_part, "grp").astype(wide)
    up_bias_grad = near[5] + far[5]
    down_bias_grad = column_sums(down_grad)
    normed2_grad = near[4][0].astype(wide) + near_back.astype(wide) + far_back.astype(wide)
    out_got = swap(jnp.stack([near[3][1], far[3][1]]), "fsdp", 1)
    out_far = swap((far[3][0].astype(wide) + out_got[1].astype(wide)).astype(low), "fsdp", 2)
    down_sum = near[3][0].astype(wide) + out_got[0].astype(wide) + out_far.astype(wide)
    output = (middle + down_sum + down_bias).astype(low)
    norm2_gain_grad = jnp.sum(normed2_grad * xhat2, axis=0)
    norm2_shift_grad = jnp.sum(normed2_grad, axis=0)
    middle_grad = upstream + norm_back(normed2_grad, xhat2, inverse2, norm2_gain)
    attended_grad = middle_grad.astype(low)
    proj_bias_grad = column_sums(attended_grad)

    context_grad = right_product(attended_grad, full_proj).astype(low)
    context_grad = context_grad.reshape(rows, HEADS // 2, 2 * head_dim).transpose(1, 0, 2)
    qkv_grad = attend_back(queries, key_values, context_grad, context_pairs, logs, shard_valid)
    normed1_grad = right_product(qkv_grad, full_qkv)
    norm1_gain_grad = jnp.sum(normed1_grad * xhat1, axis=0)
    norm1_shift_grad = jnp.sum(normed1_grad, axis=0)
    embedded_grad = (middle_grad + norm_back(normed1_grad, xhat1, inverse1, norm1_gain)).astype(low)
    agg_bias_grad = column_sums(embedded_grad)
    heads_grad = right_product(full_agg_proj, embedded_grad).astype(low)
    input_scale = (group_count * count_share)[None]
    table_grad, coeff_grad, patch_grad = aggregate_back(
        patch_rows, coeff_heads, slot_mask, table_values, heads_grad, input_scale
    )
    patches_grad = patch_grad.transpose(1, 0, 2)

    table_sum = jnp.einsum(
        "hks,su->kuh",
        table_grad.reshape(width, PIX + 1, VTOT),
        selector.astype(wide),
        precision=exact_mode,
    ).reshape((PIX + 1) * VTOT, width)
    coeff_sum = jnp.einsum(
        "hks,su->hku", coeff_grad[..., 0], selector.astype(wide), precision=exact_mode
    ).reshape(-1)
    coeff_rows = -(-coeff_sum.shape[0] // width)
    coeff_flat = jnp.pad(coeff_sum, (0, coeff_rows * width - coeff_sum.shape[0]))
    vectors = [
        agg_bias_grad,
        norm1_gain_grad,
        norm1_shift_grad,
        proj_bias_grad,
        norm2_gain_grad,
        norm2_shift_grad,
        down_bias_grad,
    ]
    up_bias_rows = lax.dynamic_update_slice_in_dim(jnp.zeros((4, width), wide), up_bias_grad, me, 0)
    pieces = [table_sum, coeff_flat.reshape(coeff_rows, width), jnp.stack(vectors), up_bias_rows]
    bundle = jnp.concatenate(pieces, axis=0) * count_share
    bundle = jnp.pad(bundle, ((0, -bundle.shape[0] % 128), (0, 0))).astype(low)
    bundle_shape = bundle.shape
    qkv_weight_grad, agg_proj_grad, proj_weight_grad, bundle = total(
        group_count,
        count_share[None],
        (normed1.T, qkv_grad),
        (heads_t, embedded_grad),
        (context.T, attended_grad),
        bundle.reshape(width, -1),
    )
    bundle = bundle.reshape(bundle_shape)
    table_total = bundle[: table_sum.shape[0]]
    at = table_sum.shape[0]
    coeff_total = bundle[at : at + coeff_rows].reshape(-1)[: coeff_sum.shape[0]]
    coeff_total = coeff_total.reshape(HEADS, (PIX + 1) * VTOT)
    at += coeff_rows
    vector_total = bundle[at : at + len(vectors)]
    at += len(vectors)
    up_bias_total = lax.dynamic_slice_in_dim(bundle, at + me, 1, 0)[0]
    vector_own = lax.dynamic_slice_in_dim(vector_total, me * own_width, own_width, 1)

    value_weight_grad = left_product(own_table, table_total.astype(low))
    key_query_grad = jnp.dot(coeff_total, own_table.astype(wide), precision=exact_mode)
    key_weight_grad = (
        key_query_grad.T[:, :, None]
        * query_vec.astype(wide).reshape(1, HEADS, head_dim)
        * score_scale
    ).reshape(own_width, width)
    query_grad = (
        jnp.einsum(
            "hx,xhj->hj",
            coeff_total,
            key_table.reshape((PIX + 1) * VTOT, HEADS, head_dim),
            precision=exact_mode,
        ).reshape(width)
        * score_scale
    )
    query_weight_grad = own_query.astype(wide)[:, None] * query_grad[None, :]
    agg_query_grad = jnp.dot(
        query_weight.astype(wide), query_grad, precision=exact_mode
    )
    own_totals = lax.dynamic_slice_in_dim(
        table_total.reshape(PIX + 1, VTOT, width), me * own_vars, own_vars, 1
    ).reshape((PIX + 1) * own_vars, width)
    own_coeffs = lax.dynamic_slice_in_dim(
        coeff_total.reshape(HEADS, PIX + 1, VTOT), me * own_vars, own_vars, 2
    ).reshape(HEADS, (PIX + 1) * own_vars)
    var_grads = right_product(own_totals.astype(low), full_value) + lax.dot_general(
        own_coeffs, key_query.astype(wide), (((0,), (0,)), ((), ())), precision=exact_mode
    )
    var_grads = var_grads.reshape(PIX + 1, own_vars, width)
    patch_weight_grad = var_grads[:PIX].transpose(1, 0, 2)
    var_embed_grad = var_grads[PIX]
    return (
        output,
        patches_grad,
        patch_weight_grad,
        var_embed_grad,
        agg_query_grad,
        query_weight_grad,
        key_weight_grad,
        value_weight_grad,
        agg_proj_grad,
        vector_own[0],
        vector_own[1],
        vector_own[2],
        qkv_weight_grad,
        proj_weight_grad,
        vector_own[3],
        vector_own[4],
        vector_own[5],
        up_weight_grad,
        up_bias_total,
        down_weight_grad,
        vector_own[6],
    )


def solution(mesh):
    shard = P("fsdp")
    shard_rows = P("fsdp", None)
    return jax.shard_map(
        on_device,
        mesh=mesh,
        in_specs=(
            P(None, None, ("grp", "fsdp")),
            P("grp"),
            P("grp", None),
            P("grp"),
            P(),
            P("fsdp", None, None),
            shard_rows,
            P(),
            shard_rows,
            shard_rows,
            shard_rows,
            shard_rows,
            P(),
            P(),
            P(),
            shard_rows,
            shard_rows,
            P(),
            P(),
            P(),
            P(None, "fsdp"),
            shard,
            shard_rows,
            P(),
            P(("grp", "fsdp"), None),
        ),
        out_specs=(
            P(("grp", "fsdp"), None),
            P(None, None, ("grp", "fsdp")),
            P("fsdp", None, None),
            shard_rows,
            shard,
            shard_rows,
            shard_rows,
            shard_rows,
            shard_rows,
            shard,
            shard,
            shard,
            shard_rows,
            shard_rows,
            shard,
            shard,
            shard,
            P(None, "fsdp"),
            shard,
            shard_rows,
            shard,
        ),
        check_vma=False,
    )
```

```python
import functools

import jax
import jax.numpy as jnp
from jax import lax
from jax.experimental import pallas as pl
from jax.experimental.pallas import tpu as pltpu
from jax.sharding import PartitionSpec as P

HEADS = 16
VTOT = 48
PIX = 4

exact_mode = lax.Precision.HIGHEST
masked_out = -1e30
VMEM_LIMIT = 56 * 1024 * 1024


def swap(value, axis, bit):
    size = lax.axis_size(axis)
    return lax.ppermute(value, axis, [(i, i ^ bit) for i in range(size)])


def product(left_side, right_side):
    return jnp.dot(left_side, right_side, preferred_element_type=jnp.float32)


def left_product(left_side, right_side):
    return lax.dot_general(
        left_side, right_side, (((0,), (0,)), ((), ())), preferred_element_type=jnp.float32
    )


def right_product(left_side, right_side):
    return lax.dot_general(
        left_side, right_side, (((1,), (1,)), ((), ())), preferred_element_type=jnp.float32
    )


def column_sums(values_in):
    return jnp.sum(values_in.astype(jnp.float32), axis=0)


def flip(index, bit):
    bit_set = (index // bit) % 2
    return index + bit - 2 * bit * bit_set, bit_set


def meet(partners):
    barrier = pltpu.get_barrier_semaphore()
    for partner in partners:
        pl.semaphore_signal(
            barrier, inc=1, device_id=partner, device_id_type=pl.DeviceIdType.MESH
        )
    pl.semaphore_wait(barrier, len(partners))


def normalise(values_in):
    row_mean = jnp.mean(values_in, axis=-1, keepdims=True)
    centred = values_in - row_mean
    spread = jnp.mean(centred * centred, axis=-1, keepdims=True)
    inverse = lax.rsqrt(spread + 1e-05)
    return centred * inverse, inverse


def norm_back(grad, xhat, inverse, gain_vec):
    scaled = grad * gain_vec
    first = jnp.mean(scaled, axis=-1, keepdims=True)
    second = jnp.mean(scaled * xhat, axis=-1, keepdims=True)
    return (scaled - first - xhat * second) * inverse


def slot_softmax(patch_ref, columns, mask_ref):
    scores = columns[PIX] + mask_ref[...]
    for k in range(PIX):
        scores = scores + patch_ref[k].astype(jnp.float32) * columns[k]
    top = jnp.max(scores, axis=0, keepdims=True)
    terms = jnp.exp(scores - top)
    return terms / jnp.sum(terms, axis=0, keepdims=True)


def mixed_of(patch_ref, weights, rows):
    parts = [
        (weights * patch_ref[k].astype(jnp.float32)).astype(jnp.bfloat16) for k in range(PIX)
    ]
    parts.append(weights.astype(jnp.bfloat16))
    used = weights.shape[0] * (PIX + 1)
    if rows > used:
        parts.append(jnp.zeros((rows - used, weights.shape[1]), jnp.bfloat16))
    return jnp.concatenate(parts, axis=0)


def head_columns(coeff_ref, head, slots):
    lane = lax.broadcasted_iota(jnp.int32, (slots, coeff_ref.shape[1]), 1)
    return [
        jnp.sum(
            jnp.where(lane == head, coeff_ref[k * slots : (k + 1) * slots, :], 0.0),
            axis=1,
            keepdims=True,
        )
        for k in range(PIX + 1)
    ]


def prepare_kernel(group_size, head_dim, *refs):
    (
        count_ref, own_query, query_w, key_w, own_table, select_ref, own_value, own_agg,
        own_qkv, own_proj, own_grad, patch_ref, mask_ref, bias_ref, gain_ref, shift_ref,
    ) = refs[:16]
    (
        count_out, tables, query_out, keys_out, full_value, full_agg, full_qkv, full_proj,
        near_grad, far_grads, table_out, coeff_out, heads_out, embed_out, norm_out,
    ) = refs[16:31]
    query_part, query_got, counts = refs[31:34]
    whole_value, whole_agg, whole_qkv, whole_proj, grads = refs[34:39]
    send_sem, recv_sem, small_send, small_recv, local_sem = refs[39:]
    wide = jnp.float32
    low = jnp.bfloat16
    me = lax.axis_index("fsdp")
    group = lax.axis_index("grp")
    near_index = flip(me, 1)[0]
    far_index = flip(me, 2)[0]
    near = {"fsdp": near_index}
    far = {"fsdp": far_index}
    block = own_value.shape[0]
    heads = keys_out.shape[0]
    slots = mask_ref.shape[0]
    rows = own_grad.shape[0]
    bits = []
    bit = 1
    while bit < group_size:
        bits.append(bit)
        bit *= 2
    meet(
        [near, far, {"fsdp": flip(far_index, 1)[0]}]
        + [{"grp": flip(group, bit)[0]} for bit in bits]
    )

    def remote(src, dst, sends, recvs, at, device):
        return pltpu.make_async_remote_copy(
            src_ref=src,
            dst_ref=dst,
            send_sem=sends.at[at],
            recv_sem=recvs.at[at],
            device_id=device,
            device_id_type=pl.DeviceIdType.MESH,
        )

    def span(start, size):
        return pl.ds(pl.multiple_of(start, 16), size)

    width = own_value.shape[1]
    items = [(own_value, whole_value, 0, width, False), (own_agg, whole_agg, 0, width, False)]
    for n in range(full_qkv.shape[1] // width):
        items.append((own_qkv, whole_qkv, n * width, width, True))
    items.append((own_proj, whole_proj, 0, width, True))
    x_bit = flip(group, 1)[1]
    piece = flip(group, 2)[1] + 2 * flip(group, 4)[1] + 4 * x_bit
    eighth = block // 8

    def weight_copy(n, stage):
        own, whole, start, size, eighths = items[n]
        cols = pl.ds(start, size)

        def region(base, offset, count):
            return whole.at[span(base * block + offset, count), cols]

        if stage == 0:
            return remote(
                own.at[:, cols], region(me, 0, block), send_sem, recv_sem, (n, 0), near
            )
        if stage == 1:
            offset, count = (piece * eighth, eighth) if eighths else (x_bit * (block // 2), block // 2)
            return remote(
                own.at[span(offset, count), cols],
                region(me, offset, count),
                send_sem,
                recv_sem,
                (n, 1),
                far,
            )
        if stage == 2:
            at = region(far_index, piece * eighth, eighth)
            return remote(at, at, send_sem, recv_sem, (n, 2), {"grp": flip(group, 2)[0]})
        if stage == 3:
            at = region(far_index, (piece // 2) * 2 * eighth, 2 * eighth)
            return remote(at, at, send_sem, recv_sem, (n, 3), {"grp": flip(group, 4)[0]})
        if stage == 4:
            at = region(far_index, x_bit * (block // 2), block // 2)
            return remote(at, at, send_sem, recv_sem, (n, 4), {"grp": flip(group, 1)[0]})
        at = region(far_index, 0, block)
        return remote(at, at, send_sem, recv_sem, (n, 5), near)

    def out_copy(n):
        own, whole, start, size, eighths = items[n]
        target = [full_value, full_agg, full_qkv, full_proj][min(n, 2) if n + 1 < len(items) else 3]
        cols = pl.ds(start, size)
        return pltpu.make_async_copy(whole.at[:, cols], target.at[:, cols], local_sem.at[2 + n])

    grad_parts = 4
    part_rows = rows // grad_parts

    def grad_near():
        return remote(own_grad, grads.at[0], small_send, small_recv, 0, near)

    def grad_far(p):
        at = pl.ds(p * part_rows, part_rows)
        return remote(
            own_grad.at[at, :], grads.at[1, at, :], small_send, small_recv, 1 + p, far
        )

    def grad_last(p):
        at = pl.ds(p * part_rows, part_rows)
        return remote(
            grads.at[1, at, :],
            grads.at[2, at, :],
            small_send,
            small_recv,
            1 + grad_parts + p,
            near,
        )

    def grad_out(n):
        if n == 0:
            return pltpu.make_async_copy(grads.at[0], near_grad, local_sem.at[0])
        return pltpu.make_async_copy(grads.at[pl.ds(1, 2)], far_grads, local_sem.at[1])

    base = 1 + 2 * grad_parts

    def table_copy(kind):
        if kind == 0:
            return remote(own_table, tables.at[me], small_send, small_recv, base, near)
        if kind == 1:
            return remote(own_table, tables.at[me], small_send, small_recv, base + 1, far)
        at = tables.at[far_index]
        return remote(at, at, small_send, small_recv, base + 2, near)

    others = [near, far, {"fsdp": flip(far_index, 1)[0]}]

    def query_copy(kind):
        return remote(
            query_part, query_got.at[kind], small_send, small_recv, base + 3 + kind, others[kind]
        )

    def key_copy(kind):
        at = keys_out.at[:, pl.ds(pl.multiple_of(me * block, 128), block)]
        return remote(at, at, small_send, small_recv, base + 6 + kind, others[kind])

    def count_copy(n):
        partner = {"grp": flip(group, bits[n])[0]}
        return remote(
            counts.at[2 * n], counts.at[2 * n + 1], small_send, small_recv, base + 9 + n, partner
        )

    def count_step(n):
        count_copy(n).wait()
        value = counts[2 * n] + counts[2 * n + 1]
        if n + 1 < len(bits):
            counts[2 * n + 2] = value
            count_copy(n + 1).start()
        else:
            count_out[...] = value

    def forward(n, stage):
        weight_copy(n, stage).wait()
        weight_copy(n, 4 if (stage == 1 and not items[n][4]) else stage + 1).start()

    def keep(n):
        weight_copy(n, 0).wait()
        weight_copy(n, 5).wait()
        out_copy(n).start()

    late = list(range(2, len(items)))

    query_part[...] = jnp.dot(own_query[...], query_w[...], preferred_element_type=wide)[:8]
    for kind in range(3):
        query_copy(kind).start()
    for n in late:
        weight_copy(n, 1).start()
    table_copy(1).start()
    table_copy(0).start()
    counts[0] = count_ref[...]
    count_copy(0).start()
    weight_copy(0, 0).start()
    weight_copy(1, 0).start()
    tables[me] = own_table[...]
    whole_value[span(me * block, block), :] = own_value[...]
    whole_agg[span(me * block, block), :] = own_agg[...]
    whole_qkv[span(me * block, block), :] = own_qkv[...]
    whole_proj[span(me * block, block), :] = own_proj[...]
    for kind in range(3):
        query_copy(kind).wait()
    query = query_part[...] + query_got[0] + query_got[1] + query_got[2]
    query_out[...] = query
    lane = lax.broadcasted_iota(jnp.int32, (heads, width), 1)
    head = lax.broadcasted_iota(jnp.int32, (heads, width), 0)
    spread = jnp.where(lane // head_dim == head, jnp.broadcast_to(query[:1], (heads, width)), 0.0)
    own_keys = lax.dot_general(
        spread.astype(low), key_w[...], (((1,), (1,)), ((), ())), preferred_element_type=wide
    ) * (head_dim ** (-0.5))
    keys_out[:, pl.ds(pl.multiple_of(me * block, 128), block)] = own_keys.astype(low)
    for kind in range(3):
        key_copy(kind).start()
    weight_copy(0, 1).start()
    weight_copy(1, 1).start()
    for p in range(grad_parts):
        grad_far(p).start()
    for n in late:
        weight_copy(n, 0).start()
    grad_near().start()
    for n in late:
        forward(n, 1)
    table_copy(0).wait()
    table_copy(1).wait()
    table_copy(2).start()
    for n in late:
        forward(n, 2)
    table_copy(2).wait()
    stacked = tables[...].reshape(select_ref.shape[1], width)
    table = jnp.dot(select_ref[...], stacked, preferred_element_type=wide).astype(low)
    for kind in range(3):
        key_copy(kind).wait()
    coeff_out[...] = lax.dot_general(
        table, keys_out[...], (((1,), (1,)), ((), ())), preferred_element_type=wide
    )
    forward(0, 1)
    forward(2, 3)
    forward(1, 1)
    forward(0, 4)
    forward(2, 4)
    weight_copy(0, 0).wait()
    weight_copy(0, 5).wait()
    out_copy(0).start()
    values = jnp.dot(table, whole_value[...], preferred_element_type=wide)
    table_out[...] = jnp.transpose(values).astype(low)
    forward(3, 3)

    def one_head(h, carry):
        weights = slot_softmax(patch_ref, head_columns(coeff_out, h, slots), mask_ref)
        mixed = mixed_of(patch_ref, weights, table_out.shape[1])
        at = pl.ds(pl.multiple_of(h * head_dim, 16), head_dim)
        heads_out[at, :] = jnp.dot(
            table_out[at, :], mixed, preferred_element_type=wide
        ).astype(low)
        return carry

    half = heads // 2
    lax.fori_loop(0, half, one_head, 0)
    forward(1, 4)
    count_step(0)
    lax.fori_loop(half, heads, one_head, 0)
    keep(2)
    forward(4, 3)
    forward(3, 4)
    keep(1)
    embedded = (
        lax.dot_general(
            heads_out[...], whole_agg[...], (((0,), (0,)), ((), ())), preferred_element_type=wide
        )
        + bias_ref[...]
    )
    embed_out[...] = embedded
    count_step(1)
    grad_far(0).wait()
    grad_last(0).start()
    xhat, inverse = normalise(embedded)
    norm_out[...] = (xhat * gain_ref[...] + shift_ref[...]).astype(low)
    forward(5, 3)
    forward(4, 4)
    keep(3)
    grad_far(1).wait()
    grad_last(1).start()
    keep(4)
    for n in range(2, len(bits)):
        count_step(n)
    forward(5, 4)
    grad_far(2).wait()
    grad_last(2).start()
    keep(5)
    grad_near().wait()
    grad_out(0).start()
    grad_far(3).wait()
    grad_last(3).start()
    for p in range(grad_parts):
        grad_last(p).wait()
    grad_out(1).start()
    for n in range(len(items)):
        out_copy(n).wait()
    for n in range(2):
        grad_out(n).wait()


def prepare(
    group_size, count_rows, own_query, query_w, key_w, own_table, select, own_value, own_agg,
    own_qkv, own_proj, own_grad, patch_rows, slot_mask, bias, gain, shift,
):
    block, width = own_value.shape
    head_dim = width // HEADS
    rows = own_grad.shape[0]
    slots = slot_mask.shape[0]
    size = select.shape[0]
    low = jnp.bfloat16
    wide = jnp.float32
    vmem = pl.BlockSpec(memory_space=pltpu.VMEM)
    hbm = pl.BlockSpec(memory_space=pl.ANY)
    steps = 0
    while 2**steps < group_size:
        steps += 1
    items = 3 + own_qkv.shape[1] // width
    small = 1 + 2 * 4 + 9 + steps

    def shape(dims, kind):
        return jax.ShapeDtypeStruct(dims, kind)

    return pl.pallas_call(
        functools.partial(prepare_kernel, group_size, head_dim),
        in_specs=[vmem] * 16,
        out_specs=[vmem] * 4 + [hbm] * 6 + [vmem] * 5,
        out_shape=[
            shape((8, 128), wide),
            shape((4,) + own_table.shape, low),
            shape((8, width), wide),
            shape((HEADS, width), low),
            shape((4 * block, width), low),
            shape((4 * block, width), low),
            shape((4 * block, own_qkv.shape[1]), low),
            shape((4 * block, width), low),
            shape((rows, width), low),
            shape((2, rows, width), low),
            shape((width, size), low),
            shape((size, HEADS), wide),
            shape((width, rows), low),
            shape((rows, width), wide),
            shape((rows, width), low),
        ],
        scratch_shapes=[
            pltpu.VMEM((8, width), wide),
            pltpu.VMEM((3, 8, width), wide),
            pltpu.VMEM((2 * steps, 8, 128), wide),
            pltpu.VMEM((4 * block, width), low),
            pltpu.VMEM((4 * block, width), low),
            pltpu.VMEM((4 * block, own_qkv.shape[1]), low),
            pltpu.VMEM((4 * block, width), low),
            pltpu.VMEM((3, rows, width), low),
            pltpu.SemaphoreType.DMA((items, 6)),
            pltpu.SemaphoreType.DMA((items, 6)),
            pltpu.SemaphoreType.DMA((small,)),
            pltpu.SemaphoreType.DMA((small,)),
            pltpu.SemaphoreType.DMA((2 + items,)),
        ],
        compiler_params=pltpu.CompilerParams(
            collective_id=3, has_side_effects=True, vmem_limit_bytes=VMEM_LIMIT
        ),
        cost_estimate=pl.CostEstimate(
            flops=8 * size * rows * width, bytes_accessed=100_000_000, transcendentals=0
        ),
        name="prepare",
    )(
        count_rows, own_query, query_w, key_w, own_table, select, own_value, own_agg,
        own_qkv, own_proj, own_grad, patch_rows, slot_mask, bias, gain, shift,
    )


def aggregate_back_kernel(
    patch_ref, coeff_ref, mask_ref, table_ref, select_ref, heads_ref, scale_ref,
    sum_ref, coeff_sum_ref, patch_grad_ref, table_s, coeff_s,
):
    slots = mask_ref.shape[0]
    head_dim = table_ref.shape[0] // HEADS
    size = table_ref.shape[1]
    wide = jnp.float32
    low = jnp.bfloat16
    patch_grad_ref[...] = jnp.zeros_like(patch_grad_ref)
    coeff_s[...] = jnp.zeros_like(coeff_s)
    lane = lax.broadcasted_iota(jnp.int32, (slots, HEADS), 1)

    def one_head(h, carry):
        columns = head_columns(coeff_ref, h, slots)
        weights = slot_softmax(patch_ref, columns, mask_ref)
        mixed = mixed_of(patch_ref, weights, size)
        at = pl.ds(pl.multiple_of(h * head_dim, 16), head_dim)
        heads_grad = heads_ref[at, :]
        table_s[at, :] = (
            lax.dot_general(
                heads_grad, mixed, (((1,), (1,)), ((), ())), preferred_element_type=wide
            )
            * scale_ref[0]
        ).astype(low)
        mixed_grad = lax.dot_general(
            table_ref[at, :], heads_grad, (((0,), (0,)), ((), ())), preferred_element_type=wide
        )
        parts = [mixed_grad[k * slots : (k + 1) * slots] for k in range(PIX + 1)]
        values = [patch_ref[k].astype(wide) for k in range(PIX)]
        weights_grad = parts[PIX]
        for k in range(PIX):
            weights_grad = weights_grad + parts[k] * values[k]
        mean_grad = jnp.sum(weights * weights_grad, axis=0, keepdims=True)
        scores_grad = weights * (weights_grad - mean_grad)
        for k in range(PIX + 1):
            value = scores_grad * values[k] if k < PIX else scores_grad
            column = jnp.sum(value, axis=1, keepdims=True)
            rows = slice(k * slots, (k + 1) * slots)
            coeff_s[rows, :] = coeff_s[rows, :] + jnp.where(lane == h, column, 0.0)
        for k in range(PIX):
            patch_grad_ref[k] += scale_ref[1] * (parts[k] * weights + scores_grad * columns[k])
        return carry

    lax.fori_loop(0, HEADS, one_head, 0)
    sum_ref[...] = lax.dot_general(
        select_ref[...], table_s[...], (((0,), (1,)), ((), ())), preferred_element_type=wide
    ).astype(low)
    coeff_sum_ref[...] = scale_ref[0] * lax.dot_general(
        select_ref[...].astype(wide),
        coeff_s[...],
        (((0,), (0,)), ((), ())),
        preferred_element_type=wide,
        precision=exact_mode,
    )


def aggregate_back(patch_rows, coeffs, slot_mask, table_values, select, heads_grad, scales):
    rows = patch_rows.shape[2]
    width, size = table_values.shape
    slots = slot_mask.shape[0]
    vmem = pl.BlockSpec(memory_space=pltpu.VMEM)
    return pl.pallas_call(
        aggregate_back_kernel,
        in_specs=[vmem] * 6 + [pl.BlockSpec(memory_space=pltpu.SMEM)],
        out_specs=[vmem] * 3,
        out_shape=[
            jax.ShapeDtypeStruct((select.shape[1], width), jnp.bfloat16),
            jax.ShapeDtypeStruct((select.shape[1], HEADS), jnp.float32),
            jax.ShapeDtypeStruct((PIX, slots, rows), jnp.float32),
        ],
        scratch_shapes=[
            pltpu.VMEM((width, size), jnp.bfloat16),
            pltpu.VMEM((size, HEADS), jnp.float32),
        ],
        compiler_params=pltpu.CompilerParams(vmem_limit_bytes=VMEM_LIMIT),
        cost_estimate=pl.CostEstimate(
            flops=16 * size * rows * width,
            bytes_accessed=8 * width * rows,
            transcendentals=HEADS * slots * rows,
        ),
        name="aggregate_back",
    )(patch_rows, coeffs, slot_mask, table_values, select, heads_grad, scales)


def lane_half(rows, pair, head_dim):
    lane = lax.broadcasted_iota(jnp.int32, (rows, 2 * head_dim), 1)
    return (lane // head_dim) == pair


def attend_kernel(
    head_dim, valid_ref, rows_ref, weight_ref, q_ref, kv_ref, out_ref, log_ref, sum_s, top_s, total_s, send_sem, recv_sem
):
    me = lax.axis_index("fsdp")
    near = {"fsdp": flip(me, 1)[0]}
    far = {"fsdp": flip(me, 2)[0]}
    wide = jnp.float32
    low = jnp.bfloat16
    rows, width = rows_ref.shape
    lanes = 2 * head_dim
    pairs = width // lanes
    scale = head_dim ** (-0.5)
    meet([near, far])

    def copy(kind, i, source, target, device):
        return pltpu.make_async_remote_copy(
            src_ref=kv_ref.at[source, i],
            dst_ref=kv_ref.at[target, i],
            send_sem=send_sem.at[kind, i],
            recv_sem=recv_sem.at[kind, i],
            device_id=device,
            device_id_type=pl.DeviceIdType.MESH,
        )

    def near_copy(i):
        return copy(0, i, 0, 1, near)

    def far_copy(i):
        return copy(1, i, 0, 2, far)

    def last_copy(i):
        return copy(2, i, 2, 3, near)

    entry = rows_ref[...]
    for g in range(pairs // 2):
        for part in range(2):
            start = (part + 1) * width + g * 2 * lanes
            value = jnp.dot(
                entry, weight_ref[:, start : start + 2 * lanes], preferred_element_type=wide
            ).astype(low)
            kv_ref[0, 2 * g, part] = value[:, :lanes]
            kv_ref[0, 2 * g + 1, part] = value[:, lanes:]
        for i in (2 * g, 2 * g + 1):
            far_copy(i).start()
            near_copy(i).start()
    for g in range(pairs // 2):
        start = g * 2 * lanes
        value = jnp.dot(
            entry, weight_ref[:, start : start + 2 * lanes], preferred_element_type=wide
        ).astype(low)
        value = value * jnp.asarray(scale, low)
        q_ref[2 * g] = value[:, :lanes]
        q_ref[2 * g + 1] = value[:, lanes:]

    tile = min(rows, 256)

    def attend(i, shards, first):
        for start in range(0, rows, tile):
            at = slice(start, start + tile)
            block = q_ref[i, at, :]
            sums, tops, totals = [], [], []
            for pair in range(2):
                query = jnp.where(lane_half(tile, pair, head_dim), block, jnp.zeros_like(block))
                logits = []
                for j in shards:
                    raw = lax.dot_general(
                        query, kv_ref[j, i, 0], (((1,), (1,)), ((), ())), preferred_element_type=wide
                    )
                    place = lax.broadcasted_iota(jnp.int32, (1, rows), 1)
                    logits.append(jnp.where(place < valid_ref[j], raw, masked_out))
                top = functools.reduce(
                    jnp.maximum, [jnp.max(part, axis=1, keepdims=True) for part in logits]
                )
                sum_now, total_now = 0.0, 0.0
                for j, part in zip(shards, logits):
                    terms = jnp.exp(part - top)
                    total_now = total_now + jnp.sum(terms, axis=1, keepdims=True)
                    sum_now = sum_now + jnp.dot(
                        terms.astype(low), kv_ref[j, i, 1], preferred_element_type=wide
                    )
                sums.append(sum_now)
                tops.append(top)
                totals.append(total_now)
            side = lane_half(tile, 0, head_dim)
            sum_now = jnp.where(side, sums[0], sums[1])
            top = jnp.where(side, tops[0], tops[1])
            total_now = jnp.where(side, totals[0], totals[1])
            if not first:
                old_top = top_s[at, :]
                new_top = jnp.maximum(top, old_top)
                mine = jnp.exp(top - new_top)
                others = jnp.exp(old_top - new_top)
                sum_now = sum_now * mine + sum_s[at, :] * others
                total_now = total_now * mine + total_s[at, :] * others
                top = new_top
            sum_s[at, :] = sum_now
            top_s[at, :] = top
            total_s[at, :] = total_now

    def one_pair(i, carry):
        near_copy(i).wait_recv()
        attend(i, (0, 1), True)
        far_copy(i).wait_recv()
        last_copy(i).start()
        attend(i, (2,), False)
        last_copy(i).wait_recv()
        attend(i, (3,), False)
        out_ref[i] = (sum_s[...] / total_s[...]).astype(low)
        log_ref[i] = top_s[...] + jnp.log(total_s[...])
        return carry

    lax.fori_loop(0, pairs, one_pair, 0)

    def end(i, carry):
        near_copy(i).wait_send()
        far_copy(i).wait_send()
        last_copy(i).wait_send()
        return carry

    lax.fori_loop(0, pairs, end, 0)


def attend(rows_in, weight, valid):
    rows, width = rows_in.shape
    head_dim = width // HEADS
    lanes = 2 * head_dim
    pairs = HEADS // 2
    whole = pl.BlockSpec(memory_space=pltpu.VMEM)
    low = jnp.bfloat16
    wide = jnp.float32
    return pl.pallas_call(
        functools.partial(attend_kernel, head_dim),
        in_specs=[pl.BlockSpec(memory_space=pltpu.SMEM), whole, whole],
        out_specs=[whole] * 4,
        out_shape=[
            jax.ShapeDtypeStruct((pairs, rows, lanes), low),
            jax.ShapeDtypeStruct((4, pairs, 2, rows, lanes), low),
            jax.ShapeDtypeStruct((pairs, rows, lanes), low),
            jax.ShapeDtypeStruct((pairs, rows, lanes), wide),
        ],
        scratch_shapes=[
            pltpu.VMEM((rows, lanes), wide),
            pltpu.VMEM((rows, lanes), wide),
            pltpu.VMEM((rows, lanes), wide),
            pltpu.SemaphoreType.DMA((3, pairs)),
            pltpu.SemaphoreType.DMA((3, pairs)),
        ],
        compiler_params=pltpu.CompilerParams(
            collective_id=1, has_side_effects=True, vmem_limit_bytes=VMEM_LIMIT
        ),
        cost_estimate=pl.CostEstimate(
            flops=64 * rows * rows * width, bytes_accessed=100_000_000, transcendentals=0
        ),
        name="attend",
    )(valid, rows_in, weight)


def attend_back_kernel(
    head_dim, valid_ref, q_ref, kv_ref, grad_ref, out_ref, log_ref, *refs
):
    result_ref, q_sum, own_s, far_s, last_s, near_s, got_far, got_last, got_near, log_rows, dot_rows = refs[:11]
    send_sem, recv_sem = refs[11:]
    me = lax.axis_index("fsdp")
    near = {"fsdp": flip(me, 1)[0]}
    far = {"fsdp": flip(me, 2)[0]}
    wide = jnp.float32
    low = jnp.bfloat16
    pairs, rows, lanes = q_ref.shape
    width = pairs * lanes
    scale = head_dim ** (-0.5)
    meet([near, far])

    def copy(kind, i, source, target, device):
        return pltpu.make_async_remote_copy(
            src_ref=source.at[i],
            dst_ref=target.at[i],
            send_sem=send_sem.at[kind, i],
            recv_sem=recv_sem.at[kind, i],
            device_id=device,
            device_id_type=pl.DeviceIdType.MESH,
        )

    def last_copy(i):
        return copy(0, i, last_s, got_last, near)

    def near_copy(i):
        return copy(1, i, near_s, got_near, near)

    def far_copy(i):
        return copy(2, i, far_s, got_far, far)

    def back(i, shards, targets):
        query = q_ref[i]
        grad = grad_ref[i]
        q_grad = None
        k_sums = [None, None]
        v_sums = [None, None]

        def plus(old, new):
            return new if old is None else old + new

        for pair in range(2):
            side = lane_half(rows, pair, head_dim)
            log_row = log_rows[i, pair : pair + 1, :]
            dot_row = dot_rows[i, pair : pair + 1, :]
            one_query = jnp.where(side, query, jnp.zeros_like(query))
            one_grad = jnp.where(side, grad, jnp.zeros_like(grad))
            for n, j in enumerate(shards):
                key = kv_ref[j, i, 0]
                one_key = jnp.where(side, key, jnp.zeros_like(key))
                raw = lax.dot_general(
                    key, one_query, (((1,), (1,)), ((), ())), preferred_element_type=wide
                )
                place = lax.broadcasted_iota(jnp.int32, raw.shape, 0)
                probs = jnp.exp(jnp.where(place < valid_ref[j], raw - log_row, masked_out))
                probs_grad = lax.dot_general(
                    kv_ref[j, i, 1], one_grad, (((1,), (1,)), ((), ())), preferred_element_type=wide
                )
                raw_grad = (probs * (probs_grad - dot_row)).astype(low)
                v_sums[n] = plus(
                    v_sums[n], jnp.dot(probs.astype(low), one_grad, preferred_element_type=wide)
                )
                k_sums[n] = plus(
                    k_sums[n], jnp.dot(raw_grad, one_query, preferred_element_type=wide)
                )
                q_grad = plus(
                    q_grad,
                    lax.dot_general(
                        raw_grad, one_key, (((0,), (0,)), ((), ())), preferred_element_type=wide
                    ),
                )
        for n, target in enumerate(targets):
            target[i, 0] = k_sums[n].astype(target.dtype)
            target[i, 1] = v_sums[n].astype(target.dtype)
        return q_grad

    def send_far(i):
        last_copy(i).wait()
        far_s[i] = (far_s[i].astype(wide) + got_last[i].astype(wide)).astype(low)
        far_copy(i).start()

    def first_loop(i, carry):
        log_t = jnp.transpose(log_ref[i])
        dots = jnp.transpose(grad_ref[i].astype(wide) * out_ref[i].astype(wide))
        for pair in range(2):
            here = slice(pair * head_dim, (pair + 1) * head_dim)
            log_rows[i, pair : pair + 1, :] = log_t[pair * head_dim : pair * head_dim + 1, :]
            dot_rows[i, pair : pair + 1, :] = jnp.sum(dots[here, :], axis=0, keepdims=True)
        q_sum[i] = back(i, (3, 2), (last_s, far_s))
        last_copy(i).start()

        @pl.when(i > 0)
        def _():
            send_far(i - 1)

        return carry

    lax.fori_loop(0, pairs, first_loop, 0)
    send_far(pairs - 1)

    def second_loop(i, carry):
        q_sum[i] = (q_sum[i] + back(i, (1, 0), (near_s, own_s))) * scale
        near_copy(i).start()
        return carry

    lax.fori_loop(0, pairs, second_loop, 0)
    for i in range(pairs):
        near_copy(i).wait()
        far_copy(i).wait()
        at = slice(i * lanes, (i + 1) * lanes)
        result_ref[:, at] = q_sum[i].astype(low)
        for part in range(2):
            value = own_s[i, part] + got_near[i, part].astype(wide) + got_far[i, part].astype(wide)
            start = (part + 1) * width + i * lanes
            result_ref[:, start : start + lanes] = value.astype(low)


def attend_back(queries, key_values, grad, out, logs, valid):
    pairs, rows, lanes = queries.shape
    head_dim = lanes // 2
    whole = pl.BlockSpec(memory_space=pltpu.VMEM)
    low = jnp.bfloat16
    wide = jnp.float32
    slab = (pairs, 2, rows, lanes)
    return pl.pallas_call(
        functools.partial(attend_back_kernel, head_dim),
        in_specs=[pl.BlockSpec(memory_space=pltpu.SMEM)] + [whole] * 5,
        out_specs=whole,
        out_shape=jax.ShapeDtypeStruct((rows, 3 * pairs * lanes), low),
        scratch_shapes=[
            pltpu.VMEM((pairs, rows, lanes), wide),
            pltpu.VMEM(slab, wide),
            pltpu.VMEM(slab, low),
            pltpu.VMEM(slab, low),
            pltpu.VMEM(slab, low),
            pltpu.VMEM(slab, low),
            pltpu.VMEM(slab, low),
            pltpu.VMEM(slab, low),
            pltpu.VMEM((pairs, 8, rows), wide),
            pltpu.VMEM((pairs, 8, rows), wide),
            pltpu.SemaphoreType.DMA((3, pairs)),
            pltpu.SemaphoreType.DMA((3, pairs)),
        ],
        compiler_params=pltpu.CompilerParams(
            collective_id=2, has_side_effects=True, vmem_limit_bytes=VMEM_LIMIT
        ),
        cost_estimate=pl.CostEstimate(
            flops=160 * rows * rows * pairs * lanes, bytes_accessed=100_000_000, transcendentals=0
        ),
        name="attend_back",
    )(valid, queries, key_values, grad, out, logs)


def feed_kernel(*refs):
    (
        share_ref, context_ref, proj_ref, embed_ref, own_grad, near_grad, far_grads, up_ref,
        down_ref, bias_ref, proj_bias, gain_ref, shift_ref,
    ) = refs[:13]
    (
        middle_ref, out_ref, down_total, up_total, middle_grad, attended, context_grad, vectors,
    ) = refs[13:21]
    entry, gelu_s, pre_s, own_back, near_s, last_s, far_s, got_near, got_last, got_far = refs[21:31]
    send_sem, recv_sem = refs[31:]
    wide = jnp.float32
    low = jnp.bfloat16
    me = lax.axis_index("fsdp")
    near = {"fsdp": flip(me, 1)[0]}
    far = {"fsdp": flip(me, 2)[0]}
    rows, width = embed_ref.shape
    hidden = up_ref.shape[1]
    tile = rows // 2
    pairs, _, lanes = context_grad.shape
    meet([near, far])

    def span(t):
        return pl.ds(t * tile, tile)

    def copy(kind, t, src, dst, device):
        return pltpu.make_async_remote_copy(
            src_ref=src.at[span(t), :],
            dst_ref=dst.at[span(t), :],
            send_sem=send_sem.at[kind, t],
            recv_sem=recv_sem.at[kind, t],
            device_id=device,
            device_id_type=pl.DeviceIdType.MESH,
        )

    def rows_near(t):
        return copy(0, t, entry.at[0], entry.at[1], near)

    def rows_far(t):
        return copy(1, t, entry.at[0], entry.at[2], far)

    def rows_last(t):
        return copy(2, t, entry.at[2], entry.at[3], near)

    def back_near(t):
        return copy(3, t, near_s, got_near, near)

    def back_last(t):
        return copy(4, t, last_s, got_last, near)

    def back_far(t):
        return copy(5, t, far_s, got_far, far)

    def grad_rows(s, t):
        if s == 0:
            return own_grad[span(t), :]
        if s == 1:
            return near_grad[span(t), :]
        return far_grads[s - 2, span(t), :]

    def feed(s, t, target):
        rows_in = entry[s, span(t), :]
        pre_act = jnp.dot(rows_in, up_ref[...], preferred_element_type=wide) + bias_ref[...]
        cdf = 0.5 * (1.0 + lax.erf(pre_act * 0.7071067811865476))
        density = jnp.exp(-0.5 * pre_act * pre_act) * 0.3989422804014327
        gelu = (pre_act * cdf).astype(low)
        gelu_s[s, span(t), :] = gelu
        act_grad = lax.dot_general(
            grad_rows(s, t), down_ref[...], (((1,), (1,)), ((), ())), preferred_element_type=wide
        )
        pre_grad = act_grad * (cdf + pre_act * density)
        pre_low = pre_grad.astype(low)
        pre_s[s, span(t), :] = pre_low
        vectors[4:5, :] += jnp.sum(pre_low.astype(wide), axis=0, keepdims=True)
        out_ref[s, span(t), :] = jnp.dot(
            gelu, down_ref[...], preferred_element_type=wide
        ).astype(low)
        target[span(t), :] = lax.dot_general(
            pre_low, up_ref[...], (((1,), (1,)), ((), ())), preferred_element_type=wide
        ).astype(target.dtype)

    vectors[...] = jnp.zeros_like(vectors)
    for t in range(2):
        middle = (
            embed_ref[span(t), :]
            + jnp.dot(context_ref[span(t), :], proj_ref[...], preferred_element_type=wide)
            + proj_bias[...]
        )
        middle_ref[span(t), :] = middle
        xhat, inverse = normalise(middle)
        entry[0, span(t), :] = (xhat * gain_ref[...] + shift_ref[...]).astype(low)
        rows_far(t).start()
        rows_near(t).start()
    for t in range(2):
        feed(0, t, own_back)
    for t in range(2):
        rows_near(t).wait()
        feed(1, t, near_s)
        back_near(t).start()

    for t in range(2):
        rows_far(t).wait()
        rows_last(t).start()
        feed(2, t, far_s)
        rows_last(t).wait()
        feed(3, t, last_s)
        back_last(t).start()
        if t > 0:
            add_last(t - 1, back_last, back_far, far_s, got_last, span)
    add_last(1, back_last, back_far, far_s, got_last, span)

    block = min(hidden, 256)
    grads = [own_grad[...], near_grad[...], far_grads[0], far_grads[1]]
    for start in range(0, hidden, block):
        value = 0.0
        for s in range(4):
            value = value + lax.dot_general(
                gelu_s[s, :, start : start + block],
                grads[s],
                (((0,), (0,)), ((), ())),
                preferred_element_type=wide,
            )
        down_total[start : start + block, :] = (value * share_ref[0]).astype(low)
    for start in range(0, width, block):
        value = 0.0
        for s in range(4):
            value = value + lax.dot_general(
                entry[s, :, start : start + block],
                pre_s[s],
                (((0,), (0,)), ((), ())),
                preferred_element_type=wide,
            )
        up_total[start : start + block, :] = (value * share_ref[0]).astype(low)

    for t in range(2):
        back_near(t).wait()
        back_far(t).wait()
        at = span(t)
        grad = own_back[at, :] + got_near[at, :].astype(wide) + got_far[at, :].astype(wide)
        xhat, inverse = normalise(middle_ref[at, :])
        vectors[0:1, :] += jnp.sum(grad * xhat, axis=0, keepdims=True)
        vectors[1:2, :] += jnp.sum(grad, axis=0, keepdims=True)
        upstream = own_grad[at, :].astype(wide)
        vectors[3:4, :] += jnp.sum(upstream, axis=0, keepdims=True)
        value = upstream + norm_back(grad, xhat, inverse, gain_ref[...])
        middle_grad[at, :] = value
        value_low = value.astype(low)
        attended[at, :] = value_low
        vectors[2:3, :] += jnp.sum(value_low.astype(wide), axis=0, keepdims=True)
        back = lax.dot_general(
            value_low, proj_ref[...], (((1,), (1,)), ((), ())), preferred_element_type=wide
        ).astype(low)
        for i in range(pairs):
            context_grad[i, at, :] = back[:, i * lanes : (i + 1) * lanes]


def add_last(t, back_last, back_far, far_s, got_last, span):
    back_last(t).wait()
    at = span(t)
    value = far_s[at, :].astype(jnp.float32) + got_last[at, :].astype(jnp.float32)
    far_s[at, :] = value.astype(jnp.bfloat16)
    back_far(t).start()


def feed(
    share, context, proj, embedded, own_grad, near_grad, far_grads, up, down, bias, proj_bias, gain, shift
):
    rows, width = embedded.shape
    hidden = up.shape[1]
    pairs = HEADS // 2
    low = jnp.bfloat16
    wide = jnp.float32
    vmem = pl.BlockSpec(memory_space=pltpu.VMEM)
    flat = (rows, width)

    def shape(dims, kind):
        return jax.ShapeDtypeStruct(dims, kind)

    return pl.pallas_call(
        feed_kernel,
        in_specs=[pl.BlockSpec(memory_space=pltpu.SMEM)] + [vmem] * 12,
        out_specs=[vmem] * 8,
        out_shape=[
            shape(flat, wide),
            shape((4,) + flat, low),
            shape((hidden, width), low),
            shape((width, hidden), low),
            shape(flat, wide),
            shape(flat, low),
            shape((pairs, rows, width // pairs), low),
            shape((8, width), wide),
        ],
        scratch_shapes=[
            pltpu.VMEM((4,) + flat, low),
            pltpu.VMEM((4, rows, hidden), low),
            pltpu.VMEM((4, rows, hidden), low),
            pltpu.VMEM(flat, wide),
            pltpu.VMEM(flat, low),
            pltpu.VMEM(flat, low),
            pltpu.VMEM(flat, low),
            pltpu.VMEM(flat, low),
            pltpu.VMEM(flat, low),
            pltpu.VMEM(flat, low),
            pltpu.SemaphoreType.DMA((6, 2)),
            pltpu.SemaphoreType.DMA((6, 2)),
        ],
        compiler_params=pltpu.CompilerParams(
            collective_id=4, has_side_effects=True, vmem_limit_bytes=VMEM_LIMIT
        ),
        cost_estimate=pl.CostEstimate(
            flops=48 * rows * width * hidden, bytes_accessed=100_000_000, transcendentals=0
        ),
        name="feed",
    )(
        share, context, proj, embedded, own_grad, near_grad, far_grads, up, down, bias,
        proj_bias, gain, shift,
    )


def total_kernel(group_size, widths, share_ref, *refs):
    pairs = [(refs[2 * i], refs[2 * i + 1]) for i in range(3)]
    bundle_ref = refs[6]
    outs = refs[7:10]
    bundle_out = refs[10]
    send1, recv1, own1, send2, recv2, hold, halves, done, full, send_sem, recv_sem = refs[11:]
    me = lax.axis_index("fsdp")
    group = lax.axis_index("grp")
    core_partner, core = flip(me, 1)
    far_partner, far = flip(me, 2)
    quarter = own1.shape[2]
    wide = jnp.float32
    low = jnp.bfloat16

    steps = []
    size, bit, offset = quarter, 1, 0
    while bit < group_size:
        partner, bit_set = flip(group, bit)
        halving = size >= 64
        steps.append((partner, bit_set, halving, size, offset))
        if halving:
            size = size // 2
            offset = offset + bit_set * size
        bit *= 2
    halvings = [i for i, step in enumerate(steps) if step[2]]

    meet([{"fsdp": core_partner}, {"fsdp": far_partner}] + [{"grp": step[0]} for step in steps])

    chunks = [(None, None, None, 0, bundle_ref.shape[1])]
    for (left, right), out in zip(pairs, outs):
        for start in range(0, right.shape[1], widths):
            chunks.append((left, right, out, start, widths))

    def copy(stage, c, src, dst, device):
        return pltpu.make_async_remote_copy(
            src_ref=src,
            dst_ref=dst,
            send_sem=send_sem.at[stage, c],
            recv_sem=recv_sem.at[stage, c],
            device_id=device,
            device_id_type=pl.DeviceIdType.MESH,
        )

    def span(start, size):
        return pl.ds(pl.multiple_of(start, 16), size)

    def columns(c):
        return pl.ds(0, chunks[c][4])

    def core_copy(c):
        cols = columns(c)
        return copy(
            0, c, send1.at[c, :, :, cols], recv1.at[c, :, :, cols], {"fsdp": core_partner}
        )

    def far_copy(c):
        cols = columns(c)
        return copy(1, c, send2.at[c, :, cols], recv2.at[c, :, cols], {"fsdp": far_partner})

    def step_copy(i, c):
        partner, bit_set, halving, size, offset = steps[i]
        cols = columns(c)
        if halving:
            size = size // 2
            offset = offset + (1 - bit_set) * size
        src = hold.at[c, span(offset, size), cols]
        dst = halves[i].at[c, :, cols]
        return copy(2 + i, c, src, dst, {"grp": partner})

    def back_copy(i, c):
        partner, bit_set, halving, size, offset = steps[i]
        size = size // 2
        offset = offset + bit_set * size
        at = done.at[c, span(offset, size), columns(c)]
        return copy(2 + len(steps) + i, c, at, at, {"grp": partner})

    def begin(c):
        left, right, out, start, width = chunks[c]
        cols = columns(c)

        def part(q):
            rows = span(q * quarter, quarter)
            if left is None:
                return bundle_ref[rows, :]
            value = jnp.dot(
                left[rows, :], right[:, start : start + width], preferred_element_type=wide
            )
            return (value * share_ref[0]).astype(low)

        for y in range(2):
            send1[c, y, :, cols] = part(2 * y + 1 - core)
        core_copy(c).start()
        for y in range(2):
            own1[c, y, :, cols] = part(2 * y + core)

    def after_core(c):
        cols = columns(c)
        core_copy(c).wait()
        value = own1[c, 1 - far, :, cols].astype(wide) + recv1[c, 1 - far, :, cols].astype(wide)
        send2[c, :, cols] = value.astype(low)
        far_copy(c).start()

    def after_far(c):
        cols = columns(c)
        far_copy(c).wait()
        value = own1[c, far, :, cols].astype(wide) + recv1[c, far, :, cols].astype(wide)
        hold[c, :, cols] = (value + recv2[c, :, cols].astype(wide)).astype(low)
        step_copy(0, c).start()

    def after_step(i, c):
        cols = columns(c)
        step_copy(i, c).wait()
        partner, bit_set, halving, size, offset = steps[i]
        if halving:
            size = size // 2
            offset = offset + bit_set * size
        at = span(offset, size)
        value = hold[c, at, cols].astype(wide) + halves[i][c, :, cols].astype(wide)
        if i + 1 < len(steps):
            hold[c, at, cols] = value.astype(low)
            step_copy(i + 1, c).start()
        else:
            done[c, at, cols] = value.astype(low)
            back_copy(halvings[-1], c).start()

    def after_back(k, c):
        back_copy(halvings[k], c).wait()
        if k > 0:
            back_copy(halvings[k - 1], c).start()
        else:
            left, right, out, start, width = chunks[c]
            if out is None:
                full[me] = done[c, :, columns(c)]
                bundle_core().start()
            else:
                out[:, start : start + width] = done[c].astype(wide)

    last = 2 + 2 * len(steps)

    def bundle_core():
        return copy(last, 0, full.at[me], full.at[me], {"fsdp": core_partner})

    def bundle_far():
        at = full.at[pl.ds(me - core, 2)]
        return copy(last, 1, at, at, {"fsdp": far_partner})

    def finish_core(c):
        bundle_core().wait()
        bundle_far().start()

    def finish_far(c):
        bundle_far().wait()
        for q in range(4):
            bundle_out[q * quarter : (q + 1) * quarter, :] = full[q].astype(wide)

    stages = [begin, after_core, after_far]
    stages += [functools.partial(after_step, i) for i in range(len(steps))]
    stages += [functools.partial(after_back, k) for k in reversed(range(len(halvings)))]
    order = [1, 0] + list(range(2, len(stages)))
    extra = [finish_core, finish_far]
    for t in range(len(chunks) + len(stages) - 1):
        for s in order:
            if 0 <= t - s < len(chunks):
                stages[s](t - s)
        if 0 <= t - len(stages) < len(extra):
            extra[t - len(stages)](0)


def total(group_size, share, qkv_pair, agg_pair, proj_pair, bundle):
    pairs = [qkv_pair, agg_pair, proj_pair]
    width = qkv_pair[0].shape[0]
    quarter = width // 4
    widths = 512
    count = 1 + sum(right.shape[1] // widths for left, right in pairs)
    steps = 0
    halves = []
    size = quarter
    while 2**steps < group_size:
        if size >= 64:
            size //= 2
        halves.append(pltpu.VMEM((count, size, widths), jnp.bfloat16))
        steps += 1
    low = jnp.bfloat16
    whole = pl.BlockSpec(memory_space=pltpu.VMEM)
    scratch = [
        pltpu.VMEM((count, 2, quarter, widths), low),
        pltpu.VMEM((count, 2, quarter, widths), low),
        pltpu.VMEM((count, 2, quarter, widths), low),
        pltpu.VMEM((count, quarter, widths), low),
        pltpu.VMEM((count, quarter, widths), low),
        pltpu.VMEM((count, quarter, widths), low),
        halves,
        pltpu.VMEM((count, quarter, widths), low),
        pltpu.VMEM((4, quarter, bundle.shape[1]), low),
        pltpu.SemaphoreType.DMA((3 + 2 * steps, count)),
        pltpu.SemaphoreType.DMA((3 + 2 * steps, count)),
    ]
    return pl.pallas_call(
        functools.partial(total_kernel, group_size, widths),
        in_specs=[pl.BlockSpec(memory_space=pltpu.SMEM)] + [whole] * 7,
        out_specs=[whole] * 4,
        out_shape=[
            jax.ShapeDtypeStruct((quarter, right.shape[1]), jnp.float32) for left, right in pairs
        ]
        + [jax.ShapeDtypeStruct(bundle.shape, jnp.float32)],
        scratch_shapes=scratch,
        compiler_params=pltpu.CompilerParams(
            collective_id=0, has_side_effects=True, vmem_limit_bytes=VMEM_LIMIT
        ),
        cost_estimate=pl.CostEstimate(
            flops=sum(2 * left.size * right.shape[1] for left, right in pairs),
            bytes_accessed=200_000_000,
            transcendentals=0,
        ),
        name="total",
    )(share, *[array for pair in pairs for array in pair], bundle)


def on_device(
    patches,
    patch_counts,
    var_present,
    item_dataset,
    var_ids,
    patch_weight,
    var_embed,
    agg_query,
    query_weight,
    key_weight,
    value_weight,
    agg_proj,
    agg_bias,
    norm1_gain,
    norm1_shift,
    qkv_weight,
    proj_weight,
    proj_bias,
    norm2_gain,
    norm2_shift,
    up_weight,
    up_bias,
    down_weight,
    down_bias,
    out_grad,
):
    low = jnp.bfloat16
    wide = jnp.float32
    rows = patches.shape[2]
    me = lax.axis_index("fsdp")
    group_count = lax.axis_size("grp")
    width = proj_weight.shape[1]
    head_dim = width // HEADS
    own_width = width // 4
    own_vars = patch_weight.shape[0]
    score_scale = head_dim ** (-0.5)

    item_count = patch_counts[0]
    own_valid = me * rows + jnp.arange(rows, dtype=jnp.int32) < item_count
    shard_valid = jnp.clip(
        item_count - (me ^ jnp.arange(4, dtype=jnp.int32)) * rows, 0, rows
    ).astype(jnp.int32)
    down_grad = jnp.where(own_valid[:, None], out_grad, jnp.zeros_like(out_grad))

    slot_vars = lax.dynamic_index_in_dim(var_ids, item_dataset[0], 0, keepdims=False)
    part_size = -(-(PIX + 1) * own_vars // 16) * 16
    size = 4 * part_size
    slot_row = jnp.arange(size, dtype=jnp.int32)
    slot_var = jnp.pad(jnp.tile(slot_vars, PIX + 1), (0, size - (PIX + 1) * VTOT))
    place = (slot_var // own_vars) * part_size + (slot_row // VTOT) * own_vars + slot_var % own_vars
    select = (
        (place[:, None] == jnp.arange(size, dtype=jnp.int32)[None, :])
        & (slot_row < (PIX + 1) * VTOT)[:, None]
    ).astype(low)
    own_table = jnp.concatenate(
        [
            patch_weight.transpose(1, 0, 2).reshape(own_vars * PIX, width),
            var_embed,
            jnp.zeros((part_size - (PIX + 1) * own_vars, width), low),
        ],
        axis=0,
    )
    own_query = lax.dynamic_slice_in_dim(agg_query, me * own_width, own_width, 0)
    patch_rows = patches.transpose(1, 0, 2)
    slot_mask = jnp.where(var_present[0] > 0, 0.0, masked_out).astype(wide)[:, None]
    (
        count_rows,
        tables,
        query_rows,
        key_query,
        full_value,
        full_agg_proj,
        full_qkv,
        full_proj,
        near_down_grad,
        far_grads,
        table_values,
        coeffs,
        heads_t,
        embedded,
        normed1,
    ) = prepare(
        group_count,
        jnp.full((8, 128), item_count.astype(wide)),
        jnp.broadcast_to(own_query[None, :], (16, own_width)),
        query_weight,
        key_weight,
        own_table,
        select,
        value_weight,
        agg_proj,
        qkv_weight,
        proj_weight,
        down_grad,
        patch_rows,
        slot_mask,
        agg_bias[None, :],
        norm1_gain[None, :],
        norm1_shift[None, :],
    )
    count_share = item_count.astype(wide) / count_rows[0, 0]
    query_vec = query_rows[0].astype(low)
    table_rows = tables.reshape(size, width)
    own_columns = lax.dynamic_slice_in_dim(table_rows, me * own_width, own_width, 1)
    key_table = product(own_columns, key_weight)
    key_table = key_table + swap(key_table.astype(low), "fsdp", 1).astype(wide)
    key_table = key_table + swap(key_table.astype(low), "fsdp", 2).astype(wide)


    queries, key_values, context_pairs, logs = attend(normed1, full_qkv, shard_valid)
    context = context_pairs.transpose(1, 0, 2).reshape(rows, width)
    (
        middle,
        out_parts,
        down_weight_part,
        up_weight_part,
        middle_grad,
        attended_grad,
        context_grad,
        feed_vectors,
    ) = feed(
        count_share[None],
        context,
        full_proj,
        embedded,
        down_grad,
        near_down_grad,
        far_grads,
        up_weight,
        down_weight,
        up_bias.astype(wide)[None, :],
        proj_bias[None, :],
        norm2_gain[None, :],
        norm2_shift[None, :],
    )
    down_weight_grad = lax.psum(down_weight_part, "grp").astype(wide)
    up_weight_grad = lax.psum(up_weight_part, "grp").astype(wide)
    out_got = swap(jnp.stack([out_parts[1], out_parts[3]]), "fsdp", 1)
    out_far = swap((out_parts[2].astype(wide) + out_got[1].astype(wide)).astype(low), "fsdp", 2)
    down_sum = out_parts[0].astype(wide) + out_got[0].astype(wide) + out_far.astype(wide)
    output = (middle + down_sum + down_bias).astype(low)

    qkv_grad = attend_back(queries, key_values, context_grad, context_pairs, logs, shard_valid)
    xhat1, inverse1 = normalise(embedded)
    normed1_grad = right_product(qkv_grad, full_qkv)
    norm1_gain_grad = jnp.sum(normed1_grad * xhat1, axis=0)
    norm1_shift_grad = jnp.sum(normed1_grad, axis=0)
    embedded_grad = (middle_grad + norm_back(normed1_grad, xhat1, inverse1, norm1_gain)).astype(low)
    agg_bias_grad = column_sums(embedded_grad)
    heads_grad = right_product(full_agg_proj, embedded_grad).astype(low)
    scales = jnp.stack([count_share, group_count * count_share])
    table_sum, coeff_sum, patch_grad = aggregate_back(
        patch_rows, coeffs, slot_mask, table_values, select, heads_grad, scales
    )
    patches_grad = patch_grad.transpose(1, 0, 2)

    vectors = [agg_bias_grad, norm1_gain_grad, norm1_shift_grad]
    up_bias_rows = lax.dynamic_update_slice_in_dim(
        jnp.zeros((4, width), wide), feed_vectors[4:5], me, 0
    )
    coeff_rows = coeff_sum.T.reshape(-1, width)
    spare = part_size - (PIX + 1) * own_vars
    extras = jnp.concatenate(
        [
            coeff_rows,
            jnp.concatenate([jnp.stack(vectors), feed_vectors[:4], up_bias_rows]) * count_share,
        ],
        axis=0,
    )
    extras = jnp.pad(extras, ((0, 4 * spare - extras.shape[0]), (0, 0))).astype(low)
    bundle = jnp.concatenate(
        [
            table_sum.reshape(4, part_size, width)[:, : part_size - spare],
            extras.reshape(4, spare, width),
        ],
        axis=1,
    ).reshape(size, width)
    qkv_weight_grad, agg_proj_grad, proj_weight_grad, bundle = total(
        group_count,
        count_share[None],
        (normed1.T, qkv_grad),
        (heads_t, embedded_grad),
        (context.T, attended_grad),
        bundle.reshape(width, -1),
    )
    table_total = bundle.reshape(size, width)
    extras = table_total.reshape(4, part_size, width)[:, part_size - spare :].reshape(-1, width)
    at = coeff_rows.shape[0]
    coeff_total = extras[:at].reshape(HEADS, size)
    vector_total = extras[at : at + 7]
    at += 7
    up_bias_total = lax.dynamic_slice_in_dim(extras, at + me, 1, 0)[0]
    vector_own = lax.dynamic_slice_in_dim(vector_total, me * own_width, own_width, 1)

    value_weight_grad = left_product(own_columns, table_total.astype(low))
    key_query_grad = jnp.dot(coeff_total, own_columns.astype(wide), precision=exact_mode)
    key_weight_grad = (
        key_query_grad.T[:, :, None]
        * query_vec.astype(wide).reshape(1, HEADS, head_dim)
        * score_scale
    ).reshape(own_width, width)
    query_grad = (
        jnp.einsum(
            "hx,xhj->hj",
            coeff_total,
            key_table.reshape(size, HEADS, head_dim),
            precision=exact_mode,
        ).reshape(width)
        * score_scale
    )
    query_weight_grad = own_query.astype(wide)[:, None] * query_grad[None, :]
    agg_query_grad = jnp.dot(
        query_weight.astype(wide), query_grad, precision=exact_mode
    )
    own_totals = lax.dynamic_slice_in_dim(table_total, me * part_size, part_size, 0)
    own_coeffs = lax.dynamic_slice_in_dim(coeff_total, me * part_size, part_size, 1)
    var_grads = right_product(own_totals.astype(low), full_value) + lax.dot_general(
        own_coeffs, key_query.astype(wide), (((0,), (0,)), ((), ())), precision=exact_mode
    )
    var_grads = var_grads[: (PIX + 1) * own_vars].reshape(PIX + 1, own_vars, width)
    patch_weight_grad = var_grads[:PIX].transpose(1, 0, 2)
    var_embed_grad = var_grads[PIX]
    return (
        output,
        patches_grad,
        patch_weight_grad,
        var_embed_grad,
        agg_query_grad,
        query_weight_grad,
        key_weight_grad,
        value_weight_grad,
        agg_proj_grad,
        vector_own[0],
        vector_own[1],
        vector_own[2],
        qkv_weight_grad,
        proj_weight_grad,
        vector_own[5],
        vector_own[3],
        vector_own[4],
        up_weight_grad,
        up_bias_total,
        down_weight_grad,
        vector_own[6],
    )


def solution(mesh):
    shard = P("fsdp")
    shard_rows = P("fsdp", None)
    return jax.shard_map(
        on_device,
        mesh=mesh,
        in_specs=(
            P(None, None, ("grp", "fsdp")),
            P("grp"),
            P("grp", None),
            P("grp"),
            P(),
            P("fsdp", None, None),
            shard_rows,
            P(),
            shard_rows,
            shard_rows,
            shard_rows,
            shard_rows,
            P(),
            P(),
            P(),
            shard_rows,
            shard_rows,
            P(),
            P(),
            P(),
            P(None, "fsdp"),
            shard,
            shard_rows,
            P(),
            P(("grp", "fsdp"), None),
        ),
        out_specs=(
            P(("grp", "fsdp"), None),
            P(None, None, ("grp", "fsdp")),
            P("fsdp", None, None),
            shard_rows,
            shard,
            shard_rows,
            shard_rows,
            shard_rows,
            shard_rows,
            shard,
            shard,
            shard,
            shard_rows,
            shard_rows,
            shard,
            shard,
            shard,
            P(None, "fsdp"),
            shard,
            shard_rows,
            shard,
        ),
        check_vma=False,
    )
```

```python
import functools

import jax
import jax.numpy as jnp
from jax import lax
from jax.experimental import pallas as pl
from jax.experimental.pallas import tpu as pltpu
from jax.sharding import PartitionSpec as P

HEADS = 16
VTOT = 48
PIX = 4

exact_mode = lax.Precision.HIGHEST
masked_out = -1e30
VMEM_LIMIT = 56 * 1024 * 1024


def swap(value, axis, bit):
    size = lax.axis_size(axis)
    return lax.ppermute(value, axis, [(i, i ^ bit) for i in range(size)])


def product(left_side, right_side):
    return jnp.dot(left_side, right_side, preferred_element_type=jnp.float32)


def left_product(left_side, right_side):
    return lax.dot_general(
        left_side, right_side, (((0,), (0,)), ((), ())), preferred_element_type=jnp.float32
    )


def right_product(left_side, right_side):
    return lax.dot_general(
        left_side, right_side, (((1,), (1,)), ((), ())), preferred_element_type=jnp.float32
    )


def column_sums(values_in):
    return jnp.sum(values_in.astype(jnp.float32), axis=0)


def flip(index, bit):
    bit_set = (index // bit) % 2
    return index + bit - 2 * bit * bit_set, bit_set


def meet(partners):
    barrier = pltpu.get_barrier_semaphore()
    for partner in partners:
        pl.semaphore_signal(
            barrier, inc=1, device_id=partner, device_id_type=pl.DeviceIdType.MESH
        )
    pl.semaphore_wait(barrier, len(partners))


def normalise(values_in):
    row_mean = jnp.mean(values_in, axis=-1, keepdims=True)
    centred = values_in - row_mean
    spread = jnp.mean(centred * centred, axis=-1, keepdims=True)
    inverse = lax.rsqrt(spread + 1e-05)
    return centred * inverse, inverse


def norm_back(grad, xhat, inverse, gain_vec):
    scaled = grad * gain_vec
    first = jnp.mean(scaled, axis=-1, keepdims=True)
    second = jnp.mean(scaled * xhat, axis=-1, keepdims=True)
    return (scaled - first - xhat * second) * inverse


def slot_softmax(patch_ref, columns, mask_ref):
    scores = columns[PIX] + mask_ref[...]
    for k in range(PIX):
        scores = scores + patch_ref[k].astype(jnp.float32) * columns[k]
    top = jnp.max(scores, axis=0, keepdims=True)
    terms = jnp.exp(scores - top)
    return terms / jnp.sum(terms, axis=0, keepdims=True)


def mixed_of(patch_ref, weights, rows):
    parts = [
        (weights * patch_ref[k].astype(jnp.float32)).astype(jnp.bfloat16) for k in range(PIX)
    ]
    parts.append(weights.astype(jnp.bfloat16))
    used = weights.shape[0] * (PIX + 1)
    if rows > used:
        parts.append(jnp.zeros((rows - used, weights.shape[1]), jnp.bfloat16))
    return jnp.concatenate(parts, axis=0)


def head_columns(coeff_ref, head, slots):
    lane = lax.broadcasted_iota(jnp.int32, (slots, coeff_ref.shape[1]), 1)
    return [
        jnp.sum(
            jnp.where(lane == head, coeff_ref[k * slots : (k + 1) * slots, :], 0.0),
            axis=1,
            keepdims=True,
        )
        for k in range(PIX + 1)
    ]


def prepare_kernel(group_size, head_dim, *refs):
    (
        count_ref, own_query, query_w, key_w, own_table, select_ref, own_value, own_agg,
        own_qkv, own_proj, own_grad, patch_ref, mask_ref, bias_ref, gain_ref, shift_ref,
    ) = refs[:16]
    (
        count_out, tables, query_out, keys_out, full_value, full_agg, full_qkv, full_proj,
        near_grad, far_grads, table_out, coeff_out, heads_out, embed_out, norm_out,
    ) = refs[16:31]
    query_part, query_got, counts = refs[31:34]
    whole_value, whole_agg, whole_qkv, whole_proj, grads = refs[34:39]
    send_sem, recv_sem, small_send, small_recv, local_sem = refs[39:]
    wide = jnp.float32
    low = jnp.bfloat16
    me = lax.axis_index("fsdp")
    group = lax.axis_index("grp")
    near_index = flip(me, 1)[0]
    far_index = flip(me, 2)[0]
    near = {"fsdp": near_index}
    far = {"fsdp": far_index}
    block = own_value.shape[0]
    heads = keys_out.shape[0]
    slots = mask_ref.shape[0]
    rows = own_grad.shape[0]
    bits = []
    bit = 1
    while bit < group_size:
        bits.append(bit)
        bit *= 2
    meet(
        [near, far, {"fsdp": flip(far_index, 1)[0]}]
        + [{"grp": flip(group, bit)[0]} for bit in bits]
    )

    def remote(src, dst, sends, recvs, at, device):
        return pltpu.make_async_remote_copy(
            src_ref=src,
            dst_ref=dst,
            send_sem=sends.at[at],
            recv_sem=recvs.at[at],
            device_id=device,
            device_id_type=pl.DeviceIdType.MESH,
        )

    def span(start, size):
        return pl.ds(pl.multiple_of(start, 16), size)

    width = own_value.shape[1]
    items = [(own_value, whole_value, 0, width, False), (own_agg, whole_agg, 0, width, False)]
    for n in range(full_qkv.shape[1] // width):
        items.append((own_qkv, whole_qkv, n * width, width, True))
    items.append((own_proj, whole_proj, 0, width, True))
    x_bit = flip(group, 1)[1]
    piece = flip(group, 2)[1] + 2 * flip(group, 4)[1] + 4 * x_bit
    eighth = block // 8

    def weight_copy(n, stage):
        own, whole, start, size, eighths = items[n]
        cols = pl.ds(start, size)

        def region(base, offset, count):
            return whole.at[span(base * block + offset, count), cols]

        if stage == 0:
            return remote(
                own.at[:, cols], region(me, 0, block), send_sem, recv_sem, (n, 0), near
            )
        if stage == 1:
            offset, count = (piece * eighth, eighth) if eighths else (x_bit * (block // 2), block // 2)
            return remote(
                own.at[span(offset, count), cols],
                region(me, offset, count),
                send_sem,
                recv_sem,
                (n, 1),
                far,
            )
        if stage == 2:
            at = region(far_index, piece * eighth, eighth)
            return remote(at, at, send_sem, recv_sem, (n, 2), {"grp": flip(group, 2)[0]})
        if stage == 3:
            at = region(far_index, (piece // 2) * 2 * eighth, 2 * eighth)
            return remote(at, at, send_sem, recv_sem, (n, 3), {"grp": flip(group, 4)[0]})
        if stage == 4:
            at = region(far_index, x_bit * (block // 2), block // 2)
            return remote(at, at, send_sem, recv_sem, (n, 4), {"grp": flip(group, 1)[0]})
        at = region(far_index, 0, block)
        return remote(at, at, send_sem, recv_sem, (n, 5), near)

    def out_copy(n):
        own, whole, start, size, eighths = items[n]
        target = [full_value, full_agg, full_qkv, full_proj][min(n, 2) if n + 1 < len(items) else 3]
        cols = pl.ds(start, size)
        return pltpu.make_async_copy(whole.at[:, cols], target.at[:, cols], local_sem.at[2 + n])

    grad_parts = 4
    part_rows = rows // grad_parts

    def grad_near():
        return remote(own_grad, grads.at[0], small_send, small_recv, 0, near)

    def grad_far(p):
        at = pl.ds(p * part_rows, part_rows)
        return remote(
            own_grad.at[at, :], grads.at[1, at, :], small_send, small_recv, 1 + p, far
        )

    def grad_last(p):
        at = pl.ds(p * part_rows, part_rows)
        return remote(
            grads.at[1, at, :],
            grads.at[2, at, :],
            small_send,
            small_recv,
            1 + grad_parts + p,
            near,
        )

    def grad_out(n):
        if n == 0:
            return pltpu.make_async_copy(grads.at[0], near_grad, local_sem.at[0])
        return pltpu.make_async_copy(grads.at[pl.ds(1, 2)], far_grads, local_sem.at[1])

    base = 1 + 2 * grad_parts

    def table_copy(kind):
        if kind == 0:
            return remote(own_table, tables.at[me], small_send, small_recv, base, near)
        if kind == 1:
            return remote(own_table, tables.at[me], small_send, small_recv, base + 1, far)
        at = tables.at[far_index]
        return remote(at, at, small_send, small_recv, base + 2, near)

    others = [near, far, {"fsdp": flip(far_index, 1)[0]}]

    def query_copy(kind):
        return remote(
            query_part, query_got.at[kind], small_send, small_recv, base + 3 + kind, others[kind]
        )

    def key_copy(kind):
        at = keys_out.at[:, pl.ds(pl.multiple_of(me * block, 128), block)]
        return remote(at, at, small_send, small_recv, base + 6 + kind, others[kind])

    def count_copy(n):
        partner = {"grp": flip(group, bits[n])[0]}
        return remote(
            counts.at[2 * n], counts.at[2 * n + 1], small_send, small_recv, base + 9 + n, partner
        )

    def count_step(n):
        count_copy(n).wait()
        value = counts[2 * n] + counts[2 * n + 1]
        if n + 1 < len(bits):
            counts[2 * n + 2] = value
            count_copy(n + 1).start()
        else:
            count_out[...] = value

    def forward(n, stage):
        weight_copy(n, stage).wait()
        weight_copy(n, 4 if (stage == 1 and not items[n][4]) else stage + 1).start()

    def keep(n):
        weight_copy(n, 0).wait()
        weight_copy(n, 5).wait()
        out_copy(n).start()

    late = list(range(2, len(items)))

    query_part[...] = jnp.dot(own_query[...], query_w[...], preferred_element_type=wide)[:8]
    for kind in range(3):
        query_copy(kind).start()
    weight_copy(0, 1).start()
    for n in late:
        weight_copy(n, 1).start()
    table_copy(1).start()
    table_copy(0).start()
    weight_copy(0, 0).start()
    counts[0] = count_ref[...]
    count_copy(0).start()
    tables[me] = own_table[...]
    whole_value[span(me * block, block), :] = own_value[...]
    for kind in range(3):
        query_copy(kind).wait()
    query = query_part[...] + query_got[0] + query_got[1] + query_got[2]
    query_out[...] = query
    lane = lax.broadcasted_iota(jnp.int32, (heads, width), 1)
    head = lax.broadcasted_iota(jnp.int32, (heads, width), 0)
    spread = jnp.where(lane // head_dim == head, jnp.broadcast_to(query[:1], (heads, width)), 0.0)
    own_keys = lax.dot_general(
        spread.astype(low), key_w[...], (((1,), (1,)), ((), ())), preferred_element_type=wide
    ) * (head_dim ** (-0.5))
    keys_out[:, pl.ds(pl.multiple_of(me * block, 128), block)] = own_keys.astype(low)
    for kind in range(3):
        key_copy(kind).start()
    weight_copy(1, 1).start()
    whole_agg[span(me * block, block), :] = own_agg[...]
    whole_qkv[span(me * block, block), :] = own_qkv[...]
    whole_proj[span(me * block, block), :] = own_proj[...]
    forward(0, 1)
    for n in late:
        forward(n, 1)
    forward(0, 4)
    forward(2, 2)
    forward(3, 2)
    table_copy(0).wait()
    table_copy(1).wait()
    table_copy(2).start()
    for p in range(grad_parts):
        grad_far(p).start()
    forward(1, 1)
    weight_copy(1, 0).start()
    table_copy(2).wait()
    stacked = tables[...].reshape(select_ref.shape[1], width)
    table = jnp.dot(select_ref[...], stacked, preferred_element_type=wide).astype(low)
    for kind in range(3):
        key_copy(kind).wait()
    coeff_out[...] = lax.dot_general(
        table, keys_out[...], (((1,), (1,)), ((), ())), preferred_element_type=wide
    )
    weight_copy(0, 0).wait()
    weight_copy(0, 5).wait()
    out_copy(0).start()
    values = jnp.dot(table, whole_value[...], preferred_element_type=wide)
    table_out[...] = jnp.transpose(values).astype(low)

    def one_head(h, carry):
        weights = slot_softmax(patch_ref, head_columns(coeff_out, h, slots), mask_ref)
        mixed = mixed_of(patch_ref, weights, table_out.shape[1])
        at = pl.ds(pl.multiple_of(h * head_dim, 16), head_dim)
        heads_out[at, :] = jnp.dot(
            table_out[at, :], mixed, preferred_element_type=wide
        ).astype(low)
        return carry

    half = heads // 2
    forward(2, 3)
    forward(4, 2)
    for n in late:
        weight_copy(n, 0).start()
    lax.fori_loop(0, half, one_head, 0)
    forward(1, 4)
    forward(3, 3)
    forward(5, 2)
    grad_near().start()
    lax.fori_loop(half, heads, one_head, 0)
    keep(1)
    embedded = (
        lax.dot_general(
            heads_out[...], whole_agg[...], (((0,), (0,)), ((), ())), preferred_element_type=wide
        )
        + bias_ref[...]
    )
    embed_out[...] = embedded
    count_step(0)
    forward(2, 4)
    grad_far(0).wait()
    grad_last(0).start()
    xhat, inverse = normalise(embedded)
    norm_out[...] = (xhat * gain_ref[...] + shift_ref[...]).astype(low)
    forward(4, 3)
    keep(2)
    forward(3, 4)
    count_step(1)
    grad_far(1).wait()
    grad_last(1).start()
    forward(5, 3)
    keep(3)
    forward(4, 4)
    for n in range(2, len(bits)):
        count_step(n)
    grad_far(2).wait()
    grad_last(2).start()
    keep(4)
    forward(5, 4)
    grad_near().wait()
    grad_out(0).start()
    grad_far(3).wait()
    grad_last(3).start()
    keep(5)
    for p in range(grad_parts):
        grad_last(p).wait()
    grad_out(1).start()
    for n in range(len(items)):
        out_copy(n).wait()
    for n in range(2):
        grad_out(n).wait()


def prepare(
    group_size, count_rows, own_query, query_w, key_w, own_table, select, own_value, own_agg,
    own_qkv, own_proj, own_grad, patch_rows, slot_mask, bias, gain, shift,
):
    block, width = own_value.shape
    head_dim = width // HEADS
    rows = own_grad.shape[0]
    slots = slot_mask.shape[0]
    size = select.shape[0]
    low = jnp.bfloat16
    wide = jnp.float32
    vmem = pl.BlockSpec(memory_space=pltpu.VMEM)
    hbm = pl.BlockSpec(memory_space=pl.ANY)
    steps = 0
    while 2**steps < group_size:
        steps += 1
    items = 3 + own_qkv.shape[1] // width
    small = 1 + 2 * 4 + 9 + steps

    def shape(dims, kind):
        return jax.ShapeDtypeStruct(dims, kind)

    return pl.pallas_call(
        functools.partial(prepare_kernel, group_size, head_dim),
        in_specs=[vmem] * 16,
        out_specs=[vmem] * 4 + [hbm] * 6 + [vmem] * 5,
        out_shape=[
            shape((8, 128), wide),
            shape((4,) + own_table.shape, low),
            shape((8, width), wide),
            shape((HEADS, width), low),
            shape((4 * block, width), low),
            shape((4 * block, width), low),
            shape((4 * block, own_qkv.shape[1]), low),
            shape((4 * block, width), low),
            shape((rows, width), low),
            shape((2, rows, width), low),
            shape((width, size), low),
            shape((size, HEADS), wide),
            shape((width, rows), low),
            shape((rows, width), wide),
            shape((rows, width), low),
        ],
        scratch_shapes=[
            pltpu.VMEM((8, width), wide),
            pltpu.VMEM((3, 8, width), wide),
            pltpu.VMEM((2 * steps, 8, 128), wide),
            pltpu.VMEM((4 * block, width), low),
            pltpu.VMEM((4 * block, width), low),
            pltpu.VMEM((4 * block, own_qkv.shape[1]), low),
            pltpu.VMEM((4 * block, width), low),
            pltpu.VMEM((3, rows, width), low),
            pltpu.SemaphoreType.DMA((items, 6)),
            pltpu.SemaphoreType.DMA((items, 6)),
            pltpu.SemaphoreType.DMA((small,)),
            pltpu.SemaphoreType.DMA((small,)),
            pltpu.SemaphoreType.DMA((2 + items,)),
        ],
        compiler_params=pltpu.CompilerParams(
            collective_id=3, has_side_effects=True, vmem_limit_bytes=VMEM_LIMIT
        ),
        cost_estimate=pl.CostEstimate(
            flops=8 * size * rows * width, bytes_accessed=100_000_000, transcendentals=0
        ),
        name="prepare",
    )(
        count_rows, own_query, query_w, key_w, own_table, select, own_value, own_agg,
        own_qkv, own_proj, own_grad, patch_rows, slot_mask, bias, gain, shift,
    )


def lane_half(rows, pair, head_dim):
    lane = lax.broadcasted_iota(jnp.int32, (rows, 2 * head_dim), 1)
    return (lane // head_dim) == pair


def attend_kernel(
    head_dim, valid_ref, rows_ref, weight_ref, q_ref, kv_out, out_ref, log_ref, kv_ref, weight_s, sum_s, top_s, total_s, send_sem, recv_sem, fetch_sem, keep_sem
):
    me = lax.axis_index("fsdp")
    near = {"fsdp": flip(me, 1)[0]}
    far = {"fsdp": flip(me, 2)[0]}
    wide = jnp.float32
    low = jnp.bfloat16
    rows, width = rows_ref.shape
    lanes = 2 * head_dim
    pairs = width // lanes
    scale = head_dim ** (-0.5)
    groups = pairs // 2

    def fetch(part, g):
        at = pl.ds(part * width + g * 2 * lanes, 2 * lanes)
        return pltpu.make_async_copy(
            weight_ref.at[:, at], weight_s.at[:, at], fetch_sem.at[part, g]
        )

    def keep(i):
        return pltpu.make_async_copy(kv_ref.at[:, i], kv_out.at[:, i], keep_sem.at[i])

    for g in range(groups):
        fetch(1, g).start()
        fetch(2, g).start()
    for g in range(groups):
        fetch(0, g).start()
    meet([near, far])

    def copy(kind, i, source, target, device):
        return pltpu.make_async_remote_copy(
            src_ref=kv_ref.at[source, i],
            dst_ref=kv_ref.at[target, i],
            send_sem=send_sem.at[kind, i],
            recv_sem=recv_sem.at[kind, i],
            device_id=device,
            device_id_type=pl.DeviceIdType.MESH,
        )

    def near_copy(i):
        return copy(0, i, 0, 1, near)

    def far_copy(i):
        return copy(1, i, 0, 2, far)

    def last_copy(i):
        return copy(2, i, 2, 3, near)

    entry = rows_ref[...]
    for g in range(groups):
        for part in range(2):
            start = (part + 1) * width + g * 2 * lanes
            fetch(part + 1, g).wait()
            value = jnp.dot(
                entry, weight_s[:, start : start + 2 * lanes], preferred_element_type=wide
            ).astype(low)
            kv_ref[0, 2 * g, part] = value[:, :lanes]
            kv_ref[0, 2 * g + 1, part] = value[:, lanes:]
        for i in (2 * g, 2 * g + 1):
            far_copy(i).start()
            near_copy(i).start()
    for g in range(groups):
        start = g * 2 * lanes
        fetch(0, g).wait()
        value = jnp.dot(
            entry, weight_s[:, start : start + 2 * lanes], preferred_element_type=wide
        ).astype(low)
        value = value * jnp.asarray(scale, low)
        q_ref[2 * g] = value[:, :lanes]
        q_ref[2 * g + 1] = value[:, lanes:]

    tile = min(rows, 256)

    def attend(i, shards, first):
        for start in range(0, rows, tile):
            at = slice(start, start + tile)
            block = q_ref[i, at, :]
            sums, tops, totals = [], [], []
            for pair in range(2):
                query = jnp.where(lane_half(tile, pair, head_dim), block, jnp.zeros_like(block))
                logits = []
                for j in shards:
                    raw = lax.dot_general(
                        query, kv_ref[j, i, 0], (((1,), (1,)), ((), ())), preferred_element_type=wide
                    )
                    place = lax.broadcasted_iota(jnp.int32, (1, rows), 1)
                    logits.append(jnp.where(place < valid_ref[j], raw, masked_out))
                top = functools.reduce(
                    jnp.maximum, [jnp.max(part, axis=1, keepdims=True) for part in logits]
                )
                sum_now, total_now = 0.0, 0.0
                for j, part in zip(shards, logits):
                    terms = jnp.exp(part - top)
                    total_now = total_now + jnp.sum(terms, axis=1, keepdims=True)
                    sum_now = sum_now + jnp.dot(
                        terms.astype(low), kv_ref[j, i, 1], preferred_element_type=wide
                    )
                sums.append(sum_now)
                tops.append(top)
                totals.append(total_now)
            side = lane_half(tile, 0, head_dim)
            sum_now = jnp.where(side, sums[0], sums[1])
            top = jnp.where(side, tops[0], tops[1])
            total_now = jnp.where(side, totals[0], totals[1])
            if not first:
                old_top = top_s[at, :]
                new_top = jnp.maximum(top, old_top)
                mine = jnp.exp(top - new_top)
                others = jnp.exp(old_top - new_top)
                sum_now = sum_now * mine + sum_s[at, :] * others
                total_now = total_now * mine + total_s[at, :] * others
                top = new_top
            sum_s[at, :] = sum_now
            top_s[at, :] = top
            total_s[at, :] = total_now

    def one_pair(i, carry):
        near_copy(i).wait_recv()
        attend(i, (0, 1), True)
        far_copy(i).wait_recv()
        last_copy(i).start()
        attend(i, (2,), False)
        last_copy(i).wait_recv()
        attend(i, (3,), False)
        keep(i).start()
        out_ref[i] = (sum_s[...] / total_s[...]).astype(low)
        log_ref[i] = top_s[...] + jnp.log(total_s[...])
        return carry

    lax.fori_loop(0, pairs, one_pair, 0)

    def end(i, carry):
        near_copy(i).wait_send()
        far_copy(i).wait_send()
        last_copy(i).wait_send()
        keep(i).wait()
        return carry

    lax.fori_loop(0, pairs, end, 0)


def attend(rows_in, weight, valid):
    rows, width = rows_in.shape
    head_dim = width // HEADS
    lanes = 2 * head_dim
    pairs = HEADS // 2
    whole = pl.BlockSpec(memory_space=pltpu.VMEM)
    hbm = pl.BlockSpec(memory_space=pl.ANY)
    low = jnp.bfloat16
    wide = jnp.float32
    return pl.pallas_call(
        functools.partial(attend_kernel, head_dim),
        in_specs=[pl.BlockSpec(memory_space=pltpu.SMEM), whole, hbm],
        out_specs=[whole, hbm, whole, whole],
        out_shape=[
            jax.ShapeDtypeStruct((pairs, rows, lanes), low),
            jax.ShapeDtypeStruct((4, pairs, 2, rows, lanes), low),
            jax.ShapeDtypeStruct((pairs, rows, lanes), low),
            jax.ShapeDtypeStruct((pairs, rows, lanes), wide),
        ],
        scratch_shapes=[
            pltpu.VMEM((4, pairs, 2, rows, lanes), low),
            pltpu.VMEM(weight.shape, low),
            pltpu.VMEM((rows, lanes), wide),
            pltpu.VMEM((rows, lanes), wide),
            pltpu.VMEM((rows, lanes), wide),
            pltpu.SemaphoreType.DMA((3, pairs)),
            pltpu.SemaphoreType.DMA((3, pairs)),
            pltpu.SemaphoreType.DMA((3, pairs // 2)),
            pltpu.SemaphoreType.DMA((pairs,)),
        ],
        compiler_params=pltpu.CompilerParams(
            collective_id=1, has_side_effects=True, vmem_limit_bytes=VMEM_LIMIT
        ),
        cost_estimate=pl.CostEstimate(
            flops=64 * rows * rows * width, bytes_accessed=100_000_000, transcendentals=0
        ),
        name="attend",
    )(valid, rows_in, weight)


def attend_back_kernel(
    head_dim, valid_ref, q_ref, kv_in, grad_ref, out_ref, log_ref, *refs
):
    result_ref, q_sum, own_s, far_s, last_s, near_s, got_far, got_last, got_near, log_rows, dot_rows = refs[:11]
    send_sem, recv_sem, kv_ref, fetch_sem = refs[11:]
    me = lax.axis_index("fsdp")
    near = {"fsdp": flip(me, 1)[0]}
    far = {"fsdp": flip(me, 2)[0]}
    wide = jnp.float32
    low = jnp.bfloat16
    pairs, rows, lanes = q_ref.shape

    def fetch(half, i):
        at = pl.ds(2 * half, 2)
        return pltpu.make_async_copy(kv_in.at[at, i], kv_ref.at[at, i], fetch_sem.at[half, i])

    for half in (1, 0):
        for i in range(pairs):
            fetch(half, i).start()
    width = pairs * lanes
    scale = head_dim ** (-0.5)
    meet([near, far])

    def copy(kind, i, source, target, device):
        return pltpu.make_async_remote_copy(
            src_ref=source.at[i],
            dst_ref=target.at[i],
            send_sem=send_sem.at[kind, i],
            recv_sem=recv_sem.at[kind, i],
            device_id=device,
            device_id_type=pl.DeviceIdType.MESH,
        )

    def last_copy(i):
        return copy(0, i, last_s, got_last, near)

    def near_copy(i):
        return copy(1, i, near_s, got_near, near)

    def far_copy(i):
        return copy(2, i, far_s, got_far, far)

    def back(i, shards, targets):
        query = q_ref[i]
        grad = grad_ref[i]
        q_grad = None
        k_sums = [None, None]
        v_sums = [None, None]

        def plus(old, new):
            return new if old is None else old + new

        for pair in range(2):
            side = lane_half(rows, pair, head_dim)
            log_row = log_rows[i, pair : pair + 1, :]
            dot_row = dot_rows[i, pair : pair + 1, :]
            one_query = jnp.where(side, query, jnp.zeros_like(query))
            one_grad = jnp.where(side, grad, jnp.zeros_like(grad))
            for n, j in enumerate(shards):
                key = kv_ref[j, i, 0]
                one_key = jnp.where(side, key, jnp.zeros_like(key))
                raw = lax.dot_general(
                    key, one_query, (((1,), (1,)), ((), ())), preferred_element_type=wide
                )
                place = lax.broadcasted_iota(jnp.int32, raw.shape, 0)
                probs = jnp.exp(jnp.where(place < valid_ref[j], raw - log_row, masked_out))
                probs_grad = lax.dot_general(
                    kv_ref[j, i, 1], one_grad, (((1,), (1,)), ((), ())), preferred_element_type=wide
                )
                raw_grad = (probs * (probs_grad - dot_row)).astype(low)
                v_sums[n] = plus(
                    v_sums[n], jnp.dot(probs.astype(low), one_grad, preferred_element_type=wide)
                )
                k_sums[n] = plus(
                    k_sums[n], jnp.dot(raw_grad, one_query, preferred_element_type=wide)
                )
                q_grad = plus(
                    q_grad,
                    lax.dot_general(
                        raw_grad, one_key, (((0,), (0,)), ((), ())), preferred_element_type=wide
                    ),
                )
        for n, target in enumerate(targets):
            target[i, 0] = k_sums[n].astype(target.dtype)
            target[i, 1] = v_sums[n].astype(target.dtype)
        return q_grad

    def send_far(i):
        last_copy(i).wait()
        far_s[i] = (far_s[i].astype(wide) + got_last[i].astype(wide)).astype(low)
        far_copy(i).start()

    def first_loop(i, carry):
        log_t = jnp.transpose(log_ref[i])
        dots = jnp.transpose(grad_ref[i].astype(wide) * out_ref[i].astype(wide))
        for pair in range(2):
            here = slice(pair * head_dim, (pair + 1) * head_dim)
            log_rows[i, pair : pair + 1, :] = log_t[pair * head_dim : pair * head_dim + 1, :]
            dot_rows[i, pair : pair + 1, :] = jnp.sum(dots[here, :], axis=0, keepdims=True)
        fetch(1, i).wait()
        q_sum[i] = back(i, (3, 2), (last_s, far_s))
        last_copy(i).start()

        @pl.when(i > 0)
        def _():
            send_far(i - 1)

        return carry

    lax.fori_loop(0, pairs, first_loop, 0)
    send_far(pairs - 1)

    def second_loop(i, carry):
        fetch(0, i).wait()
        q_sum[i] = (q_sum[i] + back(i, (1, 0), (near_s, own_s))) * scale
        near_copy(i).start()
        return carry

    lax.fori_loop(0, pairs, second_loop, 0)
    for i in range(pairs):
        near_copy(i).wait()
        far_copy(i).wait()
        at = slice(i * lanes, (i + 1) * lanes)
        result_ref[:, at] = q_sum[i].astype(low)
        for part in range(2):
            value = own_s[i, part] + got_near[i, part].astype(wide) + got_far[i, part].astype(wide)
            start = (part + 1) * width + i * lanes
            result_ref[:, start : start + lanes] = value.astype(low)


def attend_back(queries, key_values, grad, out, logs, valid):
    pairs, rows, lanes = queries.shape
    head_dim = lanes // 2
    whole = pl.BlockSpec(memory_space=pltpu.VMEM)
    low = jnp.bfloat16
    wide = jnp.float32
    slab = (pairs, 2, rows, lanes)
    return pl.pallas_call(
        functools.partial(attend_back_kernel, head_dim),
        in_specs=[
            pl.BlockSpec(memory_space=pltpu.SMEM),
            whole,
            pl.BlockSpec(memory_space=pl.ANY),
            whole,
            whole,
            whole,
        ],
        out_specs=whole,
        out_shape=jax.ShapeDtypeStruct((rows, 3 * pairs * lanes), low),
        scratch_shapes=[
            pltpu.VMEM((pairs, rows, lanes), wide),
            pltpu.VMEM(slab, wide),
            pltpu.VMEM(slab, low),
            pltpu.VMEM(slab, low),
            pltpu.VMEM(slab, low),
            pltpu.VMEM(slab, low),
            pltpu.VMEM(slab, low),
            pltpu.VMEM(slab, low),
            pltpu.VMEM((pairs, 8, rows), wide),
            pltpu.VMEM((pairs, 8, rows), wide),
            pltpu.SemaphoreType.DMA((3, pairs)),
            pltpu.SemaphoreType.DMA((3, pairs)),
            pltpu.VMEM(key_values.shape, low),
            pltpu.SemaphoreType.DMA((2, pairs)),
        ],
        compiler_params=pltpu.CompilerParams(
            collective_id=2, has_side_effects=True, vmem_limit_bytes=VMEM_LIMIT
        ),
        cost_estimate=pl.CostEstimate(
            flops=160 * rows * rows * pairs * lanes, bytes_accessed=100_000_000, transcendentals=0
        ),
        name="attend_back",
    )(valid, queries, key_values, grad, out, logs)


def feed_kernel(*refs):
    (
        share_ref, context_ref, proj_ref, embed_ref, own_in, near_in, far_in, up_in,
        down_in, bias_ref, proj_bias, gain_ref, shift_ref,
    ) = refs[:13]
    (
        middle_out, out_out, down_out, up_out, middle_grad, attended, context_grad, vectors,
    ) = refs[13:21]
    entry, gelu_s, pre_s, own_back, near_s, last_s, far_s, got_near, got_last, got_far = refs[21:31]
    grad_s, up_ref, down_ref, middle_ref, out_ref, down_total, up_total = refs[31:38]
    send_sem, recv_sem, fetch_sem, keep_sem = refs[38:]
    wide = jnp.float32
    low = jnp.bfloat16
    me = lax.axis_index("fsdp")
    near = {"fsdp": flip(me, 1)[0]}
    far = {"fsdp": flip(me, 2)[0]}
    rows, width = embed_ref.shape
    hidden = up_ref.shape[1]
    tile = rows // 2
    pairs, _, lanes = context_grad.shape
    fetches = [
        pltpu.make_async_copy(up_in, up_ref, fetch_sem.at[0]),
        pltpu.make_async_copy(own_in, grad_s.at[0], fetch_sem.at[1]),
        pltpu.make_async_copy(down_in, down_ref, fetch_sem.at[2]),
        pltpu.make_async_copy(near_in, grad_s.at[1], fetch_sem.at[3]),
        pltpu.make_async_copy(far_in, grad_s.at[pl.ds(2, 2)], fetch_sem.at[4]),
    ]
    for fetch in fetches:
        fetch.start()
    meet([near, far])

    def span(t):
        return pl.ds(t * tile, tile)

    def keep_middle(t):
        return pltpu.make_async_copy(
            middle_ref.at[span(t), :], middle_out.at[span(t), :], keep_sem.at[0, t]
        )

    def keep_out(s, t):
        return pltpu.make_async_copy(
            out_ref.at[s, span(t), :], out_out.at[s, span(t), :], keep_sem.at[1 + s, t]
        )

    def keep_total(n):
        source, target = ((down_total, down_out), (up_total, up_out))[n]
        return pltpu.make_async_copy(source, target, keep_sem.at[5, n])

    def copy(kind, t, src, dst, device):
        return pltpu.make_async_remote_copy(
            src_ref=src.at[span(t), :],
            dst_ref=dst.at[span(t), :],
            send_sem=send_sem.at[kind, t],
            recv_sem=recv_sem.at[kind, t],
            device_id=device,
            device_id_type=pl.DeviceIdType.MESH,
        )

    def rows_near(t):
        return copy(0, t, entry.at[0], entry.at[1], near)

    def rows_far(t):
        return copy(1, t, entry.at[0], entry.at[2], far)

    def rows_last(t):
        return copy(2, t, entry.at[2], entry.at[3], near)

    def back_near(t):
        return copy(3, t, near_s, got_near, near)

    def back_last(t):
        return copy(4, t, last_s, got_last, near)

    def back_far(t):
        return copy(5, t, far_s, got_far, far)

    def feed(s, t, target):
        rows_in = entry[s, span(t), :]
        pre_act = jnp.dot(rows_in, up_ref[...], preferred_element_type=wide) + bias_ref[...]
        cdf = 0.5 * (1.0 + lax.erf(pre_act * 0.7071067811865476))
        density = jnp.exp(-0.5 * pre_act * pre_act) * 0.3989422804014327
        gelu = (pre_act * cdf).astype(low)
        gelu_s[s, span(t), :] = gelu
        act_grad = lax.dot_general(
            grad_s[s, span(t), :],
            down_ref[...],
            (((1,), (1,)), ((), ())),
            preferred_element_type=wide,
        )
        pre_grad = act_grad * (cdf + pre_act * density)
        pre_low = pre_grad.astype(low)
        pre_s[s, span(t), :] = pre_low
        vectors[4:5, :] += jnp.sum(pre_low.astype(wide), axis=0, keepdims=True)
        out_ref[s, span(t), :] = jnp.dot(
            gelu, down_ref[...], preferred_element_type=wide
        ).astype(low)
        keep_out(s, t).start()
        target[span(t), :] = lax.dot_general(
            pre_low, up_ref[...], (((1,), (1,)), ((), ())), preferred_element_type=wide
        ).astype(target.dtype)

    vectors[...] = jnp.zeros_like(vectors)
    for t in range(2):
        middle = (
            embed_ref[span(t), :]
            + jnp.dot(context_ref[span(t), :], proj_ref[...], preferred_element_type=wide)
            + proj_bias[...]
        )
        middle_ref[span(t), :] = middle
        xhat, inverse = normalise(middle)
        entry[0, span(t), :] = (xhat * gain_ref[...] + shift_ref[...]).astype(low)
        rows_far(t).start()
        rows_near(t).start()
        keep_middle(t).start()
    for fetch in fetches[:3]:
        fetch.wait()
    for t in range(2):
        feed(0, t, own_back)
    for fetch in fetches[3:]:
        fetch.wait()
    for t in range(2):
        rows_near(t).wait()
        feed(1, t, near_s)
        back_near(t).start()

    for t in range(2):
        rows_far(t).wait()
        rows_last(t).start()
        feed(2, t, far_s)
        rows_last(t).wait()
        feed(3, t, last_s)
        back_last(t).start()
        if t > 0:
            add_last(t - 1, back_last, back_far, far_s, got_last, span)
    add_last(1, back_last, back_far, far_s, got_last, span)

    block = min(hidden, 256)
    for start in range(0, hidden, block):
        value = 0.0
        for s in range(4):
            value = value + lax.dot_general(
                gelu_s[s, :, start : start + block],
                grad_s[s],
                (((0,), (0,)), ((), ())),
                preferred_element_type=wide,
            )
        down_total[start : start + block, :] = (value * share_ref[0]).astype(low)
    keep_total(0).start()
    for start in range(0, width, block):
        value = 0.0
        for s in range(4):
            value = value + lax.dot_general(
                entry[s, :, start : start + block],
                pre_s[s],
                (((0,), (0,)), ((), ())),
                preferred_element_type=wide,
            )
        up_total[start : start + block, :] = (value * share_ref[0]).astype(low)
    keep_total(1).start()

    for t in range(2):
        back_near(t).wait()
        back_far(t).wait()
        at = span(t)
        grad = own_back[at, :] + got_near[at, :].astype(wide) + got_far[at, :].astype(wide)
        xhat, inverse = normalise(middle_ref[at, :])
        vectors[0:1, :] += jnp.sum(grad * xhat, axis=0, keepdims=True)
        vectors[1:2, :] += jnp.sum(grad, axis=0, keepdims=True)
        upstream = grad_s[0, at, :].astype(wide)
        vectors[3:4, :] += jnp.sum(upstream, axis=0, keepdims=True)
        value = upstream + norm_back(grad, xhat, inverse, gain_ref[...])
        middle_grad[at, :] = value
        value_low = value.astype(low)
        attended[at, :] = value_low
        vectors[2:3, :] += jnp.sum(value_low.astype(wide), axis=0, keepdims=True)
        back = lax.dot_general(
            value_low, proj_ref[...], (((1,), (1,)), ((), ())), preferred_element_type=wide
        ).astype(low)
        for i in range(pairs):
            context_grad[i, at, :] = back[:, i * lanes : (i + 1) * lanes]
    for t in range(2):
        keep_middle(t).wait()
        keep_total(t).wait()
        for s in range(4):
            keep_out(s, t).wait()


def add_last(t, back_last, back_far, far_s, got_last, span):
    back_last(t).wait()
    at = span(t)
    value = far_s[at, :].astype(jnp.float32) + got_last[at, :].astype(jnp.float32)
    far_s[at, :] = value.astype(jnp.bfloat16)
    back_far(t).start()


def feed(
    share, context, proj, embedded, own_grad, near_grad, far_grads, up, down, bias, proj_bias, gain, shift
):
    rows, width = embedded.shape
    hidden = up.shape[1]
    pairs = HEADS // 2
    low = jnp.bfloat16
    wide = jnp.float32
    vmem = pl.BlockSpec(memory_space=pltpu.VMEM)
    hbm = pl.BlockSpec(memory_space=pl.ANY)
    flat = (rows, width)

    def shape(dims, kind):
        return jax.ShapeDtypeStruct(dims, kind)

    return pl.pallas_call(
        feed_kernel,
        in_specs=[pl.BlockSpec(memory_space=pltpu.SMEM)] + [vmem] * 3 + [hbm] * 5 + [vmem] * 4,
        out_specs=[hbm] * 4 + [vmem] * 4,
        out_shape=[
            shape(flat, wide),
            shape((4,) + flat, low),
            shape((hidden, width), low),
            shape((width, hidden), low),
            shape(flat, wide),
            shape(flat, low),
            shape((pairs, rows, width // pairs), low),
            shape((8, width), wide),
        ],
        scratch_shapes=[
            pltpu.VMEM((4,) + flat, low),
            pltpu.VMEM((4, rows, hidden), low),
            pltpu.VMEM((4, rows, hidden), low),
            pltpu.VMEM(flat, wide),
            pltpu.VMEM(flat, low),
            pltpu.VMEM(flat, low),
            pltpu.VMEM(flat, low),
            pltpu.VMEM(flat, low),
            pltpu.VMEM(flat, low),
            pltpu.VMEM(flat, low),
            pltpu.VMEM((4,) + flat, low),
            pltpu.VMEM(up.shape, low),
            pltpu.VMEM(down.shape, low),
            pltpu.VMEM(flat, wide),
            pltpu.VMEM((4,) + flat, low),
            pltpu.VMEM((hidden, width), low),
            pltpu.VMEM((width, hidden), low),
            pltpu.SemaphoreType.DMA((6, 2)),
            pltpu.SemaphoreType.DMA((6, 2)),
            pltpu.SemaphoreType.DMA((5,)),
            pltpu.SemaphoreType.DMA((6, 2)),
        ],
        compiler_params=pltpu.CompilerParams(
            collective_id=4, has_side_effects=True, vmem_limit_bytes=VMEM_LIMIT
        ),
        cost_estimate=pl.CostEstimate(
            flops=48 * rows * width * hidden, bytes_accessed=100_000_000, transcendentals=0
        ),
        name="feed",
    )(
        share, context, proj, embedded, own_grad, near_grad, far_grads, up, down, bias,
        proj_bias, gain, shift,
    )


def group_steps(group, group_size, size):
    steps = []
    bit, offset = 1, 0
    while bit < group_size:
        partner, bit_set = flip(group, bit)
        halving = size >= 32
        steps.append((partner, bit_set, halving, size, offset))
        if halving:
            size = size // 2
            offset = offset + bit_set * size
        bit *= 2
    return steps


def finish_kernel(group_size, widths, head_dim, *refs):
    share_ref = refs[0]
    left_qkv, qkv_grad, left_agg_in, left_proj_in, attended_in = refs[1:6]
    (
        full_qkv, full_agg_in, full_value, embed_in, middle_in, gain_ref, vectors_ref, patch_ref,
        coeff_ref, mask_ref, table_ref, select_ref, own_columns, keys_ref, query_ref, key_w,
        query_w, own_query, out_sum,
    ) = refs[6:25]
    outs = refs[25:28]
    value_out, key_out, query_out, agg_query_out, var_out, extra_out, patch_grad = refs[28:35]
    out_far = refs[35]
    sets = [refs[36:46], refs[46:55]]
    full, query_part, query_got, var_s, last_send, last_recv = refs[55:61]
    entry_grad, embed_grad, heads_grad, table_s, coeff_s, extras, bundle = refs[61:68]
    weight_s, weight_sem, left_agg, left_proj, attended, full_agg, embed_ref, middle_grad = refs[68:76]
    fetch_sem = refs[76]
    fetches = [
        pltpu.make_async_copy(source, target, fetch_sem.at[n])
        for n, (source, target) in enumerate(
            [
                (embed_in, embed_ref),
                (middle_in, middle_grad),
                (full_agg_in, full_agg),
                (left_proj_in, left_proj),
                (attended_in, attended),
                (left_agg_in, left_agg),
            ]
        )
    ]
    me = lax.axis_index("fsdp")
    group = lax.axis_index("grp")
    core_partner, core = flip(me, 1)
    far_partner, far = flip(me, 2)
    diagonal = flip(far_partner, 1)[0]
    wide = jnp.float32
    low = jnp.bfloat16
    quarters = [buffers[2].shape[2] for buffers in sets]
    all_steps = [group_steps(group, group_size, quarter) for quarter in quarters]
    all_halvings = [[i for i, step in enumerate(steps) if step[2]] for steps in all_steps]
    count = len(all_steps[0])
    slots = sets[1][0].shape[0]
    others = [{"fsdp": core_partner}, {"fsdp": far_partner}, {"fsdp": diagonal}]
    pltpu.make_async_copy(full_qkv.at[:, pl.ds(0, key_w.shape[1])], weight_s, weight_sem.at[0]).start()
    for fetch in fetches:
        fetch.start()
    meet(others + [{"grp": step[0]} for step in all_steps[0]])

    def pieces(left, right, out):
        return [(left, right, out, start) for start in range(0, right.shape[1], widths)]

    qkv_pieces = pieces(left_qkv, qkv_grad, outs[0])
    agg_pieces = pieces(left_agg, embed_grad, outs[1])
    proj_pieces = pieces(left_proj, attended, outs[2])
    bulk = qkv_pieces + proj_pieces[:1] + [None] + proj_pieces[1:] + agg_pieces
    chunks = []
    for piece in bulk:
        if piece is None:
            chunks.append((0, 0, None, None, None, 0))
        else:
            chunks.append((1, sum(chunk[0] for chunk in chunks)) + piece)
    small = bulk.index(None)

    def remote(src, dst, send, recv, device):
        return pltpu.make_async_remote_copy(
            src_ref=src,
            dst_ref=dst,
            send_sem=send,
            recv_sem=recv,
            device_id=device,
            device_id_type=pl.DeviceIdType.MESH,
        )

    def copy(stage, c, src, dst, device):
        which, place = chunks[c][:2]
        send_sem, recv_sem = sets[which][-2:]
        return remote(src, dst, send_sem.at[stage, place], recv_sem.at[stage, place], device)

    def span(start, size):
        return pl.ds(pl.multiple_of(start, 16), size)

    def held(c):
        which, place, left, right, out, start = chunks[c]
        buffers = sets[which]
        rest = [
            buffer.at[place % slots if n in (0, 2) else place]
            for n, buffer in enumerate(buffers[:6])
        ]
        rest.append([part.at[place] for part in buffers[6]])
        rest.append(buffers[7].at[place] if out is None else out.at[:, start : start + widths])
        return rest

    def core_copy(c):
        at = held(c)
        return copy(0, c, at[0], at[1], others[0])

    def far_copy(c):
        at = held(c)
        return copy(1, c, at[3], at[4], others[1])

    def step_copy(i, c):
        partner, bit_set, halving, size, offset = all_steps[chunks[c][0]][i]
        if halving:
            size = size // 2
            offset = offset + (1 - bit_set) * size
        at = held(c)
        return copy(2 + i, c, at[5].at[span(offset, size), :], at[6][i], {"grp": partner})

    def back_copy(i, c):
        partner, bit_set, halving, size, offset = all_steps[chunks[c][0]][i]
        size = size // 2
        offset = offset + bit_set * size
        at = held(c)[7].at[span(offset, size), :]
        return copy(2 + count + i, c, at, at, {"grp": partner})

    def begin(c):
        which, place, left, right, out, start = chunks[c]
        quarter = quarters[which]
        send1, recv1, own1 = held(c)[:3]

        def part(q):
            if left is None:
                return bundle[q]
            value = jnp.dot(
                left[span(q * quarter, quarter), :],
                right[:, start : start + widths],
                preferred_element_type=wide,
            )
            return (value * share_ref[0]).astype(low)

        for y in range(2):
            send1[y] = part(2 * y + 1 - core)
        core_copy(c).start()
        for y in range(2):
            own1[y] = part(2 * y + core)

    def after_core(c):
        send1, recv1, own1, send2 = held(c)[:4]
        core_copy(c).wait()
        value = own1[1 - far].astype(wide) + recv1[1 - far].astype(wide)
        send2[...] = value.astype(low)
        far_copy(c).start()

    def after_far(c):
        send1, recv1, own1, send2, recv2, hold = held(c)[:6]
        far_copy(c).wait()
        value = own1[far].astype(wide) + recv1[far].astype(wide) + recv2[...].astype(wide)
        hold[...] = value.astype(low)
        step_copy(0, c).start()

    def after_step(i, c):
        step_copy(i, c).wait()
        hold, halves, done = held(c)[5:]
        steps, halvings = all_steps[chunks[c][0]], all_halvings[chunks[c][0]]
        partner, bit_set, halving, size, offset = steps[i]
        if halving:
            size = size // 2
            offset = offset + bit_set * size
        at = span(offset, size)
        value = hold[at, :].astype(wide) + halves[i][...].astype(wide)
        if i + 1 < count:
            hold[at, :] = value.astype(low)
            step_copy(i + 1, c).start()
        else:
            done[at, :] = value.astype(low)
            back_copy(halvings[-1], c).start()

    def after_back(k, c):
        halvings = all_halvings[chunks[c][0]]
        if k >= len(halvings):
            return
        back_copy(halvings[k], c).wait()
        if k > 0:
            back_copy(halvings[k - 1], c).start()
        elif chunks[c][0] == 0:
            full[me] = held(c)[7][...]
            bundle_core().start()

    def bundle_core():
        at = full.at[me]
        return remote(at, at, last_send.at[0], last_recv.at[0], others[0])

    def bundle_far():
        at = full.at[pl.ds(me - core, 2)]
        return remote(at, at, last_send.at[1], last_recv.at[1], others[1])

    def query_copy(kind):
        return remote(
            query_part,
            query_got.at[kind],
            last_send.at[2 + kind],
            last_recv.at[2 + kind],
            others[kind],
        )

    size = own_columns.shape[0]
    width = key_w.shape[1]
    part_rows = quarters[0]
    spare = extra_out.shape[0] // 4
    per_row = width // size
    scale = head_dim ** (-0.5)

    def coefficients():
        rows = []
        for n in range(HEADS):
            place, column = n // per_row, (n % per_row) * size
            shard, row = place // spare, part_rows - spare + place % spare
            rows.append(full[shard, row : row + 1, column : column + size].astype(wide))
        return jnp.concatenate(rows, axis=0)

    def own_head(value):
        lane = lax.broadcasted_iota(jnp.int32, (HEADS, width), 1)
        head = lax.broadcasted_iota(jnp.int32, (HEADS, width), 0)
        return jnp.where(lane // head_dim == head, value, 0.0)

    def key_grad(coeffs):
        return jnp.dot(coeffs.astype(low), own_columns[...], preferred_element_type=wide)

    def finish_core():
        bundle_core().wait()
        bundle_far().start()

    def finish_far():
        bundle_far().wait()
        spread = jnp.dot(
            key_grad(coefficients()).astype(low), key_w[...], preferred_element_type=wide
        )
        partial = jnp.sum(own_head(spread), axis=0, keepdims=True) * scale
        query_part[...] = jnp.broadcast_to(partial, query_part.shape)
        for kind in range(3):
            query_copy(kind).start()

    def finish_table():
        weights(3).wait()
        table = full[...].reshape(size, width)
        value_out[...] = lax.dot_general(
            own_columns[...], table, (((0,), (0,)), ((), ())), preferred_element_type=wide
        )
        coeffs = coefficients()
        var_s[...] = lax.dot_general(
            coeffs.astype(low), keys_ref[...], (((0,), (0,)), ((), ())), preferred_element_type=wide
        )
        var_out[...] = var_s[span(me * part_rows, part_rows), :] + lax.dot_general(
            full[me], weight_s[...], (((1,), (1,)), ((), ())), preferred_element_type=wide
        )
        for q in range(4):
            extra_out[q * spare : (q + 1) * spare, :] = full[q, part_rows - spare :, :].astype(wide)

    def finish_query():
        for kind in range(3):
            query_copy(kind).wait()
        grad = query_part[...] + query_got[0] + query_got[1] + query_got[2]
        query_out[...] = own_query[...] * grad[:1]
        agg_query_out[...] = lax.dot_general(
            grad,
            query_w[...].astype(wide),
            (((1,), (1,)), ((), ())),
            preferred_element_type=wide,
            precision=exact_mode,
        )
        spread = own_head(jnp.broadcast_to(query_ref[:1].astype(low).astype(wide), (HEADS, width)))
        key_out[...] = scale * lax.dot_general(
            key_grad(coefficients()),
            spread,
            (((0,), (0,)), ((), ())),
            preferred_element_type=wide,
            precision=exact_mode,
        )

    def weights(n):
        source = full_qkv.at[:, pl.ds(n * width, width)] if n < 3 else full_value
        return pltpu.make_async_copy(source, weight_s, weight_sem.at[0])

    def entry_part(n):
        weights(n).wait()
        value = lax.dot_general(
            qkv_grad[:, n * width : (n + 1) * width],
            weight_s[...],
            (((1,), (1,)), ((), ())),
            preferred_element_type=wide,
        )
        entry_grad[...] = value if n == 0 else entry_grad[...] + value
        weights(n + 1).start()

    def norm_part():
        for fetch in fetches:
            fetch.wait()
        grad = entry_grad[...]
        xhat, inverse = normalise(embed_ref[...])
        extras[...] = jnp.zeros_like(extras)
        value = middle_grad[...] + norm_back(grad, xhat, inverse, gain_ref[...])
        value_low = value.astype(low)
        embed_grad[...] = value_low
        first = HEADS // per_row
        extras[first : first + 1, :] = jnp.sum(value_low.astype(wide), axis=0, keepdims=True)
        extras[first + 1 : first + 2, :] = jnp.sum(grad * xhat, axis=0, keepdims=True)
        extras[first + 2 : first + 3, :] = jnp.sum(grad, axis=0, keepdims=True)
        for n in range(4):
            extras[first + 3 + n : first + 4 + n, :] = vectors_ref[n : n + 1, :]
        extras[pl.ds(first + 7 + me, 1), :] = vectors_ref[4:5, :]

    def heads_part():
        heads_grad[...] = lax.dot_general(
            full_agg[...], embed_grad[...], (((1,), (1,)), ((), ())), preferred_element_type=wide
        ).astype(low)
        patch_grad[...] = jnp.zeros_like(patch_grad)
        coeff_s[...] = jnp.zeros_like(coeff_s)

    slot_count = mask_ref.shape[0]

    def one_head(h, carry):
        lane = lax.broadcasted_iota(jnp.int32, (slot_count, HEADS), 1)
        columns = head_columns(coeff_ref, h, slot_count)
        weights = slot_softmax(patch_ref, columns, mask_ref)
        mixed = mixed_of(patch_ref, weights, table_ref.shape[1])
        at = pl.ds(pl.multiple_of(h * head_dim, 16), head_dim)
        grad = heads_grad[at, :]
        table_s[at, :] = (
            lax.dot_general(grad, mixed, (((1,), (1,)), ((), ())), preferred_element_type=wide)
            * share_ref[0]
        ).astype(low)
        mixed_grad = lax.dot_general(
            table_ref[at, :], grad, (((0,), (0,)), ((), ())), preferred_element_type=wide
        )
        parts = [
            mixed_grad[k * slot_count : (k + 1) * slot_count] for k in range(PIX + 1)
        ]
        values = [patch_ref[k].astype(wide) for k in range(PIX)]
        weights_grad = parts[PIX]
        for k in range(PIX):
            weights_grad = weights_grad + parts[k] * values[k]
        mean_grad = jnp.sum(weights * weights_grad, axis=0, keepdims=True)
        scores_grad = weights * (weights_grad - mean_grad)
        for k in range(PIX + 1):
            value = scores_grad * values[k] if k < PIX else scores_grad
            column = jnp.sum(value, axis=1, keepdims=True)
            rows = slice(k * slot_count, (k + 1) * slot_count)
            coeff_s[rows, :] = coeff_s[rows, :] + jnp.where(lane == h, column, 0.0)
        for k in range(PIX):
            patch_grad[k] += share_ref[1] * (parts[k] * weights + scores_grad * columns[k])
        return carry

    def heads_from(first, last):
        lax.fori_loop(first, last, one_head, 0)

    def bundle_part():
        sums = lax.dot_general(
            select_ref[...], table_s[...], (((0,), (1,)), ((), ())), preferred_element_type=wide
        )
        coeff_sum = lax.dot_general(
            coeff_s[...],
            select_ref[...].astype(wide),
            (((0,), (0,)), ((), ())),
            preferred_element_type=wide,
            precision=exact_mode,
        )
        for n in range(HEADS):
            place, column = n // per_row, (n % per_row) * size
            extras[place : place + 1, column : column + size] = coeff_sum[n : n + 1, :]
        row = lax.broadcasted_iota(jnp.int32, (size, extras.shape[0]), 0)
        line = lax.broadcasted_iota(jnp.int32, (size, extras.shape[0]), 1)
        spot = (row // part_rows) * spare + row % part_rows - (part_rows - spare)
        chosen = (spot == line) & (row % part_rows >= part_rows - spare)
        placed = jnp.dot(
            chosen.astype(low),
            (extras[...] * share_ref[0]).astype(low),
            preferred_element_type=wide,
        )
        bundle[...] = (sums + placed).astype(low).reshape(bundle.shape)

    middle_parts = [[functools.partial(entry_part, n)] for n in range(3)]
    middle_parts += [[norm_part, heads_part]]
    third = HEADS // 4
    middle_parts += [
        [functools.partial(heads_from, 0, third)],
        [functools.partial(heads_from, third, 2 * third)],
        [
            functools.partial(heads_from, 2 * third, HEADS),
            bundle_part,
        ],
    ]

    out_copy = remote(out_sum, out_far, last_send.at[5], last_recv.at[5], others[1])
    stages = [begin, after_core, after_far]
    stages += [functools.partial(after_step, i) for i in range(count)]
    stages += [functools.partial(after_back, k) for k in reversed(range(count))]
    extra = [finish_core, finish_far, finish_table, finish_query]
    steps = max(len(chunks), small + 1 + len(extra)) + len(stages) - 1
    for t in range(steps):
        for s in [1, 0]:
            if 0 <= t - s < len(chunks):
                stages[s](t - s)
        if t < len(middle_parts):
            for part in middle_parts[t]:
                part()
        for s in range(2, len(stages)):
            if 0 <= t - s < len(chunks):
                stages[s](t - s)
        if 0 <= t - small - len(stages) < len(extra):
            extra[t - small - len(stages)]()
        if t == len(chunks):
            out_copy.start()
    out_copy.wait()


def finish(group_size, spare, shares, lefts, rights, others):
    left_qkv, left_agg, left_proj = lefts
    qkv_grad, attended = rights
    width, rows = left_qkv.shape
    quarter = width // 4
    widths = 512
    low = jnp.bfloat16
    wide = jnp.float32
    size = others["own_columns"].shape[0]
    part = size // 4
    steps = 0
    while 2**steps < group_size:
        steps += 1

    def buffers(count, slots, rows, columns, last):
        halves = []
        size = rows
        for _ in range(steps):
            if size >= 32:
                size //= 2
            halves.append(pltpu.VMEM((count, size, columns), low))
        few = pltpu.VMEM((slots, 2, rows, columns), low)
        two = pltpu.VMEM((count, 2, rows, columns), low)
        one = pltpu.VMEM((count, rows, columns), low)
        semaphores = pltpu.SemaphoreType.DMA((2 + 2 * steps, count))
        found = [few, two, few, one, one, one, halves]
        return found + ([one] if last else []) + [semaphores, semaphores]

    shapes = [(quarter, qkv_grad.shape[1]), (quarter, width), (quarter, width)]
    count = sum(columns for _, columns in shapes) // widths
    scratch = buffers(1, 1, part, width, True) + buffers(count, 3, quarter, widths, False)
    scratch += [
        pltpu.VMEM((4, part, width), low),
        pltpu.VMEM((8, width), wide),
        pltpu.VMEM((3, 8, width), wide),
        pltpu.VMEM((size, width), wide),
        pltpu.SemaphoreType.DMA((6,)),
        pltpu.SemaphoreType.DMA((6,)),
        pltpu.VMEM((rows, width), wide),
        pltpu.VMEM((rows, width), low),
        pltpu.VMEM((width, rows), low),
        pltpu.VMEM((width, size), low),
        pltpu.VMEM((size, HEADS), wide),
        pltpu.VMEM((4 * spare, width), wide),
        pltpu.VMEM((4, part, width), low),
        pltpu.VMEM((width, width), low),
        pltpu.SemaphoreType.DMA((1,)),
        pltpu.VMEM((width, rows), low),
        pltpu.VMEM((width, rows), low),
        pltpu.VMEM((rows, width), low),
        pltpu.VMEM((width, width), low),
        pltpu.VMEM((rows, width), wide),
        pltpu.VMEM((rows, width), wide),
        pltpu.SemaphoreType.DMA((6,)),
    ]
    whole = pl.BlockSpec(memory_space=pltpu.VMEM)
    out_shape = [jax.ShapeDtypeStruct(dims, low) for dims in shapes]
    more = [(quarter, width)] * 3 + [(8, quarter), (part, width), (4 * spare, width)]
    more.append(others["patch_rows"].shape)
    out_shape += [jax.ShapeDtypeStruct(dims, wide) for dims in more]
    out_shape.append(jax.ShapeDtypeStruct(others["out_sum"].shape, low))
    hbm = pl.BlockSpec(memory_space=pl.ANY)
    far_off = ("full_qkv", "full_agg", "full_value", "embedded", "middle_grad", "out_sum")
    operands = [shares, left_qkv, qkv_grad, left_agg, left_proj, attended, *others.values()]
    return pl.pallas_call(
        functools.partial(finish_kernel, group_size, widths, width // HEADS),
        in_specs=[pl.BlockSpec(memory_space=pltpu.SMEM), whole, whole, hbm, hbm, hbm]
        + [hbm if name in far_off else whole for name in others],
        out_specs=[whole] * (len(out_shape) - 1) + [hbm],
        out_shape=out_shape,
        scratch_shapes=scratch,
        compiler_params=pltpu.CompilerParams(
            collective_id=0, has_side_effects=True, vmem_limit_bytes=62 * 1024 * 1024
        ),
        cost_estimate=pl.CostEstimate(
            flops=20 * rows * width * width, bytes_accessed=200_000_000, transcendentals=0
        ),
        name="finish",
    )(*operands)


def on_device(
    patches,
    patch_counts,
    var_present,
    item_dataset,
    var_ids,
    patch_weight,
    var_embed,
    agg_query,
    query_weight,
    key_weight,
    value_weight,
    agg_proj,
    agg_bias,
    norm1_gain,
    norm1_shift,
    qkv_weight,
    proj_weight,
    proj_bias,
    norm2_gain,
    norm2_shift,
    up_weight,
    up_bias,
    down_weight,
    down_bias,
    out_grad,
):
    low = jnp.bfloat16
    wide = jnp.float32
    rows = patches.shape[2]
    me = lax.axis_index("fsdp")
    group_count = lax.axis_size("grp")
    width = proj_weight.shape[1]
    head_dim = width // HEADS
    own_width = width // 4
    own_vars = patch_weight.shape[0]

    item_count = patch_counts[0]
    own_valid = me * rows + jnp.arange(rows, dtype=jnp.int32) < item_count
    shard_valid = jnp.clip(
        item_count - (me ^ jnp.arange(4, dtype=jnp.int32)) * rows, 0, rows
    ).astype(jnp.int32)
    down_grad = jnp.where(own_valid[:, None], out_grad, jnp.zeros_like(out_grad))

    slot_vars = lax.dynamic_index_in_dim(var_ids, item_dataset[0], 0, keepdims=False)
    part_size = -(-(PIX + 1) * own_vars // 16) * 16
    size = 4 * part_size
    slot_row = jnp.arange(size, dtype=jnp.int32)
    slot_var = jnp.pad(jnp.tile(slot_vars, PIX + 1), (0, size - (PIX + 1) * VTOT))
    place = (slot_var // own_vars) * part_size + (slot_row // VTOT) * own_vars + slot_var % own_vars
    select = (
        (place[:, None] == jnp.arange(size, dtype=jnp.int32)[None, :])
        & (slot_row < (PIX + 1) * VTOT)[:, None]
    ).astype(low)
    own_table = jnp.concatenate(
        [
            patch_weight.transpose(1, 0, 2).reshape(own_vars * PIX, width),
            var_embed,
            jnp.zeros((part_size - (PIX + 1) * own_vars, width), low),
        ],
        axis=0,
    )
    own_query = lax.dynamic_slice_in_dim(agg_query, me * own_width, own_width, 0)
    patch_rows = patches.transpose(1, 0, 2)
    slot_mask = jnp.where(var_present[0] > 0, 0.0, masked_out).astype(wide)[:, None]
    (
        count_rows,
        tables,
        query_rows,
        key_query,
        full_value,
        full_agg_proj,
        full_qkv,
        full_proj,
        near_down_grad,
        far_grads,
        table_values,
        coeffs,
        heads_t,
        embedded,
        normed1,
    ) = prepare(
        group_count,
        jnp.full((8, 128), item_count.astype(wide)),
        jnp.broadcast_to(own_query[None, :], (16, own_width)),
        query_weight,
        key_weight,
        own_table,
        select,
        value_weight,
        agg_proj,
        qkv_weight,
        proj_weight,
        down_grad,
        patch_rows,
        slot_mask,
        agg_bias[None, :],
        norm1_gain[None, :],
        norm1_shift[None, :],
    )
    count_share = item_count.astype(wide) / count_rows[0, 0]
    own_columns = lax.dynamic_slice_in_dim(
        tables.reshape(size, width), me * own_width, own_width, 1
    )

    queries, key_values, context_pairs, logs = attend(normed1, full_qkv, shard_valid)
    context = context_pairs.transpose(1, 0, 2).reshape(rows, width)
    (
        middle,
        out_parts,
        down_weight_part,
        up_weight_part,
        middle_grad,
        attended_grad,
        context_grad,
        feed_vectors,
    ) = feed(
        count_share[None],
        context,
        full_proj,
        embedded,
        down_grad,
        near_down_grad,
        far_grads,
        up_weight,
        down_weight,
        up_bias.astype(wide)[None, :],
        proj_bias[None, :],
        norm2_gain[None, :],
        norm2_shift[None, :],
    )
    down_weight_grad = lax.psum(down_weight_part, "grp").astype(wide)
    up_weight_grad = lax.psum(up_weight_part, "grp").astype(wide)
    out_got = swap(jnp.stack([out_parts[1], out_parts[3]]), "fsdp", 1)
    out_sum = (out_parts[2].astype(wide) + out_got[1].astype(wide)).astype(low)

    qkv_grad = attend_back(queries, key_values, context_grad, context_pairs, logs, shard_valid)
    spare = part_size - (PIX + 1) * own_vars
    (
        qkv_weight_grad,
        agg_proj_grad,
        proj_weight_grad,
        value_weight_grad,
        key_weight_grad,
        query_weight_grad,
        agg_query_grad,
        var_grads,
        extras,
        patch_grad,
        out_far,
    ) = finish(
        group_count,
        spare,
        jnp.stack([count_share, group_count * count_share]),
        (normed1.T, heads_t, context.T),
        (qkv_grad, attended_grad),
        dict(
            full_qkv=full_qkv,
            full_agg=full_agg_proj,
            full_value=full_value,
            embedded=embedded,
            middle_grad=middle_grad,
            gain=norm1_gain[None, :],
            vectors=feed_vectors,
            patch_rows=patch_rows,
            coeffs=coeffs,
            slot_mask=slot_mask,
            table_values=table_values,
            select=select,
            own_columns=own_columns,
            key_query=key_query,
            query_rows=query_rows,
            key_weight=key_weight,
            query_weight=query_weight,
            own_query=own_query.astype(wide)[:, None],
            out_sum=out_sum,
        ),
    )
    down_sum = out_parts[0].astype(wide) + out_got[0].astype(wide) + out_far.astype(wide)
    output = (middle + down_sum + down_bias).astype(low)
    patches_grad = patch_grad.transpose(1, 0, 2)
    qkv_weight_grad = qkv_weight_grad.astype(wide)
    agg_proj_grad = agg_proj_grad.astype(wide)
    proj_weight_grad = proj_weight_grad.astype(wide)
    at = HEADS * size // width
    vector_total = extras[at : at + 7]
    at += 7
    up_bias_total = lax.dynamic_slice_in_dim(extras, at + me, 1, 0)[0]
    vector_own = lax.dynamic_slice_in_dim(vector_total, me * own_width, own_width, 1)
    agg_query_grad = agg_query_grad[0]
    var_grads = var_grads[: (PIX + 1) * own_vars].reshape(PIX + 1, own_vars, width)
    patch_weight_grad = var_grads[:PIX].transpose(1, 0, 2)
    var_embed_grad = var_grads[PIX]
    return (
        output,
        patches_grad,
        patch_weight_grad,
        var_embed_grad,
        agg_query_grad,
        query_weight_grad,
        key_weight_grad,
        value_weight_grad,
        agg_proj_grad,
        vector_own[0],
        vector_own[1],
        vector_own[2],
        qkv_weight_grad,
        proj_weight_grad,
        vector_own[5],
        vector_own[3],
        vector_own[4],
        up_weight_grad,
        up_bias_total,
        down_weight_grad,
        vector_own[6],
    )


def solution(mesh):
    shard = P("fsdp")
    shard_rows = P("fsdp", None)
    return jax.shard_map(
        on_device,
        mesh=mesh,
        in_specs=(
            P(None, None, ("grp", "fsdp")),
            P("grp"),
            P("grp", None),
            P("grp"),
            P(),
            P("fsdp", None, None),
            shard_rows,
            P(),
            shard_rows,
            shard_rows,
            shard_rows,
            shard_rows,
            P(),
            P(),
            P(),
            shard_rows,
            shard_rows,
            P(),
            P(),
            P(),
            P(None, "fsdp"),
            shard,
            shard_rows,
            P(),
            P(("grp", "fsdp"), None),
        ),
        out_specs=(
            P(("grp", "fsdp"), None),
            P(None, None, ("grp", "fsdp")),
            P("fsdp", None, None),
            shard_rows,
            shard,
            shard_rows,
            shard_rows,
            shard_rows,
            shard_rows,
            shard,
            shard,
            shard,
            shard_rows,
            shard_rows,
            shard,
            shard,
            shard,
            P(None, "fsdp"),
            shard,
            shard_rows,
            shard,
        ),
        check_vma=False,
    )
```

```python
import functools

import jax
import jax.numpy as jnp
from jax import lax
from jax.experimental import pallas as pl
from jax.experimental.pallas import tpu as pltpu
from jax.sharding import PartitionSpec as P

HEADS = 16
VTOT = 48
PIX = 4

exact_mode = lax.Precision.HIGHEST
masked_out = -1e30
VMEM_LIMIT = 56 * 1024 * 1024


def swap(value, axis, bit):
    size = lax.axis_size(axis)
    return lax.ppermute(value, axis, [(i, i ^ bit) for i in range(size)])


def product(left_side, right_side):
    return jnp.dot(left_side, right_side, preferred_element_type=jnp.float32)


def left_product(left_side, right_side):
    return lax.dot_general(
        left_side, right_side, (((0,), (0,)), ((), ())), preferred_element_type=jnp.float32
    )


def right_product(left_side, right_side):
    return lax.dot_general(
        left_side, right_side, (((1,), (1,)), ((), ())), preferred_element_type=jnp.float32
    )


def column_sums(values_in):
    return jnp.sum(values_in.astype(jnp.float32), axis=0)


def flip(index, bit):
    bit_set = (index // bit) % 2
    return index + bit - 2 * bit * bit_set, bit_set


def meet(partners):
    barrier = pltpu.get_barrier_semaphore()
    for partner in partners:
        pl.semaphore_signal(
            barrier, inc=1, device_id=partner, device_id_type=pl.DeviceIdType.MESH
        )
    pl.semaphore_wait(barrier, len(partners))


def normalise(values_in):
    row_mean = jnp.mean(values_in, axis=-1, keepdims=True)
    centred = values_in - row_mean
    spread = jnp.mean(centred * centred, axis=-1, keepdims=True)
    inverse = lax.rsqrt(spread + 1e-05)
    return centred * inverse, inverse


def norm_back(grad, xhat, inverse, gain_vec):
    scaled = grad * gain_vec
    first = jnp.mean(scaled, axis=-1, keepdims=True)
    second = jnp.mean(scaled * xhat, axis=-1, keepdims=True)
    return (scaled - first - xhat * second) * inverse


def slot_softmax(patch_ref, columns, mask_ref):
    scores = columns[PIX] + mask_ref[...]
    for k in range(PIX):
        scores = scores + patch_ref[k].astype(jnp.float32) * columns[k]
    top = jnp.max(scores, axis=0, keepdims=True)
    terms = jnp.exp(scores - top)
    return terms / jnp.sum(terms, axis=0, keepdims=True)


def mixed_of(patch_ref, weights, rows):
    parts = [
        (weights * patch_ref[k].astype(jnp.float32)).astype(jnp.bfloat16) for k in range(PIX)
    ]
    parts.append(weights.astype(jnp.bfloat16))
    used = weights.shape[0] * (PIX + 1)
    if rows > used:
        parts.append(jnp.zeros((rows - used, weights.shape[1]), jnp.bfloat16))
    return jnp.concatenate(parts, axis=0)


def head_columns(coeff_ref, head, slots):
    lane = lax.broadcasted_iota(jnp.int32, (slots, coeff_ref.shape[1]), 1)
    return [
        jnp.sum(
            jnp.where(lane == head, coeff_ref[k * slots : (k + 1) * slots, :], 0.0),
            axis=1,
            keepdims=True,
        )
        for k in range(PIX + 1)
    ]


def prepare_kernel(group_size, head_dim, *refs):
    (
        count_ref, own_query, query_w, key_w, own_table, select_ref, own_value, own_agg,
        own_qkv, own_proj, own_grad, patch_ref, mask_ref, bias_ref, gain_ref, shift_ref,
    ) = refs[:16]
    (
        count_out, tables, query_out, keys_out, full_value, full_agg, full_qkv, full_proj,
        near_grad, far_grads, table_out, coeff_out, heads_out, embed_out, norm_out,
    ) = refs[16:31]
    query_part, query_got, counts = refs[31:34]
    whole_value, whole_agg, whole_qkv, whole_proj, grads = refs[34:39]
    send_sem, recv_sem, small_send, small_recv, local_sem = refs[39:]
    wide = jnp.float32
    low = jnp.bfloat16
    me = lax.axis_index("fsdp")
    group = lax.axis_index("grp")
    near_index = flip(me, 1)[0]
    far_index = flip(me, 2)[0]
    near = {"fsdp": near_index}
    far = {"fsdp": far_index}
    block = own_value.shape[0]
    heads = keys_out.shape[0]
    slots = mask_ref.shape[0]
    rows = own_grad.shape[0]
    bits = []
    bit = 1
    while bit < group_size:
        bits.append(bit)
        bit *= 2
    meet(
        [near, far, {"fsdp": flip(far_index, 1)[0]}]
        + [{"grp": flip(group, bit)[0]} for bit in bits]
    )

    def remote(src, dst, sends, recvs, at, device):
        return pltpu.make_async_remote_copy(
            src_ref=src,
            dst_ref=dst,
            send_sem=sends.at[at],
            recv_sem=recvs.at[at],
            device_id=device,
            device_id_type=pl.DeviceIdType.MESH,
        )

    def span(start, size):
        return pl.ds(pl.multiple_of(start, 16), size)

    width = own_value.shape[1]
    items = [(own_value, whole_value, 0, width, False), (own_agg, whole_agg, 0, width, False)]
    for n in range(full_qkv.shape[1] // width):
        items.append((own_qkv, whole_qkv, n * width, width, True))
    items.append((own_proj, whole_proj, 0, width, True))
    x_bit = flip(group, 1)[1]
    piece = flip(group, 2)[1] + 2 * flip(group, 4)[1] + 4 * x_bit
    eighth = block // 8

    def weight_copy(n, stage):
        own, whole, start, size, eighths = items[n]
        cols = pl.ds(start, size)

        def region(base, offset, count):
            return whole.at[span(base * block + offset, count), cols]

        if stage == 0:
            return remote(
                own.at[:, cols], region(me, 0, block), send_sem, recv_sem, (n, 0), near
            )
        if stage == 1:
            offset, count = (piece * eighth, eighth) if eighths else (x_bit * (block // 2), block // 2)
            return remote(
                own.at[span(offset, count), cols],
                region(me, offset, count),
                send_sem,
                recv_sem,
                (n, 1),
                far,
            )
        if stage == 2:
            at = region(far_index, piece * eighth, eighth)
            return remote(at, at, send_sem, recv_sem, (n, 2), {"grp": flip(group, 2)[0]})
        if stage == 3:
            at = region(far_index, (piece // 2) * 2 * eighth, 2 * eighth)
            return remote(at, at, send_sem, recv_sem, (n, 3), {"grp": flip(group, 4)[0]})
        if stage == 4:
            at = region(far_index, x_bit * (block // 2), block // 2)
            return remote(at, at, send_sem, recv_sem, (n, 4), {"grp": flip(group, 1)[0]})
        at = region(far_index, 0, block)
        return remote(at, at, send_sem, recv_sem, (n, 5), near)

    def out_copy(n):
        own, whole, start, size, eighths = items[n]
        target = [full_value, full_agg, full_qkv, full_proj][min(n, 2) if n + 1 < len(items) else 3]
        cols = pl.ds(start, size)
        return pltpu.make_async_copy(whole.at[:, cols], target.at[:, cols], local_sem.at[2 + n])

    grad_parts = 4
    part_rows = rows // grad_parts

    def grad_near():
        return remote(own_grad, grads.at[0], small_send, small_recv, 0, near)

    def grad_far(p):
        at = pl.ds(p * part_rows, part_rows)
        return remote(
            own_grad.at[at, :], grads.at[1, at, :], small_send, small_recv, 1 + p, far
        )

    def grad_last(p):
        at = pl.ds(p * part_rows, part_rows)
        return remote(
            grads.at[1, at, :],
            grads.at[2, at, :],
            small_send,
            small_recv,
            1 + grad_parts + p,
            near,
        )

    def grad_out(n):
        if n == 0:
            return pltpu.make_async_copy(grads.at[0], near_grad, local_sem.at[0])
        return pltpu.make_async_copy(grads.at[pl.ds(1, 2)], far_grads, local_sem.at[1])

    base = 1 + 2 * grad_parts

    def table_copy(kind):
        if kind == 0:
            return remote(own_table, tables.at[me], small_send, small_recv, base, near)
        if kind == 1:
            return remote(own_table, tables.at[me], small_send, small_recv, base + 1, far)
        at = tables.at[far_index]
        return remote(at, at, small_send, small_recv, base + 2, near)

    others = [near, far, {"fsdp": flip(far_index, 1)[0]}]

    def query_copy(kind):
        return remote(
            query_part, query_got.at[kind], small_send, small_recv, base + 3 + kind, others[kind]
        )

    def key_copy(kind):
        at = keys_out.at[:, pl.ds(pl.multiple_of(me * block, 128), block)]
        return remote(at, at, small_send, small_recv, base + 6 + kind, others[kind])

    def count_copy(n):
        partner = {"grp": flip(group, bits[n])[0]}
        return remote(
            counts.at[2 * n], counts.at[2 * n + 1], small_send, small_recv, base + 9 + n, partner
        )

    def count_step(n):
        count_copy(n).wait()
        value = counts[2 * n] + counts[2 * n + 1]
        if n + 1 < len(bits):
            counts[2 * n + 2] = value
            count_copy(n + 1).start()
        else:
            count_out[...] = value

    def forward(n, stage):
        weight_copy(n, stage).wait()
        weight_copy(n, 4 if (stage == 1 and not items[n][4]) else stage + 1).start()

    def keep(n):
        weight_copy(n, 0).wait()
        weight_copy(n, 5).wait()
        out_copy(n).start()

    late = list(range(2, len(items)))

    query_part[...] = jnp.dot(own_query[...], query_w[...], preferred_element_type=wide)[:8]
    for kind in range(3):
        query_copy(kind).start()
    weight_copy(0, 1).start()
    for n in late:
        weight_copy(n, 1).start()
    table_copy(1).start()
    table_copy(0).start()
    weight_copy(0, 0).start()
    counts[0] = count_ref[...]
    count_copy(0).start()
    tables[me] = own_table[...]
    whole_value[span(me * block, block), :] = own_value[...]
    for kind in range(3):
        query_copy(kind).wait()
    query = query_part[...] + query_got[0] + query_got[1] + query_got[2]
    query_out[...] = query
    lane = lax.broadcasted_iota(jnp.int32, (heads, width), 1)
    head = lax.broadcasted_iota(jnp.int32, (heads, width), 0)
    spread = jnp.where(lane // head_dim == head, jnp.broadcast_to(query[:1], (heads, width)), 0.0)
    own_keys = lax.dot_general(
        spread.astype(low), key_w[...], (((1,), (1,)), ((), ())), preferred_element_type=wide
    ) * (head_dim ** (-0.5))
    keys_out[:, pl.ds(pl.multiple_of(me * block, 128), block)] = own_keys.astype(low)
    for kind in range(3):
        key_copy(kind).start()
    weight_copy(1, 1).start()
    whole_agg[span(me * block, block), :] = own_agg[...]
    whole_qkv[span(me * block, block), :] = own_qkv[...]
    whole_proj[span(me * block, block), :] = own_proj[...]
    forward(0, 1)
    for n in late:
        forward(n, 1)
    forward(0, 4)
    forward(2, 2)
    forward(3, 2)
    table_copy(0).wait()
    table_copy(1).wait()
    table_copy(2).start()
    for p in range(grad_parts):
        grad_far(p).start()
    forward(1, 1)
    weight_copy(1, 0).start()
    table_copy(2).wait()
    stacked = tables[...].reshape(select_ref.shape[1], width)
    table = jnp.dot(select_ref[...], stacked, preferred_element_type=wide).astype(low)
    for kind in range(3):
        key_copy(kind).wait()
    coeff_out[...] = lax.dot_general(
        table, keys_out[...], (((1,), (1,)), ((), ())), preferred_element_type=wide
    )
    weight_copy(0, 0).wait()
    weight_copy(0, 5).wait()
    out_copy(0).start()
    values = jnp.dot(table, whole_value[...], preferred_element_type=wide)
    table_out[...] = jnp.transpose(values).astype(low)

    def one_head(h, carry):
        weights = slot_softmax(patch_ref, head_columns(coeff_out, h, slots), mask_ref)
        mixed = mixed_of(patch_ref, weights, table_out.shape[1])
        at = pl.ds(pl.multiple_of(h * head_dim, 16), head_dim)
        heads_out[at, :] = jnp.dot(
            table_out[at, :], mixed, preferred_element_type=wide
        ).astype(low)
        return carry

    half = heads // 2
    forward(2, 3)
    forward(4, 2)
    for n in late:
        weight_copy(n, 0).start()
    lax.fori_loop(0, half, one_head, 0)
    forward(1, 4)
    forward(3, 3)
    forward(5, 2)
    grad_near().start()
    lax.fori_loop(half, heads, one_head, 0)
    keep(1)
    embedded = (
        lax.dot_general(
            heads_out[...], whole_agg[...], (((0,), (0,)), ((), ())), preferred_element_type=wide
        )
        + bias_ref[...]
    )
    embed_out[...] = embedded
    count_step(0)
    forward(2, 4)
    grad_far(0).wait()
    grad_last(0).start()
    xhat, inverse = normalise(embedded)
    norm_out[...] = (xhat * gain_ref[...] + shift_ref[...]).astype(low)
    forward(4, 3)
    keep(2)
    forward(3, 4)
    count_step(1)
    grad_far(1).wait()
    grad_last(1).start()
    forward(5, 3)
    keep(3)
    forward(4, 4)
    for n in range(2, len(bits)):
        count_step(n)
    grad_far(2).wait()
    grad_last(2).start()
    keep(4)
    forward(5, 4)
    grad_near().wait()
    grad_out(0).start()
    grad_far(3).wait()
    grad_last(3).start()
    keep(5)
    for p in range(grad_parts):
        grad_last(p).wait()
    grad_out(1).start()
    for n in range(len(items)):
        out_copy(n).wait()
    for n in range(2):
        grad_out(n).wait()


def prepare(
    group_size, count_rows, own_query, query_w, key_w, own_table, select, own_value, own_agg,
    own_qkv, own_proj, own_grad, patch_rows, slot_mask, bias, gain, shift,
):
    block, width = own_value.shape
    head_dim = width // HEADS
    rows = own_grad.shape[0]
    slots = slot_mask.shape[0]
    size = select.shape[0]
    low = jnp.bfloat16
    wide = jnp.float32
    vmem = pl.BlockSpec(memory_space=pltpu.VMEM)
    hbm = pl.BlockSpec(memory_space=pl.ANY)
    steps = 0
    while 2**steps < group_size:
        steps += 1
    items = 3 + own_qkv.shape[1] // width
    small = 1 + 2 * 4 + 9 + steps

    def shape(dims, kind):
        return jax.ShapeDtypeStruct(dims, kind)

    return pl.pallas_call(
        functools.partial(prepare_kernel, group_size, head_dim),
        in_specs=[vmem] * 16,
        out_specs=[vmem] * 4 + [hbm] * 6 + [vmem] * 5,
        out_shape=[
            shape((8, 128), wide),
            shape((4,) + own_table.shape, low),
            shape((8, width), wide),
            shape((HEADS, width), low),
            shape((4 * block, width), low),
            shape((4 * block, width), low),
            shape((4 * block, own_qkv.shape[1]), low),
            shape((4 * block, width), low),
            shape((rows, width), low),
            shape((2, rows, width), low),
            shape((width, size), low),
            shape((size, HEADS), wide),
            shape((width, rows), low),
            shape((rows, width), wide),
            shape((rows, width), low),
        ],
        scratch_shapes=[
            pltpu.VMEM((8, width), wide),
            pltpu.VMEM((3, 8, width), wide),
            pltpu.VMEM((2 * steps, 8, 128), wide),
            pltpu.VMEM((4 * block, width), low),
            pltpu.VMEM((4 * block, width), low),
            pltpu.VMEM((4 * block, own_qkv.shape[1]), low),
            pltpu.VMEM((4 * block, width), low),
            pltpu.VMEM((3, rows, width), low),
            pltpu.SemaphoreType.DMA((items, 6)),
            pltpu.SemaphoreType.DMA((items, 6)),
            pltpu.SemaphoreType.DMA((small,)),
            pltpu.SemaphoreType.DMA((small,)),
            pltpu.SemaphoreType.DMA((2 + items,)),
        ],
        compiler_params=pltpu.CompilerParams(
            collective_id=3, has_side_effects=True, vmem_limit_bytes=VMEM_LIMIT
        ),
        cost_estimate=pl.CostEstimate(
            flops=8 * size * rows * width, bytes_accessed=100_000_000, transcendentals=0
        ),
        name="prepare",
    )(
        count_rows, own_query, query_w, key_w, own_table, select, own_value, own_agg,
        own_qkv, own_proj, own_grad, patch_rows, slot_mask, bias, gain, shift,
    )


def group_steps(group, order, size):
    steps = []
    offset = 0
    for bit in order:
        partner, bit_set = flip(group, bit)
        halving = size >= 32
        steps.append((partner, bit_set, halving, size, offset))
        if halving:
            size = size // 2
            offset = offset + bit_set * size
    return steps


def group_orders(group_size):
    bits = []
    while 2 ** len(bits) < group_size:
        bits.append(2 ** len(bits))
    return bits, bits[1:] + bits[:1]


def group_sum(steps, hold, halves, done, send_sem, recv_sem):
    count = len(steps)
    halvings = [i for i, step in enumerate(steps) if step[2]]
    wide = jnp.float32

    def span(start, size):
        return pl.ds(pl.multiple_of(start, 16), size)

    def copy(stage, c, src, dst, partner):
        return pltpu.make_async_remote_copy(
            src_ref=src,
            dst_ref=dst,
            send_sem=send_sem.at[stage, c],
            recv_sem=recv_sem.at[stage, c],
            device_id={"grp": partner},
            device_id_type=pl.DeviceIdType.MESH,
        )

    def step_copy(i, c):
        partner, bit_set, halving, size, offset = steps[i]
        if halving:
            size = size // 2
            offset = offset + (1 - bit_set) * size
        return copy(i, c, hold.at[c, span(offset, size), :], halves[i].at[c], partner)

    def back_copy(i, c):
        partner, bit_set, halving, size, offset = steps[i]
        size = size // 2
        at = done.at[c, span(offset + bit_set * size, size), :]
        return copy(count + i, c, at, at, partner)

    def begin(c):
        step_copy(0, c).start()

    def after_step(i, c):
        step_copy(i, c).wait()
        partner, bit_set, halving, size, offset = steps[i]
        if halving:
            size = size // 2
            offset = offset + bit_set * size
        at = span(offset, size)
        value = hold[c, at, :].astype(wide) + halves[i][c].astype(wide)
        if i + 1 < count:
            hold[c, at, :] = value.astype(hold.dtype)
            step_copy(i + 1, c).start()
        else:
            done[c, at, :] = value.astype(done.dtype)
            back_copy(halvings[-1], c).start()

    def after_back(k, c):
        back_copy(halvings[k], c).wait()
        if k > 0:
            back_copy(halvings[k - 1], c).start()

    stages = [begin] + [functools.partial(after_step, i) for i in range(count)]
    return stages + [functools.partial(after_back, k) for k in reversed(range(len(halvings)))]


def group_buffers(group_size, chunks, rows, columns):
    low = jnp.bfloat16
    steps = len(group_orders(group_size)[0])
    halves = []
    size = rows
    for _ in range(steps):
        if size >= 32:
            size //= 2
        halves.append(pltpu.VMEM((chunks, size, columns), low))
    one = pltpu.VMEM((chunks, rows, columns), low)
    semaphores = pltpu.SemaphoreType.DMA((2 * steps, chunks))
    return [one, halves, one, semaphores, semaphores]


def sum_beside(group, group_size, first, total_in, total_out, buffers):
    hold, halves, done, send_sem, recv_sem, in_sem, keep_sem = buffers
    chunks, rows, columns = hold.shape
    steps = group_steps(group, group_orders(group_size)[0], rows)
    stages = group_sum(steps, hold, halves, done, send_sem, recv_sem)

    def at(c):
        return pl.ds(pl.multiple_of((first + c) * columns, 128), columns)

    def take(c):
        return pltpu.make_async_copy(total_in.at[:, at(c)], hold.at[c], in_sem.at[c])

    def give(c):
        place = pl.ds(pl.multiple_of(c * columns, 128), columns)
        return pltpu.make_async_copy(done.at[c], total_out.at[:, place], keep_sem.at[c])

    def start():
        for c in range(chunks):
            take(c).wait()
            stages[0](c)

    def end(c):
        stages[-1](c)
        give(c).start()

    return chunks, take, start, stages[1:-1] + [end], give


def beside_buffers(group_size, chunks, rows, columns):
    return group_buffers(group_size, chunks, rows, columns) + [
        pltpu.SemaphoreType.DMA((chunks,)),
        pltpu.SemaphoreType.DMA((chunks,)),
    ]


def lane_half(rows, pair, head_dim):
    lane = lax.broadcasted_iota(jnp.int32, (rows, 2 * head_dim), 1)
    return (lane // head_dim) == pair


def attend_kernel(
    head_dim, valid_ref, rows_ref, weight_ref, q_ref, kv_out, out_ref, log_ref, kv_ref, weight_s, sum_s, top_s, total_s, send_sem, recv_sem, fetch_sem, keep_sem
):
    me = lax.axis_index("fsdp")
    near = {"fsdp": flip(me, 1)[0]}
    far = {"fsdp": flip(me, 2)[0]}
    wide = jnp.float32
    low = jnp.bfloat16
    rows, width = rows_ref.shape
    lanes = 2 * head_dim
    pairs = width // lanes
    scale = head_dim ** (-0.5)
    groups = pairs // 2

    def fetch(part, g):
        at = pl.ds(part * width + g * 2 * lanes, 2 * lanes)
        return pltpu.make_async_copy(
            weight_ref.at[:, at], weight_s.at[:, at], fetch_sem.at[part, g]
        )

    def keep(i):
        return pltpu.make_async_copy(kv_ref.at[:, i], kv_out.at[:, i], keep_sem.at[i])

    for g in range(groups):
        fetch(1, g).start()
        fetch(2, g).start()
    for g in range(groups):
        fetch(0, g).start()
    meet([near, far])

    def copy(kind, i, source, target, device):
        return pltpu.make_async_remote_copy(
            src_ref=kv_ref.at[source, i],
            dst_ref=kv_ref.at[target, i],
            send_sem=send_sem.at[kind, i],
            recv_sem=recv_sem.at[kind, i],
            device_id=device,
            device_id_type=pl.DeviceIdType.MESH,
        )

    def near_copy(i):
        return copy(0, i, 0, 1, near)

    def far_copy(i):
        return copy(1, i, 0, 2, far)

    def last_copy(i):
        return copy(2, i, 2, 3, near)

    entry = rows_ref[...]
    for g in range(groups):
        for part in range(2):
            start = (part + 1) * width + g * 2 * lanes
            fetch(part + 1, g).wait()
            value = jnp.dot(
                entry, weight_s[:, start : start + 2 * lanes], preferred_element_type=wide
            ).astype(low)
            kv_ref[0, 2 * g, part] = value[:, :lanes]
            kv_ref[0, 2 * g + 1, part] = value[:, lanes:]
        for i in (2 * g, 2 * g + 1):
            far_copy(i).start()
            near_copy(i).start()
    for g in range(groups):
        start = g * 2 * lanes
        fetch(0, g).wait()
        value = jnp.dot(
            entry, weight_s[:, start : start + 2 * lanes], preferred_element_type=wide
        ).astype(low)
        value = value * jnp.asarray(scale, low)
        q_ref[2 * g] = value[:, :lanes]
        q_ref[2 * g + 1] = value[:, lanes:]

    tile = min(rows, 256)

    def attend(i, shards, first):
        for start in range(0, rows, tile):
            at = slice(start, start + tile)
            block = q_ref[i, at, :]
            sums, tops, totals = [], [], []
            for pair in range(2):
                query = jnp.where(lane_half(tile, pair, head_dim), block, jnp.zeros_like(block))
                logits = []
                for j in shards:
                    raw = lax.dot_general(
                        query, kv_ref[j, i, 0], (((1,), (1,)), ((), ())), preferred_element_type=wide
                    )
                    place = lax.broadcasted_iota(jnp.int32, (1, rows), 1)
                    logits.append(jnp.where(place < valid_ref[j], raw, masked_out))
                top = functools.reduce(
                    jnp.maximum, [jnp.max(part, axis=1, keepdims=True) for part in logits]
                )
                sum_now, total_now = 0.0, 0.0
                for j, part in zip(shards, logits):
                    terms = jnp.exp(part - top)
                    total_now = total_now + jnp.sum(terms, axis=1, keepdims=True)
                    sum_now = sum_now + jnp.dot(
                        terms.astype(low), kv_ref[j, i, 1], preferred_element_type=wide
                    )
                sums.append(sum_now)
                tops.append(top)
                totals.append(total_now)
            side = lane_half(tile, 0, head_dim)
            sum_now = jnp.where(side, sums[0], sums[1])
            top = jnp.where(side, tops[0], tops[1])
            total_now = jnp.where(side, totals[0], totals[1])
            if not first:
                old_top = top_s[at, :]
                new_top = jnp.maximum(top, old_top)
                mine = jnp.exp(top - new_top)
                others = jnp.exp(old_top - new_top)
                sum_now = sum_now * mine + sum_s[at, :] * others
                total_now = total_now * mine + total_s[at, :] * others
                top = new_top
            sum_s[at, :] = sum_now
            top_s[at, :] = top
            total_s[at, :] = total_now

    def one_pair(i, carry):
        near_copy(i).wait_recv()
        attend(i, (0, 1), True)
        far_copy(i).wait_recv()
        last_copy(i).start()
        attend(i, (2,), False)
        last_copy(i).wait_recv()
        attend(i, (3,), False)
        keep(i).start()
        out_ref[i] = (sum_s[...] / total_s[...]).astype(low)
        log_ref[i] = top_s[...] + jnp.log(total_s[...])
        return carry

    lax.fori_loop(0, pairs, one_pair, 0)

    def end(i, carry):
        near_copy(i).wait_send()
        far_copy(i).wait_send()
        last_copy(i).wait_send()
        keep(i).wait()
        return carry

    lax.fori_loop(0, pairs, end, 0)


def attend(rows_in, weight, valid):
    rows, width = rows_in.shape
    head_dim = width // HEADS
    lanes = 2 * head_dim
    pairs = HEADS // 2
    whole = pl.BlockSpec(memory_space=pltpu.VMEM)
    hbm = pl.BlockSpec(memory_space=pl.ANY)
    low = jnp.bfloat16
    wide = jnp.float32
    return pl.pallas_call(
        functools.partial(attend_kernel, head_dim),
        in_specs=[pl.BlockSpec(memory_space=pltpu.SMEM), whole, hbm],
        out_specs=[whole, hbm, whole, whole],
        out_shape=[
            jax.ShapeDtypeStruct((pairs, rows, lanes), low),
            jax.ShapeDtypeStruct((4, pairs, 2, rows, lanes), low),
            jax.ShapeDtypeStruct((pairs, rows, lanes), low),
            jax.ShapeDtypeStruct((pairs, rows, lanes), wide),
        ],
        scratch_shapes=[
            pltpu.VMEM((4, pairs, 2, rows, lanes), low),
            pltpu.VMEM(weight.shape, low),
            pltpu.VMEM((rows, lanes), wide),
            pltpu.VMEM((rows, lanes), wide),
            pltpu.VMEM((rows, lanes), wide),
            pltpu.SemaphoreType.DMA((3, pairs)),
            pltpu.SemaphoreType.DMA((3, pairs)),
            pltpu.SemaphoreType.DMA((3, pairs // 2)),
            pltpu.SemaphoreType.DMA((pairs,)),
        ],
        compiler_params=pltpu.CompilerParams(
            collective_id=1, has_side_effects=True, vmem_limit_bytes=VMEM_LIMIT
        ),
        cost_estimate=pl.CostEstimate(
            flops=64 * rows * rows * width, bytes_accessed=100_000_000, transcendentals=0
        ),
        name="attend",
    )(valid, rows_in, weight)


def attend_back_kernel(
    head_dim, group_size, valid_ref, q_ref, kv_in, grad_ref, out_ref, log_ref, *refs
):
    total_in, result_ref, total_out = refs[:3]
    q_sum, own_s, far_s, last_s, near_s, got_far, got_last, got_near, log_rows, dot_rows = refs[3:13]
    send_sem, recv_sem, kv_ref, fetch_sem = refs[13:17]
    group = lax.axis_index("grp")
    me = lax.axis_index("fsdp")
    near = {"fsdp": flip(me, 1)[0]}
    far = {"fsdp": flip(me, 2)[0]}
    wide = jnp.float32
    low = jnp.bfloat16
    pairs, rows, lanes = q_ref.shape

    def fetch(half, i):
        at = pl.ds(2 * half, 2)
        return pltpu.make_async_copy(kv_in.at[at, i], kv_ref.at[at, i], fetch_sem.at[half, i])

    chunks, take, sum_start, sum_stages, give = sum_beside(
        group, group_size, 0, total_in, total_out, refs[17:]
    )

    waits = [s + 1 + max(0, s - len(sum_stages) + 3) for s in range(len(sum_stages))]

    def sum_step(t):
        for wait, stage in zip(waits, sum_stages):
            c = t - wait

            @pl.when((c >= 0) & (c < chunks))
            def _(stage=stage, c=c):
                stage(c)

    for i in range(pairs):
        fetch(1, i).start()
    for c in range(chunks):
        take(c).start()
    for i in range(pairs):
        fetch(0, i).start()
    width = pairs * lanes
    scale = head_dim ** (-0.5)
    meet([near, far] + [{"grp": flip(group, bit)[0]} for bit in group_orders(group_size)[0]])

    def copy(kind, i, source, target, device):
        return pltpu.make_async_remote_copy(
            src_ref=source.at[i],
            dst_ref=target.at[i],
            send_sem=send_sem.at[kind, i],
            recv_sem=recv_sem.at[kind, i],
            device_id=device,
            device_id_type=pl.DeviceIdType.MESH,
        )

    def last_copy(i):
        return copy(0, i, last_s, got_last, near)

    def near_copy(i):
        return copy(1, i, near_s, got_near, near)

    def far_copy(i):
        return copy(2, i, far_s, got_far, far)

    def back(i, shards, targets):
        query = q_ref[i]
        grad = grad_ref[i]
        q_grad = None
        k_sums = [None, None]
        v_sums = [None, None]

        def plus(old, new):
            return new if old is None else old + new

        for pair in range(2):
            side = lane_half(rows, pair, head_dim)
            log_row = log_rows[i, pair : pair + 1, :]
            dot_row = dot_rows[i, pair : pair + 1, :]
            one_query = jnp.where(side, query, jnp.zeros_like(query))
            one_grad = jnp.where(side, grad, jnp.zeros_like(grad))
            for n, j in enumerate(shards):
                key = kv_ref[j, i, 0]
                one_key = jnp.where(side, key, jnp.zeros_like(key))
                raw = lax.dot_general(
                    key, one_query, (((1,), (1,)), ((), ())), preferred_element_type=wide
                )
                place = lax.broadcasted_iota(jnp.int32, raw.shape, 0)
                probs = jnp.exp(jnp.where(place < valid_ref[j], raw - log_row, masked_out))
                probs_grad = lax.dot_general(
                    kv_ref[j, i, 1], one_grad, (((1,), (1,)), ((), ())), preferred_element_type=wide
                )
                raw_grad = (probs * (probs_grad - dot_row)).astype(low)
                v_sums[n] = plus(
                    v_sums[n], jnp.dot(probs.astype(low), one_grad, preferred_element_type=wide)
                )
                k_sums[n] = plus(
                    k_sums[n], jnp.dot(raw_grad, one_query, preferred_element_type=wide)
                )
                q_grad = plus(
                    q_grad,
                    lax.dot_general(
                        raw_grad, one_key, (((0,), (0,)), ((), ())), preferred_element_type=wide
                    ),
                )
        for n, target in enumerate(targets):
            target[i, 0] = k_sums[n].astype(target.dtype)
            target[i, 1] = v_sums[n].astype(target.dtype)
        return q_grad

    def send_far(i):
        last_copy(i).wait()
        far_s[i] = (far_s[i].astype(wide) + got_last[i].astype(wide)).astype(low)
        far_copy(i).start()

    def first_loop(i, carry):
        log_t = jnp.transpose(log_ref[i])
        dots = jnp.transpose(grad_ref[i].astype(wide) * out_ref[i].astype(wide))
        for pair in range(2):
            here = slice(pair * head_dim, (pair + 1) * head_dim)
            log_rows[i, pair : pair + 1, :] = log_t[pair * head_dim : pair * head_dim + 1, :]
            dot_rows[i, pair : pair + 1, :] = jnp.sum(dots[here, :], axis=0, keepdims=True)
        fetch(1, i).wait()
        q_sum[i] = back(i, (3, 2), (last_s, far_s))
        last_copy(i).start()

        @pl.when(i > 0)
        def _():
            send_far(i - 1)

        @pl.when(i == 0)
        def _():
            sum_start()

        sum_step(i)
        return carry

    lax.fori_loop(0, pairs, first_loop, 0)
    send_far(pairs - 1)

    def second_loop(i, carry):
        fetch(0, i).wait()
        q_sum[i] = (q_sum[i] + back(i, (1, 0), (near_s, own_s))) * scale
        near_copy(i).start()
        sum_step(pairs + i)
        return carry

    lax.fori_loop(0, pairs, second_loop, 0)
    for i in range(pairs):
        near_copy(i).wait()
        far_copy(i).wait()
        at = slice(i * lanes, (i + 1) * lanes)
        result_ref[:, at] = q_sum[i].astype(low)
        for part in range(2):
            value = own_s[i, part] + got_near[i, part].astype(wide) + got_far[i, part].astype(wide)
            start = (part + 1) * width + i * lanes
            result_ref[:, start : start + lanes] = value.astype(low)
    for t in range(2 * pairs, chunks + waits[-1]):
        for wait, stage in zip(waits, sum_stages):
            if 0 <= t - wait < chunks:
                stage(t - wait)
    for c in range(chunks):
        give(c).wait()


def attend_back(group_size, queries, key_values, grad, out, logs, valid, totals, columns, chunks):
    pairs, rows, lanes = queries.shape
    head_dim = lanes // 2
    whole = pl.BlockSpec(memory_space=pltpu.VMEM)
    low = jnp.bfloat16
    wide = jnp.float32
    slab = (pairs, 2, rows, lanes)
    return pl.pallas_call(
        functools.partial(attend_back_kernel, head_dim, group_size),
        in_specs=[
            pl.BlockSpec(memory_space=pltpu.SMEM),
            whole,
            pl.BlockSpec(memory_space=pl.ANY),
            whole,
            whole,
            whole,
            pl.BlockSpec(memory_space=pl.ANY),
        ],
        out_specs=[whole, pl.BlockSpec(memory_space=pl.ANY)],
        out_shape=[
            jax.ShapeDtypeStruct((rows, 3 * pairs * lanes), low),
            jax.ShapeDtypeStruct((totals.shape[0], chunks * columns), low),
        ],
        scratch_shapes=[
            pltpu.VMEM((pairs, rows, lanes), wide),
            pltpu.VMEM(slab, wide),
            pltpu.VMEM(slab, low),
            pltpu.VMEM(slab, low),
            pltpu.VMEM(slab, low),
            pltpu.VMEM(slab, low),
            pltpu.VMEM(slab, low),
            pltpu.VMEM(slab, low),
            pltpu.VMEM((pairs, 8, rows), wide),
            pltpu.VMEM((pairs, 8, rows), wide),
            pltpu.SemaphoreType.DMA((3, pairs)),
            pltpu.SemaphoreType.DMA((3, pairs)),
            pltpu.VMEM(key_values.shape, low),
            pltpu.SemaphoreType.DMA((2, pairs)),
        ]
        + beside_buffers(group_size, chunks, totals.shape[0], columns),
        compiler_params=pltpu.CompilerParams(
            collective_id=2, has_side_effects=True, vmem_limit_bytes=VMEM_LIMIT
        ),
        cost_estimate=pl.CostEstimate(
            flops=160 * rows * rows * pairs * lanes, bytes_accessed=100_000_000, transcendentals=0
        ),
        name="attend_back",
    )(valid, queries, key_values, grad, out, logs, totals)


def feed_kernel(*refs):
    (
        share_ref, context_ref, proj_ref, embed_ref, own_in, near_in, far_in, up_in,
        down_in, bias_ref, proj_bias, gain_ref, shift_ref,
    ) = refs[:13]
    (
        middle_out, out_out, total_out, middle_grad, attended, context_grad, vectors,
    ) = refs[13:20]
    entry, gelu_s, pre_s, own_back, near_s, last_s, far_s, got_near, got_last, got_far = refs[20:30]
    grad_s, up_ref, down_ref, middle_ref, out_ref, down_total, up_total = refs[30:37]
    send_sem, recv_sem, fetch_sem, keep_sem = refs[37:]
    wide = jnp.float32
    low = jnp.bfloat16
    me = lax.axis_index("fsdp")
    near = {"fsdp": flip(me, 1)[0]}
    far = {"fsdp": flip(me, 2)[0]}
    rows, width = embed_ref.shape
    hidden = up_ref.shape[1]
    tile = rows // 2
    pairs, _, lanes = context_grad.shape
    fetches = [
        pltpu.make_async_copy(up_in, up_ref, fetch_sem.at[0]),
        pltpu.make_async_copy(own_in, grad_s.at[0], fetch_sem.at[1]),
        pltpu.make_async_copy(down_in, down_ref, fetch_sem.at[2]),
        pltpu.make_async_copy(near_in, grad_s.at[1], fetch_sem.at[3]),
        pltpu.make_async_copy(far_in, grad_s.at[pl.ds(2, 2)], fetch_sem.at[4]),
    ]
    for fetch in fetches:
        fetch.start()
    meet([near, far])

    def span(t):
        return pl.ds(t * tile, tile)

    def keep_middle(t):
        return pltpu.make_async_copy(
            middle_ref.at[span(t), :], middle_out.at[span(t), :], keep_sem.at[0, t]
        )

    def keep_out(s, t):
        return pltpu.make_async_copy(
            out_ref.at[s, span(t), :], out_out.at[s, span(t), :], keep_sem.at[1 + s, t]
        )

    def keep_total(n):
        source = (down_total, up_total)[n]
        target = total_out.at[:, pl.ds(n * width, width)]
        return pltpu.make_async_copy(source, target, keep_sem.at[5, n])

    def copy(kind, t, src, dst, device):
        return pltpu.make_async_remote_copy(
            src_ref=src.at[span(t), :],
            dst_ref=dst.at[span(t), :],
            send_sem=send_sem.at[kind, t],
            recv_sem=recv_sem.at[kind, t],
            device_id=device,
            device_id_type=pl.DeviceIdType.MESH,
        )

    def rows_near(t):
        return copy(0, t, entry.at[0], entry.at[1], near)

    def rows_far(t):
        return copy(1, t, entry.at[0], entry.at[2], far)

    def rows_last(t):
        return copy(2, t, entry.at[2], entry.at[3], near)

    def back_near(t):
        return copy(3, t, near_s, got_near, near)

    def back_last(t):
        return copy(4, t, last_s, got_last, near)

    def back_far(t):
        return copy(5, t, far_s, got_far, far)

    def feed(s, t, target):
        rows_in = entry[s, span(t), :]
        pre_act = jnp.dot(rows_in, up_ref[...], preferred_element_type=wide) + bias_ref[...]
        cdf = 0.5 * (1.0 + lax.erf(pre_act * 0.7071067811865476))
        density = jnp.exp(-0.5 * pre_act * pre_act) * 0.3989422804014327
        gelu = (pre_act * cdf).astype(low)
        gelu_s[s, span(t), :] = gelu
        act_grad = lax.dot_general(
            grad_s[s, span(t), :],
            down_ref[...],
            (((1,), (1,)), ((), ())),
            preferred_element_type=wide,
        )
        pre_grad = act_grad * (cdf + pre_act * density)
        pre_low = pre_grad.astype(low)
        pre_s[s, span(t), :] = pre_low
        vectors[4:5, :] += jnp.sum(pre_low.astype(wide), axis=0, keepdims=True)
        out_ref[s, span(t), :] = jnp.dot(
            gelu, down_ref[...], preferred_element_type=wide
        ).astype(low)
        keep_out(s, t).start()
        target[span(t), :] = lax.dot_general(
            pre_low, up_ref[...], (((1,), (1,)), ((), ())), preferred_element_type=wide
        ).astype(target.dtype)

    vectors[...] = jnp.zeros_like(vectors)
    for t in range(2):
        middle = (
            embed_ref[span(t), :]
            + jnp.dot(context_ref[span(t), :], proj_ref[...], preferred_element_type=wide)
            + proj_bias[...]
        )
        middle_ref[span(t), :] = middle
        xhat, inverse = normalise(middle)
        entry[0, span(t), :] = (xhat * gain_ref[...] + shift_ref[...]).astype(low)
        rows_far(t).start()
        rows_near(t).start()
        keep_middle(t).start()
    for fetch in fetches[:3]:
        fetch.wait()
    for t in range(2):
        feed(0, t, own_back)
    for fetch in fetches[3:]:
        fetch.wait()
    for t in range(2):
        rows_near(t).wait()
        feed(1, t, near_s)
        back_near(t).start()

    for t in range(2):
        rows_far(t).wait()
        rows_last(t).start()
        feed(2, t, far_s)
        rows_last(t).wait()
        feed(3, t, last_s)
        back_last(t).start()
        if t > 0:
            add_last(t - 1, back_last, back_far, far_s, got_last, span)
    add_last(1, back_last, back_far, far_s, got_last, span)

    block = min(hidden, 256)
    for start in range(0, hidden, block):
        value = 0.0
        for s in range(4):
            value = value + lax.dot_general(
                gelu_s[s, :, start : start + block],
                grad_s[s],
                (((0,), (0,)), ((), ())),
                preferred_element_type=wide,
            )
        down_total[start : start + block, :] = (value * share_ref[0]).astype(low)
    keep_total(0).start()
    for start in range(0, width, block):
        value = 0.0
        for s in range(4):
            value = value + lax.dot_general(
                entry[s, :, start : start + block],
                pre_s[s],
                (((0,), (0,)), ((), ())),
                preferred_element_type=wide,
            )
        up_total[start : start + block, :] = (value * share_ref[0]).astype(low)
    keep_total(1).start()

    for t in range(2):
        back_near(t).wait()
        back_far(t).wait()
        at = span(t)
        grad = own_back[at, :] + got_near[at, :].astype(wide) + got_far[at, :].astype(wide)
        xhat, inverse = normalise(middle_ref[at, :])
        vectors[0:1, :] += jnp.sum(grad * xhat, axis=0, keepdims=True)
        vectors[1:2, :] += jnp.sum(grad, axis=0, keepdims=True)
        upstream = grad_s[0, at, :].astype(wide)
        vectors[3:4, :] += jnp.sum(upstream, axis=0, keepdims=True)
        value = upstream + norm_back(grad, xhat, inverse, gain_ref[...])
        middle_grad[at, :] = value
        value_low = value.astype(low)
        attended[at, :] = value_low
        vectors[2:3, :] += jnp.sum(value_low.astype(wide), axis=0, keepdims=True)
        back = lax.dot_general(
            value_low, proj_ref[...], (((1,), (1,)), ((), ())), preferred_element_type=wide
        ).astype(low)
        for i in range(pairs):
            context_grad[i, at, :] = back[:, i * lanes : (i + 1) * lanes]
    for t in range(2):
        keep_middle(t).wait()
        keep_total(t).wait()
        for s in range(4):
            keep_out(s, t).wait()


def add_last(t, back_last, back_far, far_s, got_last, span):
    back_last(t).wait()
    at = span(t)
    value = far_s[at, :].astype(jnp.float32) + got_last[at, :].astype(jnp.float32)
    far_s[at, :] = value.astype(jnp.bfloat16)
    back_far(t).start()


def feed(
    share, context, proj, embedded, own_grad, near_grad, far_grads, up, down, bias, proj_bias, gain, shift
):
    rows, width = embedded.shape
    hidden = up.shape[1]
    pairs = HEADS // 2
    low = jnp.bfloat16
    wide = jnp.float32
    vmem = pl.BlockSpec(memory_space=pltpu.VMEM)
    hbm = pl.BlockSpec(memory_space=pl.ANY)
    flat = (rows, width)

    def shape(dims, kind):
        return jax.ShapeDtypeStruct(dims, kind)

    return pl.pallas_call(
        feed_kernel,
        in_specs=[pl.BlockSpec(memory_space=pltpu.SMEM)] + [vmem] * 3 + [hbm] * 5 + [vmem] * 4,
        out_specs=[hbm] * 3 + [vmem] * 4,
        out_shape=[
            shape(flat, wide),
            shape((4,) + flat, low),
            shape((width, width + hidden), low),
            shape(flat, wide),
            shape(flat, low),
            shape((pairs, rows, width // pairs), low),
            shape((8, width), wide),
        ],
        scratch_shapes=[
            pltpu.VMEM((4,) + flat, low),
            pltpu.VMEM((4, rows, hidden), low),
            pltpu.VMEM((4, rows, hidden), low),
            pltpu.VMEM(flat, wide),
            pltpu.VMEM(flat, low),
            pltpu.VMEM(flat, low),
            pltpu.VMEM(flat, low),
            pltpu.VMEM(flat, low),
            pltpu.VMEM(flat, low),
            pltpu.VMEM(flat, low),
            pltpu.VMEM((4,) + flat, low),
            pltpu.VMEM(up.shape, low),
            pltpu.VMEM(down.shape, low),
            pltpu.VMEM(flat, wide),
            pltpu.VMEM((4,) + flat, low),
            pltpu.VMEM((hidden, width), low),
            pltpu.VMEM((width, hidden), low),
            pltpu.SemaphoreType.DMA((6, 2)),
            pltpu.SemaphoreType.DMA((6, 2)),
            pltpu.SemaphoreType.DMA((5,)),
            pltpu.SemaphoreType.DMA((6, 2)),
        ],
        compiler_params=pltpu.CompilerParams(
            collective_id=4, has_side_effects=True, vmem_limit_bytes=VMEM_LIMIT
        ),
        cost_estimate=pl.CostEstimate(
            flops=48 * rows * width * hidden, bytes_accessed=100_000_000, transcendentals=0
        ),
        name="feed",
    )(
        share, context, proj, embedded, own_grad, near_grad, far_grads, up, down, bias,
        proj_bias, gain, shift,
    )


def finish_kernel(group_size, widths, head_dim, first_chunk, *refs):
    share_ref = refs[0]
    left_qkv, qkv_grad, left_agg_in, left_proj_in, attended_in = refs[1:6]
    (
        full_qkv, full_agg_in, full_value, embed_in, middle_in, gain_ref, vectors_ref, patch_ref,
        coeff_ref, mask_ref, table_ref, select_ref, own_columns, keys_ref, query_ref, key_w,
        query_w, own_query, out_sum, total_in,
    ) = refs[6:26]
    outs = refs[26:29]
    value_out, key_out, query_out, agg_query_out, var_out, extra_out, patch_grad = refs[29:36]
    out_far, total_out = refs[36:38]
    sets = [refs[38:48], refs[48:57]]
    full, query_part, query_got, var_s, last_send, last_recv = refs[57:63]
    entry_grad, embed_grad, heads_grad, table_s, coeff_s, extras, bundle = refs[63:70]
    weight_s, weight_sem, left_agg, left_proj, attended, full_agg, embed_ref, middle_grad = refs[70:78]
    fetch_sem = refs[78]
    sum_chunks, sum_take, sum_start, sum_stages, sum_give = sum_beside(
        lax.axis_index("grp"), group_size, first_chunk, total_in, total_out, refs[79:]
    )
    fetches = [
        pltpu.make_async_copy(source, target, fetch_sem.at[n])
        for n, (source, target) in enumerate(
            [
                (embed_in, embed_ref),
                (middle_in, middle_grad),
                (full_agg_in, full_agg),
                (left_proj_in, left_proj),
                (attended_in, attended),
                (left_agg_in, left_agg),
            ]
        )
    ]
    me = lax.axis_index("fsdp")
    group = lax.axis_index("grp")
    core_partner, core = flip(me, 1)
    far_partner, far = flip(me, 2)
    diagonal = flip(far_partner, 1)[0]
    wide = jnp.float32
    low = jnp.bfloat16
    quarters = [buffers[2].shape[2] for buffers in sets]
    all_steps = [
        group_steps(group, group_orders(group_size)[0], quarter) for quarter in quarters
    ]
    all_halvings = [[i for i, step in enumerate(steps) if step[2]] for steps in all_steps]
    count = len(all_steps[0])
    slots = sets[1][0].shape[0]
    others = [{"fsdp": core_partner}, {"fsdp": far_partner}, {"fsdp": diagonal}]
    pltpu.make_async_copy(full_qkv.at[:, pl.ds(0, key_w.shape[1])], weight_s, weight_sem.at[0]).start()
    for c in range(sum_chunks):
        sum_take(c).start()
    for fetch in fetches:
        fetch.start()
    meet(others + [{"grp": step[0]} for step in all_steps[0]])

    def pieces(left, right, out):
        return [(left, right, out, start) for start in range(0, right.shape[1], widths)]

    qkv_pieces = pieces(left_qkv, qkv_grad, outs[0])
    agg_pieces = pieces(left_agg, embed_grad, outs[1])
    proj_pieces = pieces(left_proj, attended, outs[2])
    bulk = qkv_pieces + proj_pieces[:1] + [None] + proj_pieces[1:] + agg_pieces
    chunks = []
    for piece in bulk:
        if piece is None:
            chunks.append((0, 0, None, None, None, 0))
        else:
            chunks.append((1, sum(chunk[0] for chunk in chunks)) + piece)
    small = bulk.index(None)

    def remote(src, dst, send, recv, device):
        return pltpu.make_async_remote_copy(
            src_ref=src,
            dst_ref=dst,
            send_sem=send,
            recv_sem=recv,
            device_id=device,
            device_id_type=pl.DeviceIdType.MESH,
        )

    def copy(stage, c, src, dst, device):
        which, place = chunks[c][:2]
        send_sem, recv_sem = sets[which][-2:]
        return remote(src, dst, send_sem.at[stage, place], recv_sem.at[stage, place], device)

    def span(start, size):
        return pl.ds(pl.multiple_of(start, 16), size)

    def held(c):
        which, place, left, right, out, start = chunks[c]
        buffers = sets[which]
        rest = [
            buffer.at[place % slots if n in (0, 2) else place]
            for n, buffer in enumerate(buffers[:6])
        ]
        rest.append([part.at[place] for part in buffers[6]])
        rest.append(buffers[7].at[place] if out is None else out.at[:, start : start + widths])
        return rest

    def core_copy(c):
        at = held(c)
        return copy(0, c, at[0], at[1], others[0])

    def far_copy(c):
        at = held(c)
        return copy(1, c, at[3], at[4], others[1])

    def step_copy(i, c):
        partner, bit_set, halving, size, offset = all_steps[chunks[c][0]][i]
        if halving:
            size = size // 2
            offset = offset + (1 - bit_set) * size
        at = held(c)
        return copy(2 + i, c, at[5].at[span(offset, size), :], at[6][i], {"grp": partner})

    def back_copy(i, c):
        partner, bit_set, halving, size, offset = all_steps[chunks[c][0]][i]
        size = size // 2
        offset = offset + bit_set * size
        at = held(c)[7].at[span(offset, size), :]
        return copy(2 + count + i, c, at, at, {"grp": partner})

    def begin(c):
        which, place, left, right, out, start = chunks[c]
        quarter = quarters[which]
        send1, recv1, own1 = held(c)[:3]

        def part(q):
            if left is None:
                return bundle[q]
            value = jnp.dot(
                left[span(q * quarter, quarter), :],
                right[:, start : start + widths],
                preferred_element_type=wide,
            )
            return (value * share_ref[0]).astype(low)

        for y in range(2):
            send1[y] = part(2 * y + 1 - core)
        core_copy(c).start()
        for y in range(2):
            own1[y] = part(2 * y + core)

    def after_core(c):
        send1, recv1, own1, send2 = held(c)[:4]
        core_copy(c).wait()
        value = own1[1 - far].astype(wide) + recv1[1 - far].astype(wide)
        send2[...] = value.astype(low)
        far_copy(c).start()

    def after_far(c):
        send1, recv1, own1, send2, recv2, hold = held(c)[:6]
        far_copy(c).wait()
        value = own1[far].astype(wide) + recv1[far].astype(wide) + recv2[...].astype(wide)
        hold[...] = value.astype(low)
        step_copy(0, c).start()

    def after_step(i, c):
        step_copy(i, c).wait()
        hold, halves, done = held(c)[5:]
        steps, halvings = all_steps[chunks[c][0]], all_halvings[chunks[c][0]]
        partner, bit_set, halving, size, offset = steps[i]
        if halving:
            size = size // 2
            offset = offset + bit_set * size
        at = span(offset, size)
        value = hold[at, :].astype(wide) + halves[i][...].astype(wide)
        if i + 1 < count:
            hold[at, :] = value.astype(low)
            step_copy(i + 1, c).start()
        else:
            done[at, :] = value.astype(low)
            back_copy(halvings[-1], c).start()

    def after_back(k, c):
        halvings = all_halvings[chunks[c][0]]
        if k >= len(halvings):
            return
        back_copy(halvings[k], c).wait()
        if k > 0:
            back_copy(halvings[k - 1], c).start()
        elif chunks[c][0] == 0:
            full[me] = held(c)[7][...]
            bundle_core().start()

    def bundle_core():
        at = full.at[me]
        return remote(at, at, last_send.at[0], last_recv.at[0], others[0])

    def bundle_far():
        at = full.at[pl.ds(me - core, 2)]
        return remote(at, at, last_send.at[1], last_recv.at[1], others[1])

    def query_copy(kind):
        return remote(
            query_part,
            query_got.at[kind],
            last_send.at[2 + kind],
            last_recv.at[2 + kind],
            others[kind],
        )

    size = own_columns.shape[0]
    width = key_w.shape[1]
    part_rows = quarters[0]
    spare = extra_out.shape[0] // 4
    per_row = width // size
    scale = head_dim ** (-0.5)

    def coefficients():
        rows = []
        for n in range(HEADS):
            place, column = n // per_row, (n % per_row) * size
            shard, row = place // spare, part_rows - spare + place % spare
            rows.append(full[shard, row : row + 1, column : column + size].astype(wide))
        return jnp.concatenate(rows, axis=0)

    def own_head(value):
        lane = lax.broadcasted_iota(jnp.int32, (HEADS, width), 1)
        head = lax.broadcasted_iota(jnp.int32, (HEADS, width), 0)
        return jnp.where(lane // head_dim == head, value, 0.0)

    def key_grad(coeffs):
        return jnp.dot(coeffs.astype(low), own_columns[...], preferred_element_type=wide)

    def finish_core():
        bundle_core().wait()
        bundle_far().start()

    def finish_far():
        bundle_far().wait()
        spread = jnp.dot(
            key_grad(coefficients()).astype(low), key_w[...], preferred_element_type=wide
        )
        partial = jnp.sum(own_head(spread), axis=0, keepdims=True) * scale
        query_part[...] = jnp.broadcast_to(partial, query_part.shape)
        for kind in range(3):
            query_copy(kind).start()

    def finish_table():
        weights(3).wait()
        table = full[...].reshape(size, width)
        value_out[...] = lax.dot_general(
            own_columns[...], table, (((0,), (0,)), ((), ())), preferred_element_type=wide
        )
        coeffs = coefficients()
        var_s[...] = lax.dot_general(
            coeffs.astype(low), keys_ref[...], (((0,), (0,)), ((), ())), preferred_element_type=wide
        )
        var_out[...] = var_s[span(me * part_rows, part_rows), :] + lax.dot_general(
            full[me], weight_s[...], (((1,), (1,)), ((), ())), preferred_element_type=wide
        )
        for q in range(4):
            extra_out[q * spare : (q + 1) * spare, :] = full[q, part_rows - spare :, :].astype(wide)

    def finish_query():
        for kind in range(3):
            query_copy(kind).wait()
        grad = query_part[...] + query_got[0] + query_got[1] + query_got[2]
        query_out[...] = own_query[...] * grad[:1]
        agg_query_out[...] = lax.dot_general(
            grad,
            query_w[...].astype(wide),
            (((1,), (1,)), ((), ())),
            preferred_element_type=wide,
            precision=exact_mode,
        )
        spread = own_head(jnp.broadcast_to(query_ref[:1].astype(low).astype(wide), (HEADS, width)))
        key_out[...] = scale * lax.dot_general(
            key_grad(coefficients()),
            spread,
            (((0,), (0,)), ((), ())),
            preferred_element_type=wide,
            precision=exact_mode,
        )

    def weights(n):
        source = full_qkv.at[:, pl.ds(n * width, width)] if n < 3 else full_value
        return pltpu.make_async_copy(source, weight_s, weight_sem.at[0])

    def entry_part(n):
        weights(n).wait()
        value = lax.dot_general(
            qkv_grad[:, n * width : (n + 1) * width],
            weight_s[...],
            (((1,), (1,)), ((), ())),
            preferred_element_type=wide,
        )
        entry_grad[...] = value if n == 0 else entry_grad[...] + value
        weights(n + 1).start()

    def norm_part():
        for fetch in fetches:
            fetch.wait()
        grad = entry_grad[...]
        xhat, inverse = normalise(embed_ref[...])
        extras[...] = jnp.zeros_like(extras)
        value = middle_grad[...] + norm_back(grad, xhat, inverse, gain_ref[...])
        value_low = value.astype(low)
        embed_grad[...] = value_low
        first = HEADS // per_row
        extras[first : first + 1, :] = jnp.sum(value_low.astype(wide), axis=0, keepdims=True)
        extras[first + 1 : first + 2, :] = jnp.sum(grad * xhat, axis=0, keepdims=True)
        extras[first + 2 : first + 3, :] = jnp.sum(grad, axis=0, keepdims=True)
        for n in range(4):
            extras[first + 3 + n : first + 4 + n, :] = vectors_ref[n : n + 1, :]
        extras[pl.ds(first + 7 + me, 1), :] = vectors_ref[4:5, :]

    def heads_part():
        heads_grad[...] = lax.dot_general(
            full_agg[...], embed_grad[...], (((1,), (1,)), ((), ())), preferred_element_type=wide
        ).astype(low)
        patch_grad[...] = jnp.zeros_like(patch_grad)
        coeff_s[...] = jnp.zeros_like(coeff_s)

    slot_count = mask_ref.shape[0]

    def one_head(h, carry):
        lane = lax.broadcasted_iota(jnp.int32, (slot_count, HEADS), 1)
        columns = head_columns(coeff_ref, h, slot_count)
        weights = slot_softmax(patch_ref, columns, mask_ref)
        mixed = mixed_of(patch_ref, weights, table_ref.shape[1])
        at = pl.ds(pl.multiple_of(h * head_dim, 16), head_dim)
        grad = heads_grad[at, :]
        table_s[at, :] = (
            lax.dot_general(grad, mixed, (((1,), (1,)), ((), ())), preferred_element_type=wide)
            * share_ref[0]
        ).astype(low)
        mixed_grad = lax.dot_general(
            table_ref[at, :], grad, (((0,), (0,)), ((), ())), preferred_element_type=wide
        )
        parts = [
            mixed_grad[k * slot_count : (k + 1) * slot_count] for k in range(PIX + 1)
        ]
        values = [patch_ref[k].astype(wide) for k in range(PIX)]
        weights_grad = parts[PIX]
        for k in range(PIX):
            weights_grad = weights_grad + parts[k] * values[k]
        mean_grad = jnp.sum(weights * weights_grad, axis=0, keepdims=True)
        scores_grad = weights * (weights_grad - mean_grad)
        for k in range(PIX + 1):
            value = scores_grad * values[k] if k < PIX else scores_grad
            column = jnp.sum(value, axis=1, keepdims=True)
            rows = slice(k * slot_count, (k + 1) * slot_count)
            coeff_s[rows, :] = coeff_s[rows, :] + jnp.where(lane == h, column, 0.0)
        for k in range(PIX):
            patch_grad[k] += share_ref[1] * (parts[k] * weights + scores_grad * columns[k])
        return carry

    def heads_from(first, last):
        lax.fori_loop(first, last, one_head, 0)

    def bundle_part():
        sums = lax.dot_general(
            select_ref[...], table_s[...], (((0,), (1,)), ((), ())), preferred_element_type=wide
        )
        coeff_sum = lax.dot_general(
            coeff_s[...],
            select_ref[...].astype(wide),
            (((0,), (0,)), ((), ())),
            preferred_element_type=wide,
            precision=exact_mode,
        )
        for n in range(HEADS):
            place, column = n // per_row, (n % per_row) * size
            extras[place : place + 1, column : column + size] = coeff_sum[n : n + 1, :]
        row = lax.broadcasted_iota(jnp.int32, (size, extras.shape[0]), 0)
        line = lax.broadcasted_iota(jnp.int32, (size, extras.shape[0]), 1)
        spot = (row // part_rows) * spare + row % part_rows - (part_rows - spare)
        chosen = (spot == line) & (row % part_rows >= part_rows - spare)
        placed = jnp.dot(
            chosen.astype(low),
            (extras[...] * share_ref[0]).astype(low),
            preferred_element_type=wide,
        )
        bundle[...] = (sums + placed).astype(low).reshape(bundle.shape)

    middle_parts = [[functools.partial(entry_part, n)] for n in range(3)]
    middle_parts += [[norm_part, heads_part]]
    third = HEADS // 4
    middle_parts += [
        [functools.partial(heads_from, 0, third)],
        [functools.partial(heads_from, third, 2 * third)],
        [
            functools.partial(heads_from, 2 * third, HEADS),
            bundle_part,
        ],
    ]

    out_copy = remote(out_sum, out_far, last_send.at[5], last_recv.at[5], others[1])
    stages = [begin, after_core, after_far]
    stages += [functools.partial(after_step, i) for i in range(count)]
    stages += [functools.partial(after_back, k) for k in reversed(range(count))]
    extra = [finish_core, finish_far, finish_table, finish_query]
    steps = max(len(chunks), small + 1 + len(extra)) + len(stages) - 1
    for t in range(steps):
        for s in [1, 0]:
            if 0 <= t - s < len(chunks):
                stages[s](t - s)
        if t == 0:
            sum_start()
        if t < len(middle_parts):
            for part in middle_parts[t]:
                part()
        for s in range(2, len(stages)):
            if 0 <= t - s < len(chunks):
                stages[s](t - s)
        if 0 <= t - small - len(stages) < len(extra):
            extra[t - small - len(stages)]()
        for s, stage in enumerate(sum_stages):
            for c in range(sum_chunks):
                if t == 1 + s + c // 2:
                    stage(c)
        if t == len(chunks):
            out_copy.start()
    out_copy.wait()
    for c in range(sum_chunks):
        sum_give(c).wait()


def finish(group_size, spare, shares, lefts, rights, columns, first_chunk, others):
    left_qkv, left_agg, left_proj = lefts
    qkv_grad, attended = rights
    width, rows = left_qkv.shape
    quarter = width // 4
    widths = 512
    low = jnp.bfloat16
    wide = jnp.float32
    size = others["own_columns"].shape[0]
    part = size // 4
    steps = 0
    while 2**steps < group_size:
        steps += 1

    def buffers(count, slots, rows, columns, last):
        halves = []
        size = rows
        for _ in range(steps):
            if size >= 32:
                size //= 2
            halves.append(pltpu.VMEM((count, size, columns), low))
        few = pltpu.VMEM((slots, 2, rows, columns), low)
        two = pltpu.VMEM((count, 2, rows, columns), low)
        one = pltpu.VMEM((count, rows, columns), low)
        semaphores = pltpu.SemaphoreType.DMA((2 + 2 * steps, count))
        found = [few, two, few, one, one, one, halves]
        return found + ([one] if last else []) + [semaphores, semaphores]

    shapes = [(quarter, qkv_grad.shape[1]), (quarter, width), (quarter, width)]
    count = sum(columns for _, columns in shapes) // widths
    scratch = buffers(1, 1, part, width, True) + buffers(count, 3, quarter, widths, False)
    scratch += [
        pltpu.VMEM((4, part, width), low),
        pltpu.VMEM((8, width), wide),
        pltpu.VMEM((3, 8, width), wide),
        pltpu.VMEM((size, width), wide),
        pltpu.SemaphoreType.DMA((6,)),
        pltpu.SemaphoreType.DMA((6,)),
        pltpu.VMEM((rows, width), wide),
        pltpu.VMEM((rows, width), low),
        pltpu.VMEM((width, rows), low),
        pltpu.VMEM((width, size), low),
        pltpu.VMEM((size, HEADS), wide),
        pltpu.VMEM((4 * spare, width), wide),
        pltpu.VMEM((4, part, width), low),
        pltpu.VMEM((width, width), low),
        pltpu.SemaphoreType.DMA((1,)),
        pltpu.VMEM((width, rows), low),
        pltpu.VMEM((width, rows), low),
        pltpu.VMEM((rows, width), low),
        pltpu.VMEM((width, width), low),
        pltpu.VMEM((rows, width), wide),
        pltpu.VMEM((rows, width), wide),
        pltpu.SemaphoreType.DMA((6,)),
    ]
    totals = others["totals"]
    left_chunks = totals.shape[1] // columns - first_chunk
    scratch += beside_buffers(group_size, left_chunks, totals.shape[0], columns)
    whole = pl.BlockSpec(memory_space=pltpu.VMEM)
    out_shape = [jax.ShapeDtypeStruct(dims, low) for dims in shapes]
    more = [(quarter, width)] * 3 + [(8, quarter), (part, width), (4 * spare, width)]
    more.append(others["patch_rows"].shape)
    out_shape += [jax.ShapeDtypeStruct(dims, wide) for dims in more]
    out_shape.append(jax.ShapeDtypeStruct(others["out_sum"].shape, low))
    out_shape.append(jax.ShapeDtypeStruct((totals.shape[0], left_chunks * columns), low))
    hbm = pl.BlockSpec(memory_space=pl.ANY)
    far_off = ("full_qkv", "full_agg", "full_value", "embedded", "middle_grad", "out_sum", "totals")
    operands = [shares, left_qkv, qkv_grad, left_agg, left_proj, attended, *others.values()]
    return pl.pallas_call(
        functools.partial(finish_kernel, group_size, widths, width // HEADS, first_chunk),
        in_specs=[pl.BlockSpec(memory_space=pltpu.SMEM), whole, whole, hbm, hbm, hbm]
        + [hbm if name in far_off else whole for name in others],
        out_specs=[whole] * (len(out_shape) - 2) + [hbm] * 2,
        out_shape=out_shape,
        scratch_shapes=scratch,
        compiler_params=pltpu.CompilerParams(
            collective_id=0, has_side_effects=True, vmem_limit_bytes=62 * 1024 * 1024
        ),
        cost_estimate=pl.CostEstimate(
            flops=20 * rows * width * width, bytes_accessed=200_000_000, transcendentals=0
        ),
        name="finish",
    )(*operands)


def on_device(
    patches,
    patch_counts,
    var_present,
    item_dataset,
    var_ids,
    patch_weight,
    var_embed,
    agg_query,
    query_weight,
    key_weight,
    value_weight,
    agg_proj,
    agg_bias,
    norm1_gain,
    norm1_shift,
    qkv_weight,
    proj_weight,
    proj_bias,
    norm2_gain,
    norm2_shift,
    up_weight,
    up_bias,
    down_weight,
    down_bias,
    out_grad,
):
    low = jnp.bfloat16
    wide = jnp.float32
    rows = patches.shape[2]
    me = lax.axis_index("fsdp")
    group_count = lax.axis_size("grp")
    width = proj_weight.shape[1]
    head_dim = width // HEADS
    own_width = width // 4
    own_vars = patch_weight.shape[0]

    item_count = patch_counts[0]
    own_valid = me * rows + jnp.arange(rows, dtype=jnp.int32) < item_count
    shard_valid = jnp.clip(
        item_count - (me ^ jnp.arange(4, dtype=jnp.int32)) * rows, 0, rows
    ).astype(jnp.int32)
    down_grad = jnp.where(own_valid[:, None], out_grad, jnp.zeros_like(out_grad))

    slot_vars = lax.dynamic_index_in_dim(var_ids, item_dataset[0], 0, keepdims=False)
    part_size = -(-(PIX + 1) * own_vars // 16) * 16
    size = 4 * part_size
    slot_row = jnp.arange(size, dtype=jnp.int32)
    slot_var = jnp.pad(jnp.tile(slot_vars, PIX + 1), (0, size - (PIX + 1) * VTOT))
    place = (slot_var // own_vars) * part_size + (slot_row // VTOT) * own_vars + slot_var % own_vars
    select = (
        (place[:, None] == jnp.arange(size, dtype=jnp.int32)[None, :])
        & (slot_row < (PIX + 1) * VTOT)[:, None]
    ).astype(low)
    own_table = jnp.concatenate(
        [
            patch_weight.transpose(1, 0, 2).reshape(own_vars * PIX, width),
            var_embed,
            jnp.zeros((part_size - (PIX + 1) * own_vars, width), low),
        ],
        axis=0,
    )
    own_query = lax.dynamic_slice_in_dim(agg_query, me * own_width, own_width, 0)
    patch_rows = patches.transpose(1, 0, 2)
    slot_mask = jnp.where(var_present[0] > 0, 0.0, masked_out).astype(wide)[:, None]
    (
        count_rows,
        tables,
        query_rows,
        key_query,
        full_value,
        full_agg_proj,
        full_qkv,
        full_proj,
        near_down_grad,
        far_grads,
        table_values,
        coeffs,
        heads_t,
        embedded,
        normed1,
    ) = prepare(
        group_count,
        jnp.full((8, 128), item_count.astype(wide)),
        jnp.broadcast_to(own_query[None, :], (16, own_width)),
        query_weight,
        key_weight,
        own_table,
        select,
        value_weight,
        agg_proj,
        qkv_weight,
        proj_weight,
        down_grad,
        patch_rows,
        slot_mask,
        agg_bias[None, :],
        norm1_gain[None, :],
        norm1_shift[None, :],
    )
    count_share = item_count.astype(wide) / count_rows[0, 0]
    own_columns = lax.dynamic_slice_in_dim(
        tables.reshape(size, width), me * own_width, own_width, 1
    )

    queries, key_values, context_pairs, logs = attend(normed1, full_qkv, shard_valid)
    context = context_pairs.transpose(1, 0, 2).reshape(rows, width)
    (
        middle,
        out_parts,
        totals,
        middle_grad,
        attended_grad,
        context_grad,
        feed_vectors,
    ) = feed(
        count_share[None],
        context,
        full_proj,
        embedded,
        down_grad,
        near_down_grad,
        far_grads,
        up_weight,
        down_weight,
        up_bias.astype(wide)[None, :],
        proj_bias[None, :],
        norm2_gain[None, :],
        norm2_shift[None, :],
    )
    out_got = swap(jnp.stack([out_parts[1], out_parts[3]]), "fsdp", 1)
    out_sum = (out_parts[2].astype(wide) + out_got[1].astype(wide)).astype(low)

    columns = width // 8
    chunks = 12
    qkv_grad, summed = attend_back(
        group_count,
        queries,
        key_values,
        context_grad,
        context_pairs,
        logs,
        shard_valid,
        totals,
        columns,
        chunks,
    )
    down_weight_grad = summed[:, :width].astype(wide)
    spare = part_size - (PIX + 1) * own_vars
    (
        qkv_weight_grad,
        agg_proj_grad,
        proj_weight_grad,
        value_weight_grad,
        key_weight_grad,
        query_weight_grad,
        agg_query_grad,
        var_grads,
        extras,
        patch_grad,
        out_far,
        rest,
    ) = finish(
        group_count,
        spare,
        jnp.stack([count_share, group_count * count_share]),
        (normed1.T, heads_t, context.T),
        (qkv_grad, attended_grad),
        columns,
        chunks,
        dict(
            full_qkv=full_qkv,
            full_agg=full_agg_proj,
            full_value=full_value,
            embedded=embedded,
            middle_grad=middle_grad,
            gain=norm1_gain[None, :],
            vectors=feed_vectors,
            patch_rows=patch_rows,
            coeffs=coeffs,
            slot_mask=slot_mask,
            table_values=table_values,
            select=select,
            own_columns=own_columns,
            key_query=key_query,
            query_rows=query_rows,
            key_weight=key_weight,
            query_weight=query_weight,
            own_query=own_query.astype(wide)[:, None],
            out_sum=out_sum,
            totals=totals,
        ),
    )
    down_sum = out_parts[0].astype(wide) + out_got[0].astype(wide) + out_far.astype(wide)
    output = (middle + down_sum + down_bias).astype(low)
    up_weight_grad = jnp.concatenate([summed[:, width:], rest], axis=1).astype(wide)
    patches_grad = patch_grad.transpose(1, 0, 2)
    qkv_weight_grad = qkv_weight_grad.astype(wide)
    agg_proj_grad = agg_proj_grad.astype(wide)
    proj_weight_grad = proj_weight_grad.astype(wide)
    at = HEADS * size // width
    vector_total = extras[at : at + 7]
    at += 7
    up_bias_total = lax.dynamic_slice_in_dim(extras, at + me, 1, 0)[0]
    vector_own = lax.dynamic_slice_in_dim(vector_total, me * own_width, own_width, 1)
    agg_query_grad = agg_query_grad[0]
    var_grads = var_grads[: (PIX + 1) * own_vars].reshape(PIX + 1, own_vars, width)
    patch_weight_grad = var_grads[:PIX].transpose(1, 0, 2)
    var_embed_grad = var_grads[PIX]
    return (
        output,
        patches_grad,
        patch_weight_grad,
        var_embed_grad,
        agg_query_grad,
        query_weight_grad,
        key_weight_grad,
        value_weight_grad,
        agg_proj_grad,
        vector_own[0],
        vector_own[1],
        vector_own[2],
        qkv_weight_grad,
        proj_weight_grad,
        vector_own[5],
        vector_own[3],
        vector_own[4],
        up_weight_grad,
        up_bias_total,
        down_weight_grad,
        vector_own[6],
    )


def solution(mesh):
    shard = P("fsdp")
    shard_rows = P("fsdp", None)
    return jax.shard_map(
        on_device,
        mesh=mesh,
        in_specs=(
            P(None, None, ("grp", "fsdp")),
            P("grp"),
            P("grp", None),
            P("grp"),
            P(),
            P("fsdp", None, None),
            shard_rows,
            P(),
            shard_rows,
            shard_rows,
            shard_rows,
            shard_rows,
            P(),
            P(),
            P(),
            shard_rows,
            shard_rows,
            P(),
            P(),
            P(),
            P(None, "fsdp"),
            shard,
            shard_rows,
            P(),
            P(("grp", "fsdp"), None),
        ),
        out_specs=(
            P(("grp", "fsdp"), None),
            P(None, None, ("grp", "fsdp")),
            P("fsdp", None, None),
            shard_rows,
            shard,
            shard_rows,
            shard_rows,
            shard_rows,
            shard_rows,
            shard,
            shard,
            shard,
            shard_rows,
            shard_rows,
            shard,
            shard,
            shard,
            P(None, "fsdp"),
            shard,
            shard_rows,
            shard,
        ),
        check_vma=False,
    )
```

```python
import functools

import jax
import jax.numpy as jnp
from jax import lax
from jax.experimental import pallas as pl
from jax.experimental.pallas import tpu as pltpu
from jax.sharding import PartitionSpec as P

HEADS = 16
VTOT = 48
PIX = 4

exact_mode = lax.Precision.HIGHEST
masked_out = -1e30
VMEM_LIMIT = 56 * 1024 * 1024


def swap(value, axis, bit):
    size = lax.axis_size(axis)
    return lax.ppermute(value, axis, [(i, i ^ bit) for i in range(size)])


def product(left_side, right_side):
    return jnp.dot(left_side, right_side, preferred_element_type=jnp.float32)


def left_product(left_side, right_side):
    return lax.dot_general(
        left_side, right_side, (((0,), (0,)), ((), ())), preferred_element_type=jnp.float32
    )


def right_product(left_side, right_side):
    return lax.dot_general(
        left_side, right_side, (((1,), (1,)), ((), ())), preferred_element_type=jnp.float32
    )


def column_sums(values_in):
    return jnp.sum(values_in.astype(jnp.float32), axis=0)


def flip(index, bit):
    bit_set = (index // bit) % 2
    return index + bit - 2 * bit * bit_set, bit_set


def meet(partners):
    barrier = pltpu.get_barrier_semaphore()
    for partner in partners:
        pl.semaphore_signal(
            barrier, inc=1, device_id=partner, device_id_type=pl.DeviceIdType.MESH
        )
    pl.semaphore_wait(barrier, len(partners))


def normalise(values_in):
    row_mean = jnp.mean(values_in, axis=-1, keepdims=True)
    centred = values_in - row_mean
    spread = jnp.mean(centred * centred, axis=-1, keepdims=True)
    inverse = lax.rsqrt(spread + 1e-05)
    return centred * inverse, inverse


def norm_back(grad, xhat, inverse, gain_vec):
    scaled = grad * gain_vec
    first = jnp.mean(scaled, axis=-1, keepdims=True)
    second = jnp.mean(scaled * xhat, axis=-1, keepdims=True)
    return (scaled - first - xhat * second) * inverse


def slot_softmax(patch_ref, columns, mask_ref):
    scores = columns[PIX] + mask_ref[...]
    for k in range(PIX):
        scores = scores + patch_ref[k].astype(jnp.float32) * columns[k]
    top = jnp.max(scores, axis=0, keepdims=True)
    terms = jnp.exp(scores - top)
    return terms / jnp.sum(terms, axis=0, keepdims=True)


def mixed_of(patch_ref, weights, rows):
    parts = [
        (weights * patch_ref[k].astype(jnp.float32)).astype(jnp.bfloat16) for k in range(PIX)
    ]
    parts.append(weights.astype(jnp.bfloat16))
    used = weights.shape[0] * (PIX + 1)
    if rows > used:
        parts.append(jnp.zeros((rows - used, weights.shape[1]), jnp.bfloat16))
    return jnp.concatenate(parts, axis=0)


def head_columns(coeff_ref, head, slots):
    lane = lax.broadcasted_iota(jnp.int32, (slots, coeff_ref.shape[1]), 1)
    return [
        jnp.sum(
            jnp.where(lane == head, coeff_ref[k * slots : (k + 1) * slots, :], 0.0),
            axis=1,
            keepdims=True,
        )
        for k in range(PIX + 1)
    ]


def prepare_kernel(group_size, head_dim, *refs):
    (
        count_ref, own_query, query_w, key_w, own_table, select_ref, own_value, own_agg,
        own_qkv, own_proj, own_grad, patch_ref, mask_ref, bias_ref, gain_ref, shift_ref,
    ) = refs[:16]
    (
        count_out, tables, query_out, keys_out, full_value, full_agg, full_qkv, full_proj,
        near_grad, far_grads, table_out, coeff_out, heads_out, embed_out, norm_out,
    ) = refs[16:31]
    query_part, query_got, counts = refs[31:34]
    whole_value, whole_agg, whole_qkv, whole_proj, grads = refs[34:39]
    send_sem, recv_sem, small_send, small_recv, local_sem = refs[39:]
    wide = jnp.float32
    low = jnp.bfloat16
    me = lax.axis_index("fsdp")
    group = lax.axis_index("grp")
    near_index = flip(me, 1)[0]
    far_index = flip(me, 2)[0]
    near = {"fsdp": near_index}
    far = {"fsdp": far_index}
    block = own_value.shape[0]
    heads = keys_out.shape[0]
    slots = mask_ref.shape[0]
    rows = own_grad.shape[0]
    bits = []
    bit = 1
    while bit < group_size:
        bits.append(bit)
        bit *= 2
    meet(
        [near, far, {"fsdp": flip(far_index, 1)[0]}]
        + [{"grp": flip(group, bit)[0]} for bit in bits]
    )

    def remote(src, dst, sends, recvs, at, device):
        return pltpu.make_async_remote_copy(
            src_ref=src,
            dst_ref=dst,
            send_sem=sends.at[at],
            recv_sem=recvs.at[at],
            device_id=device,
            device_id_type=pl.DeviceIdType.MESH,
        )

    def span(start, size):
        return pl.ds(pl.multiple_of(start, 16), size)

    width = own_value.shape[1]
    items = [(own_value, whole_value, 0, width, False), (own_agg, whole_agg, 0, width, False)]
    for n in range(full_qkv.shape[1] // width):
        items.append((own_qkv, whole_qkv, n * width, width, True))
    items.append((own_proj, whole_proj, 0, width, True))
    x_bit = flip(group, 1)[1]
    piece = flip(group, 2)[1] + 2 * flip(group, 4)[1] + 4 * x_bit
    eighth = block // 8

    def weight_copy(n, stage):
        own, whole, start, size, eighths = items[n]
        cols = pl.ds(start, size)

        def region(base, offset, count):
            return whole.at[span(base * block + offset, count), cols]

        if stage == 0:
            return remote(
                own.at[:, cols], region(me, 0, block), send_sem, recv_sem, (n, 0), near
            )
        if stage == 1:
            offset, count = (piece * eighth, eighth) if eighths else (x_bit * (block // 2), block // 2)
            return remote(
                own.at[span(offset, count), cols],
                region(me, offset, count),
                send_sem,
                recv_sem,
                (n, 1),
                far,
            )
        if stage == 2:
            at = region(far_index, piece * eighth, eighth)
            return remote(at, at, send_sem, recv_sem, (n, 2), {"grp": flip(group, 2)[0]})
        if stage == 3:
            at = region(far_index, (piece // 2) * 2 * eighth, 2 * eighth)
            return remote(at, at, send_sem, recv_sem, (n, 3), {"grp": flip(group, 4)[0]})
        if stage == 4:
            at = region(far_index, x_bit * (block // 2), block // 2)
            return remote(at, at, send_sem, recv_sem, (n, 4), {"grp": flip(group, 1)[0]})
        at = region(far_index, 0, block)
        return remote(at, at, send_sem, recv_sem, (n, 5), near)

    def out_copy(n):
        own, whole, start, size, eighths = items[n]
        target = [full_value, full_agg, full_qkv, full_proj][min(n, 2) if n + 1 < len(items) else 3]
        cols = pl.ds(start, size)
        return pltpu.make_async_copy(whole.at[:, cols], target.at[:, cols], local_sem.at[2 + n])

    grad_parts = 4
    part_rows = rows // grad_parts

    def grad_near():
        return remote(own_grad, grads.at[0], small_send, small_recv, 0, near)

    def grad_far(p):
        at = pl.ds(p * part_rows, part_rows)
        return remote(
            own_grad.at[at, :], grads.at[1, at, :], small_send, small_recv, 1 + p, far
        )

    def grad_last(p):
        at = pl.ds(p * part_rows, part_rows)
        return remote(
            grads.at[1, at, :],
            grads.at[2, at, :],
            small_send,
            small_recv,
            1 + grad_parts + p,
            near,
        )

    def grad_out(n):
        if n == 0:
            return pltpu.make_async_copy(grads.at[0], near_grad, local_sem.at[0])
        return pltpu.make_async_copy(grads.at[pl.ds(1, 2)], far_grads, local_sem.at[1])

    base = 1 + 2 * grad_parts

    def table_copy(kind):
        if kind == 0:
            return remote(own_table, tables.at[me], small_send, small_recv, base, near)
        if kind == 1:
            return remote(own_table, tables.at[me], small_send, small_recv, base + 1, far)
        at = tables.at[far_index]
        return remote(at, at, small_send, small_recv, base + 2, near)

    others = [near, far, {"fsdp": flip(far_index, 1)[0]}]

    def query_copy(kind):
        return remote(
            query_part, query_got.at[kind], small_send, small_recv, base + 3 + kind, others[kind]
        )

    def key_copy(kind):
        at = keys_out.at[:, pl.ds(pl.multiple_of(me * block, 128), block)]
        return remote(at, at, small_send, small_recv, base + 6 + kind, others[kind])

    def count_copy(n):
        partner = {"grp": flip(group, bits[n])[0]}
        return remote(
            counts.at[2 * n], counts.at[2 * n + 1], small_send, small_recv, base + 9 + n, partner
        )

    def count_step(n):
        count_copy(n).wait()
        value = counts[2 * n] + counts[2 * n + 1]
        if n + 1 < len(bits):
            counts[2 * n + 2] = value
            count_copy(n + 1).start()
        else:
            count_out[...] = value

    def forward(n, stage):
        weight_copy(n, stage).wait()
        weight_copy(n, 4 if (stage == 1 and not items[n][4]) else stage + 1).start()

    def keep(n):
        weight_copy(n, 0).wait()
        weight_copy(n, 5).wait()
        out_copy(n).start()

    late = list(range(2, len(items)))

    query_part[...] = jnp.dot(own_query[...], query_w[...], preferred_element_type=wide)[:8]
    for kind in range(3):
        query_copy(kind).start()
    weight_copy(0, 1).start()
    for n in late:
        weight_copy(n, 1).start()
    table_copy(1).start()
    table_copy(0).start()
    weight_copy(0, 0).start()
    counts[0] = count_ref[...]
    count_copy(0).start()
    tables[me] = own_table[...]
    whole_value[span(me * block, block), :] = own_value[...]
    for kind in range(3):
        query_copy(kind).wait()
    query = query_part[...] + query_got[0] + query_got[1] + query_got[2]
    query_out[...] = query
    lane = lax.broadcasted_iota(jnp.int32, (heads, width), 1)
    head = lax.broadcasted_iota(jnp.int32, (heads, width), 0)
    spread = jnp.where(lane // head_dim == head, jnp.broadcast_to(query[:1], (heads, width)), 0.0)
    own_keys = lax.dot_general(
        spread.astype(low), key_w[...], (((1,), (1,)), ((), ())), preferred_element_type=wide
    ) * (head_dim ** (-0.5))
    keys_out[:, pl.ds(pl.multiple_of(me * block, 128), block)] = own_keys.astype(low)
    for kind in range(3):
        key_copy(kind).start()
    weight_copy(1, 1).start()
    whole_agg[span(me * block, block), :] = own_agg[...]
    whole_qkv[span(me * block, block), :] = own_qkv[...]
    whole_proj[span(me * block, block), :] = own_proj[...]
    forward(0, 1)
    for n in late:
        forward(n, 1)
    forward(0, 4)
    forward(2, 2)
    forward(3, 2)
    table_copy(0).wait()
    table_copy(1).wait()
    table_copy(2).start()
    for p in range(grad_parts):
        grad_far(p).start()
    forward(1, 1)
    weight_copy(1, 0).start()
    table_copy(2).wait()
    stacked = tables[...].reshape(select_ref.shape[1], width)
    table = jnp.dot(select_ref[...], stacked, preferred_element_type=wide).astype(low)
    for kind in range(3):
        key_copy(kind).wait()
    coeff_out[...] = lax.dot_general(
        table, keys_out[...], (((1,), (1,)), ((), ())), preferred_element_type=wide
    )
    weight_copy(0, 0).wait()
    weight_copy(0, 5).wait()
    out_copy(0).start()
    values = jnp.dot(table, whole_value[...], preferred_element_type=wide)
    table_out[...] = jnp.transpose(values).astype(low)

    def one_head(h, carry):
        weights = slot_softmax(patch_ref, head_columns(coeff_out, h, slots), mask_ref)
        mixed = mixed_of(patch_ref, weights, table_out.shape[1])
        at = pl.ds(pl.multiple_of(h * head_dim, 16), head_dim)
        heads_out[at, :] = jnp.dot(
            table_out[at, :], mixed, preferred_element_type=wide
        ).astype(low)
        return carry

    half = heads // 2
    forward(2, 3)
    forward(4, 2)
    for n in late:
        weight_copy(n, 0).start()
    lax.fori_loop(0, half, one_head, 0)
    forward(1, 4)
    forward(3, 3)
    forward(5, 2)
    grad_near().start()
    lax.fori_loop(half, heads, one_head, 0)
    keep(1)
    embedded = (
        lax.dot_general(
            heads_out[...], whole_agg[...], (((0,), (0,)), ((), ())), preferred_element_type=wide
        )
        + bias_ref[...]
    )
    embed_out[...] = embedded
    count_step(0)
    forward(2, 4)
    grad_far(0).wait()
    grad_last(0).start()
    xhat, inverse = normalise(embedded)
    norm_out[...] = (xhat * gain_ref[...] + shift_ref[...]).astype(low)
    forward(4, 3)
    keep(2)
    forward(3, 4)
    count_step(1)
    grad_far(1).wait()
    grad_last(1).start()
    forward(5, 3)
    keep(3)
    forward(4, 4)
    for n in range(2, len(bits)):
        count_step(n)
    grad_far(2).wait()
    grad_last(2).start()
    keep(4)
    forward(5, 4)
    grad_near().wait()
    grad_out(0).start()
    grad_far(3).wait()
    grad_last(3).start()
    keep(5)
    for p in range(grad_parts):
        grad_last(p).wait()
    grad_out(1).start()
    for n in range(len(items)):
        out_copy(n).wait()
    for n in range(2):
        grad_out(n).wait()


def prepare(
    group_size, count_rows, own_query, query_w, key_w, own_table, select, own_value, own_agg,
    own_qkv, own_proj, own_grad, patch_rows, slot_mask, bias, gain, shift,
):
    block, width = own_value.shape
    head_dim = width // HEADS
    rows = own_grad.shape[0]
    slots = slot_mask.shape[0]
    size = select.shape[0]
    low = jnp.bfloat16
    wide = jnp.float32
    vmem = pl.BlockSpec(memory_space=pltpu.VMEM)
    hbm = pl.BlockSpec(memory_space=pl.ANY)
    steps = 0
    while 2**steps < group_size:
        steps += 1
    items = 3 + own_qkv.shape[1] // width
    small = 1 + 2 * 4 + 9 + steps

    def shape(dims, kind):
        return jax.ShapeDtypeStruct(dims, kind)

    return pl.pallas_call(
        functools.partial(prepare_kernel, group_size, head_dim),
        in_specs=[vmem] * 16,
        out_specs=[vmem] * 4 + [hbm] * 6 + [vmem] * 5,
        out_shape=[
            shape((8, 128), wide),
            shape((4,) + own_table.shape, low),
            shape((8, width), wide),
            shape((HEADS, width), low),
            shape((4 * block, width), low),
            shape((4 * block, width), low),
            shape((4 * block, own_qkv.shape[1]), low),
            shape((4 * block, width), low),
            shape((rows, width), low),
            shape((2, rows, width), low),
            shape((width, size), low),
            shape((size, HEADS), wide),
            shape((width, rows), low),
            shape((rows, width), wide),
            shape((rows, width), low),
        ],
        scratch_shapes=[
            pltpu.VMEM((8, width), wide),
            pltpu.VMEM((3, 8, width), wide),
            pltpu.VMEM((2 * steps, 8, 128), wide),
            pltpu.VMEM((4 * block, width), low),
            pltpu.VMEM((4 * block, width), low),
            pltpu.VMEM((4 * block, own_qkv.shape[1]), low),
            pltpu.VMEM((4 * block, width), low),
            pltpu.VMEM((3, rows, width), low),
            pltpu.SemaphoreType.DMA((items, 6)),
            pltpu.SemaphoreType.DMA((items, 6)),
            pltpu.SemaphoreType.DMA((small,)),
            pltpu.SemaphoreType.DMA((small,)),
            pltpu.SemaphoreType.DMA((2 + items,)),
        ],
        compiler_params=pltpu.CompilerParams(
            collective_id=3, has_side_effects=True, vmem_limit_bytes=VMEM_LIMIT
        ),
        cost_estimate=pl.CostEstimate(
            flops=8 * size * rows * width, bytes_accessed=100_000_000, transcendentals=0
        ),
        name="prepare",
    )(
        count_rows, own_query, query_w, key_w, own_table, select, own_value, own_agg,
        own_qkv, own_proj, own_grad, patch_rows, slot_mask, bias, gain, shift,
    )


def group_steps(group, order, size):
    steps = []
    offset = 0
    for bit in order:
        partner, bit_set = flip(group, bit)
        halving = size >= 32
        steps.append((partner, bit_set, halving, size, offset))
        if halving:
            size = size // 2
            offset = offset + bit_set * size
    return steps


def group_orders(group_size):
    bits = []
    while 2 ** len(bits) < group_size:
        bits.append(2 ** len(bits))
    return bits, bits[1:] + bits[:1]


def group_sum(steps, hold, halves, done, send_sem, recv_sem):
    count = len(steps)
    halvings = [i for i, step in enumerate(steps) if step[2]]
    wide = jnp.float32

    def span(start, size):
        return pl.ds(pl.multiple_of(start, 16), size)

    def copy(stage, c, src, dst, partner):
        return pltpu.make_async_remote_copy(
            src_ref=src,
            dst_ref=dst,
            send_sem=send_sem.at[stage, c],
            recv_sem=recv_sem.at[stage, c],
            device_id={"grp": partner},
            device_id_type=pl.DeviceIdType.MESH,
        )

    def step_copy(i, c):
        partner, bit_set, halving, size, offset = steps[i]
        if halving:
            size = size // 2
            offset = offset + (1 - bit_set) * size
        return copy(i, c, hold.at[c, span(offset, size), :], halves[i].at[c], partner)

    def back_copy(i, c):
        partner, bit_set, halving, size, offset = steps[i]
        size = size // 2
        at = done.at[c, span(offset + bit_set * size, size), :]
        return copy(count + i, c, at, at, partner)

    def begin(c):
        step_copy(0, c).start()

    def after_step(i, c):
        step_copy(i, c).wait()
        partner, bit_set, halving, size, offset = steps[i]
        if halving:
            size = size // 2
            offset = offset + bit_set * size
        at = span(offset, size)
        value = hold[c, at, :].astype(wide) + halves[i][c].astype(wide)
        if i + 1 < count:
            hold[c, at, :] = value.astype(hold.dtype)
            step_copy(i + 1, c).start()
        else:
            done[c, at, :] = value.astype(done.dtype)
            back_copy(halvings[-1], c).start()

    def after_back(k, c):
        back_copy(halvings[k], c).wait()
        if k > 0:
            back_copy(halvings[k - 1], c).start()

    stages = [begin] + [functools.partial(after_step, i) for i in range(count)]
    return stages + [functools.partial(after_back, k) for k in reversed(range(len(halvings)))]


def group_buffers(group_size, chunks, rows, columns):
    low = jnp.bfloat16
    steps = len(group_orders(group_size)[0])
    halves = []
    size = rows
    for _ in range(steps):
        if size >= 32:
            size //= 2
        halves.append(pltpu.VMEM((chunks, size, columns), low))
    one = pltpu.VMEM((chunks, rows, columns), low)
    semaphores = pltpu.SemaphoreType.DMA((2 * steps, chunks))
    return [one, halves, one, semaphores, semaphores]


def sum_beside(group, group_size, first, total_in, total_out, buffers):
    hold, halves, done, send_sem, recv_sem, in_sem, keep_sem = buffers
    chunks, rows, columns = hold.shape
    steps = group_steps(group, group_orders(group_size)[0], rows)
    stages = group_sum(steps, hold, halves, done, send_sem, recv_sem)

    def at(c):
        return pl.ds(pl.multiple_of((first + c) * columns, 128), columns)

    def take(c):
        return pltpu.make_async_copy(total_in.at[:, at(c)], hold.at[c], in_sem.at[c])

    def give(c):
        place = pl.ds(pl.multiple_of(c * columns, 128), columns)
        return pltpu.make_async_copy(done.at[c], total_out.at[:, place], keep_sem.at[c])

    def start():
        for c in range(chunks):
            take(c).wait()
            stages[0](c)

    def end(c):
        stages[-1](c)
        give(c).start()

    return chunks, take, start, stages[1:-1] + [end], give


def beside_buffers(group_size, chunks, rows, columns):
    return group_buffers(group_size, chunks, rows, columns) + [
        pltpu.SemaphoreType.DMA((chunks,)),
        pltpu.SemaphoreType.DMA((chunks,)),
    ]


def lane_half(rows, pair, head_dim):
    lane = lax.broadcasted_iota(jnp.int32, (rows, 2 * head_dim), 1)
    return (lane // head_dim) == pair


def attend_kernel(
    head_dim, valid_ref, rows_ref, weight_ref, q_ref, kv_out, out_ref, flat_ref, log_ref, kv_ref, weight_s, sum_s, top_s, total_s, send_sem, recv_sem, fetch_sem, keep_sem
):
    me = lax.axis_index("fsdp")
    near = {"fsdp": flip(me, 1)[0]}
    far = {"fsdp": flip(me, 2)[0]}
    wide = jnp.float32
    low = jnp.bfloat16
    rows, width = rows_ref.shape
    lanes = 2 * head_dim
    pairs = width // lanes
    scale = head_dim ** (-0.5)
    groups = pairs // 2

    def fetch(part, g):
        at = pl.ds(part * width + g * 2 * lanes, 2 * lanes)
        return pltpu.make_async_copy(
            weight_ref.at[:, at], weight_s.at[:, at], fetch_sem.at[part, g]
        )

    def keep(i):
        return pltpu.make_async_copy(kv_ref.at[:, i], kv_out.at[:, i], keep_sem.at[i])

    for g in range(groups):
        fetch(1, g).start()
        fetch(2, g).start()
    for g in range(groups):
        fetch(0, g).start()
    meet([near, far])

    def copy(kind, i, source, target, device):
        return pltpu.make_async_remote_copy(
            src_ref=kv_ref.at[source, i],
            dst_ref=kv_ref.at[target, i],
            send_sem=send_sem.at[kind, i],
            recv_sem=recv_sem.at[kind, i],
            device_id=device,
            device_id_type=pl.DeviceIdType.MESH,
        )

    def near_copy(i):
        return copy(0, i, 0, 1, near)

    def far_copy(i):
        return copy(1, i, 0, 2, far)

    def last_copy(i):
        return copy(2, i, 2, 3, near)

    entry = rows_ref[...]
    for g in range(groups):
        for part in range(2):
            start = (part + 1) * width + g * 2 * lanes
            fetch(part + 1, g).wait()
            value = jnp.dot(
                entry, weight_s[:, start : start + 2 * lanes], preferred_element_type=wide
            ).astype(low)
            kv_ref[0, 2 * g, part] = value[:, :lanes]
            kv_ref[0, 2 * g + 1, part] = value[:, lanes:]
        for i in (2 * g, 2 * g + 1):
            far_copy(i).start()
            near_copy(i).start()
    for g in range(groups):
        start = g * 2 * lanes
        fetch(0, g).wait()
        value = jnp.dot(
            entry, weight_s[:, start : start + 2 * lanes], preferred_element_type=wide
        ).astype(low)
        value = value * jnp.asarray(scale, low)
        q_ref[2 * g] = value[:, :lanes]
        q_ref[2 * g + 1] = value[:, lanes:]

    tile = min(rows, 256)

    def attend(i, shards, first):
        for start in range(0, rows, tile):
            at = slice(start, start + tile)
            block = q_ref[i, at, :]
            sums, tops, totals = [], [], []
            for pair in range(2):
                query = jnp.where(lane_half(tile, pair, head_dim), block, jnp.zeros_like(block))
                logits = []
                for j in shards:
                    raw = lax.dot_general(
                        query, kv_ref[j, i, 0], (((1,), (1,)), ((), ())), preferred_element_type=wide
                    )
                    place = lax.broadcasted_iota(jnp.int32, (1, rows), 1)
                    logits.append(jnp.where(place < valid_ref[j], raw, masked_out))
                top = functools.reduce(
                    jnp.maximum, [jnp.max(part, axis=1, keepdims=True) for part in logits]
                )
                sum_now, total_now = 0.0, 0.0
                for j, part in zip(shards, logits):
                    terms = jnp.exp(part - top)
                    total_now = total_now + jnp.sum(terms, axis=1, keepdims=True)
                    sum_now = sum_now + jnp.dot(
                        terms.astype(low), kv_ref[j, i, 1], preferred_element_type=wide
                    )
                sums.append(sum_now)
                tops.append(top)
                totals.append(total_now)
            side = lane_half(tile, 0, head_dim)
            sum_now = jnp.where(side, sums[0], sums[1])
            top = jnp.where(side, tops[0], tops[1])
            total_now = jnp.where(side, totals[0], totals[1])
            if not first:
                old_top = top_s[at, :]
                new_top = jnp.maximum(top, old_top)
                mine = jnp.exp(top - new_top)
                others = jnp.exp(old_top - new_top)
                sum_now = sum_now * mine + sum_s[at, :] * others
                total_now = total_now * mine + total_s[at, :] * others
                top = new_top
            sum_s[at, :] = sum_now
            top_s[at, :] = top
            total_s[at, :] = total_now

    def one_pair(i, carry):
        near_copy(i).wait_recv()
        attend(i, (0, 1), True)
        far_copy(i).wait_recv()
        last_copy(i).start()
        attend(i, (2,), False)
        last_copy(i).wait_recv()
        attend(i, (3,), False)
        keep(i).start()
        context = (sum_s[...] / total_s[...]).astype(low)
        out_ref[i] = context
        flat_ref[:, pl.ds(pl.multiple_of(i * lanes, lanes), lanes)] = context
        logs = jnp.transpose(top_s[...] + jnp.log(total_s[...]))
        for pair in range(2):
            log_ref[i, pair : pair + 1, :] = logs[pair * head_dim : pair * head_dim + 1, :]
        return carry

    lax.fori_loop(0, pairs, one_pair, 0)

    def end(i, carry):
        near_copy(i).wait_send()
        far_copy(i).wait_send()
        last_copy(i).wait_send()
        keep(i).wait()
        return carry

    lax.fori_loop(0, pairs, end, 0)


def attend(rows_in, weight, valid):
    rows, width = rows_in.shape
    head_dim = width // HEADS
    lanes = 2 * head_dim
    pairs = HEADS // 2
    whole = pl.BlockSpec(memory_space=pltpu.VMEM)
    hbm = pl.BlockSpec(memory_space=pl.ANY)
    low = jnp.bfloat16
    wide = jnp.float32
    return pl.pallas_call(
        functools.partial(attend_kernel, head_dim),
        in_specs=[pl.BlockSpec(memory_space=pltpu.SMEM), whole, hbm],
        out_specs=[whole, hbm, whole, whole, whole],
        out_shape=[
            jax.ShapeDtypeStruct((pairs, rows, lanes), low),
            jax.ShapeDtypeStruct((4, pairs, 2, rows, lanes), low),
            jax.ShapeDtypeStruct((pairs, rows, lanes), low),
            jax.ShapeDtypeStruct((rows, width), low),
            jax.ShapeDtypeStruct((pairs, 8, rows), wide),
        ],
        scratch_shapes=[
            pltpu.VMEM((4, pairs, 2, rows, lanes), low),
            pltpu.VMEM(weight.shape, low),
            pltpu.VMEM((rows, lanes), wide),
            pltpu.VMEM((rows, lanes), wide),
            pltpu.VMEM((rows, lanes), wide),
            pltpu.SemaphoreType.DMA((3, pairs)),
            pltpu.SemaphoreType.DMA((3, pairs)),
            pltpu.SemaphoreType.DMA((3, pairs // 2)),
            pltpu.SemaphoreType.DMA((pairs,)),
        ],
        compiler_params=pltpu.CompilerParams(
            collective_id=1, has_side_effects=True, vmem_limit_bytes=VMEM_LIMIT
        ),
        cost_estimate=pl.CostEstimate(
            flops=64 * rows * rows * width, bytes_accessed=100_000_000, transcendentals=0
        ),
        name="attend",
    )(valid, rows_in, weight)


def attend_back_kernel(
    head_dim, group_size, valid_ref, q_ref, kv_in, grad_ref, out_ref, log_ref, *refs
):
    total_in, result_ref, total_out = refs[:3]
    q_sum, own_s, far_s, last_s, near_s, got_far, got_last, got_near, dot_rows = refs[3:12]
    send_sem, recv_sem, kv_ref, fetch_sem = refs[12:16]
    group = lax.axis_index("grp")
    me = lax.axis_index("fsdp")
    near = {"fsdp": flip(me, 1)[0]}
    far = {"fsdp": flip(me, 2)[0]}
    wide = jnp.float32
    low = jnp.bfloat16
    pairs, rows, lanes = q_ref.shape

    def fetch(half, i):
        at = pl.ds(2 * half, 2)
        return pltpu.make_async_copy(kv_in.at[at, i], kv_ref.at[at, i], fetch_sem.at[half, i])

    chunks, take, sum_start, sum_stages, give = sum_beside(
        group, group_size, 0, total_in, total_out, refs[16:]
    )

    waits = [s + 1 + max(0, s - len(sum_stages) + 3) for s in range(len(sum_stages))]

    def sum_step(t):
        for wait, stage in zip(waits, sum_stages):
            c = t - wait

            @pl.when((c >= 0) & (c < chunks))
            def _(stage=stage, c=c):
                stage(c)

    for i in range(pairs):
        fetch(1, i).start()
    for c in range(chunks):
        take(c).start()
    for i in range(pairs):
        fetch(0, i).start()
    width = pairs * lanes
    scale = head_dim ** (-0.5)
    meet([near, far] + [{"grp": flip(group, bit)[0]} for bit in group_orders(group_size)[0]])

    def copy(kind, i, source, target, device):
        return pltpu.make_async_remote_copy(
            src_ref=source.at[i],
            dst_ref=target.at[i],
            send_sem=send_sem.at[kind, i],
            recv_sem=recv_sem.at[kind, i],
            device_id=device,
            device_id_type=pl.DeviceIdType.MESH,
        )

    def last_copy(i):
        return copy(0, i, last_s, got_last, near)

    def near_copy(i):
        return copy(1, i, near_s, got_near, near)

    def far_copy(i):
        return copy(2, i, far_s, got_far, far)

    def back(i, shards, targets):
        query = q_ref[i]
        grad = grad_ref[i]
        q_grad = None
        k_sums = [None, None]
        v_sums = [None, None]

        def plus(old, new):
            return new if old is None else old + new

        for pair in range(2):
            side = lane_half(rows, pair, head_dim)
            log_row = log_ref[i, pair : pair + 1, :]
            dot_row = dot_rows[i, pair : pair + 1, :]
            one_query = jnp.where(side, query, jnp.zeros_like(query))
            one_grad = jnp.where(side, grad, jnp.zeros_like(grad))
            for n, j in enumerate(shards):
                key = kv_ref[j, i, 0]
                one_key = jnp.where(side, key, jnp.zeros_like(key))
                raw = lax.dot_general(
                    key, one_query, (((1,), (1,)), ((), ())), preferred_element_type=wide
                )
                place = lax.broadcasted_iota(jnp.int32, raw.shape, 0)
                probs = jnp.exp(jnp.where(place < valid_ref[j], raw - log_row, masked_out))
                probs_grad = lax.dot_general(
                    kv_ref[j, i, 1], one_grad, (((1,), (1,)), ((), ())), preferred_element_type=wide
                )
                raw_grad = (probs * (probs_grad - dot_row)).astype(low)
                v_sums[n] = plus(
                    v_sums[n], jnp.dot(probs.astype(low), one_grad, preferred_element_type=wide)
                )
                k_sums[n] = plus(
                    k_sums[n], jnp.dot(raw_grad, one_query, preferred_element_type=wide)
                )
                q_grad = plus(
                    q_grad,
                    lax.dot_general(
                        raw_grad, one_key, (((0,), (0,)), ((), ())), preferred_element_type=wide
                    ),
                )
        for n, target in enumerate(targets):
            target[i, 0] = k_sums[n].astype(target.dtype)
            target[i, 1] = v_sums[n].astype(target.dtype)
        return q_grad

    def send_far(i):
        last_copy(i).wait()
        far_s[i] = (far_s[i].astype(wide) + got_last[i].astype(wide)).astype(low)
        far_copy(i).start()

    def first_loop(i, carry):
        dots = jnp.transpose(grad_ref[i].astype(wide) * out_ref[i].astype(wide))
        for pair in range(2):
            here = slice(pair * head_dim, (pair + 1) * head_dim)
            dot_rows[i, pair : pair + 1, :] = jnp.sum(dots[here, :], axis=0, keepdims=True)
        fetch(1, i).wait()
        q_sum[i] = back(i, (3, 2), (last_s, far_s))
        last_copy(i).start()

        @pl.when(i > 0)
        def _():
            send_far(i - 1)

        @pl.when(i == 0)
        def _():
            sum_start()

        sum_step(i)
        return carry

    lax.fori_loop(0, pairs, first_loop, 0)
    send_far(pairs - 1)

    def second_loop(i, carry):
        fetch(0, i).wait()
        q_sum[i] = (q_sum[i] + back(i, (1, 0), (near_s, own_s))) * scale
        near_copy(i).start()
        sum_step(pairs + i)
        return carry

    lax.fori_loop(0, pairs, second_loop, 0)
    for i in range(pairs):
        near_copy(i).wait()
        far_copy(i).wait()
        at = slice(i * lanes, (i + 1) * lanes)
        result_ref[:, at] = q_sum[i].astype(low)
        for part in range(2):
            value = own_s[i, part] + got_near[i, part].astype(wide) + got_far[i, part].astype(wide)
            start = (part + 1) * width + i * lanes
            result_ref[:, start : start + lanes] = value.astype(low)
    for t in range(2 * pairs, chunks + waits[-1]):
        for wait, stage in zip(waits, sum_stages):
            if 0 <= t - wait < chunks:
                stage(t - wait)
    for c in range(chunks):
        give(c).wait()


def attend_back(group_size, queries, key_values, grad, out, logs, valid, totals, columns, chunks):
    pairs, rows, lanes = queries.shape
    head_dim = lanes // 2
    whole = pl.BlockSpec(memory_space=pltpu.VMEM)
    low = jnp.bfloat16
    wide = jnp.float32
    slab = (pairs, 2, rows, lanes)
    return pl.pallas_call(
        functools.partial(attend_back_kernel, head_dim, group_size),
        in_specs=[
            pl.BlockSpec(memory_space=pltpu.SMEM),
            whole,
            pl.BlockSpec(memory_space=pl.ANY),
            whole,
            whole,
            whole,
            pl.BlockSpec(memory_space=pl.ANY),
        ],
        out_specs=[whole, pl.BlockSpec(memory_space=pl.ANY)],
        out_shape=[
            jax.ShapeDtypeStruct((rows, 3 * pairs * lanes), low),
            jax.ShapeDtypeStruct((totals.shape[0], chunks * columns), low),
        ],
        scratch_shapes=[
            pltpu.VMEM((pairs, rows, lanes), wide),
            pltpu.VMEM(slab, wide),
            pltpu.VMEM(slab, low),
            pltpu.VMEM(slab, low),
            pltpu.VMEM(slab, low),
            pltpu.VMEM(slab, low),
            pltpu.VMEM(slab, low),
            pltpu.VMEM(slab, low),
            pltpu.VMEM((pairs, 8, rows), wide),
            pltpu.SemaphoreType.DMA((3, pairs)),
            pltpu.SemaphoreType.DMA((3, pairs)),
            pltpu.VMEM(key_values.shape, low),
            pltpu.SemaphoreType.DMA((2, pairs)),
        ]
        + beside_buffers(group_size, chunks, totals.shape[0], columns),
        compiler_params=pltpu.CompilerParams(
            collective_id=2, has_side_effects=True, vmem_limit_bytes=VMEM_LIMIT
        ),
        cost_estimate=pl.CostEstimate(
            flops=160 * rows * rows * pairs * lanes, bytes_accessed=100_000_000, transcendentals=0
        ),
        name="attend_back",
    )(valid, queries, key_values, grad, out, logs, totals)


def feed_kernel(*refs):
    (
        share_ref, context_ref, proj_ref, embed_ref, own_in, near_in, far_in, up_in,
        down_in, bias_ref, proj_bias, gain_ref, shift_ref,
    ) = refs[:13]
    (
        middle_out, out_out, total_out, middle_grad, attended, context_grad, vectors,
    ) = refs[13:20]
    entry, gelu_s, pre_s, own_back, near_s, last_s, far_s, got_near, got_last, got_far = refs[20:30]
    grad_s, up_ref, down_ref, middle_ref, out_ref, down_total, up_total = refs[30:37]
    send_sem, recv_sem, fetch_sem, keep_sem = refs[37:]
    wide = jnp.float32
    low = jnp.bfloat16
    me = lax.axis_index("fsdp")
    near = {"fsdp": flip(me, 1)[0]}
    far = {"fsdp": flip(me, 2)[0]}
    rows, width = embed_ref.shape
    hidden = up_ref.shape[1]
    tile = rows // 2
    pairs, _, lanes = context_grad.shape
    fetches = [
        pltpu.make_async_copy(up_in, up_ref, fetch_sem.at[0]),
        pltpu.make_async_copy(own_in, grad_s.at[0], fetch_sem.at[1]),
        pltpu.make_async_copy(down_in, down_ref, fetch_sem.at[2]),
        pltpu.make_async_copy(near_in, grad_s.at[1], fetch_sem.at[3]),
        pltpu.make_async_copy(far_in, grad_s.at[pl.ds(2, 2)], fetch_sem.at[4]),
    ]
    for fetch in fetches:
        fetch.start()
    meet([near, far])

    def span(t):
        return pl.ds(t * tile, tile)

    def keep_middle(t):
        return pltpu.make_async_copy(
            middle_ref.at[span(t), :], middle_out.at[span(t), :], keep_sem.at[0, t]
        )

    def keep_out(s, t):
        return pltpu.make_async_copy(
            out_ref.at[s, span(t), :], out_out.at[s, span(t), :], keep_sem.at[1 + s, t]
        )

    def keep_total(n):
        source = (down_total, up_total)[n]
        target = total_out.at[:, pl.ds(n * width, width)]
        return pltpu.make_async_copy(source, target, keep_sem.at[5, n])

    def copy(kind, t, src, dst, device):
        return pltpu.make_async_remote_copy(
            src_ref=src.at[span(t), :],
            dst_ref=dst.at[span(t), :],
            send_sem=send_sem.at[kind, t],
            recv_sem=recv_sem.at[kind, t],
            device_id=device,
            device_id_type=pl.DeviceIdType.MESH,
        )

    def rows_near(t):
        return copy(0, t, entry.at[0], entry.at[1], near)

    def rows_far(t):
        return copy(1, t, entry.at[0], entry.at[2], far)

    def rows_last(t):
        return copy(2, t, entry.at[2], entry.at[3], near)

    def back_near(t):
        return copy(3, t, near_s, got_near, near)

    def back_last(t):
        return copy(4, t, last_s, got_last, near)

    def back_far(t):
        return copy(5, t, far_s, got_far, far)

    def feed(s, t, target):
        rows_in = entry[s, span(t), :]
        pre_act = jnp.dot(rows_in, up_ref[...], preferred_element_type=wide) + bias_ref[...]
        cdf = 0.5 * (1.0 + lax.erf(pre_act * 0.7071067811865476))
        density = jnp.exp(-0.5 * pre_act * pre_act) * 0.3989422804014327
        gelu = (pre_act * cdf).astype(low)
        gelu_s[s, span(t), :] = gelu
        act_grad = lax.dot_general(
            grad_s[s, span(t), :],
            down_ref[...],
            (((1,), (1,)), ((), ())),
            preferred_element_type=wide,
        )
        pre_grad = act_grad * (cdf + pre_act * density)
        pre_low = pre_grad.astype(low)
        pre_s[s, span(t), :] = pre_low
        vectors[4:5, :] += jnp.sum(pre_low.astype(wide), axis=0, keepdims=True)
        out_ref[s, span(t), :] = jnp.dot(
            gelu, down_ref[...], preferred_element_type=wide
        ).astype(low)
        keep_out(s, t).start()
        target[span(t), :] = lax.dot_general(
            pre_low, up_ref[...], (((1,), (1,)), ((), ())), preferred_element_type=wide
        ).astype(target.dtype)

    vectors[...] = jnp.zeros_like(vectors)
    for t in range(2):
        middle = (
            embed_ref[span(t), :]
            + jnp.dot(context_ref[span(t), :], proj_ref[...], preferred_element_type=wide)
            + proj_bias[...]
        )
        middle_ref[span(t), :] = middle
        xhat, inverse = normalise(middle)
        entry[0, span(t), :] = (xhat * gain_ref[...] + shift_ref[...]).astype(low)
        rows_far(t).start()
        rows_near(t).start()
        keep_middle(t).start()
    for fetch in fetches[:3]:
        fetch.wait()
    for t in range(2):
        feed(0, t, own_back)
    for fetch in fetches[3:]:
        fetch.wait()
    for t in range(2):
        rows_near(t).wait()
        feed(1, t, near_s)
        back_near(t).start()

    for t in range(2):
        if t > 0:
            add_last(t - 1, back_last, back_far, far_s, got_last, span)
        rows_far(t).wait()
        rows_last(t).start()
        feed(2, t, far_s)
        rows_last(t).wait()
        feed(3, t, last_s)
        back_last(t).start()
    add_last(1, back_last, back_far, far_s, got_last, span)

    block = min(hidden, 256)
    for start in range(0, hidden, block):
        value = 0.0
        for s in range(4):
            value = value + lax.dot_general(
                gelu_s[s, :, start : start + block],
                grad_s[s],
                (((0,), (0,)), ((), ())),
                preferred_element_type=wide,
            )
        down_total[start : start + block, :] = (value * share_ref[0]).astype(low)
    keep_total(0).start()
    for start in range(0, width, block):
        value = 0.0
        for s in range(4):
            value = value + lax.dot_general(
                entry[s, :, start : start + block],
                pre_s[s],
                (((0,), (0,)), ((), ())),
                preferred_element_type=wide,
            )
        up_total[start : start + block, :] = (value * share_ref[0]).astype(low)
    keep_total(1).start()

    for t in range(2):
        back_near(t).wait()
        back_far(t).wait()
        at = span(t)
        grad = own_back[at, :] + got_near[at, :].astype(wide) + got_far[at, :].astype(wide)
        xhat, inverse = normalise(middle_ref[at, :])
        vectors[0:1, :] += jnp.sum(grad * xhat, axis=0, keepdims=True)
        vectors[1:2, :] += jnp.sum(grad, axis=0, keepdims=True)
        upstream = grad_s[0, at, :].astype(wide)
        vectors[3:4, :] += jnp.sum(upstream, axis=0, keepdims=True)
        value = upstream + norm_back(grad, xhat, inverse, gain_ref[...])
        middle_grad[at, :] = value
        value_low = value.astype(low)
        attended[at, :] = value_low
        vectors[2:3, :] += jnp.sum(value_low.astype(wide), axis=0, keepdims=True)
        back = lax.dot_general(
            value_low, proj_ref[...], (((1,), (1,)), ((), ())), preferred_element_type=wide
        ).astype(low)
        for i in range(pairs):
            context_grad[i, at, :] = back[:, i * lanes : (i + 1) * lanes]
    for t in range(2):
        keep_middle(t).wait()
        keep_total(t).wait()
        for s in range(4):
            keep_out(s, t).wait()


def add_last(t, back_last, back_far, far_s, got_last, span):
    back_last(t).wait()
    at = span(t)
    value = far_s[at, :].astype(jnp.float32) + got_last[at, :].astype(jnp.float32)
    far_s[at, :] = value.astype(jnp.bfloat16)
    back_far(t).start()


def feed(
    share, context, proj, embedded, own_grad, near_grad, far_grads, up, down, bias, proj_bias, gain, shift
):
    rows, width = embedded.shape
    hidden = up.shape[1]
    pairs = HEADS // 2
    low = jnp.bfloat16
    wide = jnp.float32
    vmem = pl.BlockSpec(memory_space=pltpu.VMEM)
    hbm = pl.BlockSpec(memory_space=pl.ANY)
    flat = (rows, width)

    def shape(dims, kind):
        return jax.ShapeDtypeStruct(dims, kind)

    return pl.pallas_call(
        feed_kernel,
        in_specs=[pl.BlockSpec(memory_space=pltpu.SMEM)] + [vmem] * 3 + [hbm] * 5 + [vmem] * 4,
        out_specs=[hbm] * 3 + [vmem] * 4,
        out_shape=[
            shape(flat, wide),
            shape((4,) + flat, low),
            shape((width, width + hidden), low),
            shape(flat, wide),
            shape(flat, low),
            shape((pairs, rows, width // pairs), low),
            shape((8, width), wide),
        ],
        scratch_shapes=[
            pltpu.VMEM((4,) + flat, low),
            pltpu.VMEM((4, rows, hidden), low),
            pltpu.VMEM((4, rows, hidden), low),
            pltpu.VMEM(flat, wide),
            pltpu.VMEM(flat, low),
            pltpu.VMEM(flat, low),
            pltpu.VMEM(flat, low),
            pltpu.VMEM(flat, low),
            pltpu.VMEM(flat, low),
            pltpu.VMEM(flat, low),
            pltpu.VMEM((4,) + flat, low),
            pltpu.VMEM(up.shape, low),
            pltpu.VMEM(down.shape, low),
            pltpu.VMEM(flat, wide),
            pltpu.VMEM((4,) + flat, low),
            pltpu.VMEM((hidden, width), low),
            pltpu.VMEM((width, hidden), low),
            pltpu.SemaphoreType.DMA((6, 2)),
            pltpu.SemaphoreType.DMA((6, 2)),
            pltpu.SemaphoreType.DMA((5,)),
            pltpu.SemaphoreType.DMA((6, 2)),
        ],
        compiler_params=pltpu.CompilerParams(
            collective_id=4, has_side_effects=True, vmem_limit_bytes=VMEM_LIMIT
        ),
        cost_estimate=pl.CostEstimate(
            flops=48 * rows * width * hidden, bytes_accessed=100_000_000, transcendentals=0
        ),
        name="feed",
    )(
        share, context, proj, embedded, own_grad, near_grad, far_grads, up, down, bias,
        proj_bias, gain, shift,
    )


def finish_kernel(group_size, widths, head_dim, first_chunk, *refs):
    share_ref = refs[0]
    left_qkv, qkv_grad, left_agg_in, left_proj_in, attended_in = refs[1:6]
    (
        full_qkv, full_agg_in, full_value, embed_in, middle_in, gain_ref, vectors_ref, patch_ref,
        coeff_ref, mask_ref, table_ref, select_ref, own_columns, keys_ref, query_ref, key_w,
        query_w, own_query, out_sum, total_in,
    ) = refs[6:26]
    outs = refs[26:29]
    value_out, key_out, query_out, agg_query_out, var_out, extra_out, patch_grad = refs[29:36]
    out_far, total_out = refs[36:38]
    sets = [refs[38:48], refs[48:57]]
    full, query_part, query_got, var_s, last_send, last_recv = refs[57:63]
    entry_grad, embed_grad, heads_grad, table_s, coeff_s, extras, bundle = refs[63:70]
    weight_s, weight_sem, left_agg, left_proj, attended, full_agg, embed_ref, middle_grad = refs[70:78]
    fetch_sem = refs[78]
    sum_chunks, sum_take, sum_start, sum_stages, sum_give = sum_beside(
        lax.axis_index("grp"), group_size, first_chunk, total_in, total_out, refs[79:]
    )
    fetches = [
        pltpu.make_async_copy(source, target, fetch_sem.at[n])
        for n, (source, target) in enumerate(
            [
                (embed_in, embed_ref),
                (middle_in, middle_grad),
                (full_agg_in, full_agg),
                (left_proj_in, left_proj),
                (attended_in, attended),
                (left_agg_in, left_agg),
            ]
        )
    ]
    me = lax.axis_index("fsdp")
    group = lax.axis_index("grp")
    core_partner, core = flip(me, 1)
    far_partner, far = flip(me, 2)
    diagonal = flip(far_partner, 1)[0]
    wide = jnp.float32
    low = jnp.bfloat16
    quarters = [buffers[2].shape[2] for buffers in sets]
    all_steps = [
        group_steps(group, group_orders(group_size)[0], quarter) for quarter in quarters
    ]
    all_halvings = [[i for i, step in enumerate(steps) if step[2]] for steps in all_steps]
    count = len(all_steps[0])
    slots = sets[1][0].shape[0]
    others = [{"fsdp": core_partner}, {"fsdp": far_partner}, {"fsdp": diagonal}]
    pltpu.make_async_copy(full_qkv.at[:, pl.ds(0, key_w.shape[1])], weight_s, weight_sem.at[0]).start()
    for c in range(sum_chunks):
        sum_take(c).start()
    for fetch in fetches:
        fetch.start()
    meet(others + [{"grp": step[0]} for step in all_steps[0]])

    def pieces(left, right, out):
        return [(left, right, out, start) for start in range(0, right.shape[1], widths)]

    qkv_pieces = pieces(left_qkv, qkv_grad, outs[0])
    agg_pieces = pieces(left_agg, embed_grad, outs[1])
    proj_pieces = pieces(left_proj, attended, outs[2])
    bulk = qkv_pieces + proj_pieces[:1] + [None] + proj_pieces[1:] + agg_pieces
    chunks = []
    for piece in bulk:
        if piece is None:
            chunks.append((0, 0, None, None, None, 0))
        else:
            chunks.append((1, sum(chunk[0] for chunk in chunks)) + piece)
    small = bulk.index(None)

    def remote(src, dst, send, recv, device):
        return pltpu.make_async_remote_copy(
            src_ref=src,
            dst_ref=dst,
            send_sem=send,
            recv_sem=recv,
            device_id=device,
            device_id_type=pl.DeviceIdType.MESH,
        )

    def copy(stage, c, src, dst, device):
        which, place = chunks[c][:2]
        send_sem, recv_sem = sets[which][-2:]
        return remote(src, dst, send_sem.at[stage, place], recv_sem.at[stage, place], device)

    def span(start, size):
        return pl.ds(pl.multiple_of(start, 16), size)

    def held(c):
        which, place, left, right, out, start = chunks[c]
        buffers = sets[which]
        rest = [
            buffer.at[place % slots if n in (0, 2) else place]
            for n, buffer in enumerate(buffers[:6])
        ]
        rest.append([part.at[place] for part in buffers[6]])
        rest.append(buffers[7].at[place] if out is None else out.at[:, start : start + widths])
        return rest

    def core_copy(c):
        at = held(c)
        return copy(0, c, at[0], at[1], others[0])

    def far_copy(c):
        at = held(c)
        return copy(1, c, at[3], at[4], others[1])

    def step_copy(i, c):
        partner, bit_set, halving, size, offset = all_steps[chunks[c][0]][i]
        if halving:
            size = size // 2
            offset = offset + (1 - bit_set) * size
        at = held(c)
        return copy(2 + i, c, at[5].at[span(offset, size), :], at[6][i], {"grp": partner})

    def back_copy(i, c):
        partner, bit_set, halving, size, offset = all_steps[chunks[c][0]][i]
        size = size // 2
        offset = offset + bit_set * size
        at = held(c)[7].at[span(offset, size), :]
        return copy(2 + count + i, c, at, at, {"grp": partner})

    def begin(c):
        which, place, left, right, out, start = chunks[c]
        quarter = quarters[which]
        send1, recv1, own1 = held(c)[:3]

        def part(q):
            if left is None:
                return bundle[q]
            value = jnp.dot(
                left[span(q * quarter, quarter), :],
                right[:, start : start + widths],
                preferred_element_type=wide,
            )
            return (value * share_ref[0]).astype(low)

        for y in range(2):
            send1[y] = part(2 * y + 1 - core)
        core_copy(c).start()
        for y in range(2):
            own1[y] = part(2 * y + core)

    def after_core(c):
        send1, recv1, own1, send2 = held(c)[:4]
        core_copy(c).wait()
        value = own1[1 - far].astype(wide) + recv1[1 - far].astype(wide)
        send2[...] = value.astype(low)
        far_copy(c).start()

    def after_far(c):
        send1, recv1, own1, send2, recv2, hold = held(c)[:6]
        far_copy(c).wait()
        value = own1[far].astype(wide) + recv1[far].astype(wide) + recv2[...].astype(wide)
        hold[...] = value.astype(low)
        step_copy(0, c).start()

    def after_step(i, c):
        step_copy(i, c).wait()
        hold, halves, done = held(c)[5:]
        steps, halvings = all_steps[chunks[c][0]], all_halvings[chunks[c][0]]
        partner, bit_set, halving, size, offset = steps[i]
        if halving:
            size = size // 2
            offset = offset + bit_set * size
        at = span(offset, size)
        value = hold[at, :].astype(wide) + halves[i][...].astype(wide)
        if i + 1 < count:
            hold[at, :] = value.astype(low)
            step_copy(i + 1, c).start()
        else:
            done[at, :] = value.astype(low)
            back_copy(halvings[-1], c).start()

    def after_back(k, c):
        halvings = all_halvings[chunks[c][0]]
        if k >= len(halvings):
            return
        back_copy(halvings[k], c).wait()
        if k > 0:
            back_copy(halvings[k - 1], c).start()
        elif chunks[c][0] == 0:
            full[me] = held(c)[7][...]
            bundle_core().start()

    def bundle_core():
        at = full.at[me]
        return remote(at, at, last_send.at[0], last_recv.at[0], others[0])

    def bundle_far():
        at = full.at[pl.ds(me - core, 2)]
        return remote(at, at, last_send.at[1], last_recv.at[1], others[1])

    def query_copy(kind):
        return remote(
            query_part,
            query_got.at[kind],
            last_send.at[2 + kind],
            last_recv.at[2 + kind],
            others[kind],
        )

    size = own_columns.shape[0]
    width = key_w.shape[1]
    part_rows = quarters[0]
    spare = extra_out.shape[0] // 4
    per_row = width // size
    scale = head_dim ** (-0.5)

    def coefficients():
        rows = []
        for n in range(HEADS):
            place, column = n // per_row, (n % per_row) * size
            shard, row = place // spare, part_rows - spare + place % spare
            rows.append(full[shard, row : row + 1, column : column + size].astype(wide))
        return jnp.concatenate(rows, axis=0)

    def own_head(value):
        lane = lax.broadcasted_iota(jnp.int32, (HEADS, width), 1)
        head = lax.broadcasted_iota(jnp.int32, (HEADS, width), 0)
        return jnp.where(lane // head_dim == head, value, 0.0)

    def key_grad(coeffs):
        return jnp.dot(coeffs.astype(low), own_columns[...], preferred_element_type=wide)

    def finish_core():
        bundle_core().wait()
        bundle_far().start()

    def finish_far():
        bundle_far().wait()
        spread = jnp.dot(
            key_grad(coefficients()).astype(low), key_w[...], preferred_element_type=wide
        )
        partial = jnp.sum(own_head(spread), axis=0, keepdims=True) * scale
        query_part[...] = jnp.broadcast_to(partial, query_part.shape)
        for kind in range(3):
            query_copy(kind).start()

    def finish_table():
        weights(3).wait()
        table = full[...].reshape(size, width)
        value_out[...] = lax.dot_general(
            own_columns[...], table, (((0,), (0,)), ((), ())), preferred_element_type=wide
        )
        coeffs = coefficients()
        var_s[...] = lax.dot_general(
            coeffs.astype(low), keys_ref[...], (((0,), (0,)), ((), ())), preferred_element_type=wide
        )
        var_out[...] = var_s[span(me * part_rows, part_rows), :] + lax.dot_general(
            full[me], weight_s[...], (((1,), (1,)), ((), ())), preferred_element_type=wide
        )
        for q in range(4):
            extra_out[q * spare : (q + 1) * spare, :] = full[q, part_rows - spare :, :].astype(wide)

    def finish_query():
        for kind in range(3):
            query_copy(kind).wait()
        grad = query_part[...] + query_got[0] + query_got[1] + query_got[2]
        query_out[...] = own_query[...] * grad[:1]
        agg_query_out[...] = lax.dot_general(
            grad,
            query_w[...].astype(wide),
            (((1,), (1,)), ((), ())),
            preferred_element_type=wide,
            precision=exact_mode,
        )
        spread = own_head(jnp.broadcast_to(query_ref[:1].astype(low).astype(wide), (HEADS, width)))
        key_out[...] = scale * lax.dot_general(
            key_grad(coefficients()),
            spread,
            (((0,), (0,)), ((), ())),
            preferred_element_type=wide,
            precision=exact_mode,
        )

    def weights(n):
        source = full_qkv.at[:, pl.ds(n * width, width)] if n < 3 else full_value
        return pltpu.make_async_copy(source, weight_s, weight_sem.at[0])

    def entry_part(n):
        weights(n).wait()
        value = lax.dot_general(
            qkv_grad[:, n * width : (n + 1) * width],
            weight_s[...],
            (((1,), (1,)), ((), ())),
            preferred_element_type=wide,
        )
        entry_grad[...] = value if n == 0 else entry_grad[...] + value
        weights(n + 1).start()

    def norm_part():
        for fetch in fetches:
            fetch.wait()
        grad = entry_grad[...]
        xhat, inverse = normalise(embed_ref[...])
        extras[...] = jnp.zeros_like(extras)
        value = middle_grad[...] + norm_back(grad, xhat, inverse, gain_ref[...])
        value_low = value.astype(low)
        embed_grad[...] = value_low
        first = HEADS // per_row
        extras[first : first + 1, :] = jnp.sum(value_low.astype(wide), axis=0, keepdims=True)
        extras[first + 1 : first + 2, :] = jnp.sum(grad * xhat, axis=0, keepdims=True)
        extras[first + 2 : first + 3, :] = jnp.sum(grad, axis=0, keepdims=True)
        for n in range(4):
            extras[first + 3 + n : first + 4 + n, :] = vectors_ref[n : n + 1, :]
        extras[pl.ds(first + 7 + me, 1), :] = vectors_ref[4:5, :]

    def heads_part():
        heads_grad[...] = lax.dot_general(
            full_agg[...], embed_grad[...], (((1,), (1,)), ((), ())), preferred_element_type=wide
        ).astype(low)
        patch_grad[...] = jnp.zeros_like(patch_grad)
        coeff_s[...] = jnp.zeros_like(coeff_s)

    slot_count = mask_ref.shape[0]

    def one_head(h, carry):
        lane = lax.broadcasted_iota(jnp.int32, (slot_count, HEADS), 1)
        columns = head_columns(coeff_ref, h, slot_count)
        weights = slot_softmax(patch_ref, columns, mask_ref)
        mixed = mixed_of(patch_ref, weights, table_ref.shape[1])
        at = pl.ds(pl.multiple_of(h * head_dim, 16), head_dim)
        grad = heads_grad[at, :]
        table_s[at, :] = (
            lax.dot_general(grad, mixed, (((1,), (1,)), ((), ())), preferred_element_type=wide)
            * share_ref[0]
        ).astype(low)
        mixed_grad = lax.dot_general(
            table_ref[at, :], grad, (((0,), (0,)), ((), ())), preferred_element_type=wide
        )
        parts = [
            mixed_grad[k * slot_count : (k + 1) * slot_count] for k in range(PIX + 1)
        ]
        values = [patch_ref[k].astype(wide) for k in range(PIX)]
        weights_grad = parts[PIX]
        for k in range(PIX):
            weights_grad = weights_grad + parts[k] * values[k]
        mean_grad = jnp.sum(weights * weights_grad, axis=0, keepdims=True)
        scores_grad = weights * (weights_grad - mean_grad)
        for k in range(PIX + 1):
            value = scores_grad * values[k] if k < PIX else scores_grad
            column = jnp.sum(value, axis=1, keepdims=True)
            rows = slice(k * slot_count, (k + 1) * slot_count)
            coeff_s[rows, :] = coeff_s[rows, :] + jnp.where(lane == h, column, 0.0)
        for k in range(PIX):
            patch_grad[k] += share_ref[1] * (parts[k] * weights + scores_grad * columns[k])
        return carry

    def heads_from(first, last):
        lax.fori_loop(first, last, one_head, 0)

    def bundle_part():
        sums = lax.dot_general(
            select_ref[...], table_s[...], (((0,), (1,)), ((), ())), preferred_element_type=wide
        )
        coeff_sum = lax.dot_general(
            coeff_s[...],
            select_ref[...].astype(wide),
            (((0,), (0,)), ((), ())),
            preferred_element_type=wide,
            precision=exact_mode,
        )
        for n in range(HEADS):
            place, column = n // per_row, (n % per_row) * size
            extras[place : place + 1, column : column + size] = coeff_sum[n : n + 1, :]
        row = lax.broadcasted_iota(jnp.int32, (size, extras.shape[0]), 0)
        line = lax.broadcasted_iota(jnp.int32, (size, extras.shape[0]), 1)
        spot = (row // part_rows) * spare + row % part_rows - (part_rows - spare)
        chosen = (spot == line) & (row % part_rows >= part_rows - spare)
        placed = jnp.dot(
            chosen.astype(low),
            (extras[...] * share_ref[0]).astype(low),
            preferred_element_type=wide,
        )
        bundle[...] = (sums + placed).astype(low).reshape(bundle.shape)

    middle_parts = [[functools.partial(entry_part, n)] for n in range(3)]
    middle_parts += [[norm_part, heads_part]]
    some = HEADS // 4
    middle_parts += [
        [functools.partial(heads_from, 0, some)],
        [functools.partial(heads_from, some, 2 * some)],
        [functools.partial(heads_from, 2 * some, HEADS), bundle_part],
    ]

    out_copy = remote(out_sum, out_far, last_send.at[5], last_recv.at[5], others[1])
    stages = [begin, after_core, after_far]
    stages += [functools.partial(after_step, i) for i in range(count)]
    stages += [functools.partial(after_back, k) for k in reversed(range(count))]
    extra = [finish_core, finish_far, finish_table, finish_query]
    steps = max(len(chunks), small + 1 + len(extra)) + len(stages) - 1
    for t in range(steps):
        for s in [1, 0]:
            if 0 <= t - s < len(chunks):
                stages[s](t - s)
        if t == 0:
            sum_start()
        if t < len(middle_parts):
            for part in middle_parts[t]:
                part()
        for s in range(2, len(stages)):
            if 0 <= t - s < len(chunks):
                stages[s](t - s)
        if 0 <= t - small - len(stages) < len(extra):
            extra[t - small - len(stages)]()
        for s, stage in enumerate(sum_stages):
            for c in range(sum_chunks):
                if t == 1 + s + c // 2:
                    stage(c)
        if t == len(chunks):
            out_copy.start()
    out_copy.wait()
    for c in range(sum_chunks):
        sum_give(c).wait()


def finish(group_size, spare, shares, lefts, rights, columns, first_chunk, others):
    left_qkv, left_agg, left_proj = lefts
    qkv_grad, attended = rights
    width, rows = left_qkv.shape
    quarter = width // 4
    widths = 512
    low = jnp.bfloat16
    wide = jnp.float32
    size = others["own_columns"].shape[0]
    part = size // 4
    steps = 0
    while 2**steps < group_size:
        steps += 1

    def buffers(count, slots, rows, columns, last):
        halves = []
        size = rows
        for _ in range(steps):
            if size >= 32:
                size //= 2
            halves.append(pltpu.VMEM((count, size, columns), low))
        few = pltpu.VMEM((slots, 2, rows, columns), low)
        two = pltpu.VMEM((count, 2, rows, columns), low)
        one = pltpu.VMEM((count, rows, columns), low)
        semaphores = pltpu.SemaphoreType.DMA((2 + 2 * steps, count))
        found = [few, two, few, one, one, one, halves]
        return found + ([one] if last else []) + [semaphores, semaphores]

    shapes = [(quarter, qkv_grad.shape[1]), (quarter, width), (quarter, width)]
    count = sum(columns for _, columns in shapes) // widths
    scratch = buffers(1, 1, part, width, True) + buffers(count, 3, quarter, widths, False)
    scratch += [
        pltpu.VMEM((4, part, width), low),
        pltpu.VMEM((8, width), wide),
        pltpu.VMEM((3, 8, width), wide),
        pltpu.VMEM((size, width), wide),
        pltpu.SemaphoreType.DMA((6,)),
        pltpu.SemaphoreType.DMA((6,)),
        pltpu.VMEM((rows, width), wide),
        pltpu.VMEM((rows, width), low),
        pltpu.VMEM((width, rows), low),
        pltpu.VMEM((width, size), low),
        pltpu.VMEM((size, HEADS), wide),
        pltpu.VMEM((4 * spare, width), wide),
        pltpu.VMEM((4, part, width), low),
        pltpu.VMEM((width, width), low),
        pltpu.SemaphoreType.DMA((1,)),
        pltpu.VMEM((width, rows), low),
        pltpu.VMEM((width, rows), low),
        pltpu.VMEM((rows, width), low),
        pltpu.VMEM((width, width), low),
        pltpu.VMEM((rows, width), wide),
        pltpu.VMEM((rows, width), wide),
        pltpu.SemaphoreType.DMA((6,)),
    ]
    totals = others["totals"]
    left_chunks = totals.shape[1] // columns - first_chunk
    scratch += beside_buffers(group_size, left_chunks, totals.shape[0], columns)
    whole = pl.BlockSpec(memory_space=pltpu.VMEM)
    out_shape = [jax.ShapeDtypeStruct(dims, low) for dims in shapes]
    more = [(quarter, width)] * 3 + [(8, quarter), (part, width), (4 * spare, width)]
    more.append(others["patch_rows"].shape)
    out_shape += [jax.ShapeDtypeStruct(dims, wide) for dims in more]
    out_shape.append(jax.ShapeDtypeStruct(others["out_sum"].shape, low))
    out_shape.append(jax.ShapeDtypeStruct((totals.shape[0], left_chunks * columns), low))
    hbm = pl.BlockSpec(memory_space=pl.ANY)
    far_off = ("full_qkv", "full_agg", "full_value", "embedded", "middle_grad", "out_sum", "totals")
    operands = [shares, left_qkv, qkv_grad, left_agg, left_proj, attended, *others.values()]
    return pl.pallas_call(
        functools.partial(finish_kernel, group_size, widths, width // HEADS, first_chunk),
        in_specs=[pl.BlockSpec(memory_space=pltpu.SMEM), whole, whole, hbm, hbm, hbm]
        + [hbm if name in far_off else whole for name in others],
        out_specs=[whole] * (len(out_shape) - 2) + [hbm] * 2,
        out_shape=out_shape,
        scratch_shapes=scratch,
        compiler_params=pltpu.CompilerParams(
            collective_id=0, has_side_effects=True, vmem_limit_bytes=62 * 1024 * 1024
        ),
        cost_estimate=pl.CostEstimate(
            flops=20 * rows * width * width, bytes_accessed=200_000_000, transcendentals=0
        ),
        name="finish",
    )(*operands)


def on_device(
    patches,
    patch_counts,
    var_present,
    item_dataset,
    var_ids,
    patch_weight,
    var_embed,
    agg_query,
    query_weight,
    key_weight,
    value_weight,
    agg_proj,
    agg_bias,
    norm1_gain,
    norm1_shift,
    qkv_weight,
    proj_weight,
    proj_bias,
    norm2_gain,
    norm2_shift,
    up_weight,
    up_bias,
    down_weight,
    down_bias,
    out_grad,
):
    low = jnp.bfloat16
    wide = jnp.float32
    rows = patches.shape[2]
    me = lax.axis_index("fsdp")
    group_count = lax.axis_size("grp")
    width = proj_weight.shape[1]
    head_dim = width // HEADS
    own_width = width // 4
    own_vars = patch_weight.shape[0]

    item_count = patch_counts[0]
    own_valid = me * rows + jnp.arange(rows, dtype=jnp.int32) < item_count
    shard_valid = jnp.clip(
        item_count - (me ^ jnp.arange(4, dtype=jnp.int32)) * rows, 0, rows
    ).astype(jnp.int32)
    down_grad = jnp.where(own_valid[:, None], out_grad, jnp.zeros_like(out_grad))

    slot_vars = lax.dynamic_index_in_dim(var_ids, item_dataset[0], 0, keepdims=False)
    part_size = -(-(PIX + 1) * own_vars // 16) * 16
    size = 4 * part_size
    slot_row = jnp.arange(size, dtype=jnp.int32)
    slot_var = jnp.pad(jnp.tile(slot_vars, PIX + 1), (0, size - (PIX + 1) * VTOT))
    place = (slot_var // own_vars) * part_size + (slot_row // VTOT) * own_vars + slot_var % own_vars
    select = (
        (place[:, None] == jnp.arange(size, dtype=jnp.int32)[None, :])
        & (slot_row < (PIX + 1) * VTOT)[:, None]
    ).astype(low)
    own_table = jnp.concatenate(
        [
            patch_weight.transpose(1, 0, 2).reshape(own_vars * PIX, width),
            var_embed,
            jnp.zeros((part_size - (PIX + 1) * own_vars, width), low),
        ],
        axis=0,
    )
    own_query = lax.dynamic_slice_in_dim(agg_query, me * own_width, own_width, 0)
    patch_rows = patches.transpose(1, 0, 2)
    slot_mask = jnp.where(var_present[0] > 0, 0.0, masked_out).astype(wide)[:, None]
    (
        count_rows,
        tables,
        query_rows,
        key_query,
        full_value,
        full_agg_proj,
        full_qkv,
        full_proj,
        near_down_grad,
        far_grads,
        table_values,
        coeffs,
        heads_t,
        embedded,
        normed1,
    ) = prepare(
        group_count,
        jnp.full((8, 128), item_count.astype(wide)),
        jnp.broadcast_to(own_query[None, :], (16, own_width)),
        query_weight,
        key_weight,
        own_table,
        select,
        value_weight,
        agg_proj,
        qkv_weight,
        proj_weight,
        down_grad,
        patch_rows,
        slot_mask,
        agg_bias[None, :],
        norm1_gain[None, :],
        norm1_shift[None, :],
    )
    count_share = item_count.astype(wide) / count_rows[0, 0]
    own_columns = lax.dynamic_slice_in_dim(
        tables.reshape(size, width), me * own_width, own_width, 1
    )

    queries, key_values, context_pairs, context, logs = attend(normed1, full_qkv, shard_valid)
    (
        middle,
        out_parts,
        totals,
        middle_grad,
        attended_grad,
        context_grad,
        feed_vectors,
    ) = feed(
        count_share[None],
        context,
        full_proj,
        embedded,
        down_grad,
        near_down_grad,
        far_grads,
        up_weight,
        down_weight,
        up_bias.astype(wide)[None, :],
        proj_bias[None, :],
        norm2_gain[None, :],
        norm2_shift[None, :],
    )
    out_got = swap(jnp.stack([out_parts[1], out_parts[3]]), "fsdp", 1)
    out_sum = (out_parts[2].astype(wide) + out_got[1].astype(wide)).astype(low)

    columns = width // 8
    chunks = 12
    qkv_grad, summed = attend_back(
        group_count,
        queries,
        key_values,
        context_grad,
        context_pairs,
        logs,
        shard_valid,
        totals,
        columns,
        chunks,
    )
    down_weight_grad = summed[:, :width].astype(wide)
    spare = part_size - (PIX + 1) * own_vars
    (
        qkv_weight_grad,
        agg_proj_grad,
        proj_weight_grad,
        value_weight_grad,
        key_weight_grad,
        query_weight_grad,
        agg_query_grad,
        var_grads,
        extras,
        patch_grad,
        out_far,
        rest,
    ) = finish(
        group_count,
        spare,
        jnp.stack([count_share, group_count * count_share]),
        (normed1.T, heads_t, context.T),
        (qkv_grad, attended_grad),
        columns,
        chunks,
        dict(
            full_qkv=full_qkv,
            full_agg=full_agg_proj,
            full_value=full_value,
            embedded=embedded,
            middle_grad=middle_grad,
            gain=norm1_gain[None, :],
            vectors=feed_vectors,
            patch_rows=patch_rows,
            coeffs=coeffs,
            slot_mask=slot_mask,
            table_values=table_values,
            select=select,
            own_columns=own_columns,
            key_query=key_query,
            query_rows=query_rows,
            key_weight=key_weight,
            query_weight=query_weight,
            own_query=own_query.astype(wide)[:, None],
            out_sum=out_sum,
            totals=totals,
        ),
    )
    down_sum = out_parts[0].astype(wide) + out_got[0].astype(wide) + out_far.astype(wide)
    output = (middle + down_sum + down_bias).astype(low)
    up_weight_grad = jnp.concatenate([summed[:, width:], rest], axis=1).astype(wide)
    patches_grad = patch_grad.transpose(1, 0, 2)
    qkv_weight_grad = qkv_weight_grad.astype(wide)
    agg_proj_grad = agg_proj_grad.astype(wide)
    proj_weight_grad = proj_weight_grad.astype(wide)
    at = HEADS * size // width
    vector_total = extras[at : at + 7]
    at += 7
    up_bias_total = lax.dynamic_slice_in_dim(extras, at + me, 1, 0)[0]
    vector_own = lax.dynamic_slice_in_dim(vector_total, me * own_width, own_width, 1)
    agg_query_grad = agg_query_grad[0]
    var_grads = var_grads[: (PIX + 1) * own_vars].reshape(PIX + 1, own_vars, width)
    patch_weight_grad = var_grads[:PIX].transpose(1, 0, 2)
    var_embed_grad = var_grads[PIX]
    return (
        output,
        patches_grad,
        patch_weight_grad,
        var_embed_grad,
        agg_query_grad,
        query_weight_grad,
        key_weight_grad,
        value_weight_grad,
        agg_proj_grad,
        vector_own[0],
        vector_own[1],
        vector_own[2],
        qkv_weight_grad,
        proj_weight_grad,
        vector_own[5],
        vector_own[3],
        vector_own[4],
        up_weight_grad,
        up_bias_total,
        down_weight_grad,
        vector_own[6],
    )


def solution(mesh):
    shard = P("fsdp")
    shard_rows = P("fsdp", None)
    return jax.shard_map(
        on_device,
        mesh=mesh,
        in_specs=(
            P(None, None, ("grp", "fsdp")),
            P("grp"),
            P("grp", None),
            P("grp"),
            P(),
            P("fsdp", None, None),
            shard_rows,
            P(),
            shard_rows,
            shard_rows,
            shard_rows,
            shard_rows,
            P(),
            P(),
            P(),
            shard_rows,
            shard_rows,
            P(),
            P(),
            P(),
            P(None, "fsdp"),
            shard,
            shard_rows,
            P(),
            P(("grp", "fsdp"), None),
        ),
        out_specs=(
            P(("grp", "fsdp"), None),
            P(None, None, ("grp", "fsdp")),
            P("fsdp", None, None),
            shard_rows,
            shard,
            shard_rows,
            shard_rows,
            shard_rows,
            shard_rows,
            shard,
            shard,
            shard,
            shard_rows,
            shard_rows,
            shard,
            shard,
            shard,
            P(None, "fsdp"),
            shard,
            shard_rows,
            shard,
        ),
        check_vma=False,
    )
```

```python
import functools

import jax
import jax.numpy as jnp
from jax import lax
from jax.experimental import pallas as pl
from jax.experimental.pallas import tpu as pltpu
from jax.sharding import PartitionSpec as P

HEADS = 16
VTOT = 48
PIX = 4

exact_mode = lax.Precision.HIGHEST
masked_out = -1e30
VMEM_LIMIT = 56 * 1024 * 1024


def swap(value, axis, bit):
    size = lax.axis_size(axis)
    return lax.ppermute(value, axis, [(i, i ^ bit) for i in range(size)])


def product(left_side, right_side):
    return jnp.dot(left_side, right_side, preferred_element_type=jnp.float32)


def left_product(left_side, right_side):
    return lax.dot_general(
        left_side, right_side, (((0,), (0,)), ((), ())), preferred_element_type=jnp.float32
    )


def right_product(left_side, right_side):
    return lax.dot_general(
        left_side, right_side, (((1,), (1,)), ((), ())), preferred_element_type=jnp.float32
    )


def column_sums(values_in):
    return jnp.sum(values_in.astype(jnp.float32), axis=0)


def flip(index, bit):
    bit_set = (index // bit) % 2
    return index + bit - 2 * bit * bit_set, bit_set


def meet(partners):
    barrier = pltpu.get_barrier_semaphore()
    for partner in partners:
        pl.semaphore_signal(
            barrier, inc=1, device_id=partner, device_id_type=pl.DeviceIdType.MESH
        )
    pl.semaphore_wait(barrier, len(partners))


def normalise(values_in):
    row_mean = jnp.mean(values_in, axis=-1, keepdims=True)
    centred = values_in - row_mean
    spread = jnp.mean(centred * centred, axis=-1, keepdims=True)
    inverse = lax.rsqrt(spread + 1e-05)
    return centred * inverse, inverse


def norm_back(grad, xhat, inverse, gain_vec):
    scaled = grad * gain_vec
    first = jnp.mean(scaled, axis=-1, keepdims=True)
    second = jnp.mean(scaled * xhat, axis=-1, keepdims=True)
    return (scaled - first - xhat * second) * inverse


def slot_softmax(patch_ref, columns, mask_ref):
    scores = columns[PIX] + mask_ref[...]
    for k in range(PIX):
        scores = scores + patch_ref[k].astype(jnp.float32) * columns[k]
    top = jnp.max(scores, axis=0, keepdims=True)
    terms = jnp.exp(scores - top)
    return terms / jnp.sum(terms, axis=0, keepdims=True)


def mixed_of(patch_ref, weights, rows):
    parts = [
        (weights * patch_ref[k].astype(jnp.float32)).astype(jnp.bfloat16) for k in range(PIX)
    ]
    parts.append(weights.astype(jnp.bfloat16))
    used = weights.shape[0] * (PIX + 1)
    if rows > used:
        parts.append(jnp.zeros((rows - used, weights.shape[1]), jnp.bfloat16))
    return jnp.concatenate(parts, axis=0)


def head_columns(coeff_ref, head, slots):
    lane = lax.broadcasted_iota(jnp.int32, (slots, coeff_ref.shape[1]), 1)
    return [
        jnp.sum(
            jnp.where(lane == head, coeff_ref[k * slots : (k + 1) * slots, :], 0.0),
            axis=1,
            keepdims=True,
        )
        for k in range(PIX + 1)
    ]


def prepare_kernel(group_size, head_dim, *refs):
    (
        count_ref, own_query, query_w, key_w, own_table, select_ref, own_value, own_agg,
        own_qkv, own_proj, own_grad, patch_ref, mask_ref, bias_ref, gain_ref, shift_ref,
    ) = refs[:16]
    (
        count_out, tables, query_out, keys_out, full_value, full_agg, full_qkv, full_proj,
        near_grad, far_grads, table_out, coeff_out, heads_out, embed_out, norm_out,
    ) = refs[16:31]
    query_part, query_got, counts = refs[31:34]
    whole_value, whole_agg, whole_qkv, whole_proj, grads = refs[34:39]
    send_sem, recv_sem, small_send, small_recv, local_sem = refs[39:]
    wide = jnp.float32
    low = jnp.bfloat16
    me = lax.axis_index("fsdp")
    group = lax.axis_index("grp")
    near_index = flip(me, 1)[0]
    far_index = flip(me, 2)[0]
    near = {"fsdp": near_index}
    far = {"fsdp": far_index}
    block = own_value.shape[0]
    heads = keys_out.shape[0]
    slots = mask_ref.shape[0]
    rows = own_grad.shape[0]
    bits = []
    bit = 1
    while bit < group_size:
        bits.append(bit)
        bit *= 2
    meet(
        [near, far, {"fsdp": flip(far_index, 1)[0]}]
        + [{"grp": flip(group, bit)[0]} for bit in bits]
    )

    def remote(src, dst, sends, recvs, at, device):
        return pltpu.make_async_remote_copy(
            src_ref=src,
            dst_ref=dst,
            send_sem=sends.at[at],
            recv_sem=recvs.at[at],
            device_id=device,
            device_id_type=pl.DeviceIdType.MESH,
        )

    def span(start, size):
        return pl.ds(pl.multiple_of(start, 16), size)

    width = own_value.shape[1]
    items = [(own_value, whole_value, 0, width, False), (own_agg, whole_agg, 0, width, False)]
    for n in range(full_qkv.shape[1] // width):
        items.append((own_qkv, whole_qkv, n * width, width, True))
    items.append((own_proj, whole_proj, 0, width, True))
    x_bit = flip(group, 1)[1]
    piece = flip(group, 2)[1] + 2 * flip(group, 4)[1] + 4 * x_bit
    eighth = block // 8

    def weight_copy(n, stage):
        own, whole, start, size, eighths = items[n]
        cols = pl.ds(start, size)

        def region(base, offset, count):
            return whole.at[span(base * block + offset, count), cols]

        if stage == 0:
            return remote(
                own.at[:, cols], region(me, 0, block), send_sem, recv_sem, (n, 0), near
            )
        if stage == 1:
            offset, count = (piece * eighth, eighth) if eighths else (x_bit * (block // 2), block // 2)
            return remote(
                own.at[span(offset, count), cols],
                region(me, offset, count),
                send_sem,
                recv_sem,
                (n, 1),
                far,
            )
        if stage == 2:
            at = region(far_index, piece * eighth, eighth)
            return remote(at, at, send_sem, recv_sem, (n, 2), {"grp": flip(group, 2)[0]})
        if stage == 3:
            at = region(far_index, (piece // 2) * 2 * eighth, 2 * eighth)
            return remote(at, at, send_sem, recv_sem, (n, 3), {"grp": flip(group, 4)[0]})
        if stage == 4:
            at = region(far_index, x_bit * (block // 2), block // 2)
            return remote(at, at, send_sem, recv_sem, (n, 4), {"grp": flip(group, 1)[0]})
        at = region(far_index, 0, block)
        return remote(at, at, send_sem, recv_sem, (n, 5), near)

    def out_copy(n):
        own, whole, start, size, eighths = items[n]
        target = [full_value, full_agg, full_qkv, full_proj][min(n, 2) if n + 1 < len(items) else 3]
        cols = pl.ds(start, size)
        return pltpu.make_async_copy(whole.at[:, cols], target.at[:, cols], local_sem.at[2 + n])

    grad_parts = 4
    part_rows = rows // grad_parts

    def grad_near():
        return remote(own_grad, grads.at[0], small_send, small_recv, 0, near)

    def grad_far(p):
        at = pl.ds(p * part_rows, part_rows)
        return remote(
            own_grad.at[at, :], grads.at[1, at, :], small_send, small_recv, 1 + p, far
        )

    def grad_last(p):
        at = pl.ds(p * part_rows, part_rows)
        return remote(
            grads.at[1, at, :],
            grads.at[2, at, :],
            small_send,
            small_recv,
            1 + grad_parts + p,
            near,
        )

    def grad_out(n):
        if n == 0:
            return pltpu.make_async_copy(grads.at[0], near_grad, local_sem.at[0])
        return pltpu.make_async_copy(grads.at[pl.ds(1, 2)], far_grads, local_sem.at[1])

    base = 1 + 2 * grad_parts

    def table_copy(kind):
        if kind == 0:
            return remote(own_table, tables.at[me], small_send, small_recv, base, near)
        if kind == 1:
            return remote(own_table, tables.at[me], small_send, small_recv, base + 1, far)
        at = tables.at[far_index]
        return remote(at, at, small_send, small_recv, base + 2, near)

    others = [near, far, {"fsdp": flip(far_index, 1)[0]}]

    def query_copy(kind):
        return remote(
            query_part, query_got.at[kind], small_send, small_recv, base + 3 + kind, others[kind]
        )

    def key_copy(kind):
        at = keys_out.at[:, pl.ds(pl.multiple_of(me * block, 128), block)]
        return remote(at, at, small_send, small_recv, base + 6 + kind, others[kind])

    def count_copy(n):
        partner = {"grp": flip(group, bits[n])[0]}
        return remote(
            counts.at[2 * n], counts.at[2 * n + 1], small_send, small_recv, base + 9 + n, partner
        )

    def count_step(n):
        count_copy(n).wait()
        value = counts[2 * n] + counts[2 * n + 1]
        if n + 1 < len(bits):
            counts[2 * n + 2] = value
            count_copy(n + 1).start()
        else:
            count_out[...] = value

    def forward(n, stage):
        weight_copy(n, stage).wait()
        weight_copy(n, 4 if (stage == 1 and not items[n][4]) else stage + 1).start()

    def keep(n):
        weight_copy(n, 0).wait()
        weight_copy(n, 5).wait()
        out_copy(n).start()

    late = list(range(2, len(items)))

    query_part[...] = jnp.dot(own_query[...], query_w[...], preferred_element_type=wide)[:8]
    for kind in range(3):
        query_copy(kind).start()
    weight_copy(0, 1).start()
    for n in late:
        weight_copy(n, 1).start()
    table_copy(1).start()
    table_copy(0).start()
    weight_copy(0, 0).start()
    counts[0] = count_ref[...]
    count_copy(0).start()
    tables[me] = own_table[...]
    whole_value[span(me * block, block), :] = own_value[...]
    for kind in range(3):
        query_copy(kind).wait()
    query = query_part[...] + query_got[0] + query_got[1] + query_got[2]
    query_out[...] = query
    lane = lax.broadcasted_iota(jnp.int32, (heads, width), 1)
    head = lax.broadcasted_iota(jnp.int32, (heads, width), 0)
    spread = jnp.where(lane // head_dim == head, jnp.broadcast_to(query[:1], (heads, width)), 0.0)
    own_keys = lax.dot_general(
        spread.astype(low), key_w[...], (((1,), (1,)), ((), ())), preferred_element_type=wide
    ) * (head_dim ** (-0.5))
    keys_out[:, pl.ds(pl.multiple_of(me * block, 128), block)] = own_keys.astype(low)
    for kind in range(3):
        key_copy(kind).start()
    weight_copy(1, 1).start()
    whole_agg[span(me * block, block), :] = own_agg[...]
    whole_qkv[span(me * block, block), :] = own_qkv[...]
    whole_proj[span(me * block, block), :] = own_proj[...]
    forward(0, 1)
    for n in late:
        forward(n, 1)
    forward(0, 4)
    forward(2, 2)
    forward(3, 2)
    table_copy(0).wait()
    table_copy(1).wait()
    table_copy(2).start()
    for p in range(grad_parts):
        grad_far(p).start()
    forward(1, 1)
    weight_copy(1, 0).start()
    table_copy(2).wait()
    stacked = tables[...].reshape(select_ref.shape[1], width)
    table = jnp.dot(select_ref[...], stacked, preferred_element_type=wide).astype(low)
    for kind in range(3):
        key_copy(kind).wait()
    coeff_out[...] = lax.dot_general(
        table, keys_out[...], (((1,), (1,)), ((), ())), preferred_element_type=wide
    )
    weight_copy(0, 0).wait()
    weight_copy(0, 5).wait()
    out_copy(0).start()
    values = jnp.dot(table, whole_value[...], preferred_element_type=wide)
    table_out[...] = jnp.transpose(values).astype(low)

    def one_head(h, carry):
        weights = slot_softmax(patch_ref, head_columns(coeff_out, h, slots), mask_ref)
        mixed = mixed_of(patch_ref, weights, table_out.shape[1])
        at = pl.ds(pl.multiple_of(h * head_dim, 16), head_dim)
        heads_out[at, :] = jnp.dot(
            table_out[at, :], mixed, preferred_element_type=wide
        ).astype(low)
        return carry

    half = heads // 2
    forward(2, 3)
    forward(4, 2)
    for n in late:
        weight_copy(n, 0).start()
    lax.fori_loop(0, half, one_head, 0)
    forward(1, 4)
    forward(3, 3)
    forward(5, 2)
    grad_near().start()
    lax.fori_loop(half, heads, one_head, 0)
    keep(1)
    embedded = (
        lax.dot_general(
            heads_out[...], whole_agg[...], (((0,), (0,)), ((), ())), preferred_element_type=wide
        )
        + bias_ref[...]
    )
    embed_out[...] = embedded
    count_step(0)
    forward(2, 4)
    grad_far(0).wait()
    grad_last(0).start()
    xhat, inverse = normalise(embedded)
    norm_out[...] = (xhat * gain_ref[...] + shift_ref[...]).astype(low)
    forward(4, 3)
    keep(2)
    forward(3, 4)
    count_step(1)
    grad_far(1).wait()
    grad_last(1).start()
    forward(5, 3)
    keep(3)
    forward(4, 4)
    for n in range(2, len(bits)):
        count_step(n)
    grad_far(2).wait()
    grad_last(2).start()
    keep(4)
    forward(5, 4)
    grad_near().wait()
    grad_out(0).start()
    grad_far(3).wait()
    grad_last(3).start()
    keep(5)
    for p in range(grad_parts):
        grad_last(p).wait()
    grad_out(1).start()
    for n in range(len(items)):
        out_copy(n).wait()
    for n in range(2):
        grad_out(n).wait()


def prepare(
    group_size, count_rows, own_query, query_w, key_w, own_table, select, own_value, own_agg,
    own_qkv, own_proj, own_grad, patch_rows, slot_mask, bias, gain, shift,
):
    block, width = own_value.shape
    head_dim = width // HEADS
    rows = own_grad.shape[0]
    slots = slot_mask.shape[0]
    size = select.shape[0]
    low = jnp.bfloat16
    wide = jnp.float32
    vmem = pl.BlockSpec(memory_space=pltpu.VMEM)
    hbm = pl.BlockSpec(memory_space=pl.ANY)
    steps = 0
    while 2**steps < group_size:
        steps += 1
    items = 3 + own_qkv.shape[1] // width
    small = 1 + 2 * 4 + 9 + steps

    def shape(dims, kind):
        return jax.ShapeDtypeStruct(dims, kind)

    return pl.pallas_call(
        functools.partial(prepare_kernel, group_size, head_dim),
        in_specs=[vmem] * 16,
        out_specs=[vmem] * 4 + [hbm] * 6 + [vmem] * 5,
        out_shape=[
            shape((8, 128), wide),
            shape((4,) + own_table.shape, low),
            shape((8, width), wide),
            shape((HEADS, width), low),
            shape((4 * block, width), low),
            shape((4 * block, width), low),
            shape((4 * block, own_qkv.shape[1]), low),
            shape((4 * block, width), low),
            shape((rows, width), low),
            shape((2, rows, width), low),
            shape((width, size), low),
            shape((size, HEADS), wide),
            shape((width, rows), low),
            shape((rows, width), wide),
            shape((rows, width), low),
        ],
        scratch_shapes=[
            pltpu.VMEM((8, width), wide),
            pltpu.VMEM((3, 8, width), wide),
            pltpu.VMEM((2 * steps, 8, 128), wide),
            pltpu.VMEM((4 * block, width), low),
            pltpu.VMEM((4 * block, width), low),
            pltpu.VMEM((4 * block, own_qkv.shape[1]), low),
            pltpu.VMEM((4 * block, width), low),
            pltpu.VMEM((3, rows, width), low),
            pltpu.SemaphoreType.DMA((items, 6)),
            pltpu.SemaphoreType.DMA((items, 6)),
            pltpu.SemaphoreType.DMA((small,)),
            pltpu.SemaphoreType.DMA((small,)),
            pltpu.SemaphoreType.DMA((2 + items,)),
        ],
        compiler_params=pltpu.CompilerParams(
            collective_id=3, has_side_effects=True, vmem_limit_bytes=VMEM_LIMIT
        ),
        cost_estimate=pl.CostEstimate(
            flops=8 * size * rows * width, bytes_accessed=100_000_000, transcendentals=0
        ),
        name="prepare",
    )(
        count_rows, own_query, query_w, key_w, own_table, select, own_value, own_agg,
        own_qkv, own_proj, own_grad, patch_rows, slot_mask, bias, gain, shift,
    )


def group_steps(group, order, size):
    steps = []
    offset = 0
    for bit in order:
        partner, bit_set = flip(group, bit)
        halving = size >= 32
        steps.append((partner, bit_set, halving, size, offset))
        if halving:
            size = size // 2
            offset = offset + bit_set * size
    return steps


def group_orders(group_size):
    bits = []
    while 2 ** len(bits) < group_size:
        bits.append(2 ** len(bits))
    return bits, bits[1:] + bits[:1]


def group_sum(steps, hold, halves, done, send_sem, recv_sem):
    count = len(steps)
    halvings = [i for i, step in enumerate(steps) if step[2]]
    wide = jnp.float32

    def span(start, size):
        return pl.ds(pl.multiple_of(start, 16), size)

    def copy(stage, c, src, dst, partner):
        return pltpu.make_async_remote_copy(
            src_ref=src,
            dst_ref=dst,
            send_sem=send_sem.at[stage, c],
            recv_sem=recv_sem.at[stage, c],
            device_id={"grp": partner},
            device_id_type=pl.DeviceIdType.MESH,
        )

    def step_copy(i, c):
        partner, bit_set, halving, size, offset = steps[i]
        if halving:
            size = size // 2
            offset = offset + (1 - bit_set) * size
        return copy(i, c, hold.at[c, span(offset, size), :], halves[i].at[c], partner)

    def back_copy(i, c):
        partner, bit_set, halving, size, offset = steps[i]
        size = size // 2
        at = done.at[c, span(offset + bit_set * size, size), :]
        return copy(count + i, c, at, at, partner)

    def begin(c):
        step_copy(0, c).start()

    def after_step(i, c):
        step_copy(i, c).wait()
        partner, bit_set, halving, size, offset = steps[i]
        if halving:
            size = size // 2
            offset = offset + bit_set * size
        at = span(offset, size)
        value = hold[c, at, :].astype(wide) + halves[i][c].astype(wide)
        if i + 1 < count:
            hold[c, at, :] = value.astype(hold.dtype)
            step_copy(i + 1, c).start()
        else:
            done[c, at, :] = value.astype(done.dtype)
            back_copy(halvings[-1], c).start()

    def after_back(k, c):
        back_copy(halvings[k], c).wait()
        if k > 0:
            back_copy(halvings[k - 1], c).start()

    stages = [begin] + [functools.partial(after_step, i) for i in range(count)]
    return stages + [functools.partial(after_back, k) for k in reversed(range(len(halvings)))]


def group_buffers(group_size, chunks, rows, columns):
    low = jnp.bfloat16
    steps = len(group_orders(group_size)[0])
    halves = []
    size = rows
    for _ in range(steps):
        if size >= 32:
            size //= 2
        halves.append(pltpu.VMEM((chunks, size, columns), low))
    one = pltpu.VMEM((chunks, rows, columns), low)
    semaphores = pltpu.SemaphoreType.DMA((2 * steps, chunks))
    return [one, halves, one, semaphores, semaphores]


def sum_beside(group, group_size, first, total_in, total_out, buffers):
    hold, halves, done, send_sem, recv_sem, in_sem, keep_sem = buffers
    chunks, rows, columns = hold.shape
    steps = group_steps(group, group_orders(group_size)[0], rows)
    stages = group_sum(steps, hold, halves, done, send_sem, recv_sem)

    def at(c):
        return pl.ds(pl.multiple_of((first + c) * columns, 128), columns)

    def take(c):
        return pltpu.make_async_copy(total_in.at[:, at(c)], hold.at[c], in_sem.at[c])

    def give(c):
        place = pl.ds(pl.multiple_of(c * columns, 128), columns)
        return pltpu.make_async_copy(done.at[c], total_out.at[:, place], keep_sem.at[c])

    def start():
        for c in range(chunks):
            take(c).wait()
            stages[0](c)

    def end(c):
        stages[-1](c)
        give(c).start()

    return chunks, take, start, stages[1:-1] + [end], give


def beside_buffers(group_size, chunks, rows, columns):
    return group_buffers(group_size, chunks, rows, columns) + [
        pltpu.SemaphoreType.DMA((chunks,)),
        pltpu.SemaphoreType.DMA((chunks,)),
    ]


def lane_half(rows, pair, head_dim):
    lane = lax.broadcasted_iota(jnp.int32, (rows, 2 * head_dim), 1)
    return (lane // head_dim) == pair


def attend_kernel(
    head_dim, valid_ref, rows_ref, weight_ref, q_ref, kv_out, out_ref, flat_ref, log_ref, kv_ref, weight_s, sum_s, top_s, total_s, send_sem, recv_sem, fetch_sem, keep_sem
):
    me = lax.axis_index("fsdp")
    near = {"fsdp": flip(me, 1)[0]}
    far = {"fsdp": flip(me, 2)[0]}
    wide = jnp.float32
    low = jnp.bfloat16
    rows, width = rows_ref.shape
    lanes = 2 * head_dim
    pairs = width // lanes
    scale = head_dim ** (-0.5)
    groups = pairs // 2

    def fetch(part, g):
        at = pl.ds(part * width + g * 2 * lanes, 2 * lanes)
        return pltpu.make_async_copy(
            weight_ref.at[:, at], weight_s.at[:, at], fetch_sem.at[part, g]
        )

    def keep(i):
        return pltpu.make_async_copy(kv_ref.at[:, i], kv_out.at[:, i], keep_sem.at[i])

    for g in range(groups):
        fetch(1, g).start()
        fetch(2, g).start()
    for g in range(groups):
        fetch(0, g).start()
    meet([near, far])

    def copy(kind, i, source, target, device):
        return pltpu.make_async_remote_copy(
            src_ref=kv_ref.at[source, i],
            dst_ref=kv_ref.at[target, i],
            send_sem=send_sem.at[kind, i],
            recv_sem=recv_sem.at[kind, i],
            device_id=device,
            device_id_type=pl.DeviceIdType.MESH,
        )

    def near_copy(i):
        return copy(0, i, 0, 1, near)

    def far_copy(i):
        return copy(1, i, 0, 2, far)

    def last_copy(i):
        return copy(2, i, 2, 3, near)

    entry = rows_ref[...]
    for g in range(groups):
        for part in range(2):
            start = (part + 1) * width + g * 2 * lanes
            fetch(part + 1, g).wait()
            value = jnp.dot(
                entry, weight_s[:, start : start + 2 * lanes], preferred_element_type=wide
            ).astype(low)
            kv_ref[0, 2 * g, part] = value[:, :lanes]
            kv_ref[0, 2 * g + 1, part] = value[:, lanes:]
        for i in (2 * g, 2 * g + 1):
            far_copy(i).start()
            near_copy(i).start()
    for g in range(groups):
        start = g * 2 * lanes
        fetch(0, g).wait()
        value = jnp.dot(
            entry, weight_s[:, start : start + 2 * lanes], preferred_element_type=wide
        ).astype(low)
        value = value * jnp.asarray(scale, low)
        q_ref[2 * g] = value[:, :lanes]
        q_ref[2 * g + 1] = value[:, lanes:]

    tile = min(rows, 256)

    def attend(i, shards, first):
        for start in range(0, rows, tile):
            at = slice(start, start + tile)
            block = q_ref[i, at, :]
            sums, tops, totals = [], [], []
            for pair in range(2):
                query = jnp.where(lane_half(tile, pair, head_dim), block, jnp.zeros_like(block))
                logits = []
                for j in shards:
                    raw = lax.dot_general(
                        query, kv_ref[j, i, 0], (((1,), (1,)), ((), ())), preferred_element_type=wide
                    )
                    place = lax.broadcasted_iota(jnp.int32, (1, rows), 1)
                    logits.append(jnp.where(place < valid_ref[j], raw, masked_out))
                top = functools.reduce(
                    jnp.maximum, [jnp.max(part, axis=1, keepdims=True) for part in logits]
                )
                sum_now, total_now = 0.0, 0.0
                for j, part in zip(shards, logits):
                    terms = jnp.exp(part - top)
                    total_now = total_now + jnp.sum(terms, axis=1, keepdims=True)
                    sum_now = sum_now + jnp.dot(
                        terms.astype(low), kv_ref[j, i, 1], preferred_element_type=wide
                    )
                sums.append(sum_now)
                tops.append(top)
                totals.append(total_now)
            side = lane_half(tile, 0, head_dim)
            sum_now = jnp.where(side, sums[0], sums[1])
            top = jnp.where(side, tops[0], tops[1])
            total_now = jnp.where(side, totals[0], totals[1])
            if not first:
                old_top = top_s[at, :]
                new_top = jnp.maximum(top, old_top)
                mine = jnp.exp(top - new_top)
                others = jnp.exp(old_top - new_top)
                sum_now = sum_now * mine + sum_s[at, :] * others
                total_now = total_now * mine + total_s[at, :] * others
                top = new_top
            sum_s[at, :] = sum_now
            top_s[at, :] = top
            total_s[at, :] = total_now

    def one_pair(i, carry):
        near_copy(i).wait_recv()
        attend(i, (0, 1), True)
        far_copy(i).wait_recv()
        last_copy(i).start()
        attend(i, (2,), False)
        last_copy(i).wait_recv()
        attend(i, (3,), False)
        keep(i).start()
        context = (sum_s[...] / total_s[...]).astype(low)
        out_ref[i] = context
        flat_ref[:, pl.ds(pl.multiple_of(i * lanes, lanes), lanes)] = context
        logs = jnp.transpose(top_s[...] + jnp.log(total_s[...]))
        for pair in range(2):
            log_ref[i, pair : pair + 1, :] = logs[pair * head_dim : pair * head_dim + 1, :]
        return carry

    lax.fori_loop(0, pairs, one_pair, 0)

    def end(i, carry):
        near_copy(i).wait_send()
        far_copy(i).wait_send()
        last_copy(i).wait_send()
        keep(i).wait()
        return carry

    lax.fori_loop(0, pairs, end, 0)


def attend(rows_in, weight, valid):
    rows, width = rows_in.shape
    head_dim = width // HEADS
    lanes = 2 * head_dim
    pairs = HEADS // 2
    whole = pl.BlockSpec(memory_space=pltpu.VMEM)
    hbm = pl.BlockSpec(memory_space=pl.ANY)
    low = jnp.bfloat16
    wide = jnp.float32
    return pl.pallas_call(
        functools.partial(attend_kernel, head_dim),
        in_specs=[pl.BlockSpec(memory_space=pltpu.SMEM), whole, hbm],
        out_specs=[whole, hbm, whole, whole, whole],
        out_shape=[
            jax.ShapeDtypeStruct((pairs, rows, lanes), low),
            jax.ShapeDtypeStruct((4, pairs, 2, rows, lanes), low),
            jax.ShapeDtypeStruct((pairs, rows, lanes), low),
            jax.ShapeDtypeStruct((rows, width), low),
            jax.ShapeDtypeStruct((pairs, 8, rows), wide),
        ],
        scratch_shapes=[
            pltpu.VMEM((4, pairs, 2, rows, lanes), low),
            pltpu.VMEM(weight.shape, low),
            pltpu.VMEM((rows, lanes), wide),
            pltpu.VMEM((rows, lanes), wide),
            pltpu.VMEM((rows, lanes), wide),
            pltpu.SemaphoreType.DMA((3, pairs)),
            pltpu.SemaphoreType.DMA((3, pairs)),
            pltpu.SemaphoreType.DMA((3, pairs // 2)),
            pltpu.SemaphoreType.DMA((pairs,)),
        ],
        compiler_params=pltpu.CompilerParams(
            collective_id=1, has_side_effects=True, vmem_limit_bytes=VMEM_LIMIT
        ),
        cost_estimate=pl.CostEstimate(
            flops=64 * rows * rows * width, bytes_accessed=100_000_000, transcendentals=0
        ),
        name="attend",
    )(valid, rows_in, weight)


def attend_back_kernel(
    head_dim, group_size, valid_ref, q_ref, kv_in, grad_ref, out_ref, log_ref, *refs
):
    total_in, result_ref, total_out = refs[:3]
    q_sum, own_s, far_s, last_s, near_s, got_far, got_last, got_near, dot_rows = refs[3:12]
    send_sem, recv_sem, kv_ref, fetch_sem = refs[12:16]
    group = lax.axis_index("grp")
    me = lax.axis_index("fsdp")
    near = {"fsdp": flip(me, 1)[0]}
    far = {"fsdp": flip(me, 2)[0]}
    wide = jnp.float32
    low = jnp.bfloat16
    pairs, rows, lanes = q_ref.shape

    def fetch(half, i):
        at = pl.ds(2 * half, 2)
        return pltpu.make_async_copy(kv_in.at[at, i], kv_ref.at[at, i], fetch_sem.at[half, i])

    chunks, take, sum_start, sum_stages, give = sum_beside(
        group, group_size, 0, total_in, total_out, refs[16:]
    )

    waits = [s + 1 + max(0, s - len(sum_stages) + 3) for s in range(len(sum_stages))]

    def sum_step(t):
        for wait, stage in zip(waits, sum_stages):
            c = t - wait

            @pl.when((c >= 0) & (c < chunks))
            def _(stage=stage, c=c):
                stage(c)

    for i in range(pairs):
        fetch(1, i).start()
    for c in range(chunks):
        take(c).start()
    for i in range(pairs):
        fetch(0, i).start()
    width = pairs * lanes
    scale = head_dim ** (-0.5)
    meet([near, far] + [{"grp": flip(group, bit)[0]} for bit in group_orders(group_size)[0]])

    def copy(kind, i, source, target, device):
        return pltpu.make_async_remote_copy(
            src_ref=source.at[i],
            dst_ref=target.at[i],
            send_sem=send_sem.at[kind, i],
            recv_sem=recv_sem.at[kind, i],
            device_id=device,
            device_id_type=pl.DeviceIdType.MESH,
        )

    def last_copy(i):
        return copy(0, i, last_s, got_last, near)

    def near_copy(i):
        return copy(1, i, near_s, got_near, near)

    def far_copy(i):
        return copy(2, i, far_s, got_far, far)

    def back(i, shards, targets):
        query = q_ref[i]
        grad = grad_ref[i]
        q_grad = None
        k_sums = [None, None]
        v_sums = [None, None]

        def plus(old, new):
            return new if old is None else old + new

        for pair in range(2):
            side = lane_half(rows, pair, head_dim)
            log_row = log_ref[i, pair : pair + 1, :]
            dot_row = dot_rows[i, pair : pair + 1, :]
            one_query = jnp.where(side, query, jnp.zeros_like(query))
            one_grad = jnp.where(side, grad, jnp.zeros_like(grad))
            for n, j in enumerate(shards):
                key = kv_ref[j, i, 0]
                one_key = jnp.where(side, key, jnp.zeros_like(key))
                raw = lax.dot_general(
                    key, one_query, (((1,), (1,)), ((), ())), preferred_element_type=wide
                )
                place = lax.broadcasted_iota(jnp.int32, raw.shape, 0)
                probs = jnp.exp(jnp.where(place < valid_ref[j], raw - log_row, masked_out))
                probs_grad = lax.dot_general(
                    kv_ref[j, i, 1], one_grad, (((1,), (1,)), ((), ())), preferred_element_type=wide
                )
                raw_grad = (probs * (probs_grad - dot_row)).astype(low)
                v_sums[n] = plus(
                    v_sums[n], jnp.dot(probs.astype(low), one_grad, preferred_element_type=wide)
                )
                k_sums[n] = plus(
                    k_sums[n], jnp.dot(raw_grad, one_query, preferred_element_type=wide)
                )
                q_grad = plus(
                    q_grad,
                    lax.dot_general(
                        raw_grad, one_key, (((0,), (0,)), ((), ())), preferred_element_type=wide
                    ),
                )
        for n, target in enumerate(targets):
            target[i, 0] = k_sums[n].astype(target.dtype)
            target[i, 1] = v_sums[n].astype(target.dtype)
        return q_grad

    def send_far(i):
        last_copy(i).wait()
        far_s[i] = (far_s[i].astype(wide) + got_last[i].astype(wide)).astype(low)
        far_copy(i).start()

    def first_loop(i, carry):
        dots = jnp.transpose(grad_ref[i].astype(wide) * out_ref[i].astype(wide))
        for pair in range(2):
            here = slice(pair * head_dim, (pair + 1) * head_dim)
            dot_rows[i, pair : pair + 1, :] = jnp.sum(dots[here, :], axis=0, keepdims=True)
        fetch(1, i).wait()
        q_sum[i] = back(i, (3, 2), (last_s, far_s))
        last_copy(i).start()

        @pl.when(i > 0)
        def _():
            send_far(i - 1)

        @pl.when(i == 0)
        def _():
            sum_start()

        sum_step(i)
        return carry

    lax.fori_loop(0, pairs, first_loop, 0)
    send_far(pairs - 1)

    def second_loop(i, carry):
        fetch(0, i).wait()
        q_sum[i] = (q_sum[i] + back(i, (1, 0), (near_s, own_s))) * scale
        near_copy(i).start()
        sum_step(pairs + i)
        return carry

    lax.fori_loop(0, pairs, second_loop, 0)
    for i in range(pairs):
        near_copy(i).wait()
        far_copy(i).wait()
        at = slice(i * lanes, (i + 1) * lanes)
        result_ref[:, at] = q_sum[i].astype(low)
        for part in range(2):
            value = own_s[i, part] + got_near[i, part].astype(wide) + got_far[i, part].astype(wide)
            start = (part + 1) * width + i * lanes
            result_ref[:, start : start + lanes] = value.astype(low)
    for t in range(2 * pairs, chunks + waits[-1]):
        for wait, stage in zip(waits, sum_stages):
            if 0 <= t - wait < chunks:
                stage(t - wait)
    for c in range(chunks):
        give(c).wait()


def attend_back(group_size, queries, key_values, grad, out, logs, valid, totals, columns, chunks):
    pairs, rows, lanes = queries.shape
    head_dim = lanes // 2
    whole = pl.BlockSpec(memory_space=pltpu.VMEM)
    low = jnp.bfloat16
    wide = jnp.float32
    slab = (pairs, 2, rows, lanes)
    return pl.pallas_call(
        functools.partial(attend_back_kernel, head_dim, group_size),
        in_specs=[
            pl.BlockSpec(memory_space=pltpu.SMEM),
            whole,
            pl.BlockSpec(memory_space=pl.ANY),
            whole,
            whole,
            whole,
            pl.BlockSpec(memory_space=pl.ANY),
        ],
        out_specs=[whole, pl.BlockSpec(memory_space=pl.ANY)],
        out_shape=[
            jax.ShapeDtypeStruct((rows, 3 * pairs * lanes), low),
            jax.ShapeDtypeStruct((totals.shape[0], chunks * columns), low),
        ],
        scratch_shapes=[
            pltpu.VMEM((pairs, rows, lanes), wide),
            pltpu.VMEM(slab, wide),
            pltpu.VMEM(slab, low),
            pltpu.VMEM(slab, low),
            pltpu.VMEM(slab, low),
            pltpu.VMEM(slab, low),
            pltpu.VMEM(slab, low),
            pltpu.VMEM(slab, low),
            pltpu.VMEM((pairs, 8, rows), wide),
            pltpu.SemaphoreType.DMA((3, pairs)),
            pltpu.SemaphoreType.DMA((3, pairs)),
            pltpu.VMEM(key_values.shape, low),
            pltpu.SemaphoreType.DMA((2, pairs)),
        ]
        + beside_buffers(group_size, chunks, totals.shape[0], columns),
        compiler_params=pltpu.CompilerParams(
            collective_id=2, has_side_effects=True, vmem_limit_bytes=VMEM_LIMIT
        ),
        cost_estimate=pl.CostEstimate(
            flops=160 * rows * rows * pairs * lanes, bytes_accessed=100_000_000, transcendentals=0
        ),
        name="attend_back",
    )(valid, queries, key_values, grad, out, logs, totals)


def feed_kernel(*refs):
    (
        share_ref, context_ref, proj_ref, embed_ref, own_in, near_in, far_in, up_in,
        down_in, bias_ref, proj_bias, gain_ref, shift_ref,
    ) = refs[:13]
    (
        middle_out, out_out, total_out, middle_grad, attended, context_grad, vectors,
    ) = refs[13:20]
    entry, gelu_s, pre_s, own_back, near_s, last_s, far_s, got_near, got_last, got_far = refs[20:30]
    grad_s, up_ref, down_ref, middle_ref, out_ref, down_total, up_total = refs[30:37]
    send_sem, recv_sem, fetch_sem, keep_sem = refs[37:]
    wide = jnp.float32
    low = jnp.bfloat16
    me = lax.axis_index("fsdp")
    near = {"fsdp": flip(me, 1)[0]}
    far = {"fsdp": flip(me, 2)[0]}
    rows, width = embed_ref.shape
    hidden = up_ref.shape[1]
    tile = rows // 2
    pairs, _, lanes = context_grad.shape
    fetches = [
        pltpu.make_async_copy(up_in, up_ref, fetch_sem.at[0]),
        pltpu.make_async_copy(own_in, grad_s.at[0], fetch_sem.at[1]),
        pltpu.make_async_copy(down_in, down_ref, fetch_sem.at[2]),
        pltpu.make_async_copy(near_in, grad_s.at[1], fetch_sem.at[3]),
        pltpu.make_async_copy(far_in, grad_s.at[pl.ds(2, 2)], fetch_sem.at[4]),
    ]
    for fetch in fetches:
        fetch.start()
    meet([near, far])

    def span(t):
        return pl.ds(t * tile, tile)

    def keep_middle(t):
        return pltpu.make_async_copy(
            middle_ref.at[span(t), :], middle_out.at[span(t), :], keep_sem.at[0, t]
        )

    def keep_out(s, t):
        return pltpu.make_async_copy(
            out_ref.at[s, span(t), :], out_out.at[s, span(t), :], keep_sem.at[1 + s, t]
        )

    def keep_total(n):
        source = (down_total, up_total)[n]
        target = total_out.at[:, pl.ds(n * width, width)]
        return pltpu.make_async_copy(source, target, keep_sem.at[5, n])

    def copy(kind, t, src, dst, device):
        return pltpu.make_async_remote_copy(
            src_ref=src.at[span(t), :],
            dst_ref=dst.at[span(t), :],
            send_sem=send_sem.at[kind, t],
            recv_sem=recv_sem.at[kind, t],
            device_id=device,
            device_id_type=pl.DeviceIdType.MESH,
        )

    def rows_near(t):
        return copy(0, t, entry.at[0], entry.at[1], near)

    def rows_far(t):
        return copy(1, t, entry.at[0], entry.at[2], far)

    def rows_last(t):
        return copy(2, t, entry.at[2], entry.at[3], near)

    def back_near(t):
        return copy(3, t, near_s, got_near, near)

    def back_last(t):
        return copy(4, t, last_s, got_last, near)

    def back_far(t):
        return copy(5, t, far_s, got_far, far)

    def feed(s, t, target):
        rows_in = entry[s, span(t), :]
        pre_act = jnp.dot(rows_in, up_ref[...], preferred_element_type=wide) + bias_ref[...]
        cdf = 0.5 * (1.0 + lax.erf(pre_act * 0.7071067811865476))
        density = jnp.exp(-0.5 * pre_act * pre_act) * 0.3989422804014327
        gelu = (pre_act * cdf).astype(low)
        gelu_s[s, span(t), :] = gelu
        act_grad = lax.dot_general(
            grad_s[s, span(t), :],
            down_ref[...],
            (((1,), (1,)), ((), ())),
            preferred_element_type=wide,
        )
        pre_grad = act_grad * (cdf + pre_act * density)
        pre_low = pre_grad.astype(low)
        pre_s[s, span(t), :] = pre_low
        vectors[4:5, :] += jnp.sum(pre_low.astype(wide), axis=0, keepdims=True)
        out_ref[s, span(t), :] = jnp.dot(
            gelu, down_ref[...], preferred_element_type=wide
        ).astype(low)
        keep_out(s, t).start()
        target[span(t), :] = lax.dot_general(
            pre_low, up_ref[...], (((1,), (1,)), ((), ())), preferred_element_type=wide
        ).astype(target.dtype)

    vectors[...] = jnp.zeros_like(vectors)
    for t in range(2):
        middle = (
            embed_ref[span(t), :]
            + jnp.dot(context_ref[span(t), :], proj_ref[...], preferred_element_type=wide)
            + proj_bias[...]
        )
        middle_ref[span(t), :] = middle
        xhat, inverse = normalise(middle)
        entry[0, span(t), :] = (xhat * gain_ref[...] + shift_ref[...]).astype(low)
        rows_far(t).start()
        rows_near(t).start()
        keep_middle(t).start()
    for fetch in fetches[:3]:
        fetch.wait()
    for t in range(2):
        feed(0, t, own_back)
    for fetch in fetches[3:]:
        fetch.wait()
    for t in range(2):
        rows_near(t).wait()
        feed(1, t, near_s)
        back_near(t).start()

    for t in range(2):
        if t > 0:
            add_last(t - 1, back_last, back_far, far_s, got_last, span)
        rows_far(t).wait()
        rows_last(t).start()
        feed(2, t, far_s)
        rows_last(t).wait()
        feed(3, t, last_s)
        back_last(t).start()
    add_last(1, back_last, back_far, far_s, got_last, span)

    block = min(hidden, 256)
    for start in range(0, hidden, block):
        value = 0.0
        for s in range(4):
            value = value + lax.dot_general(
                gelu_s[s, :, start : start + block],
                grad_s[s],
                (((0,), (0,)), ((), ())),
                preferred_element_type=wide,
            )
        down_total[start : start + block, :] = (value * share_ref[0]).astype(low)
    keep_total(0).start()
    for start in range(0, width, block):
        value = 0.0
        for s in range(4):
            value = value + lax.dot_general(
                entry[s, :, start : start + block],
                pre_s[s],
                (((0,), (0,)), ((), ())),
                preferred_element_type=wide,
            )
        up_total[start : start + block, :] = (value * share_ref[0]).astype(low)
    keep_total(1).start()

    for t in range(2):
        back_near(t).wait()
        back_far(t).wait()
        at = span(t)
        grad = own_back[at, :] + got_near[at, :].astype(wide) + got_far[at, :].astype(wide)
        xhat, inverse = normalise(middle_ref[at, :])
        vectors[0:1, :] += jnp.sum(grad * xhat, axis=0, keepdims=True)
        vectors[1:2, :] += jnp.sum(grad, axis=0, keepdims=True)
        upstream = grad_s[0, at, :].astype(wide)
        vectors[3:4, :] += jnp.sum(upstream, axis=0, keepdims=True)
        value = upstream + norm_back(grad, xhat, inverse, gain_ref[...])
        middle_grad[at, :] = value
        value_low = value.astype(low)
        attended[at, :] = value_low
        vectors[2:3, :] += jnp.sum(value_low.astype(wide), axis=0, keepdims=True)
        back = lax.dot_general(
            value_low, proj_ref[...], (((1,), (1,)), ((), ())), preferred_element_type=wide
        ).astype(low)
        for i in range(pairs):
            context_grad[i, at, :] = back[:, i * lanes : (i + 1) * lanes]
    for t in range(2):
        keep_middle(t).wait()
        keep_total(t).wait()
        for s in range(4):
            keep_out(s, t).wait()


def add_last(t, back_last, back_far, far_s, got_last, span):
    back_last(t).wait()
    at = span(t)
    value = far_s[at, :].astype(jnp.float32) + got_last[at, :].astype(jnp.float32)
    far_s[at, :] = value.astype(jnp.bfloat16)
    back_far(t).start()


def feed(
    share, context, proj, embedded, own_grad, near_grad, far_grads, up, down, bias, proj_bias, gain, shift
):
    rows, width = embedded.shape
    hidden = up.shape[1]
    pairs = HEADS // 2
    low = jnp.bfloat16
    wide = jnp.float32
    vmem = pl.BlockSpec(memory_space=pltpu.VMEM)
    hbm = pl.BlockSpec(memory_space=pl.ANY)
    flat = (rows, width)

    def shape(dims, kind):
        return jax.ShapeDtypeStruct(dims, kind)

    return pl.pallas_call(
        feed_kernel,
        in_specs=[pl.BlockSpec(memory_space=pltpu.SMEM)] + [vmem] * 3 + [hbm] * 5 + [vmem] * 4,
        out_specs=[hbm] * 3 + [vmem] * 4,
        out_shape=[
            shape(flat, wide),
            shape((4,) + flat, low),
            shape((width, width + hidden), low),
            shape(flat, wide),
            shape(flat, low),
            shape((pairs, rows, width // pairs), low),
            shape((8, width), wide),
        ],
        scratch_shapes=[
            pltpu.VMEM((4,) + flat, low),
            pltpu.VMEM((4, rows, hidden), low),
            pltpu.VMEM((4, rows, hidden), low),
            pltpu.VMEM(flat, wide),
            pltpu.VMEM(flat, low),
            pltpu.VMEM(flat, low),
            pltpu.VMEM(flat, low),
            pltpu.VMEM(flat, low),
            pltpu.VMEM(flat, low),
            pltpu.VMEM(flat, low),
            pltpu.VMEM((4,) + flat, low),
            pltpu.VMEM(up.shape, low),
            pltpu.VMEM(down.shape, low),
            pltpu.VMEM(flat, wide),
            pltpu.VMEM((4,) + flat, low),
            pltpu.VMEM((hidden, width), low),
            pltpu.VMEM((width, hidden), low),
            pltpu.SemaphoreType.DMA((6, 2)),
            pltpu.SemaphoreType.DMA((6, 2)),
            pltpu.SemaphoreType.DMA((5,)),
            pltpu.SemaphoreType.DMA((6, 2)),
        ],
        compiler_params=pltpu.CompilerParams(
            collective_id=4, has_side_effects=True, vmem_limit_bytes=VMEM_LIMIT
        ),
        cost_estimate=pl.CostEstimate(
            flops=48 * rows * width * hidden, bytes_accessed=100_000_000, transcendentals=0
        ),
        name="feed",
    )(
        share, context, proj, embedded, own_grad, near_grad, far_grads, up, down, bias,
        proj_bias, gain, shift,
    )


def finish_kernel(group_size, widths, head_dim, first_chunk, *refs):
    share_ref = refs[0]
    left_qkv, qkv_grad, left_agg_in, left_proj_in, attended_in = refs[1:6]
    (
        full_qkv, full_agg_in, full_value, embed_in, middle_in, gain_ref, vectors_ref, patch_ref,
        coeff_ref, mask_ref, table_ref, select_ref, own_columns, keys_ref, query_ref, key_w,
        query_w, own_query, out_sum, total_in,
    ) = refs[6:26]
    outs = refs[26:29]
    value_out, key_out, query_out, agg_query_out, var_out, extra_out, patch_grad = refs[29:36]
    out_far, total_out = refs[36:38]
    sets = [refs[38:48], refs[48:57]]
    full, query_part, query_got, var_s, last_send, last_recv = refs[57:63]
    entry_grad, embed_grad, heads_grad, table_s, coeff_s, extras, bundle = refs[63:70]
    weight_s, weight_sem, left_agg, left_proj, attended, full_agg, embed_ref, middle_grad = refs[70:78]
    fetch_sem = refs[78]
    sum_chunks, sum_take, sum_start, sum_stages, sum_give = sum_beside(
        lax.axis_index("grp"), group_size, first_chunk, total_in, total_out, refs[79:]
    )
    fetches = [
        pltpu.make_async_copy(source, target, fetch_sem.at[n])
        for n, (source, target) in enumerate(
            [
                (embed_in, embed_ref),
                (middle_in, middle_grad),
                (full_agg_in, full_agg),
                (left_proj_in, left_proj),
                (attended_in, attended),
                (left_agg_in, left_agg),
            ]
        )
    ]
    me = lax.axis_index("fsdp")
    group = lax.axis_index("grp")
    core_partner, core = flip(me, 1)
    far_partner, far = flip(me, 2)
    diagonal = flip(far_partner, 1)[0]
    wide = jnp.float32
    low = jnp.bfloat16
    quarters = [buffers[2].shape[2] for buffers in sets]
    all_steps = [
        group_steps(group, group_orders(group_size)[0], quarter) for quarter in quarters
    ]
    all_halvings = [[i for i, step in enumerate(steps) if step[2]] for steps in all_steps]
    count = len(all_steps[0])
    slots = sets[1][0].shape[0]
    others = [{"fsdp": core_partner}, {"fsdp": far_partner}, {"fsdp": diagonal}]
    pltpu.make_async_copy(full_qkv.at[:, pl.ds(0, key_w.shape[1])], weight_s, weight_sem.at[0]).start()
    for c in range(sum_chunks):
        sum_take(c).start()
    for fetch in fetches:
        fetch.start()
    meet(others + [{"grp": step[0]} for step in all_steps[0]])

    def pieces(left, right, out):
        return [(left, right, out, start) for start in range(0, right.shape[1], widths)]

    qkv_pieces = pieces(left_qkv, qkv_grad, outs[0])
    agg_pieces = pieces(left_agg, embed_grad, outs[1])
    proj_pieces = pieces(left_proj, attended, outs[2])
    bulk = qkv_pieces + proj_pieces[:1] + [None] + proj_pieces[1:] + agg_pieces
    chunks = []
    for piece in bulk:
        if piece is None:
            chunks.append((0, 0, None, None, None, 0))
        else:
            chunks.append((1, sum(chunk[0] for chunk in chunks)) + piece)
    small = bulk.index(None)

    def remote(src, dst, send, recv, device):
        return pltpu.make_async_remote_copy(
            src_ref=src,
            dst_ref=dst,
            send_sem=send,
            recv_sem=recv,
            device_id=device,
            device_id_type=pl.DeviceIdType.MESH,
        )

    def copy(stage, c, src, dst, device):
        which, place = chunks[c][:2]
        send_sem, recv_sem = sets[which][-2:]
        return remote(src, dst, send_sem.at[stage, place], recv_sem.at[stage, place], device)

    def span(start, size):
        return pl.ds(pl.multiple_of(start, 16), size)

    def held(c):
        which, place, left, right, out, start = chunks[c]
        buffers = sets[which]
        rest = [
            buffer.at[place % slots if n in (0, 2) else place]
            for n, buffer in enumerate(buffers[:6])
        ]
        rest.append([part.at[place] for part in buffers[6]])
        rest.append(buffers[7].at[place] if out is None else out.at[:, start : start + widths])
        return rest

    def core_copy(c):
        at = held(c)
        return copy(0, c, at[0], at[1], others[0])

    def far_copy(c):
        at = held(c)
        return copy(1, c, at[3], at[4], others[1])

    def step_copy(i, c):
        partner, bit_set, halving, size, offset = all_steps[chunks[c][0]][i]
        if halving:
            size = size // 2
            offset = offset + (1 - bit_set) * size
        at = held(c)
        return copy(2 + i, c, at[5].at[span(offset, size), :], at[6][i], {"grp": partner})

    def back_copy(i, c):
        partner, bit_set, halving, size, offset = all_steps[chunks[c][0]][i]
        size = size // 2
        offset = offset + bit_set * size
        at = held(c)[7].at[span(offset, size), :]
        return copy(2 + count + i, c, at, at, {"grp": partner})

    def begin(c):
        which, place, left, right, out, start = chunks[c]
        quarter = quarters[which]
        send1, recv1, own1 = held(c)[:3]

        def part(q):
            if left is None:
                return bundle[q]
            value = jnp.dot(
                left[span(q * quarter, quarter), :],
                right[:, start : start + widths],
                preferred_element_type=wide,
            )
            return (value * share_ref[0]).astype(low)

        for y in range(2):
            send1[y] = part(2 * y + 1 - core)
        core_copy(c).start()
        for y in range(2):
            own1[y] = part(2 * y + core)

    def after_core(c):
        send1, recv1, own1, send2 = held(c)[:4]
        core_copy(c).wait()
        value = own1[1 - far].astype(wide) + recv1[1 - far].astype(wide)
        send2[...] = value.astype(low)
        far_copy(c).start()

    def after_far(c):
        send1, recv1, own1, send2, recv2, hold = held(c)[:6]
        far_copy(c).wait()
        value = own1[far].astype(wide) + recv1[far].astype(wide) + recv2[...].astype(wide)
        hold[...] = value.astype(low)
        step_copy(0, c).start()

    def after_step(i, c):
        step_copy(i, c).wait()
        hold, halves, done = held(c)[5:]
        steps, halvings = all_steps[chunks[c][0]], all_halvings[chunks[c][0]]
        partner, bit_set, halving, size, offset = steps[i]
        if halving:
            size = size // 2
            offset = offset + bit_set * size
        at = span(offset, size)
        value = hold[at, :].astype(wide) + halves[i][...].astype(wide)
        if i + 1 < count:
            hold[at, :] = value.astype(low)
            step_copy(i + 1, c).start()
        else:
            done[at, :] = value.astype(low)
            back_copy(halvings[-1], c).start()

    def after_back(k, c):
        halvings = all_halvings[chunks[c][0]]
        if k >= len(halvings):
            return
        back_copy(halvings[k], c).wait()
        if k > 0:
            back_copy(halvings[k - 1], c).start()
        elif chunks[c][0] == 0:
            full[me] = held(c)[7][...]
            bundle_core().start()

    def bundle_core():
        at = full.at[me]
        return remote(at, at, last_send.at[0], last_recv.at[0], others[0])

    def bundle_far():
        at = full.at[pl.ds(me - core, 2)]
        return remote(at, at, last_send.at[1], last_recv.at[1], others[1])

    def query_copy(kind):
        return remote(
            query_part,
            query_got.at[kind],
            last_send.at[2 + kind],
            last_recv.at[2 + kind],
            others[kind],
        )

    size = own_columns.shape[0]
    width = key_w.shape[1]
    part_rows = quarters[0]
    spare = extra_out.shape[0] // 4
    per_row = width // size
    scale = head_dim ** (-0.5)

    def coefficients():
        rows = []
        for n in range(HEADS):
            place, column = n // per_row, (n % per_row) * size
            shard, row = place // spare, part_rows - spare + place % spare
            rows.append(full[shard, row : row + 1, column : column + size].astype(wide))
        return jnp.concatenate(rows, axis=0)

    def own_head(value):
        lane = lax.broadcasted_iota(jnp.int32, (HEADS, width), 1)
        head = lax.broadcasted_iota(jnp.int32, (HEADS, width), 0)
        return jnp.where(lane // head_dim == head, value, 0.0)

    def key_grad(coeffs):
        return jnp.dot(coeffs.astype(low), own_columns[...], preferred_element_type=wide)

    def finish_core():
        bundle_core().wait()
        bundle_far().start()

    def finish_far():
        bundle_far().wait()
        spread = jnp.dot(
            key_grad(coefficients()).astype(low), key_w[...], preferred_element_type=wide
        )
        partial = jnp.sum(own_head(spread), axis=0, keepdims=True) * scale
        query_part[...] = jnp.broadcast_to(partial, query_part.shape)
        for kind in range(3):
            query_copy(kind).start()

    def finish_table():
        weights(3).wait()
        table = full[...].reshape(size, width)
        value_out[...] = lax.dot_general(
            own_columns[...], table, (((0,), (0,)), ((), ())), preferred_element_type=wide
        )
        coeffs = coefficients()
        var_s[...] = lax.dot_general(
            coeffs.astype(low), keys_ref[...], (((0,), (0,)), ((), ())), preferred_element_type=wide
        )
        var_out[...] = var_s[span(me * part_rows, part_rows), :] + lax.dot_general(
            full[me], weight_s[...], (((1,), (1,)), ((), ())), preferred_element_type=wide
        )
        for q in range(4):
            extra_out[q * spare : (q + 1) * spare, :] = full[q, part_rows - spare :, :].astype(wide)

    def finish_query():
        for kind in range(3):
            query_copy(kind).wait()
        grad = query_part[...] + query_got[0] + query_got[1] + query_got[2]
        query_out[...] = own_query[...] * grad[:1]
        agg_query_out[...] = lax.dot_general(
            grad,
            query_w[...].astype(wide),
            (((1,), (1,)), ((), ())),
            preferred_element_type=wide,
            precision=exact_mode,
        )
        spread = own_head(jnp.broadcast_to(query_ref[:1].astype(low).astype(wide), (HEADS, width)))
        key_out[...] = scale * lax.dot_general(
            key_grad(coefficients()),
            spread,
            (((0,), (0,)), ((), ())),
            preferred_element_type=wide,
            precision=exact_mode,
        )

    def weights(n):
        source = full_qkv.at[:, pl.ds(n * width, width)] if n < 3 else full_value
        return pltpu.make_async_copy(source, weight_s, weight_sem.at[0])

    def entry_part(n):
        weights(n).wait()
        value = lax.dot_general(
            qkv_grad[:, n * width : (n + 1) * width],
            weight_s[...],
            (((1,), (1,)), ((), ())),
            preferred_element_type=wide,
        )
        entry_grad[...] = value if n == 0 else entry_grad[...] + value
        weights(n + 1).start()

    def norm_part():
        for fetch in fetches:
            fetch.wait()
        grad = entry_grad[...]
        xhat, inverse = normalise(embed_ref[...])
        extras[...] = jnp.zeros_like(extras)
        value = middle_grad[...] + norm_back(grad, xhat, inverse, gain_ref[...])
        value_low = value.astype(low)
        embed_grad[...] = value_low
        first = HEADS // per_row
        extras[first : first + 1, :] = jnp.sum(value_low.astype(wide), axis=0, keepdims=True)
        extras[first + 1 : first + 2, :] = jnp.sum(grad * xhat, axis=0, keepdims=True)
        extras[first + 2 : first + 3, :] = jnp.sum(grad, axis=0, keepdims=True)
        for n in range(4):
            extras[first + 3 + n : first + 4 + n, :] = vectors_ref[n : n + 1, :]
        extras[pl.ds(first + 7 + me, 1), :] = vectors_ref[4:5, :]

    def heads_part():
        heads_grad[...] = lax.dot_general(
            full_agg[...], embed_grad[...], (((1,), (1,)), ((), ())), preferred_element_type=wide
        ).astype(low)
        patch_grad[...] = jnp.zeros_like(patch_grad)
        coeff_s[...] = jnp.zeros_like(coeff_s)

    slot_count = mask_ref.shape[0]

    def one_head(h, carry):
        lane = lax.broadcasted_iota(jnp.int32, (slot_count, HEADS), 1)
        columns = head_columns(coeff_ref, h, slot_count)
        weights = slot_softmax(patch_ref, columns, mask_ref)
        mixed = mixed_of(patch_ref, weights, table_ref.shape[1])
        at = pl.ds(pl.multiple_of(h * head_dim, 16), head_dim)
        grad = heads_grad[at, :]
        table_s[at, :] = (
            lax.dot_general(grad, mixed, (((1,), (1,)), ((), ())), preferred_element_type=wide)
            * share_ref[0]
        ).astype(low)
        mixed_grad = lax.dot_general(
            table_ref[at, :], grad, (((0,), (0,)), ((), ())), preferred_element_type=wide
        )
        parts = [
            mixed_grad[k * slot_count : (k + 1) * slot_count] for k in range(PIX + 1)
        ]
        values = [patch_ref[k].astype(wide) for k in range(PIX)]
        weights_grad = parts[PIX]
        for k in range(PIX):
            weights_grad = weights_grad + parts[k] * values[k]
        mean_grad = jnp.sum(weights * weights_grad, axis=0, keepdims=True)
        scores_grad = weights * (weights_grad - mean_grad)
        for k in range(PIX + 1):
            value = scores_grad * values[k] if k < PIX else scores_grad
            column = jnp.sum(value, axis=1, keepdims=True)
            rows = slice(k * slot_count, (k + 1) * slot_count)
            coeff_s[rows, :] = coeff_s[rows, :] + jnp.where(lane == h, column, 0.0)
        for k in range(PIX):
            patch_grad[k] += share_ref[1] * (parts[k] * weights + scores_grad * columns[k])
        return carry

    def heads_from(first, last):
        lax.fori_loop(first, last, one_head, 0)

    def bundle_part():
        sums = lax.dot_general(
            select_ref[...], table_s[...], (((0,), (1,)), ((), ())), preferred_element_type=wide
        )
        coeff_sum = lax.dot_general(
            coeff_s[...],
            select_ref[...].astype(wide),
            (((0,), (0,)), ((), ())),
            preferred_element_type=wide,
            precision=exact_mode,
        )
        for n in range(HEADS):
            place, column = n // per_row, (n % per_row) * size
            extras[place : place + 1, column : column + size] = coeff_sum[n : n + 1, :]
        row = lax.broadcasted_iota(jnp.int32, (size, extras.shape[0]), 0)
        line = lax.broadcasted_iota(jnp.int32, (size, extras.shape[0]), 1)
        spot = (row // part_rows) * spare + row % part_rows - (part_rows - spare)
        chosen = (spot == line) & (row % part_rows >= part_rows - spare)
        placed = jnp.dot(
            chosen.astype(low),
            (extras[...] * share_ref[0]).astype(low),
            preferred_element_type=wide,
        )
        bundle[...] = (sums + placed).astype(low).reshape(bundle.shape)

    middle_parts = [[functools.partial(entry_part, n)] for n in range(3)]
    middle_parts += [[norm_part, heads_part]]
    some = HEADS // 4
    middle_parts += [
        [functools.partial(heads_from, 0, some)],
        [functools.partial(heads_from, some, 2 * some)],
        [functools.partial(heads_from, 2 * some, HEADS), bundle_part],
    ]

    out_copy = remote(out_sum, out_far, last_send.at[5], last_recv.at[5], others[1])
    stages = [begin, after_core, after_far]
    stages += [functools.partial(after_step, i) for i in range(count)]
    stages += [functools.partial(after_back, k) for k in reversed(range(count))]
    extra = [finish_core, finish_far, finish_table, finish_query]
    steps = max(len(chunks), small + 1 + len(extra)) + len(stages) - 1
    for t in range(steps):
        for s in [1, 0]:
            if 0 <= t - s < len(chunks):
                stages[s](t - s)
        if t == 0:
            sum_start()
        if t < len(middle_parts):
            for part in middle_parts[t]:
                part()
        for s in range(2, len(stages)):
            if 0 <= t - s < len(chunks):
                stages[s](t - s)
        if 0 <= t - small - len(stages) < len(extra):
            extra[t - small - len(stages)]()
        for s, stage in enumerate(sum_stages):
            for c in range(sum_chunks):
                if t == 1 + s + c // 2:
                    stage(c)
        if t == len(chunks):
            out_copy.start()
    out_copy.wait()
    for c in range(sum_chunks):
        sum_give(c).wait()


def finish(group_size, spare, shares, lefts, rights, columns, first_chunk, others):
    left_qkv, left_agg, left_proj = lefts
    qkv_grad, attended = rights
    width, rows = left_qkv.shape
    quarter = width // 4
    widths = 512
    low = jnp.bfloat16
    wide = jnp.float32
    size = others["own_columns"].shape[0]
    part = size // 4
    steps = 0
    while 2**steps < group_size:
        steps += 1

    def buffers(count, slots, rows, columns, last):
        halves = []
        size = rows
        for _ in range(steps):
            if size >= 32:
                size //= 2
            halves.append(pltpu.VMEM((count, size, columns), low))
        few = pltpu.VMEM((slots, 2, rows, columns), low)
        two = pltpu.VMEM((count, 2, rows, columns), low)
        one = pltpu.VMEM((count, rows, columns), low)
        semaphores = pltpu.SemaphoreType.DMA((2 + 2 * steps, count))
        found = [few, two, few, one, one, one, halves]
        return found + ([one] if last else []) + [semaphores, semaphores]

    shapes = [(quarter, qkv_grad.shape[1]), (quarter, width), (quarter, width)]
    count = sum(columns for _, columns in shapes) // widths
    scratch = buffers(1, 1, part, width, True) + buffers(count, 3, quarter, widths, False)
    scratch += [
        pltpu.VMEM((4, part, width), low),
        pltpu.VMEM((8, width), wide),
        pltpu.VMEM((3, 8, width), wide),
        pltpu.VMEM((size, width), wide),
        pltpu.SemaphoreType.DMA((6,)),
        pltpu.SemaphoreType.DMA((6,)),
        pltpu.VMEM((rows, width), wide),
        pltpu.VMEM((rows, width), low),
        pltpu.VMEM((width, rows), low),
        pltpu.VMEM((width, size), low),
        pltpu.VMEM((size, HEADS), wide),
        pltpu.VMEM((4 * spare, width), wide),
        pltpu.VMEM((4, part, width), low),
        pltpu.VMEM((width, width), low),
        pltpu.SemaphoreType.DMA((1,)),
        pltpu.VMEM((width, rows), low),
        pltpu.VMEM((width, rows), low),
        pltpu.VMEM((rows, width), low),
        pltpu.VMEM((width, width), low),
        pltpu.VMEM((rows, width), wide),
        pltpu.VMEM((rows, width), wide),
        pltpu.SemaphoreType.DMA((6,)),
    ]
    totals = others["totals"]
    left_chunks = totals.shape[1] // columns - first_chunk
    scratch += beside_buffers(group_size, left_chunks, totals.shape[0], columns)
    whole = pl.BlockSpec(memory_space=pltpu.VMEM)
    out_shape = [jax.ShapeDtypeStruct(dims, low) for dims in shapes]
    more = [(quarter, width)] * 3 + [(8, quarter), (part, width), (4 * spare, width)]
    more.append(others["patch_rows"].shape)
    out_shape += [jax.ShapeDtypeStruct(dims, wide) for dims in more]
    out_shape.append(jax.ShapeDtypeStruct(others["out_sum"].shape, low))
    out_shape.append(jax.ShapeDtypeStruct((totals.shape[0], left_chunks * columns), low))
    hbm = pl.BlockSpec(memory_space=pl.ANY)
    far_off = ("full_qkv", "full_agg", "full_value", "embedded", "middle_grad", "out_sum", "totals")
    operands = [shares, left_qkv, qkv_grad, left_agg, left_proj, attended, *others.values()]
    return pl.pallas_call(
        functools.partial(finish_kernel, group_size, widths, width // HEADS, first_chunk),
        in_specs=[pl.BlockSpec(memory_space=pltpu.SMEM), whole, whole, hbm, hbm, hbm]
        + [hbm if name in far_off else whole for name in others],
        out_specs=[whole] * (len(out_shape) - 2) + [hbm] * 2,
        out_shape=out_shape,
        scratch_shapes=scratch,
        compiler_params=pltpu.CompilerParams(
            collective_id=0, has_side_effects=True, vmem_limit_bytes=62 * 1024 * 1024
        ),
        cost_estimate=pl.CostEstimate(
            flops=20 * rows * width * width, bytes_accessed=200_000_000, transcendentals=0
        ),
        name="finish",
    )(*operands)


def on_device(
    patches,
    patch_counts,
    var_present,
    item_dataset,
    var_ids,
    patch_weight,
    var_embed,
    agg_query,
    query_weight,
    key_weight,
    value_weight,
    agg_proj,
    agg_bias,
    norm1_gain,
    norm1_shift,
    qkv_weight,
    proj_weight,
    proj_bias,
    norm2_gain,
    norm2_shift,
    up_weight,
    up_bias,
    down_weight,
    down_bias,
    out_grad,
):
    low = jnp.bfloat16
    wide = jnp.float32
    rows = patches.shape[2]
    me = lax.axis_index("fsdp")
    group_count = lax.axis_size("grp")
    width = proj_weight.shape[1]
    head_dim = width // HEADS
    own_width = width // 4
    own_vars = patch_weight.shape[0]

    item_count = patch_counts[0]
    own_valid = me * rows + jnp.arange(rows, dtype=jnp.int32) < item_count
    shard_valid = jnp.clip(
        item_count - (me ^ jnp.arange(4, dtype=jnp.int32)) * rows, 0, rows
    ).astype(jnp.int32)
    down_grad = jnp.where(own_valid[:, None], out_grad, jnp.zeros_like(out_grad))

    slot_vars = lax.dynamic_index_in_dim(var_ids, item_dataset[0], 0, keepdims=False)
    part_size = -(-(PIX + 1) * own_vars // 16) * 16
    size = 4 * part_size
    slot_row = jnp.arange(size, dtype=jnp.int32)
    slot_var = jnp.pad(jnp.tile(slot_vars, PIX + 1), (0, size - (PIX + 1) * VTOT))
    place = (slot_var // own_vars) * part_size + (slot_row // VTOT) * own_vars + slot_var % own_vars
    select = (
        (place[:, None] == jnp.arange(size, dtype=jnp.int32)[None, :])
        & (slot_row < (PIX + 1) * VTOT)[:, None]
    ).astype(low)
    own_table = jnp.concatenate(
        [
            patch_weight.transpose(1, 0, 2).reshape(own_vars * PIX, width),
            var_embed,
            jnp.zeros((part_size - (PIX + 1) * own_vars, width), low),
        ],
        axis=0,
    )
    own_query = lax.dynamic_slice_in_dim(agg_query, me * own_width, own_width, 0)
    patch_rows = patches.transpose(1, 0, 2)
    slot_mask = jnp.where(var_present[0] > 0, 0.0, masked_out).astype(wide)[:, None]
    (
        count_rows,
        tables,
        query_rows,
        key_query,
        full_value,
        full_agg_proj,
        full_qkv,
        full_proj,
        near_down_grad,
        far_grads,
        table_values,
        coeffs,
        heads_t,
        embedded,
        normed1,
    ) = prepare(
        group_count,
        jnp.full((8, 128), item_count.astype(wide)),
        jnp.broadcast_to(own_query[None, :], (16, own_width)),
        query_weight,
        key_weight,
        own_table,
        select,
        value_weight,
        agg_proj,
        qkv_weight,
        proj_weight,
        down_grad,
        patch_rows,
        slot_mask,
        agg_bias[None, :],
        norm1_gain[None, :],
        norm1_shift[None, :],
    )
    count_share = item_count.astype(wide) / count_rows[0, 0]
    own_columns = lax.dynamic_slice_in_dim(
        tables.reshape(size, width), me * own_width, own_width, 1
    )

    queries, key_values, context_pairs, context, logs = attend(normed1, full_qkv, shard_valid)
    (
        middle,
        out_parts,
        totals,
        middle_grad,
        attended_grad,
        context_grad,
        feed_vectors,
    ) = feed(
        count_share[None],
        context,
        full_proj,
        embedded,
        down_grad,
        near_down_grad,
        far_grads,
        up_weight,
        down_weight,
        up_bias.astype(wide)[None, :],
        proj_bias[None, :],
        norm2_gain[None, :],
        norm2_shift[None, :],
    )
    out_got = swap(jnp.stack([out_parts[1], out_parts[3]]), "fsdp", 1)
    out_sum = (out_parts[2].astype(wide) + out_got[1].astype(wide)).astype(low)

    columns = width // 8
    chunks = 11
    qkv_grad, summed = attend_back(
        group_count,
        queries,
        key_values,
        context_grad,
        context_pairs,
        logs,
        shard_valid,
        totals,
        columns,
        chunks,
    )
    down_weight_grad = summed[:, :width].astype(wide)
    spare = part_size - (PIX + 1) * own_vars
    (
        qkv_weight_grad,
        agg_proj_grad,
        proj_weight_grad,
        value_weight_grad,
        key_weight_grad,
        query_weight_grad,
        agg_query_grad,
        var_grads,
        extras,
        patch_grad,
        out_far,
        rest,
    ) = finish(
        group_count,
        spare,
        jnp.stack([count_share, group_count * count_share]),
        (normed1.T, heads_t, context.T),
        (qkv_grad, attended_grad),
        columns,
        chunks,
        dict(
            full_qkv=full_qkv,
            full_agg=full_agg_proj,
            full_value=full_value,
            embedded=embedded,
            middle_grad=middle_grad,
            gain=norm1_gain[None, :],
            vectors=feed_vectors,
            patch_rows=patch_rows,
            coeffs=coeffs,
            slot_mask=slot_mask,
            table_values=table_values,
            select=select,
            own_columns=own_columns,
            key_query=key_query,
            query_rows=query_rows,
            key_weight=key_weight,
            query_weight=query_weight,
            own_query=own_query.astype(wide)[:, None],
            out_sum=out_sum,
            totals=totals,
        ),
    )
    down_sum = out_parts[0].astype(wide) + out_got[0].astype(wide) + out_far.astype(wide)
    output = (middle + down_sum + down_bias).astype(low)
    up_weight_grad = jnp.concatenate([summed[:, width:], rest], axis=1).astype(wide)
    patches_grad = patch_grad.transpose(1, 0, 2)
    qkv_weight_grad = qkv_weight_grad.astype(wide)
    agg_proj_grad = agg_proj_grad.astype(wide)
    proj_weight_grad = proj_weight_grad.astype(wide)
    at = HEADS * size // width
    vector_total = extras[at : at + 7]
    at += 7
    up_bias_total = lax.dynamic_slice_in_dim(extras, at + me, 1, 0)[0]
    vector_own = lax.dynamic_slice_in_dim(vector_total, me * own_width, own_width, 1)
    agg_query_grad = agg_query_grad[0]
    var_grads = var_grads[: (PIX + 1) * own_vars].reshape(PIX + 1, own_vars, width)
    patch_weight_grad = var_grads[:PIX].transpose(1, 0, 2)
    var_embed_grad = var_grads[PIX]
    return (
        output,
        patches_grad,
        patch_weight_grad,
        var_embed_grad,
        agg_query_grad,
        query_weight_grad,
        key_weight_grad,
        value_weight_grad,
        agg_proj_grad,
        vector_own[0],
        vector_own[1],
        vector_own[2],
        qkv_weight_grad,
        proj_weight_grad,
        vector_own[5],
        vector_own[3],
        vector_own[4],
        up_weight_grad,
        up_bias_total,
        down_weight_grad,
        vector_own[6],
    )


def solution(mesh):
    shard = P("fsdp")
    shard_rows = P("fsdp", None)
    return jax.shard_map(
        on_device,
        mesh=mesh,
        in_specs=(
            P(None, None, ("grp", "fsdp")),
            P("grp"),
            P("grp", None),
            P("grp"),
            P(),
            P("fsdp", None, None),
            shard_rows,
            P(),
            shard_rows,
            shard_rows,
            shard_rows,
            shard_rows,
            P(),
            P(),
            P(),
            shard_rows,
            shard_rows,
            P(),
            P(),
            P(),
            P(None, "fsdp"),
            shard,
            shard_rows,
            P(),
            P(("grp", "fsdp"), None),
        ),
        out_specs=(
            P(("grp", "fsdp"), None),
            P(None, None, ("grp", "fsdp")),
            P("fsdp", None, None),
            shard_rows,
            shard,
            shard_rows,
            shard_rows,
            shard_rows,
            shard_rows,
            shard,
            shard,
            shard,
            shard_rows,
            shard_rows,
            shard,
            shard,
            shard,
            P(None, "fsdp"),
            shard,
            shard_rows,
            shard,
        ),
        check_vma=False,
    )
```
